32 devices in a mesh: src: 4 (over x, core), tgt: 8 (over z, y).
Axes of the slice: x: 2, y: 2, z: 4, core: 2. Of those that a mesh axis runs over, the one named last changes fastest.
Arguments:
- source_fields: float32 [7, 131072], P(None, ('src', 'tgt'))
- slot_source: int32 [524288], P(('src', 'tgt')), may hold values from 0 to 4095
- slot_weight: float32 [524288], P(('src', 'tgt')), may hold values from 0.05 to 1
- slot_target: int32 [524288], P(('src', 'tgt')), may hold values from -1 to 8191, as said below
- cell_mass: float32 [16, 128, 128], P('src', 'tgt'), may hold values from 0.5 to 2
- send_order: int32 [32, 8192], P(('src', 'tgt')), may hold values from 0 to 8191, each once within a row
- place_order: int32 [32, 8192], P(('src', 'tgt')), may hold values from 0 to 8191, each once within a row
Outputs:
- projected: float32 [7, 16, 128, 128], P(None, 'src', 'tgt')
- moduli: float32 [3, 262144], P(None, ('src', 'tgt'))
The draws below stay inside these ranges and needn't reach their ends.
Inputs may be any that keep to these rules, and one draw needn't show every extreme that they name: `slot_target`: within each sending partition's block of 512 slots at an owner, the live slots come first and there are 128 or more of them; some owner has all 512 slots live from every sender.
All inputs are finite; a program needn't handle non-finite values.
Results may differ from the reference program's by a relative error of at most 0.00007.
Values sent between devices are 32-bit elements; how exact they have to be, the bound alone decides.
No kernel may reach another device: no remote copies, remote signals or barrier semaphores. Data moves between devices by JAX's collectives and lax.ppermute only.
A program may use at most 64 MiB of HBM per device.

```python
import math
import jax
import jax.numpy as jnp
from jax import lax

HX = 4
HY = 16
HZ = 128
SC = 4096
CAP = 512
ITERS = 4
OWNERS = 32
TC = 8192
NX = 16
NY = 128
NZ = 128
CELLS = 262144
NSRC = 131072
SLOTS = 524288
N_SRC = 4
N_TGT = 8


def draw_source_fields(key, part):
    key = jax.random.fold_in(key, 5)
    k_poro, k_stress = jax.random.split(key, 2)
    poro = jax.random.uniform(k_poro, (1, NSRC), jnp.float32, 0.02, 0.3)
    stress = jax.random.normal(k_stress, (6, NSRC), jnp.float32)
    return jnp.concatenate([poro, stress], axis=0)


def draw_slot_target(key, part):
    key = jax.random.fold_in(key, 2)
    k_count, k_full, k_cell = jax.random.split(key, 3)
    counts = jax.random.randint(k_count, (OWNERS, OWNERS), CAP // 4, CAP + 1)
    full = jax.random.randint(k_full, (), 0, OWNERS)
    owner = jnp.arange(OWNERS, dtype=jnp.int32)[:, None]
    counts = jnp.where(owner == full, CAP, counts)
    cells = jax.random.randint(k_cell, (OWNERS, OWNERS, CAP), 0, TC)
    live = jnp.arange(CAP, dtype=jnp.int32)[None, None, :] < counts[:, :, None]
    return jnp.where(live, cells, -1).astype(jnp.int32).reshape(SLOTS)


def place_ends(result, key, least, high):
    shape = result.shape
    index_at = [jax.random.randint(jax.random.fold_in(key, axis), (), 0, shape[axis]) for axis in range(len(shape))]
    result = result.at[tuple(index_at)].set(least)
    longest = shape.index(max(shape))
    index_at[longest] = (index_at[longest] + 1) % shape[longest]
    return result.at[tuple(index_at)].set(high)


def block_scale(own_key, extent, pieces, least, largest):
    factor_of, own = 1.0, jax.random.fold_in(own_key, 6)
    for axis_at, blocks in pieces:
        steps = jnp.exp(jax.random.uniform(jax.random.fold_in(own, axis_at), (blocks,), jnp.float32, least / len(pieces), largest / len(pieces)))
        factor_of = factor_of * jnp.repeat(steps, extent[axis_at] // blocks).reshape([-1 if axis == axis_at else 1 for axis in range(len(extent))])
    return factor_of


def setup_inputs(seed: int = 0) -> dict:
    key_list = jax.random.split(jax.random.key(seed), 8)
    source_fields = draw_source_fields(jax.random.fold_in(key_list[7], 71), 0)
    slot_source = place_ends(jax.random.randint(key_list[1], (SLOTS,), 0, SC), jax.random.fold_in(key_list[1], 1), 0, SC - 1).astype(jnp.int32)
    slot_weight = jnp.clip(jnp.exp(math.log(1.0) - 2.9957323 * jax.random.uniform(key_list[2], (SLOTS,), jnp.float32) ** block_scale(key_list[2], (SLOTS,), ((0, 32),), -0.2, 0.2)), 0.05, 1.0)
    slot_target = draw_slot_target(jax.random.fold_in(key_list[7], 71), 0)
    cell_mass = jnp.clip(jnp.exp(math.log(2.0) - 1.3862944 * jax.random.uniform(key_list[4], (NX, NY, NZ), jnp.float32) ** block_scale(key_list[4], (NX, NY, NZ), ((0, 4), (1, 8)), -0.2, 0.2)), 0.5, 2.0)
    send_order = jax.vmap(lambda own: jax.random.permutation(own, TC))(jax.random.split(key_list[5], OWNERS)).reshape((OWNERS, TC)).astype(jnp.int32)
    place_order = jax.vmap(lambda own: jax.random.permutation(own, TC))(jax.random.split(key_list[6], OWNERS)).reshape((OWNERS, TC)).astype(jnp.int32)
    return {"source_fields": source_fields, "slot_source": slot_source, "slot_weight": slot_weight, "slot_target": slot_target, "cell_mass": cell_mass, "send_order": send_order, "place_order": place_order}


def mass_apply(field, root):
    w = root[None] * field
    p = jnp.pad(w, ((0, 0), (1, 1), (1, 1), (1, 1)))
    nb = p[:, 2:, 1:-1, 1:-1] + p[:, :-2, 1:-1, 1:-1]
    nb = nb + p[:, 1:-1, 2:, 1:-1] + p[:, 1:-1, :-2, 1:-1]
    nb = nb + p[:, 1:-1, 1:-1, 2:] + p[:, 1:-1, 1:-1, :-2]
    return root[None] * (w + 0.125 * nb)

def cell_moduli(vals):
    phi = vals[0]
    mean = (vals[1] + vals[2] + vals[3]) / 3.0
    q2 = 1.5 * ((vals[1] - mean) ** 2 + (vals[2] - mean) ** 2 + (vals[3] - mean) ** 2 + 2.0 * (vals[4] ** 2 + vals[5] ** 2 + vals[6] ** 2))
    bulk = 1.6 * jnp.exp(-3.0 * phi) * (1.0 + 0.25 * jnp.tanh(mean))
    shear = 0.9 * jnp.exp(-2.0 * phi) / (1.0 + q2 / 0.5)
    soften = shear * q2 / (0.5 + q2)
    return jnp.stack([bulk, shear, soften])

def reference(source_fields, slot_source, slot_weight, slot_target, cell_mass, send_order, place_order):
    fields_by = source_fields.reshape(7, OWNERS, SC).transpose(1, 0, 2)
    src_idx = slot_source.reshape(OWNERS, OWNERS * CAP)
    weights = slot_weight.reshape(OWNERS, OWNERS * CAP)
    tgt = slot_target.reshape(OWNERS, OWNERS, CAP).transpose(1, 0, 2)
    dest = jnp.arange(OWNERS, dtype=jnp.int32)[None, :, None]
    glob = jnp.where(tgt >= 0, dest * TC + tgt, CELLS).astype(jnp.int32).reshape(OWNERS, OWNERS * CAP)

    def add_sender(carry, inputs):
        fld, sidx, wgt, gidx = inputs
        vals = wgt[None, :] * jnp.take(fld, sidx, axis=1)
        return (carry.at[:, gidx].add(vals), None)
    start = jnp.zeros((7, CELLS + 1), jnp.float32)
    total, _ = lax.scan(add_sender, start, (fields_by, src_idx, weights, glob))
    local = total[:, :CELLS].reshape(7, N_SRC, N_TGT, HX, HY, HZ)
    rhs = local.transpose(0, 1, 3, 2, 4, 5).reshape(7, NX, NY, NZ)
    root = jnp.sqrt(cell_mass)
    theta = 1.0
    delta = 0.75
    sigma = theta / delta
    rho = 1.0 / sigma
    x = jnp.zeros_like(rhs)
    r = rhs
    d = r / (theta * cell_mass[None])
    for sweep in range(ITERS):
        image = mass_apply(d, root)
        x = x + d
        r = r - image
        rho_new = 1.0 / (2.0 * sigma - rho)
        d = rho_new * rho * d + 2.0 * rho_new / delta * r / cell_mass[None]
        rho = rho_new
    projected = x + d
    flat = projected.reshape(7, N_SRC, HX, N_TGT, HY, HZ).transpose(0, 1, 3, 2, 4, 5).reshape(7, OWNERS, TC)
    mods = cell_moduli(flat)
    sent = jnp.take_along_axis(mods, send_order[None], axis=2)
    quota = TC // OWNERS
    arrived = sent.reshape(3, OWNERS, OWNERS, quota).transpose(0, 2, 1, 3).reshape(3, OWNERS, TC)
    placed = jnp.take_along_axis(arrived, place_order[None], axis=2)
    return (projected, placed.reshape(3, CELLS))
```

```python
import numpy as np

import jax
import jax.numpy as jnp
from jax import lax
from jax.experimental import pallas as pl
from jax.experimental.pallas import tpu as pltpu
from jax.sharding import PartitionSpec as P

ITERS = 4
FIELDS = 7
WIDE = 256
BF16 = jnp.bfloat16
F32 = jnp.float32
NT = (((1,), (1,)), ((), ()))


def sweep_polynomial(iters, theta, delta):
    sigma = theta / delta
    rho = 1.0 / sigma
    mass = np.array([1.0, 0.125])
    poly = np.polynomial.polynomial
    resid = np.array([1.0])
    step = resid / theta
    total = np.array([0.0])
    for _ in range(iters):
        total = poly.polyadd(total, step)
        resid = poly.polysub(resid, poly.polymul(mass, step))
        rho_new = 1.0 / (2.0 * sigma - rho)
        step = poly.polyadd(rho_new * rho * step, 2.0 * rho_new / delta * resid)
        rho = rho_new
    return [float(c) for c in poly.polyadd(total, step)]


COEFS = sweep_polynomial(ITERS, 1.0, 0.75)


def halves(x):
    high = x.astype(BF16)
    return high, (x - high.astype(F32)).astype(BF16)


def log2(n):
    assert n & (n - 1) == 0
    return n.bit_length() - 1


def row_ids(rows, lanes):
    return lax.broadcasted_iota(jnp.int32, (rows, lanes), 0)


def low_onehot(low, ids):
    return jnp.where(ids == low.astype(F32).astype(BF16), jnp.ones((), BF16), jnp.zeros((), BF16))


def gather_kernel(fields_ref, index_ref, weight_ref, out_ref, table):
    owners, tiles, _, lanes = out_ref.shape
    span = tiles * lanes
    groups = fields_ref.shape[1] // WIDE
    table[...] = jnp.zeros_like(table)
    for g in range(groups):
        table[g * 8 : g * 8 + FIELDS, :] = fields_ref[:, g * WIDE : (g + 1) * WIDE]
    high, low = halves(table[...])
    both = jnp.concatenate([high, low], axis=0)
    ids = row_ids(WIDE, span).astype(F32).astype(BF16)
    rows = groups * 8

    @pl.loop(0, owners)
    def _(q):
        at = pl.multiple_of(q * span, span)
        index = index_ref[:, pl.ds(at, span)]
        weight = weight_ref[:, pl.ds(at, span)]
        onehot = low_onehot(index & (WIDE - 1), ids)
        got = jnp.dot(both, onehot, preferred_element_type=F32)
        group = jnp.broadcast_to(index >> log2(WIDE), (8, span))
        value = jnp.zeros((8, span), F32)
        for g in range(groups):
            part = got[g * 8 : (g + 1) * 8] + got[rows + g * 8 : rows + (g + 1) * 8]
            value = jnp.where(group == g, part, value)
        value = value * weight
        for t in range(tiles):
            out_ref[q, t] = value[:, t * lanes : (t + 1) * lanes]


def gather_call(fields, index, weight, owners):
    tiles = index.shape[1] // owners // 128
    return pl.pallas_call(
        gather_kernel,
        out_shape=jax.ShapeDtypeStruct((owners, tiles, 8, 128), F32),
        in_specs=[pl.BlockSpec(memory_space=pltpu.VMEM)] * 3,
        out_specs=pl.BlockSpec(memory_space=pltpu.VMEM),
        scratch_shapes=[pltpu.VMEM((fields.shape[1] // WIDE * 8, WIDE), F32)],
        compiler_params=pltpu.CompilerParams(vmem_limit_bytes=40 << 20),
    )(fields, index, weight)


def scatter_kernel(value_ref, target_ref, mass_ref, v_ref, first_ref, last_ref, total):
    owners, tiles, _, lanes = value_ref.shape
    span = tiles * lanes
    hx, hy, hz = mass_ref.shape
    groups = hx * hy * hz // WIDE
    total[...] = jnp.zeros_like(total)
    ids = row_ids(WIDE, span).astype(F32).astype(BF16)
    group_ids = row_ids(groups, span).astype(F32).astype(BF16)

    @pl.loop(0, owners)
    def _(p):
        at = pl.multiple_of(p * span, span)
        target = target_ref[:, pl.ds(at, span)]
        low = ((target >> log2(groups * hz)) << log2(hz)) + (target & (hz - 1))
        onehot = low_onehot(jnp.where(target < 0, -1, low), ids)
        group = ((target >> log2(hz)) & (groups - 1)).astype(F32).astype(BF16)
        here = group_ids == group
        value = jnp.concatenate([value_ref[p, t] for t in range(tiles)], axis=1)
        parts = []
        for half in halves(value):
            for f in range(FIELDS):
                parts.append(jnp.where(here, half[f : f + 1], jnp.zeros((), BF16)))
        spread = jnp.concatenate(parts, axis=0)
        total[...] += lax.dot_general(spread, onehot, NT, preferred_element_type=F32)

    scale = lax.rsqrt(mass_ref[...])
    half_x = hx // 2
    for f in range(FIELDS):
        s = total[f * groups : (f + 1) * groups] + total[(FIELDS + f) * groups : (FIELDS + f + 1) * groups]
        for b in range(2):
            for x in range(half_x):
                at = b * half_x + x
                v = s[x * hy : (x + 1) * hy, b * hz : (b + 1) * hz] * scale[at]
                v_ref[f, at] = v
                first_ref[f, at] = v[:ITERS]
                last_ref[f, at] = v[hy - ITERS :]


def scatter_call(values, target, mass):
    hx, hy, hz = mass.shape
    groups = hx * hy * hz // WIDE
    side = jax.ShapeDtypeStruct((FIELDS, hx, ITERS, hz), F32)
    return pl.pallas_call(
        scatter_kernel,
        out_shape=(jax.ShapeDtypeStruct((FIELDS, hx, hy, hz), F32), side, side),
        in_specs=[pl.BlockSpec(memory_space=pltpu.VMEM)] * 3,
        out_specs=(pl.BlockSpec(memory_space=pltpu.VMEM),) * 3,
        scratch_shapes=[pltpu.VMEM((2 * FIELDS * groups, WIDE), F32)],
        compiler_params=pltpu.CompilerParams(vmem_limit_bytes=40 << 20),
    )(values, target, mass)


def lookup_rows(table, index, ids, group_ids, groups, at_parts):
    group, low = at_parts(index)
    got = jnp.dot(table, low_onehot(low, ids), preferred_element_type=F32)
    here = group_ids == group
    rows = 3 * groups
    out = []
    for m in range(3):
        part = got[m * groups : (m + 1) * groups] + got[rows + m * groups : rows + (m + 1) * groups]
        out.append(jnp.sum(jnp.where(here, part, 0.0), axis=0, keepdims=True))
    return out


def cell_moduli(vals):
    phi = vals[0]
    mean = (vals[1] + vals[2] + vals[3]) / 3.0
    q2 = 1.5 * (
        (vals[1] - mean) ** 2
        + (vals[2] - mean) ** 2
        + (vals[3] - mean) ** 2
        + 2.0 * (vals[4] ** 2 + vals[5] ** 2 + vals[6] ** 2)
    )
    bulk = 1.6 * jnp.exp(-3.0 * phi) * (1.0 + 0.25 * jnp.tanh(mean))
    shear = 0.9 * jnp.exp(-2.0 * phi) / (1.0 + q2 / 0.5)
    soften = shear * q2 / (0.5 + q2)
    return [bulk, shear, soften]


def solve_kernel(
    mesh_shape, v_ref, xl_ref, xr_ref, yl_ref, yr_ref, ll_ref, lr_ref, rl_ref, rr_ref, mass_ref, order_ref,
    projected_ref, out_ref, wide,
):
    n_src, n_tgt = mesh_shape
    hx, hy, hz = mass_ref.shape
    k = ITERS
    rows = hy + 2 * k
    a, b = lax.axis_index("src"), lax.axis_index("tgt")
    wide[...] = jnp.zeros_like(wide)
    for f in range(FIELDS):
        for x in range(hx):
            wide[f, k + x, :hy] = v_ref[f, x]
            wide[f, k + x, hy : hy + k] = yr_ref[f, x]
            wide[f, k + x, hy + k :] = yl_ref[f, x]
        for x in range(k):
            wide[f, x, :hy] = xl_ref[f, hx - k + x]
            wide[f, k + hx + x, :hy] = xr_ref[f, x]
        for x in range(k - 1):
            wide[f, 1 + x, hy + k :] = ll_ref[f, x]
            wide[f, 1 + x, hy : hy + k] = lr_ref[f, x]
            wide[f, k + hx + x, hy + k :] = rl_ref[f, x]
            wide[f, k + hx + x, hy : hy + k] = rr_ref[f, x]

    def exists(flag):
        return jnp.where(flag, 1.0, 0.0).astype(F32)

    row = row_ids(rows, hz)
    lane = lax.broadcasted_iota(jnp.int32, (rows, hz), 1)
    inside = jnp.where(row < hy, 1.0, jnp.where(row < hy + k, exists(b < n_tgt - 1), exists(b > 0)))
    inside_left = inside * exists(a > 0)
    inside_right = inside * exists(a < n_src - 1)
    not_first = jnp.where(lane == 0, 0.0, 1.0)
    not_last = jnp.where(lane == hz - 1, 0.0, 1.0)
    scale = lax.rsqrt(mass_ref[...])

    @pl.loop(0, FIELDS)
    def _(f):
        base = [wide[f, x] for x in range(hx + 2 * k)]
        u = [COEFS[k] * e for e in base]
        for sweep in range(1, k + 1):
            new = list(u)
            for x in range(sweep, hx + 2 * k - sweep):
                w = u[x]
                near = u[x - 1] + u[x + 1]
                near = near + pltpu.roll(w, 1, 0) + pltpu.roll(w, rows - 1, 0)
                near = near + pltpu.roll(w, 1, 1) * not_first + pltpu.roll(w, hz - 1, 1) * not_last
                if x < k:
                    near = near * inside_left
                elif x < k + hx:
                    near = near * inside
                else:
                    near = near * inside_right
                new[x] = COEFS[k - sweep] * base[x] + near
            u = new
        for x in range(hx):
            projected_ref[f, x] = u[k + x][:hy] * scale[x]

    groups = hx * hy * hz // WIDE
    payload = cell_moduli([projected_ref[f].reshape(hx * hy, hz) for f in range(FIELDS)])
    table = jnp.concatenate([jnp.concatenate([m[:groups], m[groups:]], axis=1) for m in payload], axis=0)
    table = jnp.concatenate(halves(table), axis=0)
    ids = row_ids(WIDE, WIDE).astype(F32).astype(BF16)
    group_ids = row_ids(groups, WIDE)

    def at_parts(index):
        return (index >> log2(hz)) & (groups - 1), ((index >> log2(groups * hz)) << log2(hz)) + (index & (hz - 1))

    @pl.loop(0, out_ref.shape[0])
    def _(q):
        index = order_ref[:, pl.ds(pl.multiple_of(q * WIDE, WIDE), WIDE)]
        got = lookup_rows(table, index, ids, group_ids, groups, at_parts)
        lines = [line[:, c * 128 : (c + 1) * 128] for line in got for c in range(2)]
        out_ref[q] = jnp.concatenate(lines + [jnp.zeros((2, 128), F32)], axis=0)


def solve_call(mesh_shape, v, halos, mass, order):
    hx, hy, hz = mass.shape

    def kernel(*refs):
        solve_kernel(mesh_shape, *refs)

    return pl.pallas_call(
        kernel,
        out_shape=(
            jax.ShapeDtypeStruct((FIELDS, hx, hy, hz), F32),
            jax.ShapeDtypeStruct((order.shape[1] // WIDE, 8, 128), F32),
        ),
        in_specs=[pl.BlockSpec(memory_space=pltpu.VMEM)] * 11,
        out_specs=(pl.BlockSpec(memory_space=pltpu.VMEM),) * 2,
        scratch_shapes=[pltpu.VMEM((FIELDS, hx + 2 * ITERS, hy + 2 * ITERS, hz), F32)],
        compiler_params=pltpu.CompilerParams(vmem_limit_bytes=40 << 20),
    )(v, *halos, mass, order)


def place_kernel(arrived_ref, order_ref, out_ref, lines):
    groups = arrived_ref.shape[0]
    lines[...] = arrived_ref[...].reshape(groups * 8, 128)
    table = jnp.concatenate(
        [
            jnp.concatenate([lines[pl.ds(2 * m + c, groups, stride=8), :] for c in range(2)], axis=1)
            for m in range(3)
        ],
        axis=0,
    )
    table = jnp.concatenate(halves(table), axis=0)
    ids = row_ids(WIDE, WIDE).astype(F32).astype(BF16)
    group_ids = row_ids(groups, WIDE)

    @pl.loop(0, groups)
    def _(q):
        at = pl.ds(pl.multiple_of(q * WIDE, WIDE), WIDE)
        got = lookup_rows(
            table, order_ref[:, at], ids, group_ids, groups, lambda index: (index >> log2(WIDE), index & (WIDE - 1))
        )
        out_ref[:, at] = jnp.concatenate(got, axis=0)


def place_call(arrived, order):
    return pl.pallas_call(
        place_kernel,
        out_shape=jax.ShapeDtypeStruct((3, order.shape[1]), F32),
        in_specs=[pl.BlockSpec(memory_space=pltpu.VMEM)] * 2,
        out_specs=pl.BlockSpec(memory_space=pltpu.VMEM),
        scratch_shapes=[pltpu.VMEM((arrived.shape[0] * 8, 128), F32)],
        compiler_params=pltpu.CompilerParams(vmem_limit_bytes=40 << 20),
    )(arrived, order)


def neighbours(n_src, n_tgt, da, db):
    pairs = []
    for a in range(n_src):
        for b in range(n_tgt):
            if 0 <= a + da < n_src and 0 <= b + db < n_tgt:
                pairs.append(((a + da) * n_tgt + b + db, a * n_tgt + b))
    return pairs


def on_device(source_fields, slot_source, slot_weight, slot_target, cell_mass, send_order, place_order):
    n_src, n_tgt = lax.axis_size("src"), lax.axis_size("tgt")
    both = ("src", "tgt")
    owners = n_src * n_tgt
    cells = cell_mass.size
    quota = cells // owners

    values = gather_call(source_fields, slot_source.reshape(1, -1), slot_weight.reshape(1, -1), owners)
    values = lax.all_to_all(values, both, split_axis=0, concat_axis=0, tiled=True)
    v, first, last = scatter_call(values, slot_target.reshape(1, -1), cell_mass)

    def bring(x, da, db):
        return lax.ppermute(x, both, neighbours(n_src, n_tgt, da, db))

    hx = cell_mass.shape[0]
    halos = (
        bring(v, -1, 0),
        bring(v, 1, 0),
        bring(last, 0, -1),
        bring(first, 0, 1),
        bring(last[:, hx - ITERS + 1 :], -1, -1),
        bring(first[:, hx - ITERS + 1 :], -1, 1),
        bring(last[:, : ITERS - 1], 1, -1),
        bring(first[:, : ITERS - 1], 1, 1),
    )
    projected, outgoing = solve_call((n_src, n_tgt), v, halos, cell_mass, send_order)

    if quota == WIDE:
        incoming = lax.all_to_all(outgoing, both, split_axis=0, concat_axis=0, tiled=True)
    else:
        groups = cells // WIDE
        flat = outgoing[:, :6].reshape(groups, 3, WIDE).transpose(1, 0, 2).reshape(3, owners, quota)
        flat = lax.all_to_all(flat, both, split_axis=1, concat_axis=1, tiled=True)
        flat = flat.reshape(3, groups, WIDE).transpose(1, 0, 2).reshape(groups, 6, 128)
        incoming = jnp.pad(flat, ((0, 0), (0, 2), (0, 0)))
    return projected, place_call(incoming, place_order)


def solution(mesh):
    split = P(("src", "tgt"))
    rows = P(("src", "tgt"), None)
    return jax.shard_map(
        on_device,
        mesh=mesh,
        in_specs=(P(None, ("src", "tgt")), split, split, split, P("src", "tgt", None), rows, rows),
        out_specs=(P(None, "src", "tgt", None), P(None, ("src", "tgt"))),
        check_vma=False,
    )
```

```python
import numpy as np

import jax
import jax.numpy as jnp
from jax import lax
from jax.experimental import pallas as pl
from jax.experimental.pallas import tpu as pltpu
from jax.sharding import PartitionSpec as P

ITERS = 4
FIELDS = 7
TOGETHER = 4
WIDE = 256
BF16 = jnp.bfloat16
F32 = jnp.float32
NT = (((1,), (1,)), ((), ()))


def sweep_polynomial(iters, theta, delta):
    sigma = theta / delta
    rho = 1.0 / sigma
    mass = np.array([1.0, 0.125])
    poly = np.polynomial.polynomial
    resid = np.array([1.0])
    step = resid / theta
    total = np.array([0.0])
    for _ in range(iters):
        total = poly.polyadd(total, step)
        resid = poly.polysub(resid, poly.polymul(mass, step))
        rho_new = 1.0 / (2.0 * sigma - rho)
        step = poly.polyadd(rho_new * rho * step, 2.0 * rho_new / delta * resid)
        rho = rho_new
    return [float(c) for c in poly.polyadd(total, step)]


COEFS = sweep_polynomial(ITERS, 1.0, 0.75)


def halves(x):
    high = x.astype(BF16)
    return high, (x - high.astype(F32)).astype(BF16)


def log2(n):
    assert n & (n - 1) == 0
    return n.bit_length() - 1


def row_ids(rows, lanes):
    return lax.broadcasted_iota(jnp.int32, (rows, lanes), 0)


def low_onehot(low, ids):
    return jnp.where(ids == low.astype(F32).astype(BF16), jnp.ones((), BF16), jnp.zeros((), BF16))


def gather_kernel(fields_hbm, index_hbm, weight_hbm, out_ref, table, fields_ref, index_ref, weight_ref, sems):
    pairs = ((fields_hbm, fields_ref), (index_hbm, index_ref), (weight_hbm, weight_ref))
    copies = [pltpu.make_async_copy(src, dst, sems.at[i]) for i, (src, dst) in enumerate(pairs)]
    for copy in copies:
        copy.start()
    owners, tiles, _, lanes = out_ref.shape
    span = tiles * lanes
    groups = fields_ref.shape[1] // WIDE
    table[...] = jnp.zeros_like(table)
    for copy in copies:
        copy.wait()
    for g in range(groups):
        table[g * 8 : g * 8 + FIELDS, :] = fields_ref[:, g * WIDE : (g + 1) * WIDE]
    high, low = halves(table[...])
    both = jnp.concatenate([high, low], axis=0)
    ids = row_ids(WIDE, span).astype(F32).astype(BF16)
    rows = groups * 8

    @pl.loop(0, owners, unroll=8)
    def _(q):
        at = pl.multiple_of(q * span, span)
        index = index_ref[:, pl.ds(at, span)]
        weight = weight_ref[:, pl.ds(at, span)]
        onehot = low_onehot(index & (WIDE - 1), ids)
        got = jnp.dot(both, onehot, preferred_element_type=F32)
        group = jnp.broadcast_to(index >> log2(WIDE), (8, span))
        value = jnp.zeros((8, span), F32)
        for g in range(groups):
            part = got[g * 8 : (g + 1) * 8] + got[rows + g * 8 : rows + (g + 1) * 8]
            value = jnp.where(group == g, part, value)
        value = value * weight
        for t in range(tiles):
            out_ref[q, t] = value[:, t * lanes : (t + 1) * lanes]


def gather_call(fields, index, weight, owners):
    tiles = index.shape[1] // owners // 128
    return pl.pallas_call(
        gather_kernel,
        out_shape=jax.ShapeDtypeStruct((owners, tiles, 8, 128), F32),
        in_specs=[pl.BlockSpec(memory_space=pltpu.HBM)] * 3,
        out_specs=pl.BlockSpec(memory_space=pltpu.VMEM),
        scratch_shapes=[
            pltpu.VMEM((fields.shape[1] // WIDE * 8, WIDE), F32),
            pltpu.VMEM(fields.shape, F32),
            pltpu.VMEM(index.shape, jnp.int32),
            pltpu.VMEM(weight.shape, F32),
            pltpu.SemaphoreType.DMA((3,)),
        ],
        compiler_params=pltpu.CompilerParams(vmem_limit_bytes=40 << 20),
    )(fields, index, weight)


def scatter_kernel(value_ref, target_ref, mass_ref, v_ref, even_ref, odd_ref, total):
    owners, tiles, _, lanes = value_ref.shape
    span = TOGETHER * tiles * lanes
    hx, hy, hz = mass_ref.shape
    groups = hx * hy * hz // WIDE
    total[...] = jnp.zeros_like(total)
    ids = row_ids(WIDE, span).astype(F32).astype(BF16)
    group_ids = row_ids(groups, span).astype(F32).astype(BF16)

    @pl.loop(0, owners // TOGETHER)
    def _(p):
        at = pl.multiple_of(p * span, span)
        target = target_ref[:, pl.ds(at, span)]
        low = ((target >> log2(groups * hz)) << log2(hz)) + (target & (hz - 1))
        onehot = low_onehot(jnp.where(target < 0, -1, low), ids)
        group = ((target >> log2(hz)) & (groups - 1)).astype(F32).astype(BF16)
        here = group_ids == group
        value = jnp.concatenate([value_ref[p * TOGETHER + i, t] for i in range(TOGETHER) for t in range(tiles)], axis=1)
        parts = []
        for half in halves(value):
            for f in range(FIELDS):
                parts.append(jnp.where(here, half[f : f + 1], jnp.zeros((), BF16)))
        spread = jnp.concatenate(parts, axis=0)
        total[...] += lax.dot_general(spread, onehot, NT, preferred_element_type=F32)

    scale = lax.rsqrt(mass_ref[...])
    half_x = hx // 2
    odd = lax.axis_index("tgt") % 2 == 1
    for f in range(FIELDS):
        s = total[f * groups : (f + 1) * groups] + total[(FIELDS + f) * groups : (FIELDS + f + 1) * groups]
        for b in range(2):
            for x in range(half_x):
                at = b * half_x + x
                v = s[x * hy : (x + 1) * hy, b * hz : (b + 1) * hz] * scale[at]
                v_ref[f, at] = v
                first, last = v[:ITERS], v[hy - ITERS :]
                even_ref[f, at] = jnp.where(odd, first, last)
                odd_ref[f, at] = jnp.where(odd, last, first)


def scatter_call(values, target, mass):
    hx, hy, hz = mass.shape
    groups = hx * hy * hz // WIDE
    side = jax.ShapeDtypeStruct((FIELDS, hx, ITERS, hz), F32)
    return pl.pallas_call(
        scatter_kernel,
        out_shape=(jax.ShapeDtypeStruct((FIELDS, hx, hy, hz), F32), side, side),
        in_specs=[pl.BlockSpec(memory_space=pltpu.VMEM)] * 3,
        out_specs=(pl.BlockSpec(memory_space=pltpu.VMEM),) * 3,
        scratch_shapes=[pltpu.VMEM((2 * FIELDS * groups, WIDE), F32)],
        compiler_params=pltpu.CompilerParams(vmem_limit_bytes=40 << 20),
    )(values, target, mass)


def lookup_rows(table, index, ids, group_ids, groups, at_parts):
    group, low = at_parts(index)
    got = jnp.dot(table, low_onehot(low, ids), preferred_element_type=F32)
    here = group_ids == group
    rows = 3 * groups
    out = []
    for m in range(3):
        part = got[m * groups : (m + 1) * groups] + got[rows + m * groups : rows + (m + 1) * groups]
        out.append(jnp.sum(jnp.where(here, part, 0.0), axis=0, keepdims=True))
    return out


def cell_moduli(vals):
    phi = vals[0]
    mean = (vals[1] + vals[2] + vals[3]) / 3.0
    q2 = 1.5 * (
        (vals[1] - mean) ** 2
        + (vals[2] - mean) ** 2
        + (vals[3] - mean) ** 2
        + 2.0 * (vals[4] ** 2 + vals[5] ** 2 + vals[6] ** 2)
    )
    bulk = 1.6 * jnp.exp(-3.0 * phi) * (1.0 + 0.25 * jnp.tanh(mean))
    shear = 0.9 * jnp.exp(-2.0 * phi) / (1.0 + q2 / 0.5)
    soften = shear * q2 / (0.5 + q2)
    return [bulk, shear, soften]


def widen_kernel(v_ref, even_ref, odd_ref, wide_ref):
    hy = v_ref.shape[2]
    odd = lax.axis_index("tgt") % 2 == 1
    for f in range(FIELDS):
        for x in range(v_ref.shape[1]):
            even_side, odd_side = even_ref[f, x], odd_ref[f, x]
            wide_ref[f, x, :hy] = v_ref[f, x]
            wide_ref[f, x, hy : hy + ITERS] = jnp.where(odd, odd_side, even_side)
            wide_ref[f, x, hy + ITERS :] = jnp.where(odd, even_side, odd_side)


def widen_call(v, even, odd):
    fields, hx, hy, hz = v.shape
    return pl.pallas_call(
        widen_kernel,
        out_shape=jax.ShapeDtypeStruct((fields, hx, hy + 2 * ITERS, hz), F32),
        in_specs=[pl.BlockSpec(memory_space=pltpu.VMEM)] * 3,
        out_specs=pl.BlockSpec(memory_space=pltpu.VMEM),
    )(v, even, odd)


def solve_kernel(mesh_shape, wide_ref, even_ref, odd_ref, mass_ref, order_ref, projected_ref, out_ref):
    n_src, n_tgt = mesh_shape
    hx, hy, hz = mass_ref.shape
    k = ITERS
    rows = hy + 2 * k
    a, b = lax.axis_index("src"), lax.axis_index("tgt")

    def exists(flag):
        return jnp.where(flag, 1.0, 0.0).astype(F32)

    row = row_ids(rows, hz)
    lane = lax.broadcasted_iota(jnp.int32, (rows, hz), 1)
    inside = jnp.where(row < hy, 1.0, jnp.where(row < hy + k, exists(b < n_tgt - 1), exists(b > 0)))
    inside_left = inside * exists(a > 0)
    inside_right = inside * exists(a < n_src - 1)
    not_first = jnp.where(lane == 0, 0.0, 1.0)
    not_last = jnp.where(lane == hz - 1, 0.0, 1.0)
    scale = lax.rsqrt(mass_ref[...])

    @pl.loop(0, FIELDS)
    def _(f):
        even = [even_ref[f, x] for x in range(hx)]
        odd = [odd_ref[f, x] for x in range(hx)]
        left = [jnp.where(a % 2 == 1, p, q) for p, q in zip(even, odd)]
        right = [jnp.where(a % 2 == 1, q, p) for p, q in zip(even, odd)]
        base = left[hx - k :] + [wide_ref[f, x] for x in range(hx)] + right[:k]
        u = [COEFS[k] * e for e in base]
        for sweep in range(1, k + 1):
            new = list(u)
            for x in range(sweep, hx + 2 * k - sweep):
                w = u[x]
                near = u[x - 1] + u[x + 1]
                near = near + pltpu.roll(w, 1, 0) + pltpu.roll(w, rows - 1, 0)
                near = near + pltpu.roll(w, 1, 1) * not_first + pltpu.roll(w, hz - 1, 1) * not_last
                if x < k:
                    near = near * inside_left
                elif x < k + hx:
                    near = near * inside
                else:
                    near = near * inside_right
                new[x] = COEFS[k - sweep] * base[x] + near
            u = new
        for x in range(hx):
            projected_ref[f, x] = u[k + x][:hy] * scale[x]

    groups = hx * hy * hz // WIDE
    payload = cell_moduli([projected_ref[f].reshape(hx * hy, hz) for f in range(FIELDS)])
    table = jnp.concatenate([jnp.concatenate([m[:groups], m[groups:]], axis=1) for m in payload], axis=0)
    table = jnp.concatenate(halves(table), axis=0)
    ids = row_ids(WIDE, WIDE).astype(F32).astype(BF16)
    group_ids = row_ids(groups, WIDE)

    def at_parts(index):
        return (index >> log2(hz)) & (groups - 1), ((index >> log2(groups * hz)) << log2(hz)) + (index & (hz - 1))

    @pl.loop(0, out_ref.shape[0], unroll=8)
    def _(q):
        index = order_ref[:, pl.ds(pl.multiple_of(q * WIDE, WIDE), WIDE)]
        got = lookup_rows(table, index, ids, group_ids, groups, at_parts)
        lines = [line[:, c * 128 : (c + 1) * 128] for line in got for c in range(2)]
        out_ref[q] = jnp.concatenate(lines + [jnp.zeros((2, 128), F32)], axis=0)


def solve_call(mesh_shape, wide, even, odd, mass, order):
    hx, hy, hz = mass.shape

    def kernel(*refs):
        solve_kernel(mesh_shape, *refs)

    return pl.pallas_call(
        kernel,
        out_shape=(
            jax.ShapeDtypeStruct((FIELDS, hx, hy, hz), F32),
            jax.ShapeDtypeStruct((order.shape[1] // WIDE, 8, 128), F32),
        ),
        in_specs=[pl.BlockSpec(memory_space=pltpu.VMEM)] * 5,
        out_specs=(pl.BlockSpec(memory_space=pltpu.VMEM),) * 2,
        compiler_params=pltpu.CompilerParams(vmem_limit_bytes=40 << 20),
    )(wide, even, odd, mass, order)


def place_kernel(arrived_ref, order_ref, out_ref, lines):
    groups = arrived_ref.shape[0]
    lines[...] = arrived_ref[...].reshape(groups * 8, 128)
    table = jnp.concatenate(
        [
            jnp.concatenate([lines[pl.ds(2 * m + c, groups, stride=8), :] for c in range(2)], axis=1)
            for m in range(3)
        ],
        axis=0,
    )
    table = jnp.concatenate(halves(table), axis=0)
    ids = row_ids(WIDE, WIDE).astype(F32).astype(BF16)
    group_ids = row_ids(groups, WIDE)

    @pl.loop(0, groups, unroll=8)
    def _(q):
        at = pl.ds(pl.multiple_of(q * WIDE, WIDE), WIDE)
        got = lookup_rows(
            table, order_ref[:, at], ids, group_ids, groups, lambda index: (index >> log2(WIDE), index & (WIDE - 1))
        )
        out_ref[:, at] = jnp.concatenate(got, axis=0)


def place_call(arrived, order):
    return pl.pallas_call(
        place_kernel,
        out_shape=jax.ShapeDtypeStruct((3, order.shape[1]), F32),
        in_specs=[pl.BlockSpec(memory_space=pltpu.VMEM)] * 2,
        out_specs=pl.BlockSpec(memory_space=pltpu.VMEM),
        scratch_shapes=[pltpu.VMEM((arrived.shape[0] * 8, 128), F32)],
        compiler_params=pltpu.CompilerParams(vmem_limit_bytes=40 << 20),
    )(arrived, order)


def swap(x, axis):
    count = lax.axis_size(axis)
    out = []
    for start, part in enumerate(x):
        pairs = [(i, i + 1) for i in range(start, count - 1, 2)]
        out.append(lax.ppermute(part, axis, pairs + [(j, i) for i, j in pairs]))
    return out


def on_device(source_fields, slot_source, slot_weight, slot_target, cell_mass, send_order, place_order):
    n_src, n_tgt = lax.axis_size("src"), lax.axis_size("tgt")
    both = ("src", "tgt")
    owners = n_src * n_tgt
    cells = cell_mass.size
    quota = cells // owners

    values = gather_call(source_fields, slot_source.reshape(1, -1), slot_weight.reshape(1, -1), owners)
    values = lax.all_to_all(values, both, split_axis=0, concat_axis=0, tiled=True)
    v, even, odd = scatter_call(values, slot_target.reshape(1, -1), cell_mass)
    wide = widen_call(v, *swap((even, odd), "tgt"))
    projected, outgoing = solve_call((n_src, n_tgt), wide, *swap((wide, wide), "src"), cell_mass, send_order)

    if quota == WIDE:
        incoming = lax.all_to_all(outgoing, both, split_axis=0, concat_axis=0, tiled=True)
    else:
        groups = cells // WIDE
        flat = outgoing[:, :6].reshape(groups, 3, WIDE).transpose(1, 0, 2).reshape(3, owners, quota)
        flat = lax.all_to_all(flat, both, split_axis=1, concat_axis=1, tiled=True)
        flat = flat.reshape(3, groups, WIDE).transpose(1, 0, 2).reshape(groups, 6, 128)
        incoming = jnp.pad(flat, ((0, 0), (0, 2), (0, 0)))
    return projected, place_call(incoming, place_order)


def solution(mesh):
    split = P(("src", "tgt"))
    rows = P(("src", "tgt"), None)
    return jax.shard_map(
        on_device,
        mesh=mesh,
        in_specs=(P(None, ("src", "tgt")), split, split, split, P("src", "tgt", None), rows, rows),
        out_specs=(P(None, "src", "tgt", None), P(None, ("src", "tgt"))),
        check_vma=False,
    )
```

```python
import numpy as np

import jax
import jax.numpy as jnp
from jax import lax
from jax.experimental import pallas as pl
from jax.experimental.pallas import tpu as pltpu
from jax.sharding import PartitionSpec as P

ITERS = 4
FIELDS = 7
AT_ONCE = 8
TOGETHER = 4
WIDE = 256
BF16 = jnp.bfloat16
F32 = jnp.float32
NT = (((1,), (1,)), ((), ()))


def sweep_polynomial(iters, theta, delta):
    sigma = theta / delta
    rho = 1.0 / sigma
    mass = np.array([1.0, 0.125])
    poly = np.polynomial.polynomial
    resid = np.array([1.0])
    step = resid / theta
    total = np.array([0.0])
    for _ in range(iters):
        total = poly.polyadd(total, step)
        resid = poly.polysub(resid, poly.polymul(mass, step))
        rho_new = 1.0 / (2.0 * sigma - rho)
        step = poly.polyadd(rho_new * rho * step, 2.0 * rho_new / delta * resid)
        rho = rho_new
    return [float(c) for c in poly.polyadd(total, step)]


COEFS = sweep_polynomial(ITERS, 1.0, 0.75)


def halves(x):
    high = x.astype(BF16)
    return high, (x - high.astype(F32)).astype(BF16)


def log2(n):
    assert n & (n - 1) == 0
    return n.bit_length() - 1


def row_ids(rows, lanes):
    return lax.broadcasted_iota(jnp.int32, (rows, lanes), 0)


def low_onehot(low, ids):
    return jnp.where(ids == low.astype(F32).astype(BF16), jnp.ones((), BF16), jnp.zeros((), BF16))


def gather_kernel(fields_hbm, index_hbm, weight_hbm, out_hbm, table, fields_ref, index_ref, weight_ref, out_ref, sems, done):
    pairs = ((fields_hbm, fields_ref), (index_hbm, index_ref), (weight_hbm, weight_ref))
    copies = [pltpu.make_async_copy(src, dst, sems.at[i]) for i, (src, dst) in enumerate(pairs)]
    for copy in copies:
        copy.start()
    owners, tiles, _, lanes = out_ref.shape
    span = tiles * lanes
    groups = fields_ref.shape[1] // WIDE
    table[...] = jnp.zeros_like(table)
    for copy in copies:
        copy.wait()
    for g in range(groups):
        table[g * 8 : g * 8 + FIELDS, :] = fields_ref[:, g * WIDE : (g + 1) * WIDE]
    high, low = halves(table[...])
    both = jnp.concatenate([high, low], axis=0)
    ids = row_ids(WIDE, span).astype(F32).astype(BF16)
    rows = groups * 8

    def one_owner(q):
        at = pl.multiple_of(q * span, span)
        index = index_ref[:, pl.ds(at, span)]
        weight = weight_ref[:, pl.ds(at, span)]
        onehot = low_onehot(index & (WIDE - 1), ids)
        got = jnp.dot(both, onehot, preferred_element_type=F32)
        group = jnp.broadcast_to(index >> log2(WIDE), (8, span))
        value = jnp.zeros((8, span), F32)
        for g in range(groups):
            part = got[g * 8 : (g + 1) * 8] + got[rows + g * 8 : rows + (g + 1) * 8]
            value = jnp.where(group == g, part, value)
        value = value * weight
        for t in range(tiles):
            out_ref[q, t] = value[:, t * lanes : (t + 1) * lanes]

    def send_off(n):
        part = pl.ds(n * AT_ONCE, AT_ONCE)
        return pltpu.make_async_copy(out_ref.at[part], out_hbm.at[part], done.at[n])

    @pl.loop(0, owners // AT_ONCE)
    def _(n):
        for i in range(AT_ONCE):
            one_owner(n * AT_ONCE + i)
        send_off(n).start()

    @pl.loop(0, owners // AT_ONCE)
    def _(n):
        send_off(n).wait()


def gather_call(fields, index, weight, owners):
    tiles = index.shape[1] // owners // 128
    return pl.pallas_call(
        gather_kernel,
        out_shape=jax.ShapeDtypeStruct((owners, tiles, 8, 128), F32),
        in_specs=[pl.BlockSpec(memory_space=pltpu.HBM)] * 3,
        out_specs=pl.BlockSpec(memory_space=pltpu.HBM),
        scratch_shapes=[
            pltpu.VMEM((fields.shape[1] // WIDE * 8, WIDE), F32),
            pltpu.VMEM(fields.shape, F32),
            pltpu.VMEM(index.shape, jnp.int32),
            pltpu.VMEM(weight.shape, F32),
            pltpu.VMEM((owners, tiles, 8, 128), F32),
            pltpu.SemaphoreType.DMA((3,)),
            pltpu.SemaphoreType.DMA((owners // AT_ONCE,)),
        ],
        compiler_params=pltpu.CompilerParams(vmem_limit_bytes=60 << 20),
    )(fields, index, weight)


def scatter_kernel(value_ref, target_ref, mass_ref, v_ref, even_ref, odd_ref, total):
    owners, tiles, _, lanes = value_ref.shape
    span = TOGETHER * tiles * lanes
    hx, hy, hz = mass_ref.shape
    groups = hx * hy * hz // WIDE
    total[...] = jnp.zeros_like(total)
    ids = row_ids(WIDE, span).astype(F32).astype(BF16)
    group_ids = row_ids(groups, span).astype(F32).astype(BF16)

    @pl.loop(0, owners // TOGETHER)
    def _(p):
        at = pl.multiple_of(p * span, span)
        target = target_ref[:, pl.ds(at, span)]
        low = ((target >> log2(groups * hz)) << log2(hz)) + (target & (hz - 1))
        onehot = low_onehot(jnp.where(target < 0, -1, low), ids)
        group = ((target >> log2(hz)) & (groups - 1)).astype(F32).astype(BF16)
        here = group_ids == group
        value = jnp.concatenate([value_ref[p * TOGETHER + i, t] for i in range(TOGETHER) for t in range(tiles)], axis=1)
        parts = []
        for half in halves(value):
            for f in range(FIELDS):
                parts.append(jnp.where(here, half[f : f + 1], jnp.zeros((), BF16)))
        spread = jnp.concatenate(parts, axis=0)
        total[...] += lax.dot_general(spread, onehot, NT, preferred_element_type=F32)

    scale = lax.rsqrt(mass_ref[...])
    half_x = hx // 2
    odd = lax.axis_index("tgt") % 2 == 1
    for f in range(FIELDS):
        s = total[f * groups : (f + 1) * groups] + total[(FIELDS + f) * groups : (FIELDS + f + 1) * groups]
        for b in range(2):
            for x in range(half_x):
                at = b * half_x + x
                v = s[x * hy : (x + 1) * hy, b * hz : (b + 1) * hz] * scale[at]
                v_ref[f, at] = v
                first, last = v[:ITERS], v[hy - ITERS :]
                even_ref[f, at] = jnp.where(odd, first, last)
                odd_ref[f, at] = jnp.where(odd, last, first)


def scatter_call(values, target, mass):
    hx, hy, hz = mass.shape
    groups = hx * hy * hz // WIDE
    side = jax.ShapeDtypeStruct((FIELDS, hx, ITERS, hz), F32)
    return pl.pallas_call(
        scatter_kernel,
        out_shape=(jax.ShapeDtypeStruct((FIELDS, hx, hy, hz), F32), side, side),
        in_specs=[pl.BlockSpec(memory_space=pltpu.VMEM)] * 3,
        out_specs=(pl.BlockSpec(memory_space=pltpu.VMEM),) * 3,
        scratch_shapes=[pltpu.VMEM((2 * FIELDS * groups, WIDE), F32)],
        compiler_params=pltpu.CompilerParams(vmem_limit_bytes=40 << 20),
    )(values, target, mass)


def lookup_rows(table, index, ids, group_ids, groups, at_parts):
    group, low = at_parts(index)
    got = jnp.dot(table, low_onehot(low, ids), preferred_element_type=F32)
    here = group_ids == group
    rows = 3 * groups
    out = []
    for m in range(3):
        part = got[m * groups : (m + 1) * groups] + got[rows + m * groups : rows + (m + 1) * groups]
        out.append(jnp.sum(jnp.where(here, part, 0.0), axis=0, keepdims=True))
    return out


def cell_moduli(vals):
    phi = vals[0]
    mean = (vals[1] + vals[2] + vals[3]) / 3.0
    q2 = 1.5 * (
        (vals[1] - mean) ** 2
        + (vals[2] - mean) ** 2
        + (vals[3] - mean) ** 2
        + 2.0 * (vals[4] ** 2 + vals[5] ** 2 + vals[6] ** 2)
    )
    bulk = 1.6 * jnp.exp(-3.0 * phi) * (1.0 + 0.25 * jnp.tanh(mean))
    shear = 0.9 * jnp.exp(-2.0 * phi) / (1.0 + q2 / 0.5)
    soften = shear * q2 / (0.5 + q2)
    return [bulk, shear, soften]


def widen_kernel(v_ref, even_ref, odd_ref, wide_ref, to_even_ref, to_odd_ref):
    hx, hy = v_ref.shape[1], v_ref.shape[2]
    own = hx * hy
    b_odd = lax.axis_index("tgt") % 2 == 1
    a_odd = lax.axis_index("src") % 2 == 1
    line = row_ids(2 * ITERS, v_ref.shape[3])
    for f in range(FIELDS):
        sides = []
        for x in range(hx):
            even_side, odd_side = even_ref[f, x], odd_ref[f, x]
            right = jnp.where(b_odd, odd_side, even_side)
            left = jnp.where(b_odd, even_side, odd_side)
            sides.append(jnp.concatenate([right, left], axis=0))
            wide_ref[f, x, :hy] = v_ref[f, x]
            wide_ref[f, x, hy:] = sides[x]
            to_even_ref[f, x * hy : (x + 1) * hy] = v_ref[f, x]
            to_odd_ref[f, x * hy : (x + 1) * hy] = v_ref[f, x]
        extra = []
        for first, second, third in ((sides[hx - 1], sides[hx - 2], sides[hx - 3]), (sides[0], sides[1], sides[2])):
            far = jnp.where(line < 4, pltpu.roll(third, 2, 0), pltpu.roll(third, 6, 0))
            extra.append((first, jnp.where((line < 2) | (line > 5), second, far)))
        for i in range(2):
            at = own + i * 2 * ITERS
            to_even_ref[f, at : at + 2 * ITERS] = jnp.where(a_odd, extra[1][i], extra[0][i])
            to_odd_ref[f, at : at + 2 * ITERS] = jnp.where(a_odd, extra[0][i], extra[1][i])


def widen_call(v, even, odd):
    fields, hx, hy, hz = v.shape
    payload = jax.ShapeDtypeStruct((fields, hx * hy + 4 * ITERS, hz), F32)
    return pl.pallas_call(
        widen_kernel,
        out_shape=(jax.ShapeDtypeStruct((fields, hx, hy + 2 * ITERS, hz), F32), payload, payload),
        in_specs=[pl.BlockSpec(memory_space=pltpu.VMEM)] * 3,
        out_specs=(pl.BlockSpec(memory_space=pltpu.VMEM),) * 3,
        compiler_params=pltpu.CompilerParams(vmem_limit_bytes=40 << 20),
    )(v, even, odd)


def solve_kernel(mesh_shape, wide_ref, even_ref, odd_ref, mass_ref, order_ref, projected_ref, out_ref):
    n_src, n_tgt = mesh_shape
    hx, hy, hz = mass_ref.shape
    k = ITERS
    rows = hy + 2 * k
    a, b = lax.axis_index("src"), lax.axis_index("tgt")

    def exists(flag):
        return jnp.where(flag, 1.0, 0.0).astype(F32)

    row = row_ids(rows, hz)
    lane = lax.broadcasted_iota(jnp.int32, (rows, hz), 1)
    inside = jnp.where(row < hy, 1.0, jnp.where(row < hy + k, exists(b < n_tgt - 1), exists(b > 0)))
    inside_left = inside * exists(a > 0)
    inside_right = inside * exists(a < n_src - 1)
    not_first = jnp.where(lane == 0, 0.0, 1.0)
    not_last = jnp.where(lane == hz - 1, 0.0, 1.0)
    scale = lax.rsqrt(mass_ref[...])

    line = row_ids(2 * k, hz)

    def slabs(payload, from_left):
        first = payload[hx * hy : hx * hy + 2 * k]
        second = payload[hx * hy + 2 * k :]
        third = jnp.where(line < 4, pltpu.roll(second, 6, 0), pltpu.roll(second, 2, 0))
        sides = [first, second, third] + [jnp.zeros((2 * k, hz), F32)] * (hx - 3)
        order = reversed(sides) if from_left else sides
        return [jnp.concatenate([payload[x * hy : (x + 1) * hy], side], axis=0) for x, side in enumerate(order)]

    @pl.loop(0, FIELDS)
    def _(f):
        even, odd = even_ref[f], odd_ref[f]
        left = slabs(jnp.where(a % 2 == 1, even, odd), True)
        right = slabs(jnp.where(a % 2 == 1, odd, even), False)
        base = left + [wide_ref[f, x] for x in range(hx)] + right
        u = [COEFS[k] * e for e in base]
        for sweep in range(1, k + 1):
            new = list(u)
            for x in range(sweep, hx + 2 * k - sweep):
                w = u[x]
                near = u[x - 1] + u[x + 1]
                near = near + pltpu.roll(w, 1, 0) + pltpu.roll(w, rows - 1, 0)
                near = near + pltpu.roll(w, 1, 1) * not_first + pltpu.roll(w, hz - 1, 1) * not_last
                if x < k:
                    near = near * inside_left
                elif x < k + hx:
                    near = near * inside
                else:
                    near = near * inside_right
                new[x] = COEFS[k - sweep] * base[x] + near
            u = new
        for x in range(hx):
            projected_ref[f, x] = u[k + x][:hy] * scale[x]

    groups = hx * hy * hz // WIDE
    payload = cell_moduli([projected_ref[f].reshape(hx * hy, hz) for f in range(FIELDS)])
    table = jnp.concatenate([jnp.concatenate([m[:groups], m[groups:]], axis=1) for m in payload], axis=0)
    table = jnp.concatenate(halves(table), axis=0)
    ids = row_ids(WIDE, WIDE).astype(F32).astype(BF16)
    group_ids = row_ids(groups, WIDE)

    def at_parts(index):
        return (index >> log2(hz)) & (groups - 1), ((index >> log2(groups * hz)) << log2(hz)) + (index & (hz - 1))

    @pl.loop(0, out_ref.shape[0], unroll=8)
    def _(q):
        index = order_ref[:, pl.ds(pl.multiple_of(q * WIDE, WIDE), WIDE)]
        got = lookup_rows(table, index, ids, group_ids, groups, at_parts)
        lines = [line[:, c * 128 : (c + 1) * 128] for line in got for c in range(2)]
        out_ref[q] = jnp.concatenate(lines + [jnp.zeros((2, 128), F32)], axis=0)


def solve_call(mesh_shape, wide, even, odd, mass, order):
    hx, hy, hz = mass.shape

    def kernel(*refs):
        solve_kernel(mesh_shape, *refs)

    return pl.pallas_call(
        kernel,
        out_shape=(
            jax.ShapeDtypeStruct((FIELDS, hx, hy, hz), F32),
            jax.ShapeDtypeStruct((order.shape[1] // WIDE, 8, 128), F32),
        ),
        in_specs=[pl.BlockSpec(memory_space=pltpu.VMEM)] * 5,
        out_specs=(pl.BlockSpec(memory_space=pltpu.VMEM),) * 2,
        compiler_params=pltpu.CompilerParams(vmem_limit_bytes=40 << 20),
    )(wide, even, odd, mass, order)


def place_kernel(arrived_ref, order_ref, out_ref, lines):
    groups = arrived_ref.shape[0]
    lines[...] = arrived_ref[...].reshape(groups * 8, 128)
    table = jnp.concatenate(
        [
            jnp.concatenate([lines[pl.ds(2 * m + c, groups, stride=8), :] for c in range(2)], axis=1)
            for m in range(3)
        ],
        axis=0,
    )
    table = jnp.concatenate(halves(table), axis=0)
    ids = row_ids(WIDE, WIDE).astype(F32).astype(BF16)
    group_ids = row_ids(groups, WIDE)

    @pl.loop(0, groups, unroll=8)
    def _(q):
        at = pl.ds(pl.multiple_of(q * WIDE, WIDE), WIDE)
        got = lookup_rows(
            table, order_ref[:, at], ids, group_ids, groups, lambda index: (index >> log2(WIDE), index & (WIDE - 1))
        )
        out_ref[:, at] = jnp.concatenate(got, axis=0)


def place_call(arrived, order):
    return pl.pallas_call(
        place_kernel,
        out_shape=jax.ShapeDtypeStruct((3, order.shape[1]), F32),
        in_specs=[pl.BlockSpec(memory_space=pltpu.VMEM)] * 2,
        out_specs=pl.BlockSpec(memory_space=pltpu.VMEM),
        scratch_shapes=[pltpu.VMEM((arrived.shape[0] * 8, 128), F32)],
        compiler_params=pltpu.CompilerParams(vmem_limit_bytes=40 << 20),
    )(arrived, order)


def swap(x, axis):
    count = lax.axis_size(axis)
    out = []
    for start, part in enumerate(x):
        pairs = [(i, i + 1) for i in range(start, count - 1, 2)]
        out.append(lax.ppermute(part, axis, pairs + [(j, i) for i, j in pairs]))
    return out


def on_device(source_fields, slot_source, slot_weight, slot_target, cell_mass, send_order, place_order):
    n_src, n_tgt = lax.axis_size("src"), lax.axis_size("tgt")
    both = ("src", "tgt")
    owners = n_src * n_tgt
    cells = cell_mass.size
    quota = cells // owners

    values = gather_call(source_fields, slot_source.reshape(1, -1), slot_weight.reshape(1, -1), owners)
    values = lax.all_to_all(values, both, split_axis=0, concat_axis=0, tiled=True)
    v, even, odd = scatter_call(values, slot_target.reshape(1, -1), cell_mass)
    wide, even, odd = widen_call(v, *swap((even, odd), "tgt"))
    projected, outgoing = solve_call((n_src, n_tgt), wide, *swap((even, odd), "src"), cell_mass, send_order)

    if quota == WIDE:
        incoming = lax.all_to_all(outgoing, both, split_axis=0, concat_axis=0, tiled=True)
    else:
        groups = cells // WIDE
        flat = outgoing[:, :6].reshape(groups, 3, WIDE).transpose(1, 0, 2).reshape(3, owners, quota)
        flat = lax.all_to_all(flat, both, split_axis=1, concat_axis=1, tiled=True)
        flat = flat.reshape(3, groups, WIDE).transpose(1, 0, 2).reshape(groups, 6, 128)
        incoming = jnp.pad(flat, ((0, 0), (0, 2), (0, 0)))
    return projected, place_call(incoming, place_order)


def solution(mesh):
    split = P(("src", "tgt"))
    rows = P(("src", "tgt"), None)
    return jax.shard_map(
        on_device,
        mesh=mesh,
        in_specs=(P(None, ("src", "tgt")), split, split, split, P("src", "tgt", None), rows, rows),
        out_specs=(P(None, "src", "tgt", None), P(None, ("src", "tgt"))),
        check_vma=False,
    )
```

```python
import numpy as np

import jax
import jax.numpy as jnp
from jax import lax
from jax.experimental import pallas as pl
from jax.experimental.pallas import tpu as pltpu
from jax.sharding import PartitionSpec as P

ITERS = 4
FIELDS = 7
AT_ONCE = 8
TOGETHER = 4
WIDE = 256
BF16 = jnp.bfloat16
F32 = jnp.float32
NT = (((1,), (1,)), ((), ()))


def sweep_polynomial(iters, theta, delta):
    sigma = theta / delta
    rho = 1.0 / sigma
    mass = np.array([1.0, 0.125])
    poly = np.polynomial.polynomial
    resid = np.array([1.0])
    step = resid / theta
    total = np.array([0.0])
    for _ in range(iters):
        total = poly.polyadd(total, step)
        resid = poly.polysub(resid, poly.polymul(mass, step))
        rho_new = 1.0 / (2.0 * sigma - rho)
        step = poly.polyadd(rho_new * rho * step, 2.0 * rho_new / delta * resid)
        rho = rho_new
    return [float(c) for c in poly.polyadd(total, step)]


COEFS = sweep_polynomial(ITERS, 1.0, 0.75)


def halves(x):
    high = x.astype(BF16)
    return high, (x - high.astype(F32)).astype(BF16)


def log2(n):
    assert n & (n - 1) == 0
    return n.bit_length() - 1


def row_ids(rows, lanes):
    return lax.broadcasted_iota(jnp.int32, (rows, lanes), 0)


def low_onehot(low, ids):
    return jnp.where(ids == low.astype(F32).astype(BF16), jnp.ones((), BF16), jnp.zeros((), BF16))


def gather_kernel(fields_hbm, index_hbm, weight_hbm, out_hbm, table, fields_ref, index_ref, weight_ref, out_ref, sems, done):
    pairs = ((fields_hbm, fields_ref), (index_hbm, index_ref), (weight_hbm, weight_ref))
    copies = [pltpu.make_async_copy(src, dst, sems.at[i]) for i, (src, dst) in enumerate(pairs)]
    for copy in copies:
        copy.start()
    owners, tiles, _, lanes = out_ref.shape
    span = tiles * lanes
    groups = fields_ref.shape[1] // WIDE
    table[...] = jnp.zeros_like(table)
    for copy in copies:
        copy.wait()
    for g in range(groups):
        table[g * 8 : g * 8 + FIELDS, :] = fields_ref[:, g * WIDE : (g + 1) * WIDE]
    high, low = halves(table[...])
    both = jnp.concatenate([high, low], axis=0)
    ids = row_ids(WIDE, span).astype(F32).astype(BF16)
    rows = groups * 8

    def one_owner(q):
        at = pl.multiple_of(q * span, span)
        index = index_ref[:, pl.ds(at, span)]
        weight = weight_ref[:, pl.ds(at, span)]
        onehot = low_onehot(index & (WIDE - 1), ids)
        got = jnp.dot(both, onehot, preferred_element_type=F32)
        group = jnp.broadcast_to(index >> log2(WIDE), (8, span))
        value = jnp.zeros((8, span), F32)
        for g in range(groups):
            part = got[g * 8 : (g + 1) * 8] + got[rows + g * 8 : rows + (g + 1) * 8]
            value = jnp.where(group == g, part, value)
        value = value * weight
        for t in range(tiles):
            out_ref[q, t] = value[:, t * lanes : (t + 1) * lanes]

    def send_off(n):
        part = pl.ds(n * AT_ONCE, AT_ONCE)
        return pltpu.make_async_copy(out_ref.at[part], out_hbm.at[part], done.at[n])

    @pl.loop(0, owners // AT_ONCE)
    def _(n):
        for i in range(AT_ONCE):
            one_owner(n * AT_ONCE + i)
        send_off(n).start()

    @pl.loop(0, owners // AT_ONCE)
    def _(n):
        send_off(n).wait()


def gather_call(fields, index, weight, owners):
    tiles = index.shape[1] // owners // 128
    return pl.pallas_call(
        gather_kernel,
        out_shape=jax.ShapeDtypeStruct((owners, tiles, 8, 128), F32),
        in_specs=[pl.BlockSpec(memory_space=pltpu.HBM)] * 3,
        out_specs=pl.BlockSpec(memory_space=pltpu.HBM),
        scratch_shapes=[
            pltpu.VMEM((fields.shape[1] // WIDE * 8, WIDE), F32),
            pltpu.VMEM(fields.shape, F32),
            pltpu.VMEM(index.shape, jnp.int32),
            pltpu.VMEM(weight.shape, F32),
            pltpu.VMEM((owners, tiles, 8, 128), F32),
            pltpu.SemaphoreType.DMA((3,)),
            pltpu.SemaphoreType.DMA((owners // AT_ONCE,)),
        ],
        compiler_params=pltpu.CompilerParams(vmem_limit_bytes=60 << 20),
    )(fields, index, weight)


def scatter_kernel(value_ref, target_ref, mass_ref, v_ref, odd_ref, total):
    owners, tiles, _, lanes = value_ref.shape
    span = TOGETHER * tiles * lanes
    hx, hy, hz = mass_ref.shape
    groups = hx * hy * hz // WIDE
    total[...] = jnp.zeros_like(total)
    ids = row_ids(WIDE, span).astype(F32).astype(BF16)
    group_ids = row_ids(groups, span).astype(F32).astype(BF16)

    @pl.loop(0, owners // TOGETHER)
    def _(p):
        at = pl.multiple_of(p * span, span)
        target = target_ref[:, pl.ds(at, span)]
        low = ((target >> log2(groups * hz)) << log2(hz)) + (target & (hz - 1))
        onehot = low_onehot(jnp.where(target < 0, -1, low), ids)
        group = ((target >> log2(hz)) & (groups - 1)).astype(F32).astype(BF16)
        here = group_ids == group
        value = jnp.concatenate([value_ref[p * TOGETHER + i, t] for i in range(TOGETHER) for t in range(tiles)], axis=1)
        parts = []
        for half in halves(value):
            for f in range(FIELDS):
                parts.append(jnp.where(here, half[f : f + 1], jnp.zeros((), BF16)))
        spread = jnp.concatenate(parts, axis=0)
        total[...] += lax.dot_general(spread, onehot, NT, preferred_element_type=F32)

    scale = lax.rsqrt(mass_ref[...])
    half_x = hx // 2
    odd = lax.axis_index("tgt") % 2 == 1
    for f in range(FIELDS):
        s = total[f * groups : (f + 1) * groups] + total[(FIELDS + f) * groups : (FIELDS + f + 1) * groups]
        for b in range(2):
            for x in range(half_x):
                at = b * half_x + x
                v = s[x * hy : (x + 1) * hy, b * hz : (b + 1) * hz] * scale[at]
                v_ref[f, at] = v
                odd_ref[f, at] = jnp.where(odd, v[hy - ITERS :], v[:ITERS])


def scatter_call(values, target, mass):
    hx, hy, hz = mass.shape
    groups = hx * hy * hz // WIDE
    side = jax.ShapeDtypeStruct((FIELDS, hx, ITERS, hz), F32)
    return pl.pallas_call(
        scatter_kernel,
        out_shape=(jax.ShapeDtypeStruct((FIELDS, hx, hy, hz), F32), side),
        in_specs=[pl.BlockSpec(memory_space=pltpu.VMEM)] * 3,
        out_specs=(pl.BlockSpec(memory_space=pltpu.VMEM),) * 2,
        scratch_shapes=[pltpu.VMEM((2 * FIELDS * groups, WIDE), F32)],
        compiler_params=pltpu.CompilerParams(vmem_limit_bytes=40 << 20),
    )(values, target, mass)


def lookup_rows(table, index, ids, group_ids, groups, at_parts):
    group, low = at_parts(index)
    got = jnp.dot(table, low_onehot(low, ids), preferred_element_type=F32)
    here = group_ids == group
    rows = 3 * groups
    out = []
    for m in range(3):
        part = got[m * groups : (m + 1) * groups] + got[rows + m * groups : rows + (m + 1) * groups]
        out.append(jnp.sum(jnp.where(here, part, 0.0), axis=0, keepdims=True))
    return out


def cell_moduli(vals):
    phi = vals[0]
    mean = (vals[1] + vals[2] + vals[3]) / 3.0
    q2 = 1.5 * (
        (vals[1] - mean) ** 2
        + (vals[2] - mean) ** 2
        + (vals[3] - mean) ** 2
        + 2.0 * (vals[4] ** 2 + vals[5] ** 2 + vals[6] ** 2)
    )
    bulk = 1.6 * jnp.exp(-3.0 * phi) * (1.0 + 0.25 * jnp.tanh(mean))
    shear = 0.9 * jnp.exp(-2.0 * phi) / (1.0 + q2 / 0.5)
    soften = shear * q2 / (0.5 + q2)
    return [bulk, shear, soften]


def strips_kernel(v_ref, even_ref):
    odd = lax.axis_index("tgt") % 2 == 1
    hy = v_ref.shape[2]
    for f in range(FIELDS):
        for x in range(v_ref.shape[1]):
            even_ref[f, x] = jnp.where(odd, v_ref[f, x, :ITERS], v_ref[f, x, hy - ITERS :])


def strips_call(v):
    fields, hx, _, hz = v.shape
    return pl.pallas_call(
        strips_kernel,
        out_shape=jax.ShapeDtypeStruct((fields, hx, ITERS, hz), F32),
        in_specs=[pl.BlockSpec(memory_space=pltpu.VMEM)],
        out_specs=pl.BlockSpec(memory_space=pltpu.VMEM),
        compiler_params=pltpu.CompilerParams(vmem_limit_bytes=4 << 20),
    )(v)


def corners(sides):
    line = row_ids(2 * ITERS, sides[0].shape[1])
    far = jnp.where(line < 4, pltpu.roll(sides[2], 2, 0), pltpu.roll(sides[2], 6, 0))
    return sides[0], jnp.where((line < 2) | (line > 5), sides[1], far)


def sides_kernel(even_ref, odd_ref, block_ref, sides_ref, to_odd_ref):
    del block_ref
    b_odd = lax.axis_index("tgt") % 2 == 1
    a_odd = lax.axis_index("src") % 2 == 1
    hx = even_ref.shape[1]
    for f in range(FIELDS):
        sides = []
        for x in range(hx):
            even_side, odd_side = even_ref[f, x], odd_ref[f, x]
            right = jnp.where(b_odd, odd_side, even_side)
            left = jnp.where(b_odd, even_side, odd_side)
            sides.append(jnp.concatenate([right, left], axis=0))
            sides_ref[f, x] = sides[x]
        for i, (first, last) in enumerate(zip(corners(sides), corners(sides[::-1]))):
            to_odd_ref[f, i * 2 * ITERS : (i + 1) * 2 * ITERS] = jnp.where(a_odd, last, first)


def sides_call(even, odd, block):
    fields, hx, _, hz = even.shape
    return pl.pallas_call(
        sides_kernel,
        out_shape=(
            jax.ShapeDtypeStruct((fields, hx, 2 * ITERS, hz), F32),
            jax.ShapeDtypeStruct((fields, 4 * ITERS, hz), F32),
        ),
        in_specs=[pl.BlockSpec(memory_space=pltpu.VMEM)] * 3,
        out_specs=(pl.BlockSpec(memory_space=pltpu.VMEM),) * 2,
        compiler_params=pltpu.CompilerParams(vmem_limit_bytes=4 << 20),
    )(even, odd, block)


def payload_kernel(v_ref, sides_ref, to_even_ref):
    a_odd = lax.axis_index("src") % 2 == 1
    hx, hy = v_ref.shape[1], v_ref.shape[2]
    for f in range(FIELDS):
        for x in range(hx):
            to_even_ref[f, x * hy : (x + 1) * hy] = v_ref[f, x]
        sides = [sides_ref[f, x] for x in range(hx)]
        for i, (first, last) in enumerate(zip(corners(sides), corners(sides[::-1]))):
            at = hx * hy + i * 2 * ITERS
            to_even_ref[f, at : at + 2 * ITERS] = jnp.where(a_odd, first, last)


def payload_call(v, sides):
    fields, hx, hy, hz = v.shape
    return pl.pallas_call(
        payload_kernel,
        out_shape=jax.ShapeDtypeStruct((fields, hx * hy + 4 * ITERS, hz), F32),
        in_specs=[pl.BlockSpec(memory_space=pltpu.VMEM)] * 2,
        out_specs=pl.BlockSpec(memory_space=pltpu.VMEM),
        compiler_params=pltpu.CompilerParams(vmem_limit_bytes=4 << 20),
    )(v, sides)


def solve_kernel(
    mesh_shape, v_ref, sides_ref, even_ref, odd_ref, odd_sides_ref, mass_ref, order_ref, projected_ref, out_ref
):
    n_src, n_tgt = mesh_shape
    hx, hy, hz = mass_ref.shape
    k = ITERS
    rows = hy + 2 * k
    a, b = lax.axis_index("src"), lax.axis_index("tgt")

    def exists(flag):
        return jnp.where(flag, 1.0, 0.0).astype(F32)

    row = row_ids(rows, hz)
    lane = lax.broadcasted_iota(jnp.int32, (rows, hz), 1)
    inside = jnp.where(row < hy, 1.0, jnp.where(row < hy + k, exists(b < n_tgt - 1), exists(b > 0)))
    inside_left = inside * exists(a > 0)
    inside_right = inside * exists(a < n_src - 1)
    not_first = jnp.where(lane == 0, 0.0, 1.0)
    not_last = jnp.where(lane == hz - 1, 0.0, 1.0)
    scale = lax.rsqrt(mass_ref[...])

    line = row_ids(2 * k, hz)

    def slabs(own, sides, from_left):
        second = sides[2 * k :]
        third = jnp.where(line < 4, pltpu.roll(second, 6, 0), pltpu.roll(second, 2, 0))
        sides = [sides[: 2 * k], second, third] + [jnp.zeros((2 * k, hz), F32)] * (hx - 3)
        order = reversed(sides) if from_left else sides
        return [jnp.concatenate([own[x * hy : (x + 1) * hy], side], axis=0) for x, side in enumerate(order)]

    @pl.loop(0, FIELDS)
    def _(f):
        even, even_sides = even_ref[f, : hx * hy], even_ref[f, hx * hy :]
        odd, odd_sides = odd_ref[f].reshape(hx * hy, hz), odd_sides_ref[f]
        a_odd = a % 2 == 1
        left = slabs(jnp.where(a_odd, even, odd), jnp.where(a_odd, even_sides, odd_sides), True)
        right = slabs(jnp.where(a_odd, odd, even), jnp.where(a_odd, odd_sides, even_sides), False)
        own = [jnp.concatenate([v_ref[f, x], sides_ref[f, x]], axis=0) for x in range(hx)]
        base = left + own + right
        u = [COEFS[k] * e for e in base]
        for sweep in range(1, k + 1):
            new = list(u)
            for x in range(sweep, hx + 2 * k - sweep):
                w = u[x]
                near = u[x - 1] + u[x + 1]
                near = near + pltpu.roll(w, 1, 0) + pltpu.roll(w, rows - 1, 0)
                near = near + pltpu.roll(w, 1, 1) * not_first + pltpu.roll(w, hz - 1, 1) * not_last
                if x < k:
                    near = near * inside_left
                elif x < k + hx:
                    near = near * inside
                else:
                    near = near * inside_right
                new[x] = COEFS[k - sweep] * base[x] + near
            u = new
        for x in range(hx):
            projected_ref[f, x] = u[k + x][:hy] * scale[x]

    groups = hx * hy * hz // WIDE
    payload = cell_moduli([projected_ref[f].reshape(hx * hy, hz) for f in range(FIELDS)])
    table = jnp.concatenate([jnp.concatenate([m[:groups], m[groups:]], axis=1) for m in payload], axis=0)
    table = jnp.concatenate(halves(table), axis=0)
    ids = row_ids(WIDE, WIDE).astype(F32).astype(BF16)
    group_ids = row_ids(groups, WIDE)

    def at_parts(index):
        return (index >> log2(hz)) & (groups - 1), ((index >> log2(groups * hz)) << log2(hz)) + (index & (hz - 1))

    @pl.loop(0, out_ref.shape[0], unroll=8)
    def _(q):
        index = order_ref[:, pl.ds(pl.multiple_of(q * WIDE, WIDE), WIDE)]
        got = lookup_rows(table, index, ids, group_ids, groups, at_parts)
        lines = [line[:, c * 128 : (c + 1) * 128] for line in got for c in range(2)]
        out_ref[q] = jnp.concatenate(lines + [jnp.zeros((2, 128), F32)], axis=0)


def solve_call(mesh_shape, v, sides, even, odd, odd_sides, mass, order):
    hx, hy, hz = mass.shape

    def kernel(*refs):
        solve_kernel(mesh_shape, *refs)

    return pl.pallas_call(
        kernel,
        out_shape=(
            jax.ShapeDtypeStruct((FIELDS, hx, hy, hz), F32),
            jax.ShapeDtypeStruct((order.shape[1] // WIDE, 8, 128), F32),
        ),
        in_specs=[pl.BlockSpec(memory_space=pltpu.VMEM)] * 7,
        out_specs=(pl.BlockSpec(memory_space=pltpu.VMEM),) * 2,
        compiler_params=pltpu.CompilerParams(vmem_limit_bytes=40 << 20),
    )(v, sides, even, odd, odd_sides, mass, order)


def place_kernel(arrived_ref, order_ref, out_ref, lines):
    groups = arrived_ref.shape[0]
    lines[...] = arrived_ref[...].reshape(groups * 8, 128)
    table = jnp.concatenate(
        [
            jnp.concatenate([lines[pl.ds(2 * m + c, groups, stride=8), :] for c in range(2)], axis=1)
            for m in range(3)
        ],
        axis=0,
    )
    table = jnp.concatenate(halves(table), axis=0)
    ids = row_ids(WIDE, WIDE).astype(F32).astype(BF16)
    group_ids = row_ids(groups, WIDE)

    @pl.loop(0, groups, unroll=8)
    def _(q):
        at = pl.ds(pl.multiple_of(q * WIDE, WIDE), WIDE)
        got = lookup_rows(
            table, order_ref[:, at], ids, group_ids, groups, lambda index: (index >> log2(WIDE), index & (WIDE - 1))
        )
        out_ref[:, at] = jnp.concatenate(got, axis=0)


def place_call(arrived, order):
    return pl.pallas_call(
        place_kernel,
        out_shape=jax.ShapeDtypeStruct((3, order.shape[1]), F32),
        in_specs=[pl.BlockSpec(memory_space=pltpu.VMEM)] * 2,
        out_specs=pl.BlockSpec(memory_space=pltpu.VMEM),
        scratch_shapes=[pltpu.VMEM((arrived.shape[0] * 8, 128), F32)],
        compiler_params=pltpu.CompilerParams(vmem_limit_bytes=40 << 20),
    )(arrived, order)


def swap(x, axis, start):
    pairs = [(i, i + 1) for i in range(start, lax.axis_size(axis) - 1, 2)]
    return lax.ppermute(x, axis, pairs + [(j, i) for i, j in pairs])


def on_device(source_fields, slot_source, slot_weight, slot_target, cell_mass, send_order, place_order):
    n_src, n_tgt = lax.axis_size("src"), lax.axis_size("tgt")
    both = ("src", "tgt")
    owners = n_src * n_tgt
    cells = cell_mass.size
    quota = cells // owners

    values = gather_call(source_fields, slot_source.reshape(1, -1), slot_weight.reshape(1, -1), owners)
    values = lax.all_to_all(values, both, split_axis=0, concat_axis=0, tiled=True)
    v, odd_strips = scatter_call(values, slot_target.reshape(1, -1), cell_mass)
    odd_strips = swap(odd_strips, "tgt", 1)
    odd = swap(v, "src", 1)
    even_strips = swap(strips_call(v), "tgt", 0)
    sides, odd_sides = sides_call(even_strips, odd_strips, odd)
    odd_sides = swap(odd_sides, "src", 1)
    even = swap(payload_call(v, sides), "src", 0)
    projected, outgoing = solve_call((n_src, n_tgt), v, sides, even, odd, odd_sides, cell_mass, send_order)

    if quota == WIDE:
        incoming = lax.all_to_all(outgoing, both, split_axis=0, concat_axis=0, tiled=True)
    else:
        groups = cells // WIDE
        flat = outgoing[:, :6].reshape(groups, 3, WIDE).transpose(1, 0, 2).reshape(3, owners, quota)
        flat = lax.all_to_all(flat, both, split_axis=1, concat_axis=1, tiled=True)
        flat = flat.reshape(3, groups, WIDE).transpose(1, 0, 2).reshape(groups, 6, 128)
        incoming = jnp.pad(flat, ((0, 0), (0, 2), (0, 0)))
    return projected, place_call(incoming, place_order)


def solution(mesh):
    split = P(("src", "tgt"))
    rows = P(("src", "tgt"), None)
    return jax.shard_map(
        on_device,
        mesh=mesh,
        in_specs=(P(None, ("src", "tgt")), split, split, split, P("src", "tgt", None), rows, rows),
        out_specs=(P(None, "src", "tgt", None), P(None, ("src", "tgt"))),
        check_vma=False,
    )
```

```python
import numpy as np

import jax
import jax.numpy as jnp
from jax import lax
from jax.experimental import pallas as pl
from jax.experimental.pallas import tpu as pltpu
from jax.sharding import PartitionSpec as P

ITERS = 4
FIELDS = 7
SPAN = 512
AT_ONCE = 8
TOGETHER = 4
WIDE = 256
BF16 = jnp.bfloat16
F32 = jnp.float32
NT = (((1,), (1,)), ((), ()))


def sweep_polynomial(iters, theta, delta):
    sigma = theta / delta
    rho = 1.0 / sigma
    mass = np.array([1.0, 0.125])
    poly = np.polynomial.polynomial
    resid = np.array([1.0])
    step = resid / theta
    total = np.array([0.0])
    for _ in range(iters):
        total = poly.polyadd(total, step)
        resid = poly.polysub(resid, poly.polymul(mass, step))
        rho_new = 1.0 / (2.0 * sigma - rho)
        step = poly.polyadd(rho_new * rho * step, 2.0 * rho_new / delta * resid)
        rho = rho_new
    return [float(c) for c in poly.polyadd(total, step)]


COEFS = sweep_polynomial(ITERS, 1.0, 0.75)


def halves(x):
    high = x.astype(BF16)
    return high, (x - high.astype(F32)).astype(BF16)


def log2(n):
    assert n & (n - 1) == 0
    return n.bit_length() - 1


def row_ids(rows, lanes):
    return lax.broadcasted_iota(jnp.int32, (rows, lanes), 0)


def low_onehot(low, ids):
    return jnp.where(ids == low.astype(F32).astype(BF16), jnp.ones((), BF16), jnp.zeros((), BF16))


def gather_kernel(fields_hbm, index_hbm, weight_hbm, out_hbm, table, fields_ref, index_ref, weight_ref, out_ref, sems, done):
    pairs = ((fields_hbm, fields_ref), (index_hbm, index_ref), (weight_hbm, weight_ref))
    copies = [pltpu.make_async_copy(src, dst, sems.at[i]) for i, (src, dst) in enumerate(pairs)]
    for copy in copies:
        copy.start()
    lanes = out_ref.shape[1]
    span = SPAN
    tiles = span // lanes
    owners = index_ref.shape[1] // span
    groups = fields_ref.shape[1] // WIDE
    table[...] = jnp.zeros_like(table)
    for copy in copies:
        copy.wait()
    for g in range(groups):
        table[g * 8 : g * 8 + FIELDS, :] = fields_ref[:, g * WIDE : (g + 1) * WIDE]
    high, low = halves(table[...])
    both = jnp.concatenate([high, low], axis=0)
    ids = row_ids(WIDE, span).astype(F32).astype(BF16)
    rows = groups * 8

    def one_owner(q):
        at = pl.multiple_of(q * span, span)
        index = index_ref[:, pl.ds(at, span)]
        weight = weight_ref[:, pl.ds(at, span)]
        onehot = low_onehot(index & (WIDE - 1), ids)
        got = jnp.dot(both, onehot, preferred_element_type=F32)
        group = jnp.broadcast_to(index >> log2(WIDE), (8, span))
        value = jnp.zeros((8, span), F32)
        for g in range(groups):
            part = got[g * 8 : (g + 1) * 8] + got[rows + g * 8 : rows + (g + 1) * 8]
            value = jnp.where(group == g, part, value)
        value = value * weight
        for t in range(tiles):
            out_ref[pl.ds(q * (FIELDS * tiles) + t, FIELDS, stride=tiles), :] = value[
                :FIELDS, t * lanes : (t + 1) * lanes
            ]

    def send_off(n):
        rows = AT_ONCE * FIELDS * tiles
        part = pl.ds(pl.multiple_of(n * rows, 8), rows)
        return pltpu.make_async_copy(out_ref.at[part], out_hbm.at[part], done.at[n])

    @pl.loop(0, owners // AT_ONCE)
    def _(n):
        for i in range(AT_ONCE):
            one_owner(n * AT_ONCE + i)
        send_off(n).start()

    @pl.loop(0, owners // AT_ONCE)
    def _(n):
        send_off(n).wait()


def gather_call(fields, index, weight):
    owners = index.shape[1] // SPAN
    rows = FIELDS * index.shape[1] // 128
    return pl.pallas_call(
        gather_kernel,
        out_shape=jax.ShapeDtypeStruct((rows, 128), F32),
        in_specs=[pl.BlockSpec(memory_space=pltpu.HBM)] * 3,
        out_specs=pl.BlockSpec(memory_space=pltpu.HBM),
        scratch_shapes=[
            pltpu.VMEM((fields.shape[1] // WIDE * 8, WIDE), F32),
            pltpu.VMEM(fields.shape, F32),
            pltpu.VMEM(index.shape, jnp.int32),
            pltpu.VMEM(weight.shape, F32),
            pltpu.VMEM((rows, 128), F32),
            pltpu.SemaphoreType.DMA((3,)),
            pltpu.SemaphoreType.DMA((owners // AT_ONCE,)),
        ],
        compiler_params=pltpu.CompilerParams(vmem_limit_bytes=60 << 20),
    )(fields, index, weight)


def scatter_kernel(value_ref, target_ref, mass_ref, v_ref, even_ref, odd_ref, total):
    lanes = value_ref.shape[1]
    tiles = SPAN // lanes
    owners = target_ref.shape[1] // SPAN
    span = TOGETHER * SPAN
    hx, hy, hz = mass_ref.shape
    groups = hx * hy * hz // WIDE
    total[...] = jnp.zeros_like(total)
    ids = row_ids(WIDE, span).astype(F32).astype(BF16)
    group_ids = row_ids(groups, span).astype(F32).astype(BF16)

    @pl.loop(0, owners // TOGETHER)
    def _(p):
        at = pl.multiple_of(p * span, span)
        target = target_ref[:, pl.ds(at, span)]
        low = ((target >> log2(groups * hz)) << log2(hz)) + (target & (hz - 1))
        onehot = low_onehot(jnp.where(target < 0, -1, low), ids)
        group = ((target >> log2(hz)) & (groups - 1)).astype(F32).astype(BF16)
        here = group_ids == group
        row = p * (TOGETHER * FIELDS * tiles)
        pieces = [i * FIELDS * tiles + t for i in range(TOGETHER) for t in range(tiles)]
        value = jnp.concatenate([value_ref[pl.ds(row + i, FIELDS, stride=tiles), :] for i in pieces], axis=1)
        parts = []
        for half in halves(value):
            for f in range(FIELDS):
                parts.append(jnp.where(here, half[f : f + 1], jnp.zeros((), BF16)))
        spread = jnp.concatenate(parts, axis=0)
        total[...] += lax.dot_general(spread, onehot, NT, preferred_element_type=F32)

    odd_ref[FIELDS * hx] = jnp.zeros((ITERS, hz), F32)
    scale = lax.rsqrt(mass_ref[...])
    half_x = hx // 2
    odd = lax.axis_index("tgt") % 2 == 1
    for f in range(FIELDS):
        s = total[f * groups : (f + 1) * groups] + total[(FIELDS + f) * groups : (FIELDS + f + 1) * groups]
        for b in range(2):
            for x in range(half_x):
                at = b * half_x + x
                v = s[x * hy : (x + 1) * hy, b * hz : (b + 1) * hz] * scale[at]
                v_ref[f, at] = v
                first, last = v[:ITERS], v[hy - ITERS :]
                even_ref[f * hx + at] = jnp.where(odd, first, last)
                odd_ref[f * hx + at] = jnp.where(odd, last, first)


def scatter_call(values, target, mass):
    hx, hy, hz = mass.shape
    groups = hx * hy * hz // WIDE
    even = jax.ShapeDtypeStruct((FIELDS * hx, ITERS, hz), F32)
    odd = jax.ShapeDtypeStruct((FIELDS * hx + 1, ITERS, hz), F32)
    return pl.pallas_call(
        scatter_kernel,
        out_shape=(jax.ShapeDtypeStruct((FIELDS, hx, hy, hz), F32), even, odd),
        in_specs=[pl.BlockSpec(memory_space=pltpu.VMEM)] * 3,
        out_specs=(pl.BlockSpec(memory_space=pltpu.VMEM),) * 3,
        scratch_shapes=[pltpu.VMEM((2 * FIELDS * groups, WIDE), F32)],
        compiler_params=pltpu.CompilerParams(vmem_limit_bytes=40 << 20),
    )(values, target, mass)


def lookup_rows(table, index, ids, group_ids, groups, at_parts):
    group, low = at_parts(index)
    got = jnp.dot(table, low_onehot(low, ids), preferred_element_type=F32)
    here = group_ids == group
    rows = 3 * groups
    out = []
    for m in range(3):
        part = got[m * groups : (m + 1) * groups] + got[rows + m * groups : rows + (m + 1) * groups]
        out.append(jnp.sum(jnp.where(here, part, 0.0), axis=0, keepdims=True))
    return out


def cell_moduli(vals):
    phi = vals[0]
    mean = (vals[1] + vals[2] + vals[3]) / 3.0
    q2 = 1.5 * (
        (vals[1] - mean) ** 2
        + (vals[2] - mean) ** 2
        + (vals[3] - mean) ** 2
        + 2.0 * (vals[4] ** 2 + vals[5] ** 2 + vals[6] ** 2)
    )
    bulk = 1.6 * jnp.exp(-3.0 * phi) * (1.0 + 0.25 * jnp.tanh(mean))
    shear = 0.9 * jnp.exp(-2.0 * phi) / (1.0 + q2 / 0.5)
    soften = shear * q2 / (0.5 + q2)
    return [bulk, shear, soften]


def widen_kernel(v_ref, even_ref, odd_ref, wide_ref, to_even_ref, to_odd_ref):
    hx, hy = v_ref.shape[1], v_ref.shape[2]
    own = hx * hy
    b_odd = lax.axis_index("tgt") % 2 == 1
    a_odd = lax.axis_index("src") % 2 == 1
    line = row_ids(2 * ITERS, v_ref.shape[3])
    for f in range(FIELDS):
        sides = []
        for x in range(hx):
            even_side, odd_side = even_ref[f * hx + x], odd_ref[f * hx + x]
            right = jnp.where(b_odd, odd_side, even_side)
            left = jnp.where(b_odd, even_side, odd_side)
            sides.append(jnp.concatenate([right, left], axis=0))
            wide_ref[f, x, :hy] = v_ref[f, x]
            wide_ref[f, x, hy:] = sides[x]
            to_even_ref[f, x * hy : (x + 1) * hy] = v_ref[f, x]
            to_odd_ref[f, x * hy : (x + 1) * hy] = v_ref[f, x]
        extra = []
        for first, second, third in ((sides[hx - 1], sides[hx - 2], sides[hx - 3]), (sides[0], sides[1], sides[2])):
            near = pltpu.roll(second, 2, 0)
            far = jnp.where(line == 4, pltpu.roll(third, 4, 0), pltpu.roll(third, 6, 0))
            extra.append((first, jnp.where(line < 4, near, far)))
        at = own + 2 * ITERS
        to_even_ref[f, own:at] = jnp.where(a_odd, extra[1][0], extra[0][0])
        to_odd_ref[f, own:at] = jnp.where(a_odd, extra[0][0], extra[1][0])
        to_even_ref[f, at : at + 6] = jnp.where(a_odd, extra[1][1], extra[0][1])[:6]
        to_odd_ref[f, at : at + 8] = jnp.where(a_odd, extra[0][1], extra[1][1])


def widen_call(v, even, odd):
    fields, hx, hy, hz = v.shape
    even_rows = jax.ShapeDtypeStruct((fields, hx * hy + 4 * ITERS - 2, hz), F32)
    odd_rows = jax.ShapeDtypeStruct((fields, hx * hy + 4 * ITERS, hz), F32)
    return pl.pallas_call(
        widen_kernel,
        out_shape=(jax.ShapeDtypeStruct((fields, hx, hy + 2 * ITERS, hz), F32), even_rows, odd_rows),
        in_specs=[pl.BlockSpec(memory_space=pltpu.VMEM)] * 3,
        out_specs=(pl.BlockSpec(memory_space=pltpu.VMEM),) * 3,
        compiler_params=pltpu.CompilerParams(vmem_limit_bytes=40 << 20),
    )(v, even, odd)


def solve_kernel(mesh_shape, wide_ref, even_ref, odd_ref, mass_ref, order_ref, projected_ref, out_ref):
    n_src, n_tgt = mesh_shape
    hx, hy, hz = mass_ref.shape
    k = ITERS
    rows = hy + 2 * k
    a, b = lax.axis_index("src"), lax.axis_index("tgt")

    def exists(flag):
        return jnp.where(flag, 1.0, 0.0).astype(F32)

    row = row_ids(rows, hz)
    lane = lax.broadcasted_iota(jnp.int32, (rows, hz), 1)
    inside = jnp.where(row < hy, 1.0, jnp.where(row < hy + k, exists(b < n_tgt - 1), exists(b > 0)))
    inside_left = inside * exists(a > 0)
    inside_right = inside * exists(a < n_src - 1)
    not_first = jnp.where(lane == 0, 0.0, 1.0)
    not_last = jnp.where(lane == hz - 1, 0.0, 1.0)
    scale = lax.rsqrt(mass_ref[...])

    line = row_ids(2 * k, hz)

    def slabs(payload, from_left):
        first = payload[hx * hy : hx * hy + 2 * k]
        packed = payload[hx * hy + 2 * k :]
        second = pltpu.roll(packed, 6, 0)
        third = jnp.where(line < 4, pltpu.roll(packed, 4, 0), pltpu.roll(packed, 2, 0))
        sides = [first, second, third] + [jnp.zeros((2 * k, hz), F32)] * (hx - 3)
        order = reversed(sides) if from_left else sides
        return [jnp.concatenate([payload[x * hy : (x + 1) * hy], side], axis=0) for x, side in enumerate(order)]

    @pl.loop(0, FIELDS)
    def _(f):
        even, odd = jnp.concatenate([even_ref[f], jnp.zeros((2, hz), F32)], axis=0), odd_ref[f]
        left = slabs(jnp.where(a % 2 == 1, even, odd), True)
        right = slabs(jnp.where(a % 2 == 1, odd, even), False)
        base = left + [wide_ref[f, x] for x in range(hx)] + right
        u = [COEFS[k] * e for e in base]
        for sweep in range(1, k + 1):
            new = list(u)
            for x in range(sweep, hx + 2 * k - sweep):
                w = u[x]
                near = u[x - 1] + u[x + 1]
                near = near + pltpu.roll(w, 1, 0) + pltpu.roll(w, rows - 1, 0)
                near = near + pltpu.roll(w, 1, 1) * not_first + pltpu.roll(w, hz - 1, 1) * not_last
                if x < k:
                    near = near * inside_left
                elif x < k + hx:
                    near = near * inside
                else:
                    near = near * inside_right
                new[x] = COEFS[k - sweep] * base[x] + near
            u = new
        for x in range(hx):
            projected_ref[f, x] = u[k + x][:hy] * scale[x]

    groups = hx * hy * hz // WIDE
    payload = cell_moduli([projected_ref[f].reshape(hx * hy, hz) for f in range(FIELDS)])
    table = jnp.concatenate([jnp.concatenate([m[:groups], m[groups:]], axis=1) for m in payload], axis=0)
    table = jnp.concatenate(halves(table), axis=0)
    ids = row_ids(WIDE, WIDE).astype(F32).astype(BF16)
    group_ids = row_ids(groups, WIDE)

    def at_parts(index):
        return (index >> log2(hz)) & (groups - 1), ((index >> log2(groups * hz)) << log2(hz)) + (index & (hz - 1))

    @pl.loop(0, groups // 4)
    def _(q):
        lines = []
        for i in range(4):
            index = order_ref[:, pl.ds(pl.multiple_of((q * 4 + i) * WIDE, WIDE), WIDE)]
            got = lookup_rows(table, index, ids, group_ids, groups, at_parts)
            lines += [line[:, c * 128 : (c + 1) * 128] for line in got for c in range(2)]
        out_ref[pl.ds(pl.multiple_of(q * 24, 8), 24), :] = jnp.concatenate(lines, axis=0)


def solve_call(mesh_shape, wide, even, odd, mass, order):
    hx, hy, hz = mass.shape

    def kernel(*refs):
        solve_kernel(mesh_shape, *refs)

    return pl.pallas_call(
        kernel,
        out_shape=(
            jax.ShapeDtypeStruct((FIELDS, hx, hy, hz), F32),
            jax.ShapeDtypeStruct((order.shape[1] // WIDE * 6, 128), F32),
        ),
        in_specs=[pl.BlockSpec(memory_space=pltpu.VMEM)] * 5,
        out_specs=(pl.BlockSpec(memory_space=pltpu.VMEM),) * 2,
        compiler_params=pltpu.CompilerParams(vmem_limit_bytes=40 << 20),
    )(wide, even, odd, mass, order)


def place_kernel(arrived_ref, order_ref, out_ref):
    groups = arrived_ref.shape[0] // 6
    table = jnp.concatenate(
        [
            jnp.concatenate([arrived_ref[pl.ds(2 * m + c, groups, stride=6), :] for c in range(2)], axis=1)
            for m in range(3)
        ],
        axis=0,
    )
    table = jnp.concatenate(halves(table), axis=0)
    ids = row_ids(WIDE, WIDE).astype(F32).astype(BF16)
    group_ids = row_ids(groups, WIDE)

    @pl.loop(0, groups, unroll=8)
    def _(q):
        at = pl.ds(pl.multiple_of(q * WIDE, WIDE), WIDE)
        got = lookup_rows(
            table, order_ref[:, at], ids, group_ids, groups, lambda index: (index >> log2(WIDE), index & (WIDE - 1))
        )
        out_ref[:, at] = jnp.concatenate(got, axis=0)


def place_call(arrived, order):
    return pl.pallas_call(
        place_kernel,
        out_shape=jax.ShapeDtypeStruct((3, order.shape[1]), F32),
        in_specs=[pl.BlockSpec(memory_space=pltpu.VMEM)] * 2,
        out_specs=pl.BlockSpec(memory_space=pltpu.VMEM),
        compiler_params=pltpu.CompilerParams(vmem_limit_bytes=40 << 20),
    )(arrived, order)


def swap(x, axis):
    count = lax.axis_size(axis)
    out = []
    for start, part in enumerate(x):
        pairs = [(i, i + 1) for i in range(start, count - 1, 2)]
        out.append(lax.ppermute(part, axis, pairs + [(j, i) for i, j in pairs]))
    return out


def on_device(source_fields, slot_source, slot_weight, slot_target, cell_mass, send_order, place_order):
    n_src, n_tgt = lax.axis_size("src"), lax.axis_size("tgt")
    both = ("src", "tgt")
    owners = n_src * n_tgt
    cells = cell_mass.size
    quota = cells // owners

    values = gather_call(source_fields, slot_source.reshape(1, -1), slot_weight.reshape(1, -1))
    values = values.reshape(owners, FIELDS, SPAN // 128, 128)
    values = lax.all_to_all(values, both, split_axis=0, concat_axis=0, tiled=True).reshape(-1, 128)
    v, even, odd = scatter_call(values, slot_target.reshape(1, -1), cell_mass)
    wide, even, odd = widen_call(v, *swap((even, odd), "tgt"))
    projected, outgoing = solve_call((n_src, n_tgt), wide, *swap((even, odd), "src"), cell_mass, send_order)

    if quota == WIDE:
        outgoing = outgoing.reshape(owners, 3, 2, 128)
        incoming = lax.all_to_all(outgoing, both, split_axis=0, concat_axis=0, tiled=True)
    else:
        groups = cells // WIDE
        flat = outgoing.reshape(groups, 3, WIDE).transpose(1, 0, 2).reshape(3, owners, quota)
        flat = lax.all_to_all(flat, both, split_axis=1, concat_axis=1, tiled=True)
        incoming = flat.reshape(3, groups, WIDE).transpose(1, 0, 2)
    incoming = incoming.reshape(-1, 128)
    return projected, place_call(incoming, place_order)


def solution(mesh):
    split = P(("src", "tgt"))
    rows = P(("src", "tgt"), None)
    return jax.shard_map(
        on_device,
        mesh=mesh,
        in_specs=(P(None, ("src", "tgt")), split, split, split, P("src", "tgt", None), rows, rows),
        out_specs=(P(None, "src", "tgt", None), P(None, ("src", "tgt"))),
        check_vma=False,
    )
```

```python
import functools

import numpy as np

import jax
import jax.numpy as jnp
from jax import lax
from jax.experimental import pallas as pl
from jax.experimental.pallas import tpu as pltpu
from jax.sharding import PartitionSpec as P

ITERS = 4
FIELDS = 7
HALVES = 2
SPAN = 512
AT_ONCE = 8
TOGETHER = 8
WIDE = 256
BF16 = jnp.bfloat16
F32 = jnp.float32
NT = (((1,), (1,)), ((), ()))


def sweep_polynomial(iters, theta, delta):
    sigma = theta / delta
    rho = 1.0 / sigma
    mass = np.array([1.0, 0.125])
    poly = np.polynomial.polynomial
    resid = np.array([1.0])
    step = resid / theta
    total = np.array([0.0])
    for _ in range(iters):
        total = poly.polyadd(total, step)
        resid = poly.polysub(resid, poly.polymul(mass, step))
        rho_new = 1.0 / (2.0 * sigma - rho)
        step = poly.polyadd(rho_new * rho * step, 2.0 * rho_new / delta * resid)
        rho = rho_new
    return [float(c) for c in poly.polyadd(total, step)]


COEFS = sweep_polynomial(ITERS, 1.0, 0.75)


def halves(x):
    high = x.astype(BF16)
    return high, (x - high.astype(F32)).astype(BF16)


def log2(n):
    assert n & (n - 1) == 0
    return n.bit_length() - 1


def cost(flops):
    return pl.CostEstimate(flops=flops, bytes_accessed=1 << 20, transcendentals=0)


def row_ids(rows, lanes):
    return lax.broadcasted_iota(jnp.int32, (rows, lanes), 0)


def low_onehot(low, ids):
    return jnp.where(ids == low.astype(F32).astype(BF16), jnp.ones((), BF16), jnp.zeros((), BF16))


def gather_kernel(first, fields_hbm, index_hbm, weight_hbm, out_hbm, table, fields_ref, index_ref, weight_ref, out_ref, sems, done):
    pairs = ((fields_hbm, fields_ref), (index_hbm, index_ref), (weight_hbm, weight_ref))
    copies = [pltpu.make_async_copy(src, dst, sems.at[i]) for i, (src, dst) in enumerate(pairs)]
    for copy in copies:
        copy.start()
    lanes = out_ref.shape[1]
    span = SPAN // HALVES
    tiles = span // lanes
    owners = index_ref.shape[1] // SPAN
    groups = fields_ref.shape[1] // WIDE
    table[...] = jnp.zeros_like(table)
    for copy in copies:
        copy.wait()
    for g in range(groups):
        table[g * 8 : g * 8 + FIELDS, :] = fields_ref[:, g * WIDE : (g + 1) * WIDE]
    high, low = halves(table[...])
    both = jnp.concatenate([high, low], axis=0)
    ids = row_ids(WIDE, span).astype(F32).astype(BF16)
    rows = groups * 8

    def one_owner(q):
        at = pl.multiple_of(q * SPAN + first, span)
        index = index_ref[:, pl.ds(at, span)]
        weight = weight_ref[:, pl.ds(at, span)]
        onehot = low_onehot(index & (WIDE - 1), ids)
        got = jnp.dot(both, onehot, preferred_element_type=F32)
        group = jnp.broadcast_to(index >> log2(WIDE), (8, span))
        value = jnp.zeros((8, span), F32)
        for g in range(groups):
            part = got[g * 8 : (g + 1) * 8] + got[rows + g * 8 : rows + (g + 1) * 8]
            value = jnp.where(group == g, part, value)
        value = value * weight
        for t in range(tiles):
            out_ref[pl.ds(q * (FIELDS * tiles) + t, FIELDS, stride=tiles), :] = value[
                :FIELDS, t * lanes : (t + 1) * lanes
            ]

    def send_off(n):
        rows = AT_ONCE * FIELDS * tiles
        part = pl.ds(pl.multiple_of(n * rows, 8), rows)
        return pltpu.make_async_copy(out_ref.at[part], out_hbm.at[part], done.at[n])

    @pl.loop(0, owners // AT_ONCE)
    def _(n):
        for i in range(AT_ONCE):
            one_owner(n * AT_ONCE + i)
        send_off(n).start()

    @pl.loop(0, owners // AT_ONCE)
    def _(n):
        send_off(n).wait()


def gather_call(fields, index, weight, half):
    owners = index.shape[1] // SPAN
    rows = FIELDS * index.shape[1] // HALVES // 128
    return pl.pallas_call(
        functools.partial(gather_kernel, half * SPAN // HALVES),
        out_shape=jax.ShapeDtypeStruct((rows, 128), F32),
        in_specs=[pl.BlockSpec(memory_space=pltpu.HBM)] * 3,
        out_specs=pl.BlockSpec(memory_space=pltpu.HBM),
        scratch_shapes=[
            pltpu.VMEM((fields.shape[1] // WIDE * 8, WIDE), F32),
            pltpu.VMEM(fields.shape, F32),
            pltpu.VMEM(index.shape, jnp.int32),
            pltpu.VMEM(weight.shape, F32),
            pltpu.VMEM((rows, 128), F32),
            pltpu.SemaphoreType.DMA((3,)),
            pltpu.SemaphoreType.DMA((owners // AT_ONCE,)),
        ],
        compiler_params=pltpu.CompilerParams(vmem_limit_bytes=60 << 20),
        cost_estimate=cost(2 * 2 * 8 * fields.shape[1] * index.shape[1] // HALVES),
    )(fields, index, weight)


def add_slots(first, value_ref, target_ref, total, groups, hz):
    lanes = value_ref.shape[1]
    part = SPAN // HALVES
    tiles = part // lanes
    owners = target_ref.shape[1] // SPAN
    total[...] = jnp.zeros_like(total)
    ids = row_ids(WIDE, TOGETHER * part).astype(F32).astype(BF16)
    group_ids = row_ids(groups, TOGETHER * part).astype(F32).astype(BF16)

    @pl.loop(0, owners // TOGETHER)
    def _(p):
        starts = [pl.multiple_of((p * TOGETHER + i) * SPAN + first, part) for i in range(TOGETHER)]
        target = jnp.concatenate([target_ref[:, pl.ds(at, part)] for at in starts], axis=1)
        low = ((target >> log2(groups * hz)) << log2(hz)) + (target & (hz - 1))
        onehot = low_onehot(jnp.where(target < 0, -1, low), ids)
        group = ((target >> log2(hz)) & (groups - 1)).astype(F32).astype(BF16)
        here = group_ids == group
        row = p * (TOGETHER * FIELDS * tiles)
        pieces = [i * FIELDS * tiles + t for i in range(TOGETHER) for t in range(tiles)]
        value = jnp.concatenate([value_ref[pl.ds(row + i, FIELDS, stride=tiles), :] for i in pieces], axis=1)
        parts = []
        for half in halves(value):
            for f in range(FIELDS):
                parts.append(jnp.where(here, half[f : f + 1], jnp.zeros((), BF16)))
        spread = jnp.concatenate(parts, axis=0)
        total[...] += lax.dot_general(spread, onehot, NT, preferred_element_type=F32)


def first_sums_kernel(hz, value_ref, target_ref, total_ref):
    add_slots(0, value_ref, target_ref, total_ref, total_ref.shape[0] // (2 * FIELDS), hz)


def first_sums_call(values, target, mass):
    return pl.pallas_call(
        functools.partial(first_sums_kernel, mass.shape[2]),
        out_shape=jax.ShapeDtypeStruct((2 * FIELDS * mass.size // WIDE, WIDE), F32),
        in_specs=[pl.BlockSpec(memory_space=pltpu.VMEM)] * 2,
        out_specs=pl.BlockSpec(memory_space=pltpu.VMEM),
        compiler_params=pltpu.CompilerParams(vmem_limit_bytes=40 << 20),
        cost_estimate=cost(4 * FIELDS * mass.size * target.shape[1] // HALVES),
    )(values, target)


def scatter_kernel(value_ref, target_ref, before_ref, mass_ref, v_ref, even_ref, odd_ref, total):
    hx, hy, hz = mass_ref.shape
    groups = hx * hy * hz // WIDE
    add_slots(SPAN // HALVES, value_ref, target_ref, total, groups, hz)
    total[...] += before_ref[...]
    scale = lax.rsqrt(mass_ref[...])
    half_x = hx // 2
    odd = lax.axis_index("tgt") % 2 == 1
    for f in range(FIELDS):
        s = total[f * groups : (f + 1) * groups] + total[(FIELDS + f) * groups : (FIELDS + f + 1) * groups]
        for b in range(2):
            for x in range(half_x):
                at = b * half_x + x
                v = s[x * hy : (x + 1) * hy, b * hz : (b + 1) * hz] * scale[at]
                v_ref[f, at] = v
                first, last = v[:ITERS], v[hy - ITERS :]
                even_ref[f * hx + at] = jnp.where(odd, first, last)
                odd_ref[f * hx + at] = jnp.where(odd, last, first)


def scatter_call(values, target, before, mass):
    hx, hy, hz = mass.shape
    groups = hx * hy * hz // WIDE
    even = jax.ShapeDtypeStruct((FIELDS * hx, ITERS, hz), F32)
    odd = jax.ShapeDtypeStruct((FIELDS * hx + 1, ITERS, hz), F32)
    return pl.pallas_call(
        scatter_kernel,
        out_shape=(jax.ShapeDtypeStruct((FIELDS, hx, hy, hz), F32), even, odd),
        in_specs=[pl.BlockSpec(memory_space=pltpu.VMEM)] * 4,
        out_specs=(pl.BlockSpec(memory_space=pltpu.VMEM),) * 3,
        scratch_shapes=[pltpu.VMEM((2 * FIELDS * groups, WIDE), F32)],
        compiler_params=pltpu.CompilerParams(vmem_limit_bytes=40 << 20),
        cost_estimate=cost(4 * FIELDS * mass.size * target.shape[1] // HALVES),
    )(values, target, before, mass)


def lookup_rows(table, index, ids, group_ids, groups, at_parts):
    group, low = at_parts(index)
    got = jnp.dot(table, low_onehot(low, ids), preferred_element_type=F32)
    here = group_ids == group
    rows = 3 * groups
    out = []
    for m in range(3):
        part = got[m * groups : (m + 1) * groups] + got[rows + m * groups : rows + (m + 1) * groups]
        out.append(jnp.sum(jnp.where(here, part, 0.0), axis=0, keepdims=True))
    return out


def cell_moduli(vals):
    phi = vals[0]
    mean = (vals[1] + vals[2] + vals[3]) / 3.0
    q2 = 1.5 * (
        (vals[1] - mean) ** 2
        + (vals[2] - mean) ** 2
        + (vals[3] - mean) ** 2
        + 2.0 * (vals[4] ** 2 + vals[5] ** 2 + vals[6] ** 2)
    )
    bulk = 1.6 * jnp.exp(-3.0 * phi) * (1.0 + 0.25 * jnp.tanh(mean))
    shear = 0.9 * jnp.exp(-2.0 * phi) / (1.0 + q2 / 0.5)
    soften = shear * q2 / (0.5 + q2)
    return [bulk, shear, soften]


def widen_kernel(v_ref, even_ref, odd_ref, wide_ref, to_even_ref, to_odd_ref):
    hx, hy = v_ref.shape[1], v_ref.shape[2]
    own = hx * hy
    b_odd = lax.axis_index("tgt") % 2 == 1
    a_odd = lax.axis_index("src") % 2 == 1
    line = row_ids(2 * ITERS, v_ref.shape[3])
    for f in range(FIELDS):
        sides = []
        for x in range(hx):
            even_side, odd_side = even_ref[f * hx + x], odd_ref[f * hx + x]
            right = jnp.where(b_odd, odd_side, even_side)
            left = jnp.where(b_odd, even_side, odd_side)
            sides.append(jnp.concatenate([right, left], axis=0))
            wide_ref[f, x, :hy] = v_ref[f, x]
            wide_ref[f, x, hy:] = sides[x]
            to_even_ref[f, x * hy : (x + 1) * hy] = v_ref[f, x]
            to_odd_ref[f, x * hy : (x + 1) * hy] = v_ref[f, x]
        extra = []
        for first, second, third in ((sides[hx - 1], sides[hx - 2], sides[hx - 3]), (sides[0], sides[1], sides[2])):
            near = pltpu.roll(second, 2, 0)
            far = jnp.where(line == 4, pltpu.roll(third, 4, 0), pltpu.roll(third, 6, 0))
            extra.append((first, jnp.where(line < 4, near, far)))
        at = own + 2 * ITERS
        to_even_ref[f, own:at] = jnp.where(a_odd, extra[1][0], extra[0][0])
        to_odd_ref[f, own:at] = jnp.where(a_odd, extra[0][0], extra[1][0])
        to_even_ref[f, at : at + 6] = jnp.where(a_odd, extra[1][1], extra[0][1])[:6]
        to_odd_ref[f, at : at + 8] = jnp.where(a_odd, extra[0][1], extra[1][1])


def widen_call(v, even, odd):
    fields, hx, hy, hz = v.shape
    even_rows = jax.ShapeDtypeStruct((fields, hx * hy + 4 * ITERS - 2, hz), F32)
    odd_rows = jax.ShapeDtypeStruct((fields, hx * hy + 4 * ITERS, hz), F32)
    return pl.pallas_call(
        widen_kernel,
        out_shape=(jax.ShapeDtypeStruct((fields, hx, hy + 2 * ITERS, hz), F32), even_rows, odd_rows),
        in_specs=[pl.BlockSpec(memory_space=pltpu.VMEM)] * 3,
        out_specs=(pl.BlockSpec(memory_space=pltpu.VMEM),) * 3,
        compiler_params=pltpu.CompilerParams(vmem_limit_bytes=40 << 20),
    )(v, even, odd)


def solve_kernel(mesh_shape, wide_ref, even_ref, odd_ref, mass_ref, order_ref, projected_ref, out_ref):
    n_src, n_tgt = mesh_shape
    hx, hy, hz = mass_ref.shape
    k = ITERS
    rows = hy + 2 * k
    a, b = lax.axis_index("src"), lax.axis_index("tgt")

    def exists(flag):
        return jnp.where(flag, 1.0, 0.0).astype(F32)

    row = row_ids(rows, hz)
    lane = lax.broadcasted_iota(jnp.int32, (rows, hz), 1)
    inside = jnp.where(row < hy, 1.0, jnp.where(row < hy + k, exists(b < n_tgt - 1), exists(b > 0)))
    inside_left = inside * exists(a > 0)
    inside_right = inside * exists(a < n_src - 1)
    not_first = jnp.where(lane == 0, 0.0, 1.0)
    not_last = jnp.where(lane == hz - 1, 0.0, 1.0)
    scale = lax.rsqrt(mass_ref[...])

    line = row_ids(2 * k, hz)

    def slabs(payload, from_left):
        first = payload[hx * hy : hx * hy + 2 * k]
        packed = payload[hx * hy + 2 * k :]
        second = pltpu.roll(packed, 6, 0)
        third = jnp.where(line < 4, pltpu.roll(packed, 4, 0), pltpu.roll(packed, 2, 0))
        sides = [first, second, third] + [jnp.zeros((2 * k, hz), F32)] * (hx - 3)
        order = reversed(sides) if from_left else sides
        return [jnp.concatenate([payload[x * hy : (x + 1) * hy], side], axis=0) for x, side in enumerate(order)]

    @pl.loop(0, FIELDS)
    def _(f):
        even, odd = jnp.concatenate([even_ref[f], jnp.zeros((2, hz), F32)], axis=0), odd_ref[f]
        left = slabs(jnp.where(a % 2 == 1, even, odd), True)
        right = slabs(jnp.where(a % 2 == 1, odd, even), False)
        base = left + [wide_ref[f, x] for x in range(hx)] + right
        u = [COEFS[k] * e for e in base]
        for sweep in range(1, k + 1):
            new = list(u)
            for x in range(sweep, hx + 2 * k - sweep):
                w = u[x]
                near = u[x - 1] + u[x + 1]
                near = near + pltpu.roll(w, 1, 0) + pltpu.roll(w, rows - 1, 0)
                near = near + pltpu.roll(w, 1, 1) * not_first + pltpu.roll(w, hz - 1, 1) * not_last
                if x < k:
                    near = near * inside_left
                elif x < k + hx:
                    near = near * inside
                else:
                    near = near * inside_right
                new[x] = COEFS[k - sweep] * base[x] + near
            u = new
        for x in range(hx):
            projected_ref[f, x] = u[k + x][:hy] * scale[x]

    groups = hx * hy * hz // WIDE
    payload = cell_moduli([projected_ref[f].reshape(hx * hy, hz) for f in range(FIELDS)])
    table = jnp.concatenate([jnp.concatenate([m[:groups], m[groups:]], axis=1) for m in payload], axis=0)
    table = jnp.concatenate(halves(table), axis=0)
    ids = row_ids(WIDE, WIDE).astype(F32).astype(BF16)
    group_ids = row_ids(groups, WIDE)

    def at_parts(index):
        return (index >> log2(hz)) & (groups - 1), ((index >> log2(groups * hz)) << log2(hz)) + (index & (hz - 1))

    @pl.loop(0, groups // 8)
    def _(q):
        lines = []
        for i in range(8):
            index = order_ref[:, pl.ds(pl.multiple_of((q * 8 + i) * WIDE, WIDE), WIDE)]
            got = lookup_rows(table, index, ids, group_ids, groups, at_parts)
            lines += [line[:, c * 128 : (c + 1) * 128] for line in got for c in range(2)]
        out_ref[pl.ds(pl.multiple_of(q * 48, 8), 48), :] = jnp.concatenate(lines, axis=0)


def solve_call(mesh_shape, wide, even, odd, mass, order):
    hx, hy, hz = mass.shape

    def kernel(*refs):
        solve_kernel(mesh_shape, *refs)

    return pl.pallas_call(
        kernel,
        out_shape=(
            jax.ShapeDtypeStruct((FIELDS, hx, hy, hz), F32),
            jax.ShapeDtypeStruct((order.shape[1] // WIDE * 6, 128), F32),
        ),
        in_specs=[pl.BlockSpec(memory_space=pltpu.VMEM)] * 5,
        out_specs=(pl.BlockSpec(memory_space=pltpu.VMEM),) * 2,
        compiler_params=pltpu.CompilerParams(vmem_limit_bytes=40 << 20),
    )(wide, even, odd, mass, order)


def place_kernel(arrived_ref, order_ref, out_ref):
    groups = arrived_ref.shape[0] // 6
    table = jnp.concatenate(
        [
            jnp.concatenate([arrived_ref[pl.ds(2 * m + c, groups, stride=6), :] for c in range(2)], axis=1)
            for m in range(3)
        ],
        axis=0,
    )
    table = jnp.concatenate(halves(table), axis=0)
    ids = row_ids(WIDE, WIDE).astype(F32).astype(BF16)
    group_ids = row_ids(groups, WIDE)

    @pl.loop(0, groups, unroll=8)
    def _(q):
        at = pl.ds(pl.multiple_of(q * WIDE, WIDE), WIDE)
        got = lookup_rows(
            table, order_ref[:, at], ids, group_ids, groups, lambda index: (index >> log2(WIDE), index & (WIDE - 1))
        )
        out_ref[:, at] = jnp.concatenate(got, axis=0)


def place_call(arrived, order):
    return pl.pallas_call(
        place_kernel,
        out_shape=jax.ShapeDtypeStruct((3, order.shape[1]), F32),
        in_specs=[pl.BlockSpec(memory_space=pltpu.VMEM)] * 2,
        out_specs=pl.BlockSpec(memory_space=pltpu.VMEM),
        compiler_params=pltpu.CompilerParams(vmem_limit_bytes=40 << 20),
    )(arrived, order)


def swap(x, axis):
    count = lax.axis_size(axis)
    out = []
    for start, part in enumerate(x):
        pairs = [(i, i + 1) for i in range(start, count - 1, 2)]
        out.append(lax.ppermute(part, axis, pairs + [(j, i) for i, j in pairs]))
    return out


def on_device(source_fields, slot_source, slot_weight, slot_target, cell_mass, send_order, place_order):
    n_src, n_tgt = lax.axis_size("src"), lax.axis_size("tgt")
    both = ("src", "tgt")
    owners = n_src * n_tgt
    cells = cell_mass.size
    quota = cells // owners

    arrived = []
    for half in range(HALVES):
        values = gather_call(source_fields, slot_source.reshape(1, -1), slot_weight.reshape(1, -1), half)
        values = values.reshape(owners, FIELDS, SPAN // HALVES // 128, 128)
        values = lax.all_to_all(values, both, split_axis=0, concat_axis=0, tiled=True)
        arrived.append(values.reshape(-1, 128))
    target = slot_target.reshape(1, -1)
    before = first_sums_call(arrived[0], target, cell_mass)
    v, even, odd = scatter_call(arrived[1], target, before, cell_mass)
    wide, even, odd = widen_call(v, *swap((even, odd), "tgt"))
    projected, outgoing = solve_call((n_src, n_tgt), wide, *swap((even, odd), "src"), cell_mass, send_order)

    if quota == WIDE:
        outgoing = outgoing.reshape(owners, 3, 2, 128)
        incoming = lax.all_to_all(outgoing, both, split_axis=0, concat_axis=0, tiled=True)
    else:
        groups = cells // WIDE
        flat = outgoing.reshape(groups, 3, WIDE).transpose(1, 0, 2).reshape(3, owners, quota)
        flat = lax.all_to_all(flat, both, split_axis=1, concat_axis=1, tiled=True)
        incoming = flat.reshape(3, groups, WIDE).transpose(1, 0, 2)
    incoming = incoming.reshape(-1, 128)
    return projected, place_call(incoming, place_order)


def solution(mesh):
    split = P(("src", "tgt"))
    rows = P(("src", "tgt"), None)
    return jax.shard_map(
        on_device,
        mesh=mesh,
        in_specs=(P(None, ("src", "tgt")), split, split, split, P("src", "tgt", None), rows, rows),
        out_specs=(P(None, "src", "tgt", None), P(None, ("src", "tgt"))),
        check_vma=False,
    )
```

```python
import functools

import numpy as np

import jax
import jax.numpy as jnp
from jax import lax
from jax.experimental import pallas as pl
from jax.experimental.pallas import tpu as pltpu
from jax.sharding import PartitionSpec as P

ITERS = 4
FIELDS = 7
VMEM = 28 << 20
READY = 16384
SPAN = 512
AT_ONCE = 8
TOGETHER = 4
WIDE = 256
BF16 = jnp.bfloat16
F32 = jnp.float32
NT = (((1,), (1,)), ((), ()))


def sweep_polynomial(iters, theta, delta):
    sigma = theta / delta
    rho = 1.0 / sigma
    mass = np.array([1.0, 0.125])
    poly = np.polynomial.polynomial
    resid = np.array([1.0])
    step = resid / theta
    total = np.array([0.0])
    for _ in range(iters):
        total = poly.polyadd(total, step)
        resid = poly.polysub(resid, poly.polymul(mass, step))
        rho_new = 1.0 / (2.0 * sigma - rho)
        step = poly.polyadd(rho_new * rho * step, 2.0 * rho_new / delta * resid)
        rho = rho_new
    return [float(c) for c in poly.polyadd(total, step)]


COEFS = sweep_polynomial(ITERS, 1.0, 0.75)


def halves(x):
    high = x.astype(BF16)
    return high, (x - high.astype(F32)).astype(BF16)


def log2(n):
    assert n & (n - 1) == 0
    return n.bit_length() - 1


def cost(flops):
    return pl.CostEstimate(flops=flops, bytes_accessed=1 << 20, transcendentals=0)


def row_ids(rows, lanes):
    return lax.broadcasted_iota(jnp.int32, (rows, lanes), 0)


def low_onehot(low, ids):
    return jnp.where(ids == low.astype(F32).astype(BF16), jnp.ones((), BF16), jnp.zeros((), BF16))


def gather_kernel(fields_hbm, index_hbm, weight_hbm, out_hbm, table, fields_ref, index_ref, weight_ref, out_ref, sems, done):
    pairs = ((fields_hbm, fields_ref), (index_hbm, index_ref), (weight_hbm, weight_ref))
    copies = [pltpu.make_async_copy(src, dst, sems.at[i]) for i, (src, dst) in enumerate(pairs)]
    for copy in copies:
        copy.start()
    lanes = out_ref.shape[1]
    span = SPAN
    tiles = span // lanes
    owners = index_ref.shape[1] // span
    groups = fields_ref.shape[1] // WIDE
    table[...] = jnp.zeros_like(table)
    for copy in copies:
        copy.wait()
    for g in range(groups):
        table[g * 8 : g * 8 + FIELDS, :] = fields_ref[:, g * WIDE : (g + 1) * WIDE]
    high, low = halves(table[...])
    both = jnp.concatenate([high, low], axis=0)
    ids = row_ids(WIDE, span).astype(F32).astype(BF16)
    rows = groups * 8

    def one_owner(q):
        at = pl.multiple_of(q * span, span)
        index = index_ref[:, pl.ds(at, span)]
        weight = weight_ref[:, pl.ds(at, span)]
        onehot = low_onehot(index & (WIDE - 1), ids)
        got = jnp.dot(both, onehot, preferred_element_type=F32)
        group = jnp.broadcast_to(index >> log2(WIDE), (8, span))
        value = jnp.zeros((8, span), F32)
        for g in range(groups):
            part = got[g * 8 : (g + 1) * 8] + got[rows + g * 8 : rows + (g + 1) * 8]
            value = jnp.where(group == g, part, value)
        value = value * weight
        for t in range(tiles):
            out_ref[pl.ds(q * (FIELDS * tiles) + t, FIELDS, stride=tiles), :] = value[
                :FIELDS, t * lanes : (t + 1) * lanes
            ]

    def send_off(n):
        rows = AT_ONCE * FIELDS * tiles
        part = pl.ds(pl.multiple_of(n * rows, 8), rows)
        return pltpu.make_async_copy(out_ref.at[part], out_hbm.at[part], done.at[n])

    @pl.loop(0, owners // AT_ONCE)
    def _(n):
        for i in range(AT_ONCE):
            one_owner(n * AT_ONCE + i)
        send_off(n).start()

    @pl.loop(0, owners // AT_ONCE)
    def _(n):
        send_off(n).wait()


def gather_call(fields, index, weight):
    owners = index.shape[1] // SPAN
    rows = FIELDS * index.shape[1] // 128
    return pl.pallas_call(
        gather_kernel,
        out_shape=jax.ShapeDtypeStruct((rows, 128), F32),
        in_specs=[pl.BlockSpec(memory_space=pltpu.HBM)] * 3,
        out_specs=pl.BlockSpec(memory_space=pltpu.HBM),
        scratch_shapes=[
            pltpu.VMEM((fields.shape[1] // WIDE * 8, WIDE), F32),
            pltpu.VMEM(fields.shape, F32),
            pltpu.VMEM(index.shape, jnp.int32),
            pltpu.VMEM(weight.shape, F32),
            pltpu.VMEM((rows, 128), F32),
            pltpu.SemaphoreType.DMA((3,)),
            pltpu.SemaphoreType.DMA((owners // AT_ONCE,)),
        ],
        compiler_params=pltpu.CompilerParams(vmem_limit_bytes=60 << 20),
    )(fields, index, weight)


def cell_parts(cell, groups, hz):
    return (cell >> log2(hz)) & (groups - 1), ((cell >> log2(groups * hz)) << log2(hz)) + (cell & (hz - 1))


def prepare_kernel(groups, hz, target_ref, send_ref, place_ref, target_hot, send_hot, place_hot):
    span = 1024
    ids = row_ids(WIDE, span).astype(F32).astype(BF16)

    def build(index_ref, hot_ref, low_of):
        @pl.loop(0, hot_ref.shape[1] // span)
        def _(n):
            at = pl.ds(pl.multiple_of(n * span, span), span)
            hot_ref[:, at] = low_onehot(low_of(index_ref[:, at]), ids)

    def low_of_cell(cell):
        return jnp.where(cell < 0, -1, cell_parts(cell, groups, hz)[1])

    build(target_ref, target_hot, low_of_cell)
    build(send_ref, send_hot, low_of_cell)
    build(place_ref, place_hot, lambda index: index & (WIDE - 1))


def prepare_call(target, send, place, mass):
    hz = mass.shape[2]
    columns = (min(target.shape[1], READY), send.shape[1], place.shape[1])
    out = [jax.ShapeDtypeStruct((WIDE, n), BF16) for n in columns]
    return pl.pallas_call(
        functools.partial(prepare_kernel, mass.size // WIDE, hz),
        out_shape=out,
        in_specs=[pl.BlockSpec(memory_space=pltpu.VMEM)] * 3,
        out_specs=[pl.BlockSpec(memory_space=pltpu.VMEM)] * 3,
        compiler_params=pltpu.CompilerParams(vmem_limit_bytes=VMEM),
        cost_estimate=cost(4 * 10**9),
    )(target, send, place)


def scatter_kernel(value_ref, target_ref, hot_ref, mass_ref, v_ref, even_ref, odd_ref, total):
    lanes = value_ref.shape[1]
    tiles = SPAN // lanes
    owners = target_ref.shape[1] // SPAN
    span = TOGETHER * SPAN
    hx, hy, hz = mass_ref.shape
    groups = hx * hy * hz // WIDE
    total[...] = jnp.zeros_like(total)
    group_ids = row_ids(groups, span).astype(F32).astype(BF16)

    def step(p, onehot_at):
        at = pl.ds(pl.multiple_of(p * span, span), span)
        target = target_ref[:, at]
        group, low = cell_parts(target, groups, hz)
        here = group_ids == group.astype(F32).astype(BF16)
        row = p * (TOGETHER * FIELDS * tiles)
        pieces = [i * FIELDS * tiles + t for i in range(TOGETHER) for t in range(tiles)]
        value = jnp.concatenate([value_ref[pl.ds(row + i, FIELDS, stride=tiles), :] for i in pieces], axis=1)
        parts = []
        for half in halves(value):
            for f in range(FIELDS):
                parts.append(jnp.where(here, half[f : f + 1], jnp.zeros((), BF16)))
        spread = jnp.concatenate(parts, axis=0)
        onehot = onehot_at(at, jnp.where(target < 0, -1, low))
        total[...] += lax.dot_general(spread, onehot, NT, preferred_element_type=F32)

    ready = hot_ref.shape[1] // span

    @pl.loop(0, ready)
    def _(p):
        step(p, lambda at, low: hot_ref[:, at])

    if ready < owners // TOGETHER:
        ids = row_ids(WIDE, span).astype(F32).astype(BF16)

        @pl.loop(ready, owners // TOGETHER)
        def _(p):
            step(p, lambda at, low: low_onehot(low, ids))

    odd_ref[FIELDS * hx] = jnp.zeros((ITERS, hz), F32)
    scale = lax.rsqrt(mass_ref[...])
    half_x = hx // 2
    odd = lax.axis_index("tgt") % 2 == 1
    for f in range(FIELDS):
        s = total[f * groups : (f + 1) * groups] + total[(FIELDS + f) * groups : (FIELDS + f + 1) * groups]
        for b in range(2):
            for x in range(half_x):
                at = b * half_x + x
                v = s[x * hy : (x + 1) * hy, b * hz : (b + 1) * hz] * scale[at]
                v_ref[f, at] = v
                first, last = v[:ITERS], v[hy - ITERS :]
                even_ref[f * hx + at] = jnp.where(odd, first, last)
                odd_ref[f * hx + at] = jnp.where(odd, last, first)


def scatter_call(values, target, hot, mass):
    hx, hy, hz = mass.shape
    groups = hx * hy * hz // WIDE
    even = jax.ShapeDtypeStruct((FIELDS * hx, ITERS, hz), F32)
    odd = jax.ShapeDtypeStruct((FIELDS * hx + 1, ITERS, hz), F32)
    return pl.pallas_call(
        scatter_kernel,
        out_shape=(jax.ShapeDtypeStruct((FIELDS, hx, hy, hz), F32), even, odd),
        in_specs=[pl.BlockSpec(memory_space=pltpu.VMEM)] * 4,
        out_specs=(pl.BlockSpec(memory_space=pltpu.VMEM),) * 3,
        scratch_shapes=[pltpu.VMEM((2 * FIELDS * groups, WIDE), F32)],
        compiler_params=pltpu.CompilerParams(vmem_limit_bytes=VMEM),
    )(values, target, hot, mass)


def lookup_rows(table, group, hot, group_ids, groups):
    got = jnp.dot(table, hot, preferred_element_type=F32)
    here = group_ids == group
    rows = 3 * groups
    out = []
    for m in range(3):
        part = got[m * groups : (m + 1) * groups] + got[rows + m * groups : rows + (m + 1) * groups]
        out.append(jnp.sum(jnp.where(here, part, 0.0), axis=0, keepdims=True))
    return out


def cell_moduli(vals):
    phi = vals[0]
    mean = (vals[1] + vals[2] + vals[3]) / 3.0
    q2 = 1.5 * (
        (vals[1] - mean) ** 2
        + (vals[2] - mean) ** 2
        + (vals[3] - mean) ** 2
        + 2.0 * (vals[4] ** 2 + vals[5] ** 2 + vals[6] ** 2)
    )
    bulk = 1.6 * jnp.exp(-3.0 * phi) * (1.0 + 0.25 * jnp.tanh(mean))
    shear = 0.9 * jnp.exp(-2.0 * phi) / (1.0 + q2 / 0.5)
    soften = shear * q2 / (0.5 + q2)
    return [bulk, shear, soften]


def widen_kernel(v_ref, even_ref, odd_ref, wide_ref, to_even_ref, to_odd_ref):
    hx, hy = v_ref.shape[1], v_ref.shape[2]
    own = hx * hy
    b_odd = lax.axis_index("tgt") % 2 == 1
    a_odd = lax.axis_index("src") % 2 == 1
    line = row_ids(2 * ITERS, v_ref.shape[3])
    for f in range(FIELDS):
        sides = []
        for x in range(hx):
            even_side, odd_side = even_ref[f * hx + x], odd_ref[f * hx + x]
            right = jnp.where(b_odd, odd_side, even_side)
            left = jnp.where(b_odd, even_side, odd_side)
            sides.append(jnp.concatenate([right, left], axis=0))
            wide_ref[f, x, :hy] = v_ref[f, x]
            wide_ref[f, x, hy:] = sides[x]
            to_even_ref[f, x * hy : (x + 1) * hy] = v_ref[f, x]
            to_odd_ref[f, x * hy : (x + 1) * hy] = v_ref[f, x]
        extra = []
        for first, second, third in ((sides[hx - 1], sides[hx - 2], sides[hx - 3]), (sides[0], sides[1], sides[2])):
            near = pltpu.roll(second, 2, 0)
            far = jnp.where(line == 4, pltpu.roll(third, 4, 0), pltpu.roll(third, 6, 0))
            extra.append((first, jnp.where(line < 4, near, far)))
        at = own + 2 * ITERS
        to_even_ref[f, own:at] = jnp.where(a_odd, extra[1][0], extra[0][0])
        to_odd_ref[f, own:at] = jnp.where(a_odd, extra[0][0], extra[1][0])
        to_even_ref[f, at : at + 6] = jnp.where(a_odd, extra[1][1], extra[0][1])[:6]
        to_odd_ref[f, at : at + 8] = jnp.where(a_odd, extra[0][1], extra[1][1])


def widen_call(v, even, odd):
    fields, hx, hy, hz = v.shape
    even_rows = jax.ShapeDtypeStruct((fields, hx * hy + 4 * ITERS - 2, hz), F32)
    odd_rows = jax.ShapeDtypeStruct((fields, hx * hy + 4 * ITERS, hz), F32)
    return pl.pallas_call(
        widen_kernel,
        out_shape=(jax.ShapeDtypeStruct((fields, hx, hy + 2 * ITERS, hz), F32), even_rows, odd_rows),
        in_specs=[pl.BlockSpec(memory_space=pltpu.VMEM)] * 3,
        out_specs=(pl.BlockSpec(memory_space=pltpu.VMEM),) * 3,
        compiler_params=pltpu.CompilerParams(vmem_limit_bytes=VMEM),
    )(v, even, odd)


def solve_kernel(
    mesh_shape, wide_ref, even_ref, odd_ref, mass_ref, order_ref, hot_ref, projected_ref, out_ref
):
    n_src, n_tgt = mesh_shape
    hx, hy, hz = mass_ref.shape
    k = ITERS
    rows = hy + 2 * k
    a, b = lax.axis_index("src"), lax.axis_index("tgt")

    def exists(flag):
        return jnp.where(flag, 1.0, 0.0).astype(F32)

    row = row_ids(rows, hz)
    lane = lax.broadcasted_iota(jnp.int32, (rows, hz), 1)
    inside = jnp.where(row < hy, 1.0, jnp.where(row < hy + k, exists(b < n_tgt - 1), exists(b > 0)))
    inside_left = inside * exists(a > 0)
    inside_right = inside * exists(a < n_src - 1)
    not_first = jnp.where(lane == 0, 0.0, 1.0)
    not_last = jnp.where(lane == hz - 1, 0.0, 1.0)
    scale = lax.rsqrt(mass_ref[...])

    line = row_ids(2 * k, hz)

    def slabs(payload, from_left):
        first = payload[hx * hy : hx * hy + 2 * k]
        packed = payload[hx * hy + 2 * k :]
        second = pltpu.roll(packed, 6, 0)
        third = jnp.where(line < 4, pltpu.roll(packed, 4, 0), pltpu.roll(packed, 2, 0))
        sides = [first, second, third] + [jnp.zeros((2 * k, hz), F32)] * (hx - 3)
        order = reversed(sides) if from_left else sides
        return [jnp.concatenate([payload[x * hy : (x + 1) * hy], side], axis=0) for x, side in enumerate(order)]

    @pl.loop(0, FIELDS)
    def _(f):
        even, odd = jnp.concatenate([even_ref[f], jnp.zeros((2, hz), F32)], axis=0), odd_ref[f]
        left = slabs(jnp.where(a % 2 == 1, even, odd), True)
        right = slabs(jnp.where(a % 2 == 1, odd, even), False)
        base = left + [wide_ref[f, x] for x in range(hx)] + right
        u = [COEFS[k] * e for e in base]
        for sweep in range(1, k + 1):
            new = list(u)
            for x in range(sweep, hx + 2 * k - sweep):
                w = u[x]
                near = u[x - 1] + u[x + 1]
                near = near + pltpu.roll(w, 1, 0) + pltpu.roll(w, rows - 1, 0)
                near = near + pltpu.roll(w, 1, 1) * not_first + pltpu.roll(w, hz - 1, 1) * not_last
                if x < k:
                    near = near * inside_left
                elif x < k + hx:
                    near = near * inside
                else:
                    near = near * inside_right
                new[x] = COEFS[k - sweep] * base[x] + near
            u = new
        for x in range(hx):
            projected_ref[f, x] = u[k + x][:hy] * scale[x]

    groups = hx * hy * hz // WIDE
    payload = cell_moduli([projected_ref[f].reshape(hx * hy, hz) for f in range(FIELDS)])
    table = jnp.concatenate([jnp.concatenate([m[:groups], m[groups:]], axis=1) for m in payload], axis=0)
    table = jnp.concatenate(halves(table), axis=0)
    group_ids = row_ids(groups, WIDE)

    @pl.loop(0, groups // 8)
    def _(q):
        lines = []
        for i in range(8):
            at = pl.ds(pl.multiple_of((q * 8 + i) * WIDE, WIDE), WIDE)
            group, _ = cell_parts(order_ref[:, at], groups, hz)
            got = lookup_rows(table, group, hot_ref[:, at], group_ids, groups)
            lines += [line[:, c * 128 : (c + 1) * 128] for line in got for c in range(2)]
        out_ref[pl.ds(pl.multiple_of(q * 48, 8), 48), :] = jnp.concatenate(lines, axis=0)


def solve_call(mesh_shape, wide, even, odd, mass, order, hot):
    hx, hy, hz = mass.shape

    def kernel(*refs):
        solve_kernel(mesh_shape, *refs)

    return pl.pallas_call(
        kernel,
        out_shape=(
            jax.ShapeDtypeStruct((FIELDS, hx, hy, hz), F32),
            jax.ShapeDtypeStruct((order.shape[1] // WIDE * 6, 128), F32),
        ),
        in_specs=[pl.BlockSpec(memory_space=pltpu.VMEM)] * 6,
        out_specs=(pl.BlockSpec(memory_space=pltpu.VMEM),) * 2,
        compiler_params=pltpu.CompilerParams(vmem_limit_bytes=VMEM),
    )(wide, even, odd, mass, order, hot)


def place_kernel(arrived_ref, order_ref, hot_ref, out_ref):
    groups = arrived_ref.shape[0] // 6
    table = jnp.concatenate(
        [
            jnp.concatenate([arrived_ref[pl.ds(2 * m + c, groups, stride=6), :] for c in range(2)], axis=1)
            for m in range(3)
        ],
        axis=0,
    )
    table = jnp.concatenate(halves(table), axis=0)
    group_ids = row_ids(groups, WIDE)

    @pl.loop(0, groups, unroll=8)
    def _(q):
        at = pl.ds(pl.multiple_of(q * WIDE, WIDE), WIDE)
        got = lookup_rows(table, order_ref[:, at] >> log2(WIDE), hot_ref[:, at], group_ids, groups)
        out_ref[:, at] = jnp.concatenate(got, axis=0)


def place_call(arrived, order, hot):
    return pl.pallas_call(
        place_kernel,
        out_shape=jax.ShapeDtypeStruct((3, order.shape[1]), F32),
        in_specs=[pl.BlockSpec(memory_space=pltpu.VMEM)] * 3,
        out_specs=pl.BlockSpec(memory_space=pltpu.VMEM),
        compiler_params=pltpu.CompilerParams(vmem_limit_bytes=VMEM),
    )(arrived, order, hot)


def swap(x, axis):
    count = lax.axis_size(axis)
    out = []
    for start, part in enumerate(x):
        pairs = [(i, i + 1) for i in range(start, count - 1, 2)]
        out.append(lax.ppermute(part, axis, pairs + [(j, i) for i, j in pairs]))
    return out


def on_device(source_fields, slot_source, slot_weight, slot_target, cell_mass, send_order, place_order):
    n_src, n_tgt = lax.axis_size("src"), lax.axis_size("tgt")
    both = ("src", "tgt")
    owners = n_src * n_tgt
    cells = cell_mass.size
    quota = cells // owners

    values = gather_call(source_fields, slot_source.reshape(1, -1), slot_weight.reshape(1, -1))
    values = values.reshape(owners, FIELDS, SPAN // 128, 128)
    values = lax.all_to_all(values, both, split_axis=0, concat_axis=0, tiled=True).reshape(-1, 128)
    target = slot_target.reshape(1, -1)
    target_hot, send_hot, place_hot = prepare_call(target, send_order, place_order, cell_mass)
    v, even, odd = scatter_call(values, target, target_hot, cell_mass)
    wide, even, odd = widen_call(v, *swap((even, odd), "tgt"))
    projected, outgoing = solve_call((n_src, n_tgt), wide, *swap((even, odd), "src"), cell_mass, send_order, send_hot)

    if quota == WIDE:
        outgoing = outgoing.reshape(owners, 3, 2, 128)
        incoming = lax.all_to_all(outgoing, both, split_axis=0, concat_axis=0, tiled=True)
    else:
        groups = cells // WIDE
        flat = outgoing.reshape(groups, 3, WIDE).transpose(1, 0, 2).reshape(3, owners, quota)
        flat = lax.all_to_all(flat, both, split_axis=1, concat_axis=1, tiled=True)
        incoming = flat.reshape(3, groups, WIDE).transpose(1, 0, 2)
    incoming = incoming.reshape(-1, 128)
    return projected, place_call(incoming, place_order, place_hot)


def solution(mesh):
    split = P(("src", "tgt"))
    rows = P(("src", "tgt"), None)
    return jax.shard_map(
        on_device,
        mesh=mesh,
        in_specs=(P(None, ("src", "tgt")), split, split, split, P("src", "tgt", None), rows, rows),
        out_specs=(P(None, "src", "tgt", None), P(None, ("src", "tgt"))),
        check_vma=False,
    )
```

```python
import numpy as np

import jax
import jax.numpy as jnp
from jax import lax
from jax.experimental import pallas as pl
from jax.experimental.pallas import tpu as pltpu
from jax.sharding import PartitionSpec as P

ITERS = 4
FIELDS = 7
SPAN = 512
AT_ONCE = 8
TOGETHER = 8
WIDE = 256
BF16 = jnp.bfloat16
F32 = jnp.float32
NT = (((1,), (1,)), ((), ()))


def sweep_polynomial(iters, theta, delta):
    sigma = theta / delta
    rho = 1.0 / sigma
    mass = np.array([1.0, 0.125])
    poly = np.polynomial.polynomial
    resid = np.array([1.0])
    step = resid / theta
    total = np.array([0.0])
    for _ in range(iters):
        total = poly.polyadd(total, step)
        resid = poly.polysub(resid, poly.polymul(mass, step))
        rho_new = 1.0 / (2.0 * sigma - rho)
        step = poly.polyadd(rho_new * rho * step, 2.0 * rho_new / delta * resid)
        rho = rho_new
    return [float(c) for c in poly.polyadd(total, step)]


COEFS = sweep_polynomial(ITERS, 1.0, 0.75)


def halves(x):
    high = x.astype(BF16)
    return high, (x - high.astype(F32)).astype(BF16)


def log2(n):
    assert n & (n - 1) == 0
    return n.bit_length() - 1


def row_ids(rows, lanes):
    return lax.broadcasted_iota(jnp.int32, (rows, lanes), 0)


def low_onehot(low, ids):
    return jnp.where(ids == low.astype(F32).astype(BF16), jnp.ones((), BF16), jnp.zeros((), BF16))


def gather_kernel(fields_hbm, index_hbm, weight_hbm, out_hbm, table, fields_ref, index_ref, weight_ref, out_ref, sems, done):
    pairs = ((fields_hbm, fields_ref), (index_hbm, index_ref), (weight_hbm, weight_ref))
    copies = [pltpu.make_async_copy(src, dst, sems.at[i]) for i, (src, dst) in enumerate(pairs)]
    for copy in copies:
        copy.start()
    lanes = out_ref.shape[1]
    span = SPAN
    tiles = span // lanes
    owners = index_ref.shape[1] // span
    groups = fields_ref.shape[1] // WIDE
    table[...] = jnp.zeros_like(table)
    for copy in copies:
        copy.wait()
    for g in range(groups):
        table[g * 8 : g * 8 + FIELDS, :] = fields_ref[:, g * WIDE : (g + 1) * WIDE]
    high, low = halves(table[...])
    both = jnp.concatenate([high, low], axis=0)
    ids = row_ids(WIDE, span).astype(F32).astype(BF16)
    rows = groups * 8

    def one_owner(q):
        at = pl.multiple_of(q * span, span)
        index = index_ref[:, pl.ds(at, span)]
        weight = weight_ref[:, pl.ds(at, span)]
        onehot = low_onehot(index & (WIDE - 1), ids)
        got = jnp.dot(both, onehot, preferred_element_type=F32)
        group = jnp.broadcast_to(index >> log2(WIDE), (8, span))
        value = jnp.zeros((8, span), F32)
        for g in range(groups):
            part = got[g * 8 : (g + 1) * 8] + got[rows + g * 8 : rows + (g + 1) * 8]
            value = jnp.where(group == g, part, value)
        value = value * weight
        for t in range(tiles):
            out_ref[pl.ds(q * (FIELDS * tiles) + t, FIELDS, stride=tiles), :] = value[
                :FIELDS, t * lanes : (t + 1) * lanes
            ]

    def send_off(n):
        rows = AT_ONCE * FIELDS * tiles
        part = pl.ds(pl.multiple_of(n * rows, 8), rows)
        return pltpu.make_async_copy(out_ref.at[part], out_hbm.at[part], done.at[n])

    @pl.loop(0, owners // AT_ONCE // 4)
    def _(m):
        for j in range(4):
            for i in range(AT_ONCE):
                one_owner((m * 4 + j) * AT_ONCE + i)
            send_off(m * 4 + j).start()

    @pl.loop(0, owners // AT_ONCE)
    def _(n):
        send_off(n).wait()


def gather_call(fields, index, weight):
    owners = index.shape[1] // SPAN
    rows = FIELDS * index.shape[1] // 128
    return pl.pallas_call(
        gather_kernel,
        out_shape=jax.ShapeDtypeStruct((rows, 128), F32),
        in_specs=[pl.BlockSpec(memory_space=pltpu.HBM)] * 3,
        out_specs=pl.BlockSpec(memory_space=pltpu.HBM),
        scratch_shapes=[
            pltpu.VMEM((fields.shape[1] // WIDE * 8, WIDE), F32),
            pltpu.VMEM(fields.shape, F32),
            pltpu.VMEM(index.shape, jnp.int32),
            pltpu.VMEM(weight.shape, F32),
            pltpu.VMEM((rows, 128), F32),
            pltpu.SemaphoreType.DMA((3,)),
            pltpu.SemaphoreType.DMA((owners // AT_ONCE,)),
        ],
        compiler_params=pltpu.CompilerParams(vmem_limit_bytes=60 << 20),
    )(fields, index, weight)


def scatter_kernel(value_ref, target_ref, mass_ref, v_ref, even_ref, odd_ref, total):
    lanes = value_ref.shape[1]
    tiles = SPAN // lanes
    owners = target_ref.shape[1] // SPAN
    span = TOGETHER * SPAN
    hx, hy, hz = mass_ref.shape
    groups = hx * hy * hz // WIDE
    total[...] = jnp.zeros_like(total)
    ids = row_ids(WIDE, span).astype(F32).astype(BF16)
    group_ids = row_ids(groups, span).astype(F32).astype(BF16)

    @pl.loop(0, owners // TOGETHER)
    def _(p):
        at = pl.multiple_of(p * span, span)
        target = target_ref[:, pl.ds(at, span)]
        low = ((target >> log2(groups * hz)) << log2(hz)) + (target & (hz - 1))
        onehot = low_onehot(jnp.where(target < 0, -1, low), ids)
        group = ((target >> log2(hz)) & (groups - 1)).astype(F32).astype(BF16)
        here = group_ids == group
        row = p * (TOGETHER * FIELDS * tiles)
        pieces = [i * FIELDS * tiles + t for i in range(TOGETHER) for t in range(tiles)]
        value = jnp.concatenate([value_ref[pl.ds(row + i, FIELDS, stride=tiles), :] for i in pieces], axis=1)
        parts = []
        for half in halves(value):
            for f in range(FIELDS):
                parts.append(jnp.where(here, half[f : f + 1], jnp.zeros((), BF16)))
        spread = jnp.concatenate(parts, axis=0)
        total[...] += lax.dot_general(spread, onehot, NT, preferred_element_type=F32)

    odd_ref[FIELDS * hx] = jnp.zeros((ITERS, hz), F32)
    scale = lax.rsqrt(mass_ref[...])
    half_x = hx // 2
    odd = lax.axis_index("tgt") % 2 == 1
    for f in range(FIELDS):
        s = total[f * groups : (f + 1) * groups] + total[(FIELDS + f) * groups : (FIELDS + f + 1) * groups]
        for b in range(2):
            for x in range(half_x):
                at = b * half_x + x
                v = s[x * hy : (x + 1) * hy, b * hz : (b + 1) * hz] * scale[at]
                v_ref[f, at] = v
                first, last = v[:ITERS], v[hy - ITERS :]
                even_ref[f * hx + at] = jnp.where(odd, first, last)
                odd_ref[f * hx + at] = jnp.where(odd, last, first)


def scatter_call(values, target, mass):
    hx, hy, hz = mass.shape
    groups = hx * hy * hz // WIDE
    even = jax.ShapeDtypeStruct((FIELDS * hx, ITERS, hz), F32)
    odd = jax.ShapeDtypeStruct((FIELDS * hx + 1, ITERS, hz), F32)
    return pl.pallas_call(
        scatter_kernel,
        out_shape=(jax.ShapeDtypeStruct((FIELDS, hx, hy, hz), F32), even, odd),
        in_specs=[pl.BlockSpec(memory_space=pltpu.VMEM)] * 3,
        out_specs=(pl.BlockSpec(memory_space=pltpu.VMEM),) * 3,
        scratch_shapes=[pltpu.VMEM((2 * FIELDS * groups, WIDE), F32)],
        compiler_params=pltpu.CompilerParams(vmem_limit_bytes=40 << 20),
    )(values, target, mass)


def lookup_rows(table, index, ids, group_ids, groups, at_parts):
    group, low = at_parts(index)
    got = jnp.dot(table, low_onehot(low, ids), preferred_element_type=F32)
    here = group_ids == group
    rows = 3 * groups
    out = []
    for m in range(3):
        part = got[m * groups : (m + 1) * groups] + got[rows + m * groups : rows + (m + 1) * groups]
        out.append(jnp.sum(jnp.where(here, part, 0.0), axis=0, keepdims=True))
    return out


def cell_moduli(vals):
    phi = vals[0]
    mean = (vals[1] + vals[2] + vals[3]) / 3.0
    q2 = 1.5 * (
        (vals[1] - mean) ** 2
        + (vals[2] - mean) ** 2
        + (vals[3] - mean) ** 2
        + 2.0 * (vals[4] ** 2 + vals[5] ** 2 + vals[6] ** 2)
    )
    bulk = 1.6 * jnp.exp(-3.0 * phi) * (1.0 + 0.25 * jnp.tanh(mean))
    shear = 0.9 * jnp.exp(-2.0 * phi) / (1.0 + q2 / 0.5)
    soften = shear * q2 / (0.5 + q2)
    return [bulk, shear, soften]


def widen_kernel(v_ref, even_ref, odd_ref, wide_ref, to_even_ref, to_odd_ref):
    hx, hy = v_ref.shape[1], v_ref.shape[2]
    own = hx * hy
    b_odd = lax.axis_index("tgt") % 2 == 1
    a_odd = lax.axis_index("src") % 2 == 1
    line = row_ids(2 * ITERS, v_ref.shape[3])
    for f in range(FIELDS):
        sides = []
        for x in range(hx):
            even_side, odd_side = even_ref[f * hx + x], odd_ref[f * hx + x]
            right = jnp.where(b_odd, odd_side, even_side)
            left = jnp.where(b_odd, even_side, odd_side)
            sides.append(jnp.concatenate([right, left], axis=0))
            wide_ref[f, x, :hy] = v_ref[f, x]
            wide_ref[f, x, hy:] = sides[x]
            to_even_ref[f, x * hy : (x + 1) * hy] = v_ref[f, x]
            to_odd_ref[f, x * hy : (x + 1) * hy] = v_ref[f, x]
        extra = []
        for first, second, third in ((sides[hx - 1], sides[hx - 2], sides[hx - 3]), (sides[0], sides[1], sides[2])):
            near = pltpu.roll(second, 2, 0)
            far = jnp.where(line == 4, pltpu.roll(third, 4, 0), pltpu.roll(third, 6, 0))
            extra.append((first, jnp.where(line < 4, near, far)))
        at = own + 2 * ITERS
        to_even_ref[f, own:at] = jnp.where(a_odd, extra[1][0], extra[0][0])
        to_odd_ref[f, own:at] = jnp.where(a_odd, extra[0][0], extra[1][0])
        to_even_ref[f, at : at + 6] = jnp.where(a_odd, extra[1][1], extra[0][1])[:6]
        to_odd_ref[f, at : at + 8] = jnp.where(a_odd, extra[0][1], extra[1][1])


def widen_call(v, even, odd):
    fields, hx, hy, hz = v.shape
    even_rows = jax.ShapeDtypeStruct((fields, hx * hy + 4 * ITERS - 2, hz), F32)
    odd_rows = jax.ShapeDtypeStruct((fields, hx * hy + 4 * ITERS, hz), F32)
    return pl.pallas_call(
        widen_kernel,
        out_shape=(jax.ShapeDtypeStruct((fields, hx, hy + 2 * ITERS, hz), F32), even_rows, odd_rows),
        in_specs=[pl.BlockSpec(memory_space=pltpu.VMEM)] * 3,
        out_specs=(pl.BlockSpec(memory_space=pltpu.VMEM),) * 3,
        compiler_params=pltpu.CompilerParams(vmem_limit_bytes=40 << 20),
    )(v, even, odd)


def solve_kernel(mesh_shape, wide_ref, even_ref, odd_ref, mass_ref, order_ref, projected_ref, out_ref):
    n_src, n_tgt = mesh_shape
    hx, hy, hz = mass_ref.shape
    k = ITERS
    rows = hy + 2 * k
    a, b = lax.axis_index("src"), lax.axis_index("tgt")

    def exists(flag):
        return jnp.where(flag, 1.0, 0.0).astype(F32)

    row = row_ids(rows, hz)
    lane = lax.broadcasted_iota(jnp.int32, (rows, hz), 1)
    inside = jnp.where(row < hy, 1.0, jnp.where(row < hy + k, exists(b < n_tgt - 1), exists(b > 0)))
    inside_left = inside * exists(a > 0)
    inside_right = inside * exists(a < n_src - 1)
    not_first = jnp.where(lane == 0, 0.0, 1.0)
    not_last = jnp.where(lane == hz - 1, 0.0, 1.0)
    scale = lax.rsqrt(mass_ref[...])

    line = row_ids(2 * k, hz)

    def slabs(payload, from_left):
        first = payload[hx * hy : hx * hy + 2 * k]
        packed = payload[hx * hy + 2 * k :]
        second = pltpu.roll(packed, 6, 0)
        third = jnp.where(line < 4, pltpu.roll(packed, 4, 0), pltpu.roll(packed, 2, 0))
        sides = [first, second, third] + [jnp.zeros((2 * k, hz), F32)] * (hx - 3)
        order = reversed(sides) if from_left else sides
        return [jnp.concatenate([payload[x * hy : (x + 1) * hy], side], axis=0) for x, side in enumerate(order)]

    @pl.loop(0, FIELDS)
    def _(f):
        even, odd = jnp.concatenate([even_ref[f], jnp.zeros((2, hz), F32)], axis=0), odd_ref[f]
        left = slabs(jnp.where(a % 2 == 1, even, odd), True)
        right = slabs(jnp.where(a % 2 == 1, odd, even), False)
        base = left + [wide_ref[f, x] for x in range(hx)] + right
        u = [COEFS[k] * e for e in base]
        for sweep in range(1, k + 1):
            new = list(u)
            for x in range(sweep, hx + 2 * k - sweep):
                w = u[x]
                near = u[x - 1] + u[x + 1]
                near = near + pltpu.roll(w, 1, 0) + pltpu.roll(w, rows - 1, 0)
                near = near + pltpu.roll(w, 1, 1) * not_first + pltpu.roll(w, hz - 1, 1) * not_last
                if x < k:
                    near = near * inside_left
                elif x < k + hx:
                    near = near * inside
                else:
                    near = near * inside_right
                new[x] = COEFS[k - sweep] * base[x] + near
            u = new
        for x in range(hx):
            projected_ref[f, x] = u[k + x][:hy] * scale[x]

    groups = hx * hy * hz // WIDE
    payload = cell_moduli([projected_ref[f].reshape(hx * hy, hz) for f in range(FIELDS)])
    table = jnp.concatenate([jnp.concatenate([m[:groups], m[groups:]], axis=1) for m in payload], axis=0)
    table = jnp.concatenate(halves(table), axis=0)
    ids = row_ids(WIDE, WIDE).astype(F32).astype(BF16)
    group_ids = row_ids(groups, WIDE)

    def at_parts(index):
        return (index >> log2(hz)) & (groups - 1), ((index >> log2(groups * hz)) << log2(hz)) + (index & (hz - 1))

    for q in range(0, groups, 4):
        lines = []
        for i in range(q, q + 4):
            index = order_ref[:, i * WIDE : (i + 1) * WIDE]
            got = lookup_rows(table, index, ids, group_ids, groups, at_parts)
            lines += [line[:, c * 128 : (c + 1) * 128] for line in got for c in range(2)]
        out_ref[q * 6 : q * 6 + 24, :] = jnp.concatenate(lines, axis=0)


def solve_call(mesh_shape, wide, even, odd, mass, order):
    hx, hy, hz = mass.shape

    def kernel(*refs):
        solve_kernel(mesh_shape, *refs)

    return pl.pallas_call(
        kernel,
        out_shape=(
            jax.ShapeDtypeStruct((FIELDS, hx, hy, hz), F32),
            jax.ShapeDtypeStruct((order.shape[1] // WIDE * 6, 128), F32),
        ),
        in_specs=[pl.BlockSpec(memory_space=pltpu.VMEM)] * 5,
        out_specs=(pl.BlockSpec(memory_space=pltpu.VMEM),) * 2,
        compiler_params=pltpu.CompilerParams(vmem_limit_bytes=40 << 20),
    )(wide, even, odd, mass, order)


def place_kernel(arrived_ref, order_ref, out_ref):
    groups = arrived_ref.shape[0] // 6
    table = jnp.concatenate(
        [
            jnp.concatenate([arrived_ref[pl.ds(2 * m + c, groups, stride=6), :] for c in range(2)], axis=1)
            for m in range(3)
        ],
        axis=0,
    )
    table = jnp.concatenate(halves(table), axis=0)
    ids = row_ids(WIDE, WIDE).astype(F32).astype(BF16)
    group_ids = row_ids(groups, WIDE)

    for q in range(groups):
        at = pl.ds(q * WIDE, WIDE)
        got = lookup_rows(
            table, order_ref[:, at], ids, group_ids, groups, lambda index: (index >> log2(WIDE), index & (WIDE - 1))
        )
        out_ref[:, at] = jnp.concatenate(got, axis=0)


def place_call(arrived, order):
    return pl.pallas_call(
        place_kernel,
        out_shape=jax.ShapeDtypeStruct((3, order.shape[1]), F32),
        in_specs=[pl.BlockSpec(memory_space=pltpu.VMEM)] * 2,
        out_specs=pl.BlockSpec(memory_space=pltpu.VMEM),
        compiler_params=pltpu.CompilerParams(vmem_limit_bytes=40 << 20),
    )(arrived, order)


def swap(x, axis):
    count = lax.axis_size(axis)
    out = []
    for start, part in enumerate(x):
        pairs = [(i, i + 1) for i in range(start, count - 1, 2)]
        out.append(lax.ppermute(part, axis, pairs + [(j, i) for i, j in pairs]))
    return out


def on_device(source_fields, slot_source, slot_weight, slot_target, cell_mass, send_order, place_order):
    n_src, n_tgt = lax.axis_size("src"), lax.axis_size("tgt")
    both = ("src", "tgt")
    owners = n_src * n_tgt
    cells = cell_mass.size
    quota = cells // owners

    values = gather_call(source_fields, slot_source.reshape(1, -1), slot_weight.reshape(1, -1))
    values = values.reshape(owners, FIELDS, SPAN // 128, 128)
    values = lax.all_to_all(values, both, split_axis=0, concat_axis=0, tiled=True).reshape(-1, 128)
    v, even, odd = scatter_call(values, slot_target.reshape(1, -1), cell_mass)
    wide, even, odd = widen_call(v, *swap((even, odd), "tgt"))
    projected, outgoing = solve_call((n_src, n_tgt), wide, *swap((even, odd), "src"), cell_mass, send_order)

    if quota == WIDE:
        outgoing = outgoing.reshape(owners, 3, 2, 128)
        incoming = lax.all_to_all(outgoing, both, split_axis=0, concat_axis=0, tiled=True)
    else:
        groups = cells // WIDE
        flat = outgoing.reshape(groups, 3, WIDE).transpose(1, 0, 2).reshape(3, owners, quota)
        flat = lax.all_to_all(flat, both, split_axis=1, concat_axis=1, tiled=True)
        incoming = flat.reshape(3, groups, WIDE).transpose(1, 0, 2)
    incoming = incoming.reshape(-1, 128)
    return projected, place_call(incoming, place_order)


def solution(mesh):
    split = P(("src", "tgt"))
    rows = P(("src", "tgt"), None)
    return jax.shard_map(
        on_device,
        mesh=mesh,
        in_specs=(P(None, ("src", "tgt")), split, split, split, P("src", "tgt", None), rows, rows),
        out_specs=(P(None, "src", "tgt", None), P(None, ("src", "tgt"))),
        check_vma=False,
    )
```

```python
import numpy as np

import jax
import jax.numpy as jnp
from jax import lax
from jax.experimental import pallas as pl
from jax.experimental.pallas import tpu as pltpu
from jax.sharding import PartitionSpec as P

ITERS = 4
FIELDS = 7
PIECES = 4
SPAN = 512
AT_ONCE = 8
TOGETHER = 8
WIDE = 256
BF16 = jnp.bfloat16
F32 = jnp.float32
NT = (((1,), (1,)), ((), ()))


def sweep_polynomial(iters, theta, delta):
    sigma = theta / delta
    rho = 1.0 / sigma
    mass = np.array([1.0, 0.125])
    poly = np.polynomial.polynomial
    resid = np.array([1.0])
    step = resid / theta
    total = np.array([0.0])
    for _ in range(iters):
        total = poly.polyadd(total, step)
        resid = poly.polysub(resid, poly.polymul(mass, step))
        rho_new = 1.0 / (2.0 * sigma - rho)
        step = poly.polyadd(rho_new * rho * step, 2.0 * rho_new / delta * resid)
        rho = rho_new
    return [float(c) for c in poly.polyadd(total, step)]


COEFS = sweep_polynomial(ITERS, 1.0, 0.75)


def halves(x):
    high = x.astype(BF16)
    return high, (x - high.astype(F32)).astype(BF16)


def log2(n):
    assert n & (n - 1) == 0
    return n.bit_length() - 1


def row_ids(rows, lanes):
    return lax.broadcasted_iota(jnp.int32, (rows, lanes), 0)


def low_onehot(low, ids):
    return jnp.where(ids == low.astype(F32).astype(BF16), jnp.ones((), BF16), jnp.zeros((), BF16))


def gather_kernel(fields_hbm, index_hbm, weight_hbm, out_hbm, table, fields_ref, index_ref, weight_ref, out_ref, sems, done):
    pairs = ((fields_hbm, fields_ref), (index_hbm, index_ref), (weight_hbm, weight_ref))
    copies = [pltpu.make_async_copy(src, dst, sems.at[i]) for i, (src, dst) in enumerate(pairs)]
    for copy in copies:
        copy.start()
    lanes = out_ref.shape[1]
    span = SPAN
    tiles = span // lanes
    owners = index_ref.shape[1] // span
    groups = fields_ref.shape[1] // WIDE
    table[...] = jnp.zeros_like(table)
    for copy in copies:
        copy.wait()
    for g in range(groups):
        table[g * 8 : g * 8 + FIELDS, :] = fields_ref[:, g * WIDE : (g + 1) * WIDE]
    high, low = halves(table[...])
    both = jnp.concatenate([high, low], axis=0)
    ids = row_ids(WIDE, span).astype(F32).astype(BF16)
    rows = groups * 8

    def one_owner(q):
        at = pl.multiple_of(q * span, span)
        index = index_ref[:, pl.ds(at, span)]
        weight = weight_ref[:, pl.ds(at, span)]
        onehot = low_onehot(index & (WIDE - 1), ids)
        got = jnp.dot(both, onehot, preferred_element_type=F32)
        group = jnp.broadcast_to(index >> log2(WIDE), (8, span))
        value = jnp.zeros((8, span), F32)
        for g in range(groups):
            part = got[g * 8 : (g + 1) * 8] + got[rows + g * 8 : rows + (g + 1) * 8]
            value = jnp.where(group == g, part, value)
        value = value * weight
        for t in range(tiles):
            out_ref[pl.ds(q * (FIELDS * tiles) + t, FIELDS, stride=tiles), :] = value[
                :FIELDS, t * lanes : (t + 1) * lanes
            ]

    def send_off(n):
        rows = AT_ONCE * FIELDS * tiles
        part = pl.ds(pl.multiple_of(n * rows, 8), rows)
        return pltpu.make_async_copy(out_ref.at[part], out_hbm.at[part], done.at[n])

    @pl.loop(0, owners // AT_ONCE // 4)
    def _(m):
        for j in range(4):
            for i in range(AT_ONCE):
                one_owner((m * 4 + j) * AT_ONCE + i)
            send_off(m * 4 + j).start()

    @pl.loop(0, owners // AT_ONCE)
    def _(n):
        send_off(n).wait()


def gather_call(fields, index, weight):
    owners = index.shape[1] // SPAN
    rows = FIELDS * index.shape[1] // 128
    return pl.pallas_call(
        gather_kernel,
        out_shape=jax.ShapeDtypeStruct((rows, 128), F32),
        in_specs=[pl.BlockSpec(memory_space=pltpu.HBM)] * 3,
        out_specs=pl.BlockSpec(memory_space=pltpu.HBM),
        scratch_shapes=[
            pltpu.VMEM((fields.shape[1] // WIDE * 8, WIDE), F32),
            pltpu.VMEM(fields.shape, F32),
            pltpu.VMEM(index.shape, jnp.int32),
            pltpu.VMEM(weight.shape, F32),
            pltpu.VMEM((rows, 128), F32),
            pltpu.SemaphoreType.DMA((3,)),
            pltpu.SemaphoreType.DMA((owners // AT_ONCE,)),
        ],
        compiler_params=pltpu.CompilerParams(vmem_limit_bytes=60 << 20),
    )(fields, index, weight)


def scatter_kernel(value_ref, target_ref, mass_ref, v_ref, even_ref, odd_ref, total):
    lanes = value_ref.shape[1]
    tiles = SPAN // lanes
    owners = target_ref.shape[1] // SPAN
    span = TOGETHER * SPAN
    hx, hy, hz = mass_ref.shape
    groups = hx * hy * hz // WIDE
    total[...] = jnp.zeros_like(total)
    ids = row_ids(WIDE, span).astype(F32).astype(BF16)
    group_ids = row_ids(groups, span).astype(F32).astype(BF16)

    def step(p):
        at = pl.multiple_of(p * span, span)
        target = target_ref[:, pl.ds(at, span)]
        low = ((target >> log2(groups * hz)) << log2(hz)) + (target & (hz - 1))
        onehot = low_onehot(jnp.where(target < 0, -1, low), ids)
        group = ((target >> log2(hz)) & (groups - 1)).astype(F32).astype(BF16)
        here = group_ids == group
        row = p * (TOGETHER * FIELDS * tiles)
        pieces = [i * FIELDS * tiles + t for i in range(TOGETHER) for t in range(tiles)]
        value = jnp.concatenate([value_ref[pl.ds(row + i, FIELDS, stride=tiles), :] for i in pieces], axis=1)
        parts = []
        for half in halves(value):
            for f in range(FIELDS):
                parts.append(jnp.where(here, half[f : f + 1], jnp.zeros((), BF16)))
        spread = jnp.concatenate(parts, axis=0)
        total[...] += lax.dot_general(spread, onehot, NT, preferred_element_type=F32)

    @pl.loop(0, owners // TOGETHER // 4)
    def _(n):
        for i in range(4):
            step(n * 4 + i)

    odd_ref[FIELDS * hx] = jnp.zeros((ITERS, hz), F32)
    scale = lax.rsqrt(mass_ref[...])
    half_x = hx // 2
    odd = lax.axis_index("tgt") % 2 == 1
    for f in range(FIELDS):
        s = total[f * groups : (f + 1) * groups] + total[(FIELDS + f) * groups : (FIELDS + f + 1) * groups]
        for b in range(2):
            for x in range(half_x):
                at = b * half_x + x
                v = s[x * hy : (x + 1) * hy, b * hz : (b + 1) * hz] * scale[at]
                v_ref[f, at] = v
                first, last = v[:ITERS], v[hy - ITERS :]
                even_ref[f * hx + at] = jnp.where(odd, first, last)
                odd_ref[f * hx + at] = jnp.where(odd, last, first)


def scatter_call(values, target, mass):
    hx, hy, hz = mass.shape
    groups = hx * hy * hz // WIDE
    even = jax.ShapeDtypeStruct((FIELDS * hx, ITERS, hz), F32)
    odd = jax.ShapeDtypeStruct((FIELDS * hx + 1, ITERS, hz), F32)
    return pl.pallas_call(
        scatter_kernel,
        out_shape=(jax.ShapeDtypeStruct((FIELDS, hx, hy, hz), F32), even, odd),
        in_specs=[pl.BlockSpec(memory_space=pltpu.VMEM)] * 3,
        out_specs=(pl.BlockSpec(memory_space=pltpu.VMEM),) * 3,
        scratch_shapes=[pltpu.VMEM((2 * FIELDS * groups, WIDE), F32)],
        compiler_params=pltpu.CompilerParams(vmem_limit_bytes=40 << 20),
    )(values, target, mass)


def lookup_rows(table, index, ids, group_ids, groups, at_parts):
    group, low = at_parts(index)
    got = jnp.dot(table, low_onehot(low, ids), preferred_element_type=F32)
    here = group_ids == group
    rows = 3 * groups
    out = []
    for m in range(3):
        part = got[m * groups : (m + 1) * groups] + got[rows + m * groups : rows + (m + 1) * groups]
        out.append(jnp.sum(jnp.where(here, part, 0.0), axis=0, keepdims=True))
    return out


def cell_moduli(vals):
    phi = vals[0]
    mean = (vals[1] + vals[2] + vals[3]) / 3.0
    q2 = 1.5 * (
        (vals[1] - mean) ** 2
        + (vals[2] - mean) ** 2
        + (vals[3] - mean) ** 2
        + 2.0 * (vals[4] ** 2 + vals[5] ** 2 + vals[6] ** 2)
    )
    bulk = 1.6 * jnp.exp(-3.0 * phi) * (1.0 + 0.25 * jnp.tanh(mean))
    shear = 0.9 * jnp.exp(-2.0 * phi) / (1.0 + q2 / 0.5)
    soften = shear * q2 / (0.5 + q2)
    return [bulk, shear, soften]


def widen_kernel(v_ref, even_ref, odd_ref, wide_ref, to_even_ref, to_odd_ref):
    hx, hy = v_ref.shape[1], v_ref.shape[2]
    own = hx * hy
    b_odd = lax.axis_index("tgt") % 2 == 1
    a_odd = lax.axis_index("src") % 2 == 1
    line = row_ids(2 * ITERS, v_ref.shape[3])
    for f in range(FIELDS):
        sides = []
        for x in range(hx):
            even_side, odd_side = even_ref[f * hx + x], odd_ref[f * hx + x]
            right = jnp.where(b_odd, odd_side, even_side)
            left = jnp.where(b_odd, even_side, odd_side)
            sides.append(jnp.concatenate([right, left], axis=0))
            wide_ref[f, x, :hy] = v_ref[f, x]
            wide_ref[f, x, hy:] = sides[x]
            to_even_ref[f, x * hy : (x + 1) * hy] = v_ref[f, x]
            to_odd_ref[f, x * hy : (x + 1) * hy] = v_ref[f, x]
        extra = []
        for first, second, third in ((sides[hx - 1], sides[hx - 2], sides[hx - 3]), (sides[0], sides[1], sides[2])):
            near = pltpu.roll(second, 2, 0)
            far = jnp.where(line == 4, pltpu.roll(third, 4, 0), pltpu.roll(third, 6, 0))
            extra.append((first, jnp.where(line < 4, near, far)))
        at = own + 2 * ITERS
        to_even_ref[f, own:at] = jnp.where(a_odd, extra[1][0], extra[0][0])
        to_odd_ref[f, own:at] = jnp.where(a_odd, extra[0][0], extra[1][0])
        to_even_ref[f, at : at + 6] = jnp.where(a_odd, extra[1][1], extra[0][1])[:6]
        to_odd_ref[f, at : at + 8] = jnp.where(a_odd, extra[0][1], extra[1][1])


def widen_call(v, even, odd):
    fields, hx, hy, hz = v.shape
    even_rows = jax.ShapeDtypeStruct((fields, hx * hy + 4 * ITERS - 2, hz), F32)
    odd_rows = jax.ShapeDtypeStruct((fields, hx * hy + 4 * ITERS, hz), F32)
    return pl.pallas_call(
        widen_kernel,
        out_shape=(jax.ShapeDtypeStruct((fields, hx, hy + 2 * ITERS, hz), F32), even_rows, odd_rows),
        in_specs=[pl.BlockSpec(memory_space=pltpu.VMEM)] * 3,
        out_specs=(pl.BlockSpec(memory_space=pltpu.VMEM),) * 3,
        compiler_params=pltpu.CompilerParams(vmem_limit_bytes=40 << 20),
    )(v, even, odd)


def solve_kernel(mesh_shape, wide_ref, even_ref, odd_ref, mass_ref, order_ref, projected_hbm, out_ref, projected_ref, sem):
    n_src, n_tgt = mesh_shape
    hx, hy, hz = mass_ref.shape
    k = ITERS
    rows = hy + 2 * k
    a, b = lax.axis_index("src"), lax.axis_index("tgt")

    def exists(flag):
        return jnp.where(flag, 1.0, 0.0).astype(F32)

    row = row_ids(rows, hz)
    lane = lax.broadcasted_iota(jnp.int32, (rows, hz), 1)
    inside = jnp.where(row < hy, 1.0, jnp.where(row < hy + k, exists(b < n_tgt - 1), exists(b > 0)))
    inside_left = inside * exists(a > 0)
    inside_right = inside * exists(a < n_src - 1)
    not_first = jnp.where(lane == 0, 0.0, 1.0)
    not_last = jnp.where(lane == hz - 1, 0.0, 1.0)
    scale = lax.rsqrt(mass_ref[...])

    line = row_ids(2 * k, hz)

    def slabs(payload, from_left):
        first = payload[hx * hy : hx * hy + 2 * k]
        packed = payload[hx * hy + 2 * k :]
        second = pltpu.roll(packed, 6, 0)
        third = jnp.where(line < 4, pltpu.roll(packed, 4, 0), pltpu.roll(packed, 2, 0))
        sides = [first, second, third] + [jnp.zeros((2 * k, hz), F32)] * (hx - 3)
        order = reversed(sides) if from_left else sides
        return [jnp.concatenate([payload[x * hy : (x + 1) * hy], side], axis=0) for x, side in enumerate(order)]

    @pl.loop(0, FIELDS)
    def _(f):
        even, odd = jnp.concatenate([even_ref[f], jnp.zeros((2, hz), F32)], axis=0), odd_ref[f]
        left = slabs(jnp.where(a % 2 == 1, even, odd), True)
        right = slabs(jnp.where(a % 2 == 1, odd, even), False)
        base = left + [wide_ref[f, x] for x in range(hx)] + right
        u = [COEFS[k] * e for e in base]
        for sweep in range(1, k + 1):
            new = list(u)
            for x in range(sweep, hx + 2 * k - sweep):
                far = max(k - x, x - (k + hx - 1), 0)
                n = rows if sweep + far < k else hy
                w = u[x]
                near = u[x - 1][:n] + u[x + 1][:n]
                near = near + pltpu.roll(w, 1, 0)[:n] + pltpu.roll(w, rows - 1, 0)[:n]
                w = w[:n]
                near = near + pltpu.roll(w, 1, 1) * not_first[:n] + pltpu.roll(w, hz - 1, 1) * not_last[:n]
                if x < k:
                    near = near * inside_left[:n]
                elif x >= k + hx:
                    near = near * inside_right[:n]
                elif n > hy:
                    near = near * inside
                new[x] = COEFS[k - sweep] * base[x][:n] + near
            u = new
        for x in range(hx):
            projected_ref[f, x] = u[k + x][:hy] * scale[x]

    leave = pltpu.make_async_copy(projected_ref, projected_hbm, sem)
    leave.start()
    groups = hx * hy * hz // WIDE
    payload = cell_moduli([projected_ref[f].reshape(hx * hy, hz) for f in range(FIELDS)])
    table = jnp.concatenate([jnp.concatenate([m[:groups], m[groups:]], axis=1) for m in payload], axis=0)
    table = jnp.concatenate(halves(table), axis=0)
    ids = row_ids(WIDE, WIDE).astype(F32).astype(BF16)
    group_ids = row_ids(groups, WIDE)

    def at_parts(index):
        return (index >> log2(hz)) & (groups - 1), ((index >> log2(groups * hz)) << log2(hz)) + (index & (hz - 1))

    for q in range(0, groups, 4):
        lines = []
        for i in range(q, q + 4):
            index = order_ref[:, i * WIDE : (i + 1) * WIDE]
            got = lookup_rows(table, index, ids, group_ids, groups, at_parts)
            lines += [line[:, c * 128 : (c + 1) * 128] for line in got for c in range(2)]
        out_ref[q * 6 : q * 6 + 24, :] = jnp.concatenate(lines, axis=0)
    leave.wait()


def solve_call(mesh_shape, wide, even, odd, mass, order):
    hx, hy, hz = mass.shape

    def kernel(*refs):
        solve_kernel(mesh_shape, *refs)

    return pl.pallas_call(
        kernel,
        out_shape=(
            jax.ShapeDtypeStruct((FIELDS, hx, hy, hz), F32),
            jax.ShapeDtypeStruct((order.shape[1] // WIDE * 6, 128), F32),
        ),
        in_specs=[pl.BlockSpec(memory_space=pltpu.VMEM)] * 5,
        out_specs=(pl.BlockSpec(memory_space=pltpu.HBM), pl.BlockSpec(memory_space=pltpu.VMEM)),
        scratch_shapes=[pltpu.VMEM((FIELDS, hx, hy, hz), F32), pltpu.SemaphoreType.DMA],
        compiler_params=pltpu.CompilerParams(vmem_limit_bytes=40 << 20),
    )(wide, even, odd, mass, order)


def place_kernel(arrived_ref, order_ref, out_hbm, out_ref, sems):
    groups = arrived_ref.shape[0] // 6
    table = jnp.concatenate(
        [
            jnp.concatenate([arrived_ref[pl.ds(2 * m + c, groups, stride=6), :] for c in range(2)], axis=1)
            for m in range(3)
        ],
        axis=0,
    )
    table = jnp.concatenate(halves(table), axis=0)
    ids = row_ids(WIDE, WIDE).astype(F32).astype(BF16)
    group_ids = row_ids(groups, WIDE)

    copies = []
    for n in range(PIECES):
        for q in range(n * groups // PIECES, (n + 1) * groups // PIECES):
            at = pl.ds(q * WIDE, WIDE)
            got = lookup_rows(
                table, order_ref[:, at], ids, group_ids, groups, lambda index: (index >> log2(WIDE), index & (WIDE - 1))
            )
            out_ref[:, at] = jnp.concatenate(got, axis=0)
        piece = pl.ds(n * groups // PIECES * WIDE, groups // PIECES * WIDE)
        copies.append(pltpu.make_async_copy(out_ref.at[:, piece], out_hbm.at[:, piece], sems.at[n]))
        copies[n].start()
    for copy in copies:
        copy.wait()


def place_call(arrived, order):
    return pl.pallas_call(
        place_kernel,
        out_shape=jax.ShapeDtypeStruct((3, order.shape[1]), F32),
        in_specs=[pl.BlockSpec(memory_space=pltpu.VMEM)] * 2,
        out_specs=pl.BlockSpec(memory_space=pltpu.HBM),
        scratch_shapes=[pltpu.VMEM((3, order.shape[1]), F32), pltpu.SemaphoreType.DMA((PIECES,))],
        compiler_params=pltpu.CompilerParams(vmem_limit_bytes=40 << 20),
    )(arrived, order)


def swap(x, axis):
    count = lax.axis_size(axis)
    out = []
    for start, part in enumerate(x):
        pairs = [(i, i + 1) for i in range(start, count - 1, 2)]
        out.append(lax.ppermute(part, axis, pairs + [(j, i) for i, j in pairs]))
    return out


def on_device(source_fields, slot_source, slot_weight, slot_target, cell_mass, send_order, place_order):
    n_src, n_tgt = lax.axis_size("src"), lax.axis_size("tgt")
    both = ("src", "tgt")
    owners = n_src * n_tgt
    cells = cell_mass.size
    quota = cells // owners

    values = gather_call(source_fields, slot_source.reshape(1, -1), slot_weight.reshape(1, -1))
    values = values.reshape(owners, FIELDS, SPAN // 128, 128)
    values = lax.all_to_all(values, both, split_axis=0, concat_axis=0, tiled=True).reshape(-1, 128)
    v, even, odd = scatter_call(values, slot_target.reshape(1, -1), cell_mass)
    wide, even, odd = widen_call(v, *swap((even, odd), "tgt"))
    projected, outgoing = solve_call((n_src, n_tgt), wide, *swap((even, odd), "src"), cell_mass, send_order)

    if quota == WIDE:
        outgoing = outgoing.reshape(owners, 3, 2, 128)
        incoming = lax.all_to_all(outgoing, both, split_axis=0, concat_axis=0, tiled=True)
    else:
        groups = cells // WIDE
        flat = outgoing.reshape(groups, 3, WIDE).transpose(1, 0, 2).reshape(3, owners, quota)
        flat = lax.all_to_all(flat, both, split_axis=1, concat_axis=1, tiled=True)
        incoming = flat.reshape(3, groups, WIDE).transpose(1, 0, 2)
    incoming = incoming.reshape(-1, 128)
    return projected, place_call(incoming, place_order)


def solution(mesh):
    split = P(("src", "tgt"))
    rows = P(("src", "tgt"), None)
    return jax.shard_map(
        on_device,
        mesh=mesh,
        in_specs=(P(None, ("src", "tgt")), split, split, split, P("src", "tgt", None), rows, rows),
        out_specs=(P(None, "src", "tgt", None), P(None, ("src", "tgt"))),
        check_vma=False,
    )
```

```python
import numpy as np

import jax
import jax.numpy as jnp
from jax import lax
from jax.experimental import pallas as pl
from jax.experimental.pallas import tpu as pltpu
from jax.sharding import PartitionSpec as P

ITERS = 4
FIELDS = 7
PIECES = 4
SPAN = 512
AT_ONCE = 8
TOGETHER = 8
WIDE = 256
BF16 = jnp.bfloat16
F32 = jnp.float32
NT = (((1,), (1,)), ((), ()))


def sweep_polynomial(iters, theta, delta):
    sigma = theta / delta
    rho = 1.0 / sigma
    mass = np.array([1.0, 0.125])
    poly = np.polynomial.polynomial
    resid = np.array([1.0])
    step = resid / theta
    total = np.array([0.0])
    for _ in range(iters):
        total = poly.polyadd(total, step)
        resid = poly.polysub(resid, poly.polymul(mass, step))
        rho_new = 1.0 / (2.0 * sigma - rho)
        step = poly.polyadd(rho_new * rho * step, 2.0 * rho_new / delta * resid)
        rho = rho_new
    return [float(c) for c in poly.polyadd(total, step)]


COEFS = sweep_polynomial(ITERS, 1.0, 0.75)


def halves(x):
    high = x.astype(BF16)
    return high, (x - high.astype(F32)).astype(BF16)


def log2(n):
    assert n & (n - 1) == 0
    return n.bit_length() - 1


def row_ids(rows, lanes):
    return lax.broadcasted_iota(jnp.int32, (rows, lanes), 0)


def low_onehot(low, ids):
    return jnp.where(ids == low.astype(F32).astype(BF16), jnp.ones((), BF16), jnp.zeros((), BF16))


def gather_kernel(fields_hbm, index_hbm, weight_hbm, out_hbm, table, fields_ref, index_ref, weight_ref, out_ref, sems, done):
    pairs = ((fields_hbm, fields_ref), (index_hbm, index_ref), (weight_hbm, weight_ref))
    copies = [pltpu.make_async_copy(src, dst, sems.at[i]) for i, (src, dst) in enumerate(pairs)]
    for copy in copies:
        copy.start()
    lanes = out_ref.shape[1]
    span = SPAN
    tiles = span // lanes
    owners = index_ref.shape[1] // span
    groups = fields_ref.shape[1] // WIDE
    table[...] = jnp.zeros_like(table)
    for copy in copies:
        copy.wait()
    for g in range(groups):
        table[g * 8 : g * 8 + FIELDS, :] = fields_ref[:, g * WIDE : (g + 1) * WIDE]
    high, low = halves(table[...])
    both = jnp.concatenate([high, low], axis=0)
    ids = row_ids(WIDE, span).astype(F32).astype(BF16)
    rows = groups * 8

    def one_owner(q):
        at = pl.multiple_of(q * span, span)
        index = index_ref[:, pl.ds(at, span)]
        weight = weight_ref[:, pl.ds(at, span)]
        onehot = low_onehot(index & (WIDE - 1), ids)
        got = jnp.dot(both, onehot, preferred_element_type=F32)
        group = jnp.broadcast_to(index >> log2(WIDE), (8, span))
        value = jnp.zeros((8, span), F32)
        for g in range(groups):
            part = got[g * 8 : (g + 1) * 8] + got[rows + g * 8 : rows + (g + 1) * 8]
            value = jnp.where(group == g, part, value)
        value = value * weight
        for t in range(tiles):
            out_ref[pl.ds(q * (FIELDS * tiles) + t, FIELDS, stride=tiles), :] = value[
                :FIELDS, t * lanes : (t + 1) * lanes
            ]

    def send_off(n):
        rows = AT_ONCE * FIELDS * tiles
        part = pl.ds(pl.multiple_of(n * rows, 8), rows)
        return pltpu.make_async_copy(out_ref.at[part], out_hbm.at[part], done.at[n])

    @pl.loop(0, owners // AT_ONCE // 4)
    def _(m):
        for j in range(4):
            for i in range(AT_ONCE):
                one_owner((m * 4 + j) * AT_ONCE + i)
            send_off(m * 4 + j).start()

    @pl.loop(0, owners // AT_ONCE)
    def _(n):
        send_off(n).wait()


def gather_call(fields, index, weight):
    owners = index.shape[1] // SPAN
    rows = FIELDS * index.shape[1] // 128
    return pl.pallas_call(
        gather_kernel,
        out_shape=jax.ShapeDtypeStruct((rows, 128), F32),
        in_specs=[pl.BlockSpec(memory_space=pltpu.HBM)] * 3,
        out_specs=pl.BlockSpec(memory_space=pltpu.HBM),
        scratch_shapes=[
            pltpu.VMEM((fields.shape[1] // WIDE * 8, WIDE), F32),
            pltpu.VMEM(fields.shape, F32),
            pltpu.VMEM(index.shape, jnp.int32),
            pltpu.VMEM(weight.shape, F32),
            pltpu.VMEM((rows, 128), F32),
            pltpu.SemaphoreType.DMA((3,)),
            pltpu.SemaphoreType.DMA((owners // AT_ONCE,)),
        ],
        compiler_params=pltpu.CompilerParams(vmem_limit_bytes=60 << 20),
    )(fields, index, weight)


def scatter_kernel(value_ref, target_ref, mass_ref, v_ref, even_ref, odd_ref, total):
    lanes = value_ref.shape[1]
    tiles = SPAN // lanes
    owners = target_ref.shape[1] // SPAN
    span = TOGETHER * SPAN
    hx, hy, hz = mass_ref.shape
    groups = hx * hy * hz // WIDE
    total[...] = jnp.zeros_like(total)
    ids = row_ids(WIDE, span).astype(F32).astype(BF16)
    group_ids = row_ids(groups, span).astype(F32).astype(BF16)

    def step(p):
        at = pl.multiple_of(p * span, span)
        target = target_ref[:, pl.ds(at, span)]
        low = ((target >> log2(groups * hz)) << log2(hz)) + (target & (hz - 1))
        onehot = low_onehot(jnp.where(target < 0, -1, low), ids)
        group = ((target >> log2(hz)) & (groups - 1)).astype(F32).astype(BF16)
        here = group_ids == group
        row = p * (TOGETHER * FIELDS * tiles)
        pieces = [i * FIELDS * tiles + t for i in range(TOGETHER) for t in range(tiles)]
        value = jnp.concatenate([value_ref[pl.ds(row + i, FIELDS, stride=tiles), :] for i in pieces], axis=1)
        parts = []
        for half in halves(value):
            for f in range(FIELDS):
                parts.append(jnp.where(here, half[f : f + 1], jnp.zeros((), BF16)))
        spread = jnp.concatenate(parts, axis=0)
        total[...] += lax.dot_general(spread, onehot, NT, preferred_element_type=F32)

    @pl.loop(0, owners // TOGETHER // 4)
    def _(n):
        for i in range(4):
            step(n * 4 + i)

    odd_ref[FIELDS * hx] = jnp.zeros((ITERS, hz), F32)
    scale = lax.rsqrt(mass_ref[...])
    half_x = hx // 2
    odd = lax.axis_index("tgt") % 2 == 1
    for f in range(FIELDS):
        s = total[f * groups : (f + 1) * groups] + total[(FIELDS + f) * groups : (FIELDS + f + 1) * groups]
        for b in range(2):
            for x in range(half_x):
                at = b * half_x + x
                v = s[x * hy : (x + 1) * hy, b * hz : (b + 1) * hz] * scale[at]
                v_ref[f, at] = v
                first, last = v[:ITERS], v[hy - ITERS :]
                even_ref[f * hx + at] = jnp.where(odd, first, last)
                odd_ref[f * hx + at] = jnp.where(odd, last, first)


def scatter_call(values, target, mass):
    hx, hy, hz = mass.shape
    groups = hx * hy * hz // WIDE
    even = jax.ShapeDtypeStruct((FIELDS * hx, ITERS, hz), F32)
    odd = jax.ShapeDtypeStruct((FIELDS * hx + 1, ITERS, hz), F32)
    return pl.pallas_call(
        scatter_kernel,
        out_shape=(jax.ShapeDtypeStruct((FIELDS, hx, hy, hz), F32), even, odd),
        in_specs=[pl.BlockSpec(memory_space=pltpu.VMEM)] * 3,
        out_specs=(pl.BlockSpec(memory_space=pltpu.VMEM),) * 3,
        scratch_shapes=[pltpu.VMEM((2 * FIELDS * groups, WIDE), F32)],
        compiler_params=pltpu.CompilerParams(vmem_limit_bytes=40 << 20),
    )(values, target, mass)


def lookup_rows(table, index, ids, group_ids, groups, at_parts):
    group, low = at_parts(index)
    got = jnp.dot(table, low_onehot(low, ids), preferred_element_type=F32)
    here = group_ids == group
    rows = 3 * groups
    out = []
    for m in range(3):
        part = got[m * groups : (m + 1) * groups] + got[rows + m * groups : rows + (m + 1) * groups]
        out.append(jnp.sum(jnp.where(here, part, 0.0), axis=0, keepdims=True))
    return out


def cell_moduli(vals):
    phi = vals[0]
    mean = (vals[1] + vals[2] + vals[3]) / 3.0
    q2 = 1.5 * (
        (vals[1] - mean) ** 2
        + (vals[2] - mean) ** 2
        + (vals[3] - mean) ** 2
        + 2.0 * (vals[4] ** 2 + vals[5] ** 2 + vals[6] ** 2)
    )
    bulk = 1.6 * jnp.exp(-3.0 * phi) * (1.0 + 0.25 * jnp.tanh(mean))
    shear = 0.9 * jnp.exp(-2.0 * phi) / (1.0 + q2 / 0.5)
    soften = shear * q2 / (0.5 + q2)
    return [bulk, shear, soften]


def corners(sides):
    line = row_ids(2 * ITERS, sides[0].shape[1])
    near = pltpu.roll(sides[1], 2, 0)
    far = jnp.where(line == 4, pltpu.roll(sides[2], 4, 0), pltpu.roll(sides[2], 6, 0))
    return sides[0], jnp.where(line < 4, near, far)


def sides_kernel(even_ref, odd_ref, sides_ref, to_even_ref, to_odd_ref):
    hx = sides_ref.shape[1]
    b_odd = lax.axis_index("tgt") % 2 == 1
    a_odd = lax.axis_index("src") % 2 == 1
    for f in range(FIELDS):
        sides = []
        for x in range(hx):
            even_side, odd_side = even_ref[f * hx + x], odd_ref[f * hx + x]
            right = jnp.where(b_odd, odd_side, even_side)
            left = jnp.where(b_odd, even_side, odd_side)
            sides.append(jnp.concatenate([right, left], axis=0))
            sides_ref[f, x] = sides[x]
        to_left, to_right = corners(sides), corners(sides[::-1])
        to_even_ref[f, :8] = jnp.where(a_odd, to_left[0], to_right[0])
        to_even_ref[f, 8:14] = jnp.where(a_odd, to_left[1], to_right[1])[:6]
        to_odd_ref[f, :8] = jnp.where(a_odd, to_right[0], to_left[0])
        to_odd_ref[f, 8:] = jnp.where(a_odd, to_right[1], to_left[1])


def sides_call(even, odd, hx):
    hz = even.shape[2]
    return pl.pallas_call(
        sides_kernel,
        out_shape=(
            jax.ShapeDtypeStruct((FIELDS, hx, 2 * ITERS, hz), F32),
            jax.ShapeDtypeStruct((FIELDS, 4 * ITERS - 2, hz), F32),
            jax.ShapeDtypeStruct((FIELDS, 4 * ITERS, hz), F32),
        ),
        in_specs=[pl.BlockSpec(memory_space=pltpu.VMEM)] * 2,
        out_specs=(pl.BlockSpec(memory_space=pltpu.VMEM),) * 3,
        compiler_params=pltpu.CompilerParams(vmem_limit_bytes=4 << 20),
        cost_estimate=pl.CostEstimate(flops=40 * 10**9, bytes_accessed=40 * 10**6, transcendentals=0),
    )(even, odd)


def solve_kernel(
    mesh_shape, v_ref, sides_ref, even_ref, odd_ref, even_corners_ref, odd_corners_ref, mass_ref, order_ref,
    projected_hbm, out_ref, projected_ref, sem,
):
    n_src, n_tgt = mesh_shape
    hx, hy, hz = mass_ref.shape
    k = ITERS
    rows = hy + 2 * k
    a, b = lax.axis_index("src"), lax.axis_index("tgt")

    def exists(flag):
        return jnp.where(flag, 1.0, 0.0).astype(F32)

    row = row_ids(rows, hz)
    lane = lax.broadcasted_iota(jnp.int32, (rows, hz), 1)
    inside = jnp.where(row < hy, 1.0, jnp.where(row < hy + k, exists(b < n_tgt - 1), exists(b > 0)))
    inside_left = inside * exists(a > 0)
    inside_right = inside * exists(a < n_src - 1)
    not_first = jnp.where(lane == 0, 0.0, 1.0)
    not_last = jnp.where(lane == hz - 1, 0.0, 1.0)
    scale = lax.rsqrt(mass_ref[...])

    line = row_ids(2 * k, hz)

    def slabs(own, first, packed, from_left):
        second = pltpu.roll(packed, 6, 0)
        third = jnp.where(line < 4, pltpu.roll(packed, 4, 0), pltpu.roll(packed, 2, 0))
        sides = [first, second, third] + [jnp.zeros((2 * k, hz), F32)] * (hx - 3)
        if from_left:
            sides = sides[::-1]
        return [jnp.concatenate([own[x], side], axis=0) for x, side in enumerate(sides)]

    a_odd = a % 2 == 1

    @pl.loop(0, FIELDS)
    def _(f):
        packed = jnp.concatenate([even_corners_ref[f, 2 * k :], jnp.zeros((2, hz), F32)], axis=0)
        even = (even_ref[f], even_corners_ref[f, : 2 * k], packed)
        odd = (odd_ref[f], odd_corners_ref[f, : 2 * k], odd_corners_ref[f, 2 * k :])
        left = slabs(*[jnp.where(a_odd, p, q) for p, q in zip(even, odd)], True)
        right = slabs(*[jnp.where(a_odd, q, p) for p, q in zip(even, odd)], False)
        own = [jnp.concatenate([v_ref[f, x], sides_ref[f, x]], axis=0) for x in range(hx)]
        base = left + own + right
        u = [COEFS[k] * e for e in base]
        for sweep in range(1, k + 1):
            new = list(u)
            for x in range(sweep, hx + 2 * k - sweep):
                far = max(k - x, x - (k + hx - 1), 0)
                n = rows if sweep + far < k else hy
                w = u[x]
                near = u[x - 1][:n] + u[x + 1][:n]
                near = near + pltpu.roll(w, 1, 0)[:n] + pltpu.roll(w, rows - 1, 0)[:n]
                w = w[:n]
                near = near + pltpu.roll(w, 1, 1) * not_first[:n] + pltpu.roll(w, hz - 1, 1) * not_last[:n]
                if x < k:
                    near = near * inside_left[:n]
                elif x >= k + hx:
                    near = near * inside_right[:n]
                elif n > hy:
                    near = near * inside
                new[x] = COEFS[k - sweep] * base[x][:n] + near
            u = new
        for x in range(hx):
            projected_ref[f, x] = u[k + x][:hy] * scale[x]

    leave = pltpu.make_async_copy(projected_ref, projected_hbm, sem)
    leave.start()
    groups = hx * hy * hz // WIDE
    payload = cell_moduli([projected_ref[f].reshape(hx * hy, hz) for f in range(FIELDS)])
    table = jnp.concatenate([jnp.concatenate([m[:groups], m[groups:]], axis=1) for m in payload], axis=0)
    table = jnp.concatenate(halves(table), axis=0)
    ids = row_ids(WIDE, WIDE).astype(F32).astype(BF16)
    group_ids = row_ids(groups, WIDE)

    def at_parts(index):
        return (index >> log2(hz)) & (groups - 1), ((index >> log2(groups * hz)) << log2(hz)) + (index & (hz - 1))

    for q in range(0, groups, 4):
        lines = []
        for i in range(q, q + 4):
            index = order_ref[:, i * WIDE : (i + 1) * WIDE]
            got = lookup_rows(table, index, ids, group_ids, groups, at_parts)
            lines += [line[:, c * 128 : (c + 1) * 128] for line in got for c in range(2)]
        out_ref[q * 6 : q * 6 + 24, :] = jnp.concatenate(lines, axis=0)
    leave.wait()


def solve_call(mesh_shape, *args):
    mass, order = args[-2:]
    hx, hy, hz = mass.shape

    def kernel(*refs):
        solve_kernel(mesh_shape, *refs)

    return pl.pallas_call(
        kernel,
        out_shape=(
            jax.ShapeDtypeStruct((FIELDS, hx, hy, hz), F32),
            jax.ShapeDtypeStruct((order.shape[1] // WIDE * 6, 128), F32),
        ),
        in_specs=[pl.BlockSpec(memory_space=pltpu.VMEM)] * 8,
        out_specs=(pl.BlockSpec(memory_space=pltpu.HBM), pl.BlockSpec(memory_space=pltpu.VMEM)),
        scratch_shapes=[pltpu.VMEM((FIELDS, hx, hy, hz), F32), pltpu.SemaphoreType.DMA],
        compiler_params=pltpu.CompilerParams(vmem_limit_bytes=40 << 20),
    )(*args)


def place_kernel(arrived_ref, order_ref, out_hbm, out_ref, sems):
    groups = arrived_ref.shape[0] // 6
    table = jnp.concatenate(
        [
            jnp.concatenate([arrived_ref[pl.ds(2 * m + c, groups, stride=6), :] for c in range(2)], axis=1)
            for m in range(3)
        ],
        axis=0,
    )
    table = jnp.concatenate(halves(table), axis=0)
    ids = row_ids(WIDE, WIDE).astype(F32).astype(BF16)
    group_ids = row_ids(groups, WIDE)

    copies = []
    for n in range(PIECES):
        for q in range(n * groups // PIECES, (n + 1) * groups // PIECES):
            at = pl.ds(q * WIDE, WIDE)
            got = lookup_rows(
                table, order_ref[:, at], ids, group_ids, groups, lambda index: (index >> log2(WIDE), index & (WIDE - 1))
            )
            out_ref[:, at] = jnp.concatenate(got, axis=0)
        piece = pl.ds(n * groups // PIECES * WIDE, groups // PIECES * WIDE)
        copies.append(pltpu.make_async_copy(out_ref.at[:, piece], out_hbm.at[:, piece], sems.at[n]))
        copies[n].start()
    for copy in copies:
        copy.wait()


def place_call(arrived, order):
    return pl.pallas_call(
        place_kernel,
        out_shape=jax.ShapeDtypeStruct((3, order.shape[1]), F32),
        in_specs=[pl.BlockSpec(memory_space=pltpu.VMEM)] * 2,
        out_specs=pl.BlockSpec(memory_space=pltpu.HBM),
        scratch_shapes=[pltpu.VMEM((3, order.shape[1]), F32), pltpu.SemaphoreType.DMA((PIECES,))],
        compiler_params=pltpu.CompilerParams(vmem_limit_bytes=40 << 20),
    )(arrived, order)


def swap(x, axis, start):
    pairs = [(i, i + 1) for i in range(start, lax.axis_size(axis) - 1, 2)]
    return lax.ppermute(x, axis, pairs + [(j, i) for i, j in pairs])


def on_device(source_fields, slot_source, slot_weight, slot_target, cell_mass, send_order, place_order):
    n_src, n_tgt = lax.axis_size("src"), lax.axis_size("tgt")
    both = ("src", "tgt")
    owners = n_src * n_tgt
    cells = cell_mass.size
    quota = cells // owners

    values = gather_call(source_fields, slot_source.reshape(1, -1), slot_weight.reshape(1, -1))
    values = values.reshape(owners, FIELDS, SPAN // 128, 128)
    values = lax.all_to_all(values, both, split_axis=0, concat_axis=0, tiled=True).reshape(-1, 128)
    v, even, odd = scatter_call(values, slot_target.reshape(1, -1), cell_mass)
    even_block, odd_block = swap(v, "src", 0), swap(v, "src", 1)
    even, odd = swap(even, "tgt", 0), swap(odd, "tgt", 1)
    sides, even, odd = sides_call(even, odd, cell_mass.shape[0])
    even, odd = swap(even, "src", 0), swap(odd, "src", 1)
    projected, outgoing = solve_call(
        (n_src, n_tgt), v, sides, even_block, odd_block, even, odd, cell_mass, send_order
    )

    if quota == WIDE:
        outgoing = outgoing.reshape(owners, 3, 2, 128)
        incoming = lax.all_to_all(outgoing, both, split_axis=0, concat_axis=0, tiled=True)
    else:
        groups = cells // WIDE
        flat = outgoing.reshape(groups, 3, WIDE).transpose(1, 0, 2).reshape(3, owners, quota)
        flat = lax.all_to_all(flat, both, split_axis=1, concat_axis=1, tiled=True)
        incoming = flat.reshape(3, groups, WIDE).transpose(1, 0, 2)
    incoming = incoming.reshape(-1, 128)
    return projected, place_call(incoming, place_order)


def solution(mesh):
    split = P(("src", "tgt"))
    rows = P(("src", "tgt"), None)
    return jax.shard_map(
        on_device,
        mesh=mesh,
        in_specs=(P(None, ("src", "tgt")), split, split, split, P("src", "tgt", None), rows, rows),
        out_specs=(P(None, "src", "tgt", None), P(None, ("src", "tgt"))),
        check_vma=False,
    )
```

```python
import numpy as np

import jax
import jax.numpy as jnp
from jax import lax
from jax.experimental import pallas as pl
from jax.experimental.pallas import tpu as pltpu
from jax.sharding import PartitionSpec as P

ITERS = 4
FIELDS = 7
PIECES = 4
SPAN = 512
AT_ONCE = 32
TOGETHER = 8
WIDE = 256
BF16 = jnp.bfloat16
F32 = jnp.float32
NT = (((1,), (1,)), ((), ()))


def sweep_polynomial(iters, theta, delta):
    sigma = theta / delta
    rho = 1.0 / sigma
    mass = np.array([1.0, 0.125])
    poly = np.polynomial.polynomial
    resid = np.array([1.0])
    step = resid / theta
    total = np.array([0.0])
    for _ in range(iters):
        total = poly.polyadd(total, step)
        resid = poly.polysub(resid, poly.polymul(mass, step))
        rho_new = 1.0 / (2.0 * sigma - rho)
        step = poly.polyadd(rho_new * rho * step, 2.0 * rho_new / delta * resid)
        rho = rho_new
    return [float(c) for c in poly.polyadd(total, step)]


COEFS = sweep_polynomial(ITERS, 1.0, 0.75)


def halves(x):
    high = x.astype(BF16)
    return high, (x - high.astype(F32)).astype(BF16)


def log2(n):
    assert n & (n - 1) == 0
    return n.bit_length() - 1


def row_ids(rows, lanes):
    return lax.broadcasted_iota(jnp.int32, (rows, lanes), 0)


def low_onehot(low, ids):
    return jnp.where(ids == low.astype(F32).astype(BF16), jnp.ones((), BF16), jnp.zeros((), BF16))


def gather_kernel(fields_hbm, index_hbm, weight_hbm, out_ref, table, fields_ref, index_ref, weight_ref, sems):
    pairs = ((fields_hbm, fields_ref), (index_hbm, index_ref), (weight_hbm, weight_ref))
    copies = [pltpu.make_async_copy(src, dst, sems.at[i]) for i, (src, dst) in enumerate(pairs)]
    for copy in copies:
        copy.start()
    lanes = out_ref.shape[1]
    span = SPAN
    tiles = span // lanes
    owners = index_ref.shape[1] // span
    groups = fields_ref.shape[1] // WIDE
    table[...] = jnp.zeros_like(table)
    for copy in copies:
        copy.wait()
    for g in range(groups):
        table[g * 8 : g * 8 + FIELDS, :] = fields_ref[:, g * WIDE : (g + 1) * WIDE]
    high, low = halves(table[...])
    both = jnp.concatenate([high, low], axis=0)
    ids = row_ids(WIDE, span).astype(F32).astype(BF16)
    rows = groups * 8

    def one_owner(q):
        at = pl.multiple_of(q * span, span)
        index = index_ref[:, pl.ds(at, span)]
        weight = weight_ref[:, pl.ds(at, span)]
        onehot = low_onehot(index & (WIDE - 1), ids)
        got = jnp.dot(both, onehot, preferred_element_type=F32)
        group = jnp.broadcast_to(index >> log2(WIDE), (8, span))
        value = jnp.zeros((8, span), F32)
        for g in range(groups):
            part = got[g * 8 : (g + 1) * 8] + got[rows + g * 8 : rows + (g + 1) * 8]
            value = jnp.where(group == g, part, value)
        value = value * weight
        for t in range(tiles):
            out_ref[pl.ds(q * (FIELDS * tiles) + t, FIELDS, stride=tiles), :] = value[
                :FIELDS, t * lanes : (t + 1) * lanes
            ]

    @pl.loop(0, owners // AT_ONCE)
    def _(m):
        for i in range(AT_ONCE):
            one_owner(m * AT_ONCE + i)


def gather_call(fields, index, weight):
    rows = FIELDS * index.shape[1] // 128
    return pl.pallas_call(
        gather_kernel,
        out_shape=jax.ShapeDtypeStruct((rows, 128), F32),
        in_specs=[pl.BlockSpec(memory_space=pltpu.HBM)] * 3,
        out_specs=pl.BlockSpec(memory_space=pltpu.VMEM),
        scratch_shapes=[
            pltpu.VMEM((fields.shape[1] // WIDE * 8, WIDE), F32),
            pltpu.VMEM(fields.shape, F32),
            pltpu.VMEM(index.shape, jnp.int32),
            pltpu.VMEM(weight.shape, F32),
            pltpu.SemaphoreType.DMA((3,)),
        ],
        compiler_params=pltpu.CompilerParams(vmem_limit_bytes=40 << 20),
    )(*[pltpu.with_memory_space_constraint(x, pltpu.HBM) for x in (fields, index, weight)])


def scatter_kernel(value_ref, target_ref, mass_ref, v_ref, even_ref, odd_ref, total):
    lanes = value_ref.shape[1]
    tiles = SPAN // lanes
    owners = target_ref.shape[1] // SPAN
    span = TOGETHER * SPAN
    hx, hy, hz = mass_ref.shape
    groups = hx * hy * hz // WIDE
    total[...] = jnp.zeros_like(total)
    ids = row_ids(WIDE, span).astype(F32).astype(BF16)
    group_ids = row_ids(groups, span).astype(F32).astype(BF16)

    def step(p):
        at = pl.multiple_of(p * span, span)
        target = target_ref[:, pl.ds(at, span)]
        low = ((target >> log2(groups * hz)) << log2(hz)) + (target & (hz - 1))
        onehot = low_onehot(jnp.where(target < 0, -1, low), ids)
        group = ((target >> log2(hz)) & (groups - 1)).astype(F32).astype(BF16)
        here = group_ids == group
        row = p * (TOGETHER * FIELDS * tiles)
        pieces = [i * FIELDS * tiles + t for i in range(TOGETHER) for t in range(tiles)]
        value = jnp.concatenate([value_ref[pl.ds(row + i, FIELDS, stride=tiles), :] for i in pieces], axis=1)
        parts = []
        for half in halves(value):
            for f in range(FIELDS):
                parts.append(jnp.where(here, half[f : f + 1], jnp.zeros((), BF16)))
        spread = jnp.concatenate(parts, axis=0)
        total[...] += lax.dot_general(spread, onehot, NT, preferred_element_type=F32)

    @pl.loop(0, owners // TOGETHER // 4)
    def _(n):
        for i in range(4):
            step(n * 4 + i)

    odd_ref[FIELDS * hx] = jnp.zeros((ITERS, hz), F32)
    scale = lax.rsqrt(mass_ref[...])
    half_x = hx // 2
    odd = lax.axis_index("tgt") % 2 == 1
    for f in range(FIELDS):
        s = total[f * groups : (f + 1) * groups] + total[(FIELDS + f) * groups : (FIELDS + f + 1) * groups]
        for b in range(2):
            for x in range(half_x):
                at = b * half_x + x
                v = s[x * hy : (x + 1) * hy, b * hz : (b + 1) * hz] * scale[at]
                v_ref[f, at] = v
                first, last = v[:ITERS], v[hy - ITERS :]
                even_ref[f * hx + at] = jnp.where(odd, first, last)
                odd_ref[f * hx + at] = jnp.where(odd, last, first)


def scatter_call(values, target, mass):
    hx, hy, hz = mass.shape
    groups = hx * hy * hz // WIDE
    even = jax.ShapeDtypeStruct((FIELDS * hx, ITERS, hz), F32)
    odd = jax.ShapeDtypeStruct((FIELDS * hx + 1, ITERS, hz), F32)
    return pl.pallas_call(
        scatter_kernel,
        out_shape=(jax.ShapeDtypeStruct((FIELDS, hx, hy, hz), F32), even, odd),
        in_specs=[pl.BlockSpec(memory_space=pltpu.VMEM)] * 3,
        out_specs=(pl.BlockSpec(memory_space=pltpu.VMEM),) * 3,
        scratch_shapes=[pltpu.VMEM((2 * FIELDS * groups, WIDE), F32)],
        compiler_params=pltpu.CompilerParams(vmem_limit_bytes=40 << 20),
    )(values, target, mass)


def lookup_rows(table, index, ids, group_ids, groups, at_parts):
    group, low = at_parts(index)
    got = jnp.dot(table, low_onehot(low, ids), preferred_element_type=F32)
    here = group_ids == group
    rows = 3 * groups
    out = []
    for m in range(3):
        part = got[m * groups : (m + 1) * groups] + got[rows + m * groups : rows + (m + 1) * groups]
        out.append(jnp.sum(jnp.where(here, part, 0.0), axis=0, keepdims=True))
    return out


def cell_moduli(vals):
    phi = vals[0]
    mean = (vals[1] + vals[2] + vals[3]) / 3.0
    q2 = 1.5 * (
        (vals[1] - mean) ** 2
        + (vals[2] - mean) ** 2
        + (vals[3] - mean) ** 2
        + 2.0 * (vals[4] ** 2 + vals[5] ** 2 + vals[6] ** 2)
    )
    bulk = 1.6 * jnp.exp(-3.0 * phi) * (1.0 + 0.25 * jnp.tanh(mean))
    shear = 0.9 * jnp.exp(-2.0 * phi) / (1.0 + q2 / 0.5)
    soften = shear * q2 / (0.5 + q2)
    return [bulk, shear, soften]


def corners(sides):
    line = row_ids(2 * ITERS, sides[0].shape[1])
    near = pltpu.roll(sides[1], 2, 0)
    far = jnp.where(line == 4, pltpu.roll(sides[2], 4, 0), pltpu.roll(sides[2], 6, 0))
    return sides[0], jnp.where(line < 4, near, far)


def sides_kernel(even_ref, odd_ref, sides_ref, to_even_ref, to_odd_ref):
    hx = sides_ref.shape[1]
    b_odd = lax.axis_index("tgt") % 2 == 1
    a_odd = lax.axis_index("src") % 2 == 1
    for f in range(FIELDS):
        sides = []
        for x in range(hx):
            even_side, odd_side = even_ref[f * hx + x], odd_ref[f * hx + x]
            right = jnp.where(b_odd, odd_side, even_side)
            left = jnp.where(b_odd, even_side, odd_side)
            sides.append(jnp.concatenate([right, left], axis=0))
            sides_ref[f, x] = sides[x]
        to_left, to_right = corners(sides), corners(sides[::-1])
        to_even_ref[f, :8] = jnp.where(a_odd, to_left[0], to_right[0])
        to_even_ref[f, 8:14] = jnp.where(a_odd, to_left[1], to_right[1])[:6]
        to_odd_ref[f, :8] = jnp.where(a_odd, to_right[0], to_left[0])
        to_odd_ref[f, 8:] = jnp.where(a_odd, to_right[1], to_left[1])


def sides_call(even, odd, hx):
    hz = even.shape[2]
    return pl.pallas_call(
        sides_kernel,
        out_shape=(
            jax.ShapeDtypeStruct((FIELDS, hx, 2 * ITERS, hz), F32),
            jax.ShapeDtypeStruct((FIELDS, 4 * ITERS - 2, hz), F32),
            jax.ShapeDtypeStruct((FIELDS, 4 * ITERS, hz), F32),
        ),
        in_specs=[pl.BlockSpec(memory_space=pltpu.VMEM)] * 2,
        out_specs=(pl.BlockSpec(memory_space=pltpu.VMEM),) * 3,
        compiler_params=pltpu.CompilerParams(vmem_limit_bytes=4 << 20),
        cost_estimate=pl.CostEstimate(flops=40 * 10**9, bytes_accessed=40 * 10**6, transcendentals=0),
    )(even, odd)


def solve_kernel(
    mesh_shape, v_ref, sides_ref, even_ref, odd_ref, even_corners_ref, odd_corners_ref, mass_ref, order_ref,
    projected_hbm, out_ref, projected_ref, sem,
):
    n_src, n_tgt = mesh_shape
    hx, hy, hz = mass_ref.shape
    k = ITERS
    rows = hy + 2 * k
    a, b = lax.axis_index("src"), lax.axis_index("tgt")

    def exists(flag):
        return jnp.where(flag, 1.0, 0.0).astype(F32)

    row = row_ids(rows, hz)
    lane = lax.broadcasted_iota(jnp.int32, (rows, hz), 1)
    inside = jnp.where(row < hy, 1.0, jnp.where(row < hy + k, exists(b < n_tgt - 1), exists(b > 0)))
    inside_left = inside * exists(a > 0)
    inside_right = inside * exists(a < n_src - 1)
    not_first = jnp.where(lane == 0, 0.0, 1.0)
    not_last = jnp.where(lane == hz - 1, 0.0, 1.0)
    scale = lax.rsqrt(mass_ref[...])

    line = row_ids(2 * k, hz)

    def slabs(own, first, packed, from_left):
        second = pltpu.roll(packed, 6, 0)
        third = jnp.where(line < 4, pltpu.roll(packed, 4, 0), pltpu.roll(packed, 2, 0))
        sides = [first, second, third] + [jnp.zeros((2 * k, hz), F32)] * (hx - 3)
        if from_left:
            sides = sides[::-1]
        return [jnp.concatenate([own[x], side], axis=0) for x, side in enumerate(sides)]

    a_odd = a % 2 == 1

    for f in range(FIELDS):
        packed = jnp.concatenate([even_corners_ref[f, 2 * k :], jnp.zeros((2, hz), F32)], axis=0)
        even = (even_ref[f], even_corners_ref[f, : 2 * k], packed)
        odd = (odd_ref[f], odd_corners_ref[f, : 2 * k], odd_corners_ref[f, 2 * k :])
        left = slabs(*[jnp.where(a_odd, p, q) for p, q in zip(even, odd)], True)
        right = slabs(*[jnp.where(a_odd, q, p) for p, q in zip(even, odd)], False)
        own = [jnp.concatenate([v_ref[f, x], sides_ref[f, x]], axis=0) for x in range(hx)]
        base = left + own + right
        u = [COEFS[k] * e for e in base]
        for sweep in range(1, k + 1):
            new = list(u)
            for x in range(sweep, hx + 2 * k - sweep):
                far = max(k - x, x - (k + hx - 1), 0)
                n = rows if sweep + far < k else hy
                w = u[x]
                near = u[x - 1][:n] + u[x + 1][:n]
                near = near + pltpu.roll(w, 1, 0)[:n] + pltpu.roll(w, rows - 1, 0)[:n]
                w = w[:n]
                near = near + pltpu.roll(w, 1, 1) * not_first[:n] + pltpu.roll(w, hz - 1, 1) * not_last[:n]
                if x < k:
                    near = near * inside_left[:n]
                elif x >= k + hx:
                    near = near * inside_right[:n]
                elif n > hy:
                    near = near * inside
                new[x] = COEFS[k - sweep] * base[x][:n] + near
            u = new
        for x in range(hx):
            projected_ref[f, x] = u[k + x][:hy] * scale[x]

    leave = pltpu.make_async_copy(projected_ref, projected_hbm, sem)
    leave.start()
    groups = hx * hy * hz // WIDE
    payload = cell_moduli([projected_ref[f].reshape(hx * hy, hz) for f in range(FIELDS)])
    table = jnp.concatenate([jnp.concatenate([m[:groups], m[groups:]], axis=1) for m in payload], axis=0)
    table = jnp.concatenate(halves(table), axis=0)
    ids = row_ids(WIDE, WIDE).astype(F32).astype(BF16)
    group_ids = row_ids(groups, WIDE)

    def at_parts(index):
        return (index >> log2(hz)) & (groups - 1), ((index >> log2(groups * hz)) << log2(hz)) + (index & (hz - 1))

    for q in range(0, groups, 4):
        lines = []
        for i in range(q, q + 4):
            index = order_ref[:, i * WIDE : (i + 1) * WIDE]
            got = lookup_rows(table, index, ids, group_ids, groups, at_parts)
            lines += [line[:, c * 128 : (c + 1) * 128] for line in got for c in range(2)]
        out_ref[q * 6 : q * 6 + 24, :] = jnp.concatenate(lines, axis=0)
    leave.wait()


def solve_call(mesh_shape, *args):
    mass, order = args[-2:]
    hx, hy, hz = mass.shape

    def kernel(*refs):
        solve_kernel(mesh_shape, *refs)

    return pl.pallas_call(
        kernel,
        out_shape=(
            jax.ShapeDtypeStruct((FIELDS, hx, hy, hz), F32),
            jax.ShapeDtypeStruct((order.shape[1] // WIDE * 6, 128), F32),
        ),
        in_specs=[pl.BlockSpec(memory_space=pltpu.VMEM)] * 8,
        out_specs=(pl.BlockSpec(memory_space=pltpu.HBM), pl.BlockSpec(memory_space=pltpu.VMEM)),
        scratch_shapes=[pltpu.VMEM((FIELDS, hx, hy, hz), F32), pltpu.SemaphoreType.DMA],
        compiler_params=pltpu.CompilerParams(vmem_limit_bytes=40 << 20),
    )(*args)


def place_kernel(arrived_ref, order_ref, out_hbm, out_ref, sems):
    groups = arrived_ref.shape[0] // 6
    table = jnp.concatenate(
        [
            jnp.concatenate([arrived_ref[pl.ds(2 * m + c, groups, stride=6), :] for c in range(2)], axis=1)
            for m in range(3)
        ],
        axis=0,
    )
    table = jnp.concatenate(halves(table), axis=0)
    ids = row_ids(WIDE, WIDE).astype(F32).astype(BF16)
    group_ids = row_ids(groups, WIDE)

    copies = []
    for n in range(PIECES):
        for q in range(n * groups // PIECES, (n + 1) * groups // PIECES):
            at = pl.ds(q * WIDE, WIDE)
            got = lookup_rows(
                table, order_ref[:, at], ids, group_ids, groups, lambda index: (index >> log2(WIDE), index & (WIDE - 1))
            )
            out_ref[:, at] = jnp.concatenate(got, axis=0)
        piece = pl.ds(n * groups // PIECES * WIDE, groups // PIECES * WIDE)
        copies.append(pltpu.make_async_copy(out_ref.at[:, piece], out_hbm.at[:, piece], sems.at[n]))
        copies[n].start()
    for copy in copies:
        copy.wait()


def place_call(arrived, order):
    return pl.pallas_call(
        place_kernel,
        out_shape=jax.ShapeDtypeStruct((3, order.shape[1]), F32),
        in_specs=[pl.BlockSpec(memory_space=pltpu.VMEM)] * 2,
        out_specs=pl.BlockSpec(memory_space=pltpu.HBM),
        scratch_shapes=[pltpu.VMEM((3, order.shape[1]), F32), pltpu.SemaphoreType.DMA((PIECES,))],
        compiler_params=pltpu.CompilerParams(vmem_limit_bytes=40 << 20),
    )(arrived, order)


def swap(x, axis, start):
    pairs = [(i, i + 1) for i in range(start, lax.axis_size(axis) - 1, 2)]
    return lax.ppermute(x, axis, pairs + [(j, i) for i, j in pairs])


def on_device(source_fields, slot_source, slot_weight, slot_target, cell_mass, send_order, place_order):
    n_src, n_tgt = lax.axis_size("src"), lax.axis_size("tgt")
    both = ("src", "tgt")
    owners = n_src * n_tgt
    cells = cell_mass.size
    quota = cells // owners

    values = gather_call(source_fields, slot_source.reshape(1, -1), slot_weight.reshape(1, -1))
    values = values.reshape(owners, FIELDS, SPAN // 128, 128)
    values = lax.all_to_all(values, both, split_axis=0, concat_axis=0, tiled=True).reshape(-1, 128)
    v, even, odd = scatter_call(values, slot_target.reshape(1, -1), cell_mass)
    even_block, odd_block = swap(v, "src", 0), swap(v, "src", 1)
    even, odd = swap(even, "tgt", 0), swap(odd, "tgt", 1)
    sides, even, odd = sides_call(even, odd, cell_mass.shape[0])
    even, odd = swap(even, "src", 0), swap(odd, "src", 1)
    projected, outgoing = solve_call(
        (n_src, n_tgt), v, sides, even_block, odd_block, even, odd, cell_mass, send_order
    )

    if quota == WIDE:
        outgoing = outgoing.reshape(owners, 3, 2, 128)
        incoming = lax.all_to_all(outgoing, both, split_axis=0, concat_axis=0, tiled=True)
    else:
        groups = cells // WIDE
        flat = outgoing.reshape(groups, 3, WIDE).transpose(1, 0, 2).reshape(3, owners, quota)
        flat = lax.all_to_all(flat, both, split_axis=1, concat_axis=1, tiled=True)
        incoming = flat.reshape(3, groups, WIDE).transpose(1, 0, 2)
    incoming = incoming.reshape(-1, 128)
    return projected, place_call(incoming, place_order)


def solution(mesh):
    split = P(("src", "tgt"))
    rows = P(("src", "tgt"), None)
    return jax.shard_map(
        on_device,
        mesh=mesh,
        in_specs=(P(None, ("src", "tgt")), split, split, split, P("src", "tgt", None), rows, rows),
        out_specs=(P(None, "src", "tgt", None), P(None, ("src", "tgt"))),
        check_vma=False,
    )
```

```python
import numpy as np

import jax
import jax.numpy as jnp
from jax import lax
from jax.experimental import pallas as pl
from jax.experimental.pallas import tpu as pltpu
from jax.sharding import PartitionSpec as P

ITERS = 4
FIELDS = 7
HEAD = 4
PIECES = 4
SPAN = 512
AT_ONCE = 32
TOGETHER = 8
WIDE = 256
BF16 = jnp.bfloat16
F32 = jnp.float32
NT = (((1,), (1,)), ((), ()))


def sweep_polynomial(iters, theta, delta):
    sigma = theta / delta
    rho = 1.0 / sigma
    mass = np.array([1.0, 0.125])
    poly = np.polynomial.polynomial
    resid = np.array([1.0])
    step = resid / theta
    total = np.array([0.0])
    for _ in range(iters):
        total = poly.polyadd(total, step)
        resid = poly.polysub(resid, poly.polymul(mass, step))
        rho_new = 1.0 / (2.0 * sigma - rho)
        step = poly.polyadd(rho_new * rho * step, 2.0 * rho_new / delta * resid)
        rho = rho_new
    return [float(c) for c in poly.polyadd(total, step)]


COEFS = sweep_polynomial(ITERS, 1.0, 0.75)


def halves(x):
    high = x.astype(BF16)
    return high, (x - high.astype(F32)).astype(BF16)


def log2(n):
    assert n & (n - 1) == 0
    return n.bit_length() - 1


def row_ids(rows, lanes):
    return lax.broadcasted_iota(jnp.int32, (rows, lanes), 0)


def low_onehot(low, ids):
    return jnp.where(ids == low.astype(F32).astype(BF16), jnp.ones((), BF16), jnp.zeros((), BF16))


def gather_kernel(fields_hbm, index_hbm, weight_hbm, out_ref, table, fields_ref, index_ref, weight_ref, sems):
    pairs = ((fields_hbm, fields_ref), (index_hbm, index_ref), (weight_hbm, weight_ref))
    copies = [pltpu.make_async_copy(src, dst, sems.at[i]) for i, (src, dst) in enumerate(pairs)]
    for copy in copies:
        copy.start()
    lanes = out_ref.shape[1]
    span = SPAN
    tiles = span // lanes
    owners = index_ref.shape[1] // span
    groups = fields_ref.shape[1] // WIDE
    table[...] = jnp.zeros_like(table)
    for copy in copies:
        copy.wait()
    for g in range(groups):
        table[g * 8 : g * 8 + FIELDS, :] = fields_ref[:, g * WIDE : (g + 1) * WIDE]
    high, low = halves(table[...])
    both = jnp.concatenate([high, low], axis=0)
    ids = row_ids(WIDE, span).astype(F32).astype(BF16)
    rows = groups * 8

    def one_owner(q):
        at = pl.multiple_of(q * span, span)
        index = index_ref[:, pl.ds(at, span)]
        weight = weight_ref[:, pl.ds(at, span)]
        onehot = low_onehot(index & (WIDE - 1), ids)
        got = jnp.dot(both, onehot, preferred_element_type=F32)
        group = jnp.broadcast_to(index >> log2(WIDE), (8, span))
        value = jnp.zeros((8, span), F32)
        for g in range(groups):
            part = got[g * 8 : (g + 1) * 8] + got[rows + g * 8 : rows + (g + 1) * 8]
            value = jnp.where(group == g, part, value)
        value = value * weight
        for t in range(tiles):
            out_ref[pl.ds(q * (FIELDS * tiles) + t, FIELDS, stride=tiles), :] = value[
                :FIELDS, t * lanes : (t + 1) * lanes
            ]

    @pl.loop(0, owners // AT_ONCE)
    def _(m):
        for i in range(AT_ONCE):
            one_owner(m * AT_ONCE + i)


def gather_call(fields, index, weight):
    rows = FIELDS * index.shape[1] // 128
    return pl.pallas_call(
        gather_kernel,
        out_shape=jax.ShapeDtypeStruct((rows, 128), F32),
        in_specs=[pl.BlockSpec(memory_space=pltpu.HBM)] * 3,
        out_specs=pl.BlockSpec(memory_space=pltpu.VMEM),
        scratch_shapes=[
            pltpu.VMEM((fields.shape[1] // WIDE * 8, WIDE), F32),
            pltpu.VMEM(fields.shape, F32),
            pltpu.VMEM(index.shape, jnp.int32),
            pltpu.VMEM(weight.shape, F32),
            pltpu.SemaphoreType.DMA((3,)),
        ],
        compiler_params=pltpu.CompilerParams(vmem_limit_bytes=40 << 20),
    )(*[pltpu.with_memory_space_constraint(x, pltpu.HBM) for x in (fields, index, weight)])


def scatter_kernel(value_ref, target_ref, mass_ref, v_ref, even_ref, odd_ref, total):
    lanes = value_ref.shape[1]
    tiles = SPAN // lanes
    owners = target_ref.shape[1] // SPAN
    span = TOGETHER * SPAN
    hx, hy, hz = mass_ref.shape
    groups = hx * hy * hz // WIDE
    total[...] = jnp.zeros_like(total)
    ids = row_ids(WIDE, span).astype(F32).astype(BF16)
    group_ids = row_ids(groups, span).astype(F32).astype(BF16)

    def step(p):
        at = pl.multiple_of(p * span, span)
        target = target_ref[:, pl.ds(at, span)]
        low = ((target >> log2(groups * hz)) << log2(hz)) + (target & (hz - 1))
        onehot = low_onehot(jnp.where(target < 0, -1, low), ids)
        group = ((target >> log2(hz)) & (groups - 1)).astype(F32).astype(BF16)
        here = group_ids == group
        row = p * (TOGETHER * FIELDS * tiles)
        pieces = [i * FIELDS * tiles + t for i in range(TOGETHER) for t in range(tiles)]
        value = jnp.concatenate([value_ref[pl.ds(row + i, FIELDS, stride=tiles), :] for i in pieces], axis=1)
        parts = []
        for half in halves(value):
            for f in range(FIELDS):
                parts.append(jnp.where(here, half[f : f + 1], jnp.zeros((), BF16)))
        spread = jnp.concatenate(parts, axis=0)
        total[...] += lax.dot_general(spread, onehot, NT, preferred_element_type=F32)

    @pl.loop(0, owners // TOGETHER // 4)
    def _(n):
        for i in range(4):
            step(n * 4 + i)

    odd_ref[FIELDS * hx] = jnp.zeros((ITERS, hz), F32)
    scale = lax.rsqrt(mass_ref[...])
    half_x = hx // 2
    odd = lax.axis_index("tgt") % 2 == 1
    for f in range(FIELDS):
        s = total[f * groups : (f + 1) * groups] + total[(FIELDS + f) * groups : (FIELDS + f + 1) * groups]
        for b in range(2):
            for x in range(half_x):
                at = b * half_x + x
                v = s[x * hy : (x + 1) * hy, b * hz : (b + 1) * hz] * scale[at]
                v_ref[f, at] = v
                first, last = v[:ITERS], v[hy - ITERS :]
                even_ref[f * hx + at] = jnp.where(odd, first, last)
                odd_ref[f * hx + at] = jnp.where(odd, last, first)


def scatter_call(values, target, mass):
    hx, hy, hz = mass.shape
    groups = hx * hy * hz // WIDE
    even = jax.ShapeDtypeStruct((FIELDS * hx, ITERS, hz), F32)
    odd = jax.ShapeDtypeStruct((FIELDS * hx + 1, ITERS, hz), F32)
    return pl.pallas_call(
        scatter_kernel,
        out_shape=(jax.ShapeDtypeStruct((FIELDS, hx, hy, hz), F32), even, odd),
        in_specs=[pl.BlockSpec(memory_space=pltpu.VMEM)] * 3,
        out_specs=(pl.BlockSpec(memory_space=pltpu.VMEM),) * 3,
        scratch_shapes=[pltpu.VMEM((2 * FIELDS * groups, WIDE), F32)],
        compiler_params=pltpu.CompilerParams(vmem_limit_bytes=40 << 20),
    )(values, target, mass)


def lookup_rows(table, index, ids, group_ids, groups, at_parts):
    group, low = at_parts(index)
    got = jnp.dot(table, low_onehot(low, ids), preferred_element_type=F32)
    here = group_ids == group
    rows = 3 * groups
    out = []
    for m in range(3):
        part = got[m * groups : (m + 1) * groups] + got[rows + m * groups : rows + (m + 1) * groups]
        out.append(jnp.sum(jnp.where(here, part, 0.0), axis=0, keepdims=True))
    return out


def cell_moduli(vals):
    phi = vals[0]
    mean = (vals[1] + vals[2] + vals[3]) / 3.0
    q2 = 1.5 * (
        (vals[1] - mean) ** 2
        + (vals[2] - mean) ** 2
        + (vals[3] - mean) ** 2
        + 2.0 * (vals[4] ** 2 + vals[5] ** 2 + vals[6] ** 2)
    )
    bulk = 1.6 * jnp.exp(-3.0 * phi) * (1.0 + 0.25 * jnp.tanh(mean))
    shear = 0.9 * jnp.exp(-2.0 * phi) / (1.0 + q2 / 0.5)
    soften = shear * q2 / (0.5 + q2)
    return [bulk, shear, soften]


def corners(sides):
    line = row_ids(2 * ITERS, sides[0].shape[1])
    near = pltpu.roll(sides[1], 2, 0)
    far = jnp.where(line == 4, pltpu.roll(sides[2], 4, 0), pltpu.roll(sides[2], 6, 0))
    return sides[0], jnp.where(line < 4, near, far)


def sides_kernel(even_ref, odd_ref, sides_ref, to_even_ref, to_odd_ref):
    hx = sides_ref.shape[1]
    b_odd = lax.axis_index("tgt") % 2 == 1
    a_odd = lax.axis_index("src") % 2 == 1
    for f in range(FIELDS):
        sides = []
        for x in range(hx):
            even_side, odd_side = even_ref[f * hx + x], odd_ref[f * hx + x]
            right = jnp.where(b_odd, odd_side, even_side)
            left = jnp.where(b_odd, even_side, odd_side)
            sides.append(jnp.concatenate([right, left], axis=0))
            sides_ref[f, x] = sides[x]
        to_left, to_right = corners(sides), corners(sides[::-1])
        to_even_ref[f, :8] = jnp.where(a_odd, to_left[0], to_right[0])
        to_even_ref[f, 8:14] = jnp.where(a_odd, to_left[1], to_right[1])[:6]
        to_odd_ref[f, :8] = jnp.where(a_odd, to_right[0], to_left[0])
        to_odd_ref[f, 8:] = jnp.where(a_odd, to_right[1], to_left[1])


def sides_call(even, odd, hx):
    hz = even.shape[2]
    return pl.pallas_call(
        sides_kernel,
        out_shape=(
            jax.ShapeDtypeStruct((FIELDS, hx, 2 * ITERS, hz), F32),
            jax.ShapeDtypeStruct((FIELDS, 4 * ITERS - 2, hz), F32),
            jax.ShapeDtypeStruct((FIELDS, 4 * ITERS, hz), F32),
        ),
        in_specs=[pl.BlockSpec(memory_space=pltpu.VMEM)] * 2,
        out_specs=(pl.BlockSpec(memory_space=pltpu.VMEM),) * 3,
        compiler_params=pltpu.CompilerParams(vmem_limit_bytes=4 << 20),
        cost_estimate=pl.CostEstimate(flops=40 * 10**9, bytes_accessed=40 * 10**6, transcendentals=0),
    )(even, odd)


def solve_kernel(
    mesh_shape, v_ref, sides_ref, even_ref, head_ref, tail_ref, even_corners_ref, odd_corners_ref, mass_ref, order_ref,
    projected_hbm, out_ref, projected_ref, sem,
):
    n_src, n_tgt = mesh_shape
    hx, hy, hz = mass_ref.shape
    k = ITERS
    rows = hy + 2 * k
    a, b = lax.axis_index("src"), lax.axis_index("tgt")

    def exists(flag):
        return jnp.where(flag, 1.0, 0.0).astype(F32)

    row = row_ids(rows, hz)
    lane = lax.broadcasted_iota(jnp.int32, (rows, hz), 1)
    inside = jnp.where(row < hy, 1.0, jnp.where(row < hy + k, exists(b < n_tgt - 1), exists(b > 0)))
    inside_left = inside * exists(a > 0)
    inside_right = inside * exists(a < n_src - 1)
    not_first = jnp.where(lane == 0, 0.0, 1.0)
    not_last = jnp.where(lane == hz - 1, 0.0, 1.0)
    scale = lax.rsqrt(mass_ref[...])

    line = row_ids(2 * k, hz)

    def slabs(own, first, packed, from_left):
        second = pltpu.roll(packed, 6, 0)
        third = jnp.where(line < 4, pltpu.roll(packed, 4, 0), pltpu.roll(packed, 2, 0))
        sides = [first, second, third] + [jnp.zeros((2 * k, hz), F32)] * (hx - 3)
        if from_left:
            sides = sides[::-1]
        return [jnp.concatenate([own[x], side], axis=0) for x, side in enumerate(sides)]

    a_odd = a % 2 == 1

    for f in range(FIELDS):
        packed = jnp.concatenate([even_corners_ref[f, 2 * k :], jnp.zeros((2, hz), F32)], axis=0)
        even = (even_ref[f], even_corners_ref[f, : 2 * k], packed)
        odd_block = head_ref[f] if f < HEAD else tail_ref[f - HEAD]
        odd = (odd_block, odd_corners_ref[f, : 2 * k], odd_corners_ref[f, 2 * k :])
        left = slabs(*[jnp.where(a_odd, p, q) for p, q in zip(even, odd)], True)
        right = slabs(*[jnp.where(a_odd, q, p) for p, q in zip(even, odd)], False)
        own = [jnp.concatenate([v_ref[f, x], sides_ref[f, x]], axis=0) for x in range(hx)]
        base = left + own + right
        u = [COEFS[k] * e for e in base]
        for sweep in range(1, k + 1):
            new = list(u)
            for x in range(sweep, hx + 2 * k - sweep):
                far = max(k - x, x - (k + hx - 1), 0)
                n = rows if sweep + far < k else hy
                w = u[x]
                near = u[x - 1][:n] + u[x + 1][:n]
                near = near + pltpu.roll(w, 1, 0)[:n] + pltpu.roll(w, rows - 1, 0)[:n]
                w = w[:n]
                near = near + pltpu.roll(w, 1, 1) * not_first[:n] + pltpu.roll(w, hz - 1, 1) * not_last[:n]
                if x < k:
                    near = near * inside_left[:n]
                elif x >= k + hx:
                    near = near * inside_right[:n]
                elif n > hy:
                    near = near * inside
                new[x] = COEFS[k - sweep] * base[x][:n] + near
            u = new
        for x in range(hx):
            projected_ref[f, x] = u[k + x][:hy] * scale[x]

    leave = pltpu.make_async_copy(projected_ref, projected_hbm, sem)
    leave.start()
    groups = hx * hy * hz // WIDE
    payload = cell_moduli([projected_ref[f].reshape(hx * hy, hz) for f in range(FIELDS)])
    table = jnp.concatenate([jnp.concatenate([m[:groups], m[groups:]], axis=1) for m in payload], axis=0)
    table = jnp.concatenate(halves(table), axis=0)
    ids = row_ids(WIDE, WIDE).astype(F32).astype(BF16)
    group_ids = row_ids(groups, WIDE)

    def at_parts(index):
        return (index >> log2(hz)) & (groups - 1), ((index >> log2(groups * hz)) << log2(hz)) + (index & (hz - 1))

    for q in range(0, groups, 4):
        lines = []
        for i in range(q, q + 4):
            index = order_ref[:, i * WIDE : (i + 1) * WIDE]
            got = lookup_rows(table, index, ids, group_ids, groups, at_parts)
            lines += [line[:, c * 128 : (c + 1) * 128] for line in got for c in range(2)]
        out_ref[q * 6 : q * 6 + 24, :] = jnp.concatenate(lines, axis=0)
    leave.wait()


def solve_call(mesh_shape, *args):
    mass, order = args[-2:]
    hx, hy, hz = mass.shape

    def kernel(*refs):
        solve_kernel(mesh_shape, *refs)

    return pl.pallas_call(
        kernel,
        out_shape=(
            jax.ShapeDtypeStruct((FIELDS, hx, hy, hz), F32),
            jax.ShapeDtypeStruct((order.shape[1] // WIDE * 6, 128), F32),
        ),
        in_specs=[pl.BlockSpec(memory_space=pltpu.VMEM)] * 9,
        out_specs=(pl.BlockSpec(memory_space=pltpu.HBM), pl.BlockSpec(memory_space=pltpu.VMEM)),
        scratch_shapes=[pltpu.VMEM((FIELDS, hx, hy, hz), F32), pltpu.SemaphoreType.DMA],
        compiler_params=pltpu.CompilerParams(vmem_limit_bytes=40 << 20),
    )(*args)


def place_kernel(arrived_ref, order_ref, out_hbm, out_ref, sems):
    groups = arrived_ref.shape[0] // 6
    table = jnp.concatenate(
        [
            jnp.concatenate([arrived_ref[pl.ds(2 * m + c, groups, stride=6), :] for c in range(2)], axis=1)
            for m in range(3)
        ],
        axis=0,
    )
    table = jnp.concatenate(halves(table), axis=0)
    ids = row_ids(WIDE, WIDE).astype(F32).astype(BF16)
    group_ids = row_ids(groups, WIDE)

    copies = []
    for n in range(PIECES):
        for q in range(n * groups // PIECES, (n + 1) * groups // PIECES):
            at = pl.ds(q * WIDE, WIDE)
            got = lookup_rows(
                table, order_ref[:, at], ids, group_ids, groups, lambda index: (index >> log2(WIDE), index & (WIDE - 1))
            )
            out_ref[:, at] = jnp.concatenate(got, axis=0)
        piece = pl.ds(n * groups // PIECES * WIDE, groups // PIECES * WIDE)
        copies.append(pltpu.make_async_copy(out_ref.at[:, piece], out_hbm.at[:, piece], sems.at[n]))
        copies[n].start()
    for copy in copies:
        copy.wait()


def place_call(arrived, order):
    return pl.pallas_call(
        place_kernel,
        out_shape=jax.ShapeDtypeStruct((3, order.shape[1]), F32),
        in_specs=[pl.BlockSpec(memory_space=pltpu.VMEM)] * 2,
        out_specs=pl.BlockSpec(memory_space=pltpu.HBM),
        scratch_shapes=[pltpu.VMEM((3, order.shape[1]), F32), pltpu.SemaphoreType.DMA((PIECES,))],
        compiler_params=pltpu.CompilerParams(vmem_limit_bytes=40 << 20),
    )(arrived, order)


def swap(x, axis, start):
    pairs = [(i, i + 1) for i in range(start, lax.axis_size(axis) - 1, 2)]
    return lax.ppermute(x, axis, pairs + [(j, i) for i, j in pairs])


def on_device(source_fields, slot_source, slot_weight, slot_target, cell_mass, send_order, place_order):
    n_src, n_tgt = lax.axis_size("src"), lax.axis_size("tgt")
    both = ("src", "tgt")
    owners = n_src * n_tgt
    cells = cell_mass.size
    quota = cells // owners

    values = gather_call(source_fields, slot_source.reshape(1, -1), slot_weight.reshape(1, -1))
    values = values.reshape(owners, FIELDS, SPAN // 128, 128)
    values = lax.all_to_all(values, both, split_axis=0, concat_axis=0, tiled=True).reshape(-1, 128)
    v, even, odd = scatter_call(values, slot_target.reshape(1, -1), cell_mass)
    even_block, head = swap(v, "src", 0), swap(v[:HEAD], "src", 1)
    across = [(i, i + 2 if i % 2 == 0 else i - 2) for i in range(n_src)]
    tail = lax.ppermute(even_block[HEAD:], "src", [(i, j) for i, j in across if 0 <= j < n_src])
    even, odd = swap(even, "tgt", 0), swap(odd, "tgt", 1)
    sides, even, odd = sides_call(even, odd, cell_mass.shape[0])
    even, odd = swap(even, "src", 0), swap(odd, "src", 1)
    projected, outgoing = solve_call(
        (n_src, n_tgt), v, sides, even_block, head, tail, even, odd, cell_mass, send_order
    )

    if quota == WIDE:
        outgoing = outgoing.reshape(owners, 3, 2, 128)
        incoming = lax.all_to_all(outgoing, both, split_axis=0, concat_axis=0, tiled=True)
    else:
        groups = cells // WIDE
        flat = outgoing.reshape(groups, 3, WIDE).transpose(1, 0, 2).reshape(3, owners, quota)
        flat = lax.all_to_all(flat, both, split_axis=1, concat_axis=1, tiled=True)
        incoming = flat.reshape(3, groups, WIDE).transpose(1, 0, 2)
    incoming = incoming.reshape(-1, 128)
    return projected, place_call(incoming, place_order)


def solution(mesh):
    split = P(("src", "tgt"))
    rows = P(("src", "tgt"), None)
    return jax.shard_map(
        on_device,
        mesh=mesh,
        in_specs=(P(None, ("src", "tgt")), split, split, split, P("src", "tgt", None), rows, rows),
        out_specs=(P(None, "src", "tgt", None), P(None, ("src", "tgt"))),
        check_vma=False,
    )
```

```python
import functools

import numpy as np

import jax
import jax.numpy as jnp
from jax import lax
from jax.experimental import pallas as pl
from jax.experimental.pallas import tpu as pltpu
from jax.sharding import PartitionSpec as P

ITERS = 4
FIELDS = 7
PIECES = 4
SPAN = 512
AT_ONCE = 32
TOGETHER = 8
WIDE = 256
BF16 = jnp.bfloat16
F32 = jnp.float32
NT = (((1,), (1,)), ((), ()))


def sweep_polynomial(iters, theta, delta):
    sigma = theta / delta
    rho = 1.0 / sigma
    mass = np.array([1.0, 0.125])
    poly = np.polynomial.polynomial
    resid = np.array([1.0])
    step = resid / theta
    total = np.array([0.0])
    for _ in range(iters):
        total = poly.polyadd(total, step)
        resid = poly.polysub(resid, poly.polymul(mass, step))
        rho_new = 1.0 / (2.0 * sigma - rho)
        step = poly.polyadd(rho_new * rho * step, 2.0 * rho_new / delta * resid)
        rho = rho_new
    return [float(c) for c in poly.polyadd(total, step)]


COEFS = sweep_polynomial(ITERS, 1.0, 0.75)


def halves(x):
    high = x.astype(BF16)
    return high, (x - high.astype(F32)).astype(BF16)


def log2(n):
    assert n & (n - 1) == 0
    return n.bit_length() - 1


def row_ids(rows, lanes):
    return lax.broadcasted_iota(jnp.int32, (rows, lanes), 0)


def low_onehot(low, ids):
    return jnp.where(ids == low.astype(F32).astype(BF16), jnp.ones((), BF16), jnp.zeros((), BF16))


def gather_kernel(fields_hbm, index_hbm, weight_hbm, out_ref, table, fields_ref, index_ref, weight_ref, sems):
    pairs = ((fields_hbm, fields_ref), (index_hbm, index_ref), (weight_hbm, weight_ref))
    copies = [pltpu.make_async_copy(src, dst, sems.at[i]) for i, (src, dst) in enumerate(pairs)]
    for copy in copies:
        copy.start()
    lanes = out_ref.shape[1]
    span = SPAN
    tiles = span // lanes
    owners = index_ref.shape[1] // span
    groups = fields_ref.shape[1] // WIDE
    table[...] = jnp.zeros_like(table)
    for copy in copies:
        copy.wait()
    for g in range(groups):
        table[g * 8 : g * 8 + FIELDS, :] = fields_ref[:, g * WIDE : (g + 1) * WIDE]
    high, low = halves(table[...])
    both = jnp.concatenate([high, low], axis=0)
    ids = row_ids(WIDE, span).astype(F32).astype(BF16)
    rows = groups * 8

    def one_owner(q):
        at = pl.multiple_of(q * span, span)
        index = index_ref[:, pl.ds(at, span)]
        weight = weight_ref[:, pl.ds(at, span)]
        onehot = low_onehot(index & (WIDE - 1), ids)
        got = jnp.dot(both, onehot, preferred_element_type=F32)
        group = jnp.broadcast_to(index >> log2(WIDE), (8, span))
        value = jnp.zeros((8, span), F32)
        for g in range(groups):
            part = got[g * 8 : (g + 1) * 8] + got[rows + g * 8 : rows + (g + 1) * 8]
            value = jnp.where(group == g, part, value)
        value = value * weight
        for t in range(tiles):
            out_ref[pl.ds(q * (FIELDS * tiles) + t, FIELDS, stride=tiles), :] = value[
                :FIELDS, t * lanes : (t + 1) * lanes
            ]

    @pl.loop(0, owners // AT_ONCE)
    def _(m):
        for i in range(AT_ONCE):
            one_owner(m * AT_ONCE + i)


def gather_call(fields, index, weight):
    rows = FIELDS * index.shape[1] // 128
    return pl.pallas_call(
        gather_kernel,
        out_shape=jax.ShapeDtypeStruct((rows, 128), F32),
        in_specs=[pl.BlockSpec(memory_space=pltpu.HBM)] * 3,
        out_specs=pl.BlockSpec(memory_space=pltpu.VMEM),
        scratch_shapes=[
            pltpu.VMEM((fields.shape[1] // WIDE * 8, WIDE), F32),
            pltpu.VMEM(fields.shape, F32),
            pltpu.VMEM(index.shape, jnp.int32),
            pltpu.VMEM(weight.shape, F32),
            pltpu.SemaphoreType.DMA((3,)),
        ],
        compiler_params=pltpu.CompilerParams(vmem_limit_bytes=40 << 20),
    )(*[pltpu.with_memory_space_constraint(x, pltpu.HBM) for x in (fields, index, weight)])


def scatter_kernel(value_ref, target_ref, mass_ref, v_ref, strips_ref, total):
    lanes = value_ref.shape[1]
    tiles = SPAN // lanes
    owners = target_ref.shape[1] // SPAN
    span = TOGETHER * SPAN
    hx, hy, hz = mass_ref.shape
    groups = hx * hy * hz // WIDE
    total[...] = jnp.zeros_like(total)
    ids = row_ids(WIDE, span).astype(F32).astype(BF16)
    group_ids = row_ids(groups, span).astype(F32).astype(BF16)

    def step(p):
        at = pl.multiple_of(p * span, span)
        target = target_ref[:, pl.ds(at, span)]
        low = ((target >> log2(groups * hz)) << log2(hz)) + (target & (hz - 1))
        onehot = low_onehot(jnp.where(target < 0, -1, low), ids)
        group = ((target >> log2(hz)) & (groups - 1)).astype(F32).astype(BF16)
        here = group_ids == group
        row = p * (TOGETHER * FIELDS * tiles)
        pieces = [i * FIELDS * tiles + t for i in range(TOGETHER) for t in range(tiles)]
        value = jnp.concatenate([value_ref[pl.ds(row + i, FIELDS, stride=tiles), :] for i in pieces], axis=1)
        parts = []
        for half in halves(value):
            for f in range(FIELDS):
                parts.append(jnp.where(here, half[f : f + 1], jnp.zeros((), BF16)))
        spread = jnp.concatenate(parts, axis=0)
        total[...] += lax.dot_general(spread, onehot, NT, preferred_element_type=F32)

    @pl.loop(0, owners // TOGETHER // 4)
    def _(n):
        for i in range(4):
            step(n * 4 + i)

    scale = lax.rsqrt(mass_ref[...])
    half_x = hx // 2
    odd = lax.axis_index("tgt") % 2 == 1
    for f in range(FIELDS):
        s = total[f * groups : (f + 1) * groups] + total[(FIELDS + f) * groups : (FIELDS + f + 1) * groups]
        for b in range(2):
            for x in range(half_x):
                at = b * half_x + x
                v = s[x * hy : (x + 1) * hy, b * hz : (b + 1) * hz] * scale[at]
                v_ref[f, at] = v
                first, last = v[:ITERS], v[hy - ITERS :]
                strips_ref[0, f * hx + at] = jnp.where(odd, first, last)
                strips_ref[1, f * hx + at] = jnp.where(odd, last, first)


def scatter_call(values, target, mass):
    hx, hy, hz = mass.shape
    groups = hx * hy * hz // WIDE
    strips = jax.ShapeDtypeStruct((2, FIELDS * hx, ITERS, hz), F32)
    return pl.pallas_call(
        scatter_kernel,
        out_shape=(jax.ShapeDtypeStruct((FIELDS, hx, hy, hz), F32), strips),
        in_specs=[pl.BlockSpec(memory_space=pltpu.VMEM)] * 3,
        out_specs=(pl.BlockSpec(memory_space=pltpu.VMEM),) * 2,
        scratch_shapes=[pltpu.VMEM((2 * FIELDS * groups, WIDE), F32)],
        compiler_params=pltpu.CompilerParams(vmem_limit_bytes=40 << 20),
    )(values, target, mass)


def lookup_rows(table, index, ids, group_ids, groups, at_parts):
    group, low = at_parts(index)
    got = jnp.dot(table, low_onehot(low, ids), preferred_element_type=F32)
    here = group_ids == group
    rows = 3 * groups
    out = []
    for m in range(3):
        part = got[m * groups : (m + 1) * groups] + got[rows + m * groups : rows + (m + 1) * groups]
        out.append(jnp.sum(jnp.where(here, part, 0.0), axis=0, keepdims=True))
    return out


def cell_moduli(vals):
    phi = vals[0]
    mean = (vals[1] + vals[2] + vals[3]) / 3.0
    q2 = 1.5 * (
        (vals[1] - mean) ** 2
        + (vals[2] - mean) ** 2
        + (vals[3] - mean) ** 2
        + 2.0 * (vals[4] ** 2 + vals[5] ** 2 + vals[6] ** 2)
    )
    bulk = 1.6 * jnp.exp(-3.0 * phi) * (1.0 + 0.25 * jnp.tanh(mean))
    shear = 0.9 * jnp.exp(-2.0 * phi) / (1.0 + q2 / 0.5)
    soften = shear * q2 / (0.5 + q2)
    return [bulk, shear, soften]


def pack_corners(sides):
    first, second, third = sides[:3]
    line = row_ids(2 * ITERS, first.shape[1])
    far = jnp.where(line == 3, pltpu.roll(third, 3, 0), pltpu.roll(third, 5, 0))
    first = jnp.where((line == 3) | (line == 4), far, first)
    return first[:4], first[4:], pltpu.roll(second, 2, 0)[:4]


def unpack_corners(pieces):
    first = jnp.concatenate([pieces[0], pieces[1]], axis=0)
    line = row_ids(2 * ITERS, first.shape[1])
    second = pltpu.roll(jnp.concatenate([pieces[2], pieces[2]], axis=0), 6, 0)
    third = jnp.where(line < 4, pltpu.roll(first, 5, 0), pltpu.roll(first, 3, 0))
    return [first, second, third]


def inner(axis, count):
    index = lax.axis_index(axis)
    return (index > 0) & (index < count - 1)


def sides_kernel(n_tgt, even_ref, odd_ref, block_ref, sides_ref, corners_ref):
    del block_ref
    hx = sides_ref.shape[1]
    b_odd = lax.axis_index("tgt") % 2 == 1
    a_odd = lax.axis_index("src") % 2 == 1
    has_odd = inner("tgt", n_tgt)
    for f in range(FIELDS):
        sides = []
        for x in range(hx):
            even_side = even_ref[0, f * hx + x]
            odd_side = jnp.where(has_odd, odd_ref[f * hx + x], 0.0)
            right = jnp.where(b_odd, odd_side, even_side)
            left = jnp.where(b_odd, even_side, odd_side)
            sides.append(jnp.concatenate([right, left], axis=0))
            sides_ref[f, x] = sides[x]
        for i, (to_left, to_right) in enumerate(zip(pack_corners(sides), pack_corners(sides[::-1]))):
            corners_ref[0, f * 3 + i] = jnp.where(a_odd, to_left, to_right)
            corners_ref[1, f * 3 + i] = jnp.where(a_odd, to_right, to_left)


def sides_call(n_tgt, even, odd, block):
    hx, _, hz = block.shape[1:]
    return pl.pallas_call(
        functools.partial(sides_kernel, n_tgt),
        out_shape=(
            jax.ShapeDtypeStruct((FIELDS, hx, 2 * ITERS, hz), F32),
            jax.ShapeDtypeStruct((2, FIELDS * 3, 4, hz), F32),
        ),
        in_specs=[pl.BlockSpec(memory_space=pltpu.VMEM)] * 2 + [pl.BlockSpec(memory_space=pl.ANY)],
        out_specs=(pl.BlockSpec(memory_space=pltpu.VMEM),) * 2,
        compiler_params=pltpu.CompilerParams(vmem_limit_bytes=4 << 20),
    )(even, odd, block)


def solve_kernel(
    mesh_shape, v_ref, sides_ref, even_ref, odd_ref, even_corners_ref, odd_corners_ref, mass_ref, order_ref,
    projected_hbm, out_ref, projected_ref, sem,
):
    n_src, n_tgt = mesh_shape
    hx, hy, hz = mass_ref.shape
    k = ITERS
    rows = hy + 2 * k
    a, b = lax.axis_index("src"), lax.axis_index("tgt")

    def exists(flag):
        return jnp.where(flag, 1.0, 0.0).astype(F32)

    row = row_ids(rows, hz)
    lane = lax.broadcasted_iota(jnp.int32, (rows, hz), 1)
    inside = jnp.where(row < hy, 1.0, jnp.where(row < hy + k, exists(b < n_tgt - 1), exists(b > 0)))
    inside_left = inside * exists(a > 0)
    inside_right = inside * exists(a < n_src - 1)
    not_first = jnp.where(lane == 0, 0.0, 1.0)
    not_last = jnp.where(lane == hz - 1, 0.0, 1.0)
    scale = lax.rsqrt(mass_ref[...])

    line = row_ids(2 * k, hz)

    def slabs(own, ends, from_left):
        sides = unpack_corners(ends) + [jnp.zeros((2 * k, hz), F32)] * (hx - 3)
        if from_left:
            sides = sides[::-1]
        return [jnp.concatenate([own[x], side], axis=0) for x, side in enumerate(sides)]

    a_odd = a % 2 == 1
    has_odd = inner("src", n_src)

    for f in range(FIELDS):
        even = [even_corners_ref[0, f * 3 + i] for i in range(3)]
        odd = [jnp.where(has_odd, odd_corners_ref[f * 3 + i], 0.0) for i in range(3)]
        odd_block = jnp.where(has_odd, odd_ref[f], 0.0)
        left = slabs(jnp.where(a_odd, even_ref[f], odd_block), [jnp.where(a_odd, p, q) for p, q in zip(even, odd)], True)
        right = slabs(jnp.where(a_odd, odd_block, even_ref[f]), [jnp.where(a_odd, q, p) for p, q in zip(even, odd)], False)
        own = [jnp.concatenate([v_ref[f, x], sides_ref[f, x]], axis=0) for x in range(hx)]
        base = left + own + right
        u = [COEFS[k] * e for e in base]
        for sweep in range(1, k + 1):
            new = list(u)
            for x in range(sweep, hx + 2 * k - sweep):
                far = max(k - x, x - (k + hx - 1), 0)
                n = rows if sweep + far < k else hy
                w = u[x]
                near = u[x - 1][:n] + u[x + 1][:n]
                near = near + pltpu.roll(w, 1, 0)[:n] + pltpu.roll(w, rows - 1, 0)[:n]
                w = w[:n]
                near = near + pltpu.roll(w, 1, 1) * not_first[:n] + pltpu.roll(w, hz - 1, 1) * not_last[:n]
                if x < k:
                    near = near * inside_left[:n]
                elif x >= k + hx:
                    near = near * inside_right[:n]
                elif n > hy:
                    near = near * inside
                new[x] = COEFS[k - sweep] * base[x][:n] + near
            u = new
        for x in range(hx):
            projected_ref[f, x] = u[k + x][:hy] * scale[x]

    leave = pltpu.make_async_copy(projected_ref, projected_hbm, sem)
    leave.start()
    groups = hx * hy * hz // WIDE
    payload = cell_moduli([projected_ref[f].reshape(hx * hy, hz) for f in range(FIELDS)])
    table = jnp.concatenate([jnp.concatenate([m[:groups], m[groups:]], axis=1) for m in payload], axis=0)
    table = jnp.concatenate(halves(table), axis=0)
    ids = row_ids(WIDE, WIDE).astype(F32).astype(BF16)
    group_ids = row_ids(groups, WIDE)

    def at_parts(index):
        return (index >> log2(hz)) & (groups - 1), ((index >> log2(groups * hz)) << log2(hz)) + (index & (hz - 1))

    for q in range(0, groups, 4):
        lines = []
        for i in range(q, q + 4):
            index = order_ref[:, i * WIDE : (i + 1) * WIDE]
            got = lookup_rows(table, index, ids, group_ids, groups, at_parts)
            lines += [line[:, c * 128 : (c + 1) * 128] for line in got for c in range(2)]
        out_ref[q * 6 : q * 6 + 24, :] = jnp.concatenate(lines, axis=0)
    leave.wait()


def solve_call(mesh_shape, *args):
    mass, order = args[-2:]
    hx, hy, hz = mass.shape

    def kernel(*refs):
        solve_kernel(mesh_shape, *refs)

    return pl.pallas_call(
        kernel,
        out_shape=(
            jax.ShapeDtypeStruct((FIELDS, hx, hy, hz), F32),
            jax.ShapeDtypeStruct((order.shape[1] // WIDE * 6, 128), F32),
        ),
        in_specs=[pl.BlockSpec(memory_space=pltpu.VMEM)] * 8,
        out_specs=(pl.BlockSpec(memory_space=pltpu.HBM), pl.BlockSpec(memory_space=pltpu.VMEM)),
        scratch_shapes=[pltpu.VMEM((FIELDS, hx, hy, hz), F32), pltpu.SemaphoreType.DMA],
        compiler_params=pltpu.CompilerParams(vmem_limit_bytes=40 << 20),
    )(*args)


def place_kernel(arrived_ref, order_ref, out_hbm, out_ref, sems):
    groups = arrived_ref.shape[0] // 6
    table = jnp.concatenate(
        [
            jnp.concatenate([arrived_ref[pl.ds(2 * m + c, groups, stride=6), :] for c in range(2)], axis=1)
            for m in range(3)
        ],
        axis=0,
    )
    table = jnp.concatenate(halves(table), axis=0)
    ids = row_ids(WIDE, WIDE).astype(F32).astype(BF16)
    group_ids = row_ids(groups, WIDE)

    copies = []
    for n in range(PIECES):
        for q in range(n * groups // PIECES, (n + 1) * groups // PIECES):
            at = pl.ds(q * WIDE, WIDE)
            got = lookup_rows(
                table, order_ref[:, at], ids, group_ids, groups, lambda index: (index >> log2(WIDE), index & (WIDE - 1))
            )
            out_ref[:, at] = jnp.concatenate(got, axis=0)
        piece = pl.ds(n * groups // PIECES * WIDE, groups // PIECES * WIDE)
        copies.append(pltpu.make_async_copy(out_ref.at[:, piece], out_hbm.at[:, piece], sems.at[n]))
        copies[n].start()
    for copy in copies:
        copy.wait()


def place_call(arrived, order):
    return pl.pallas_call(
        place_kernel,
        out_shape=jax.ShapeDtypeStruct((3, order.shape[1]), F32),
        in_specs=[pl.BlockSpec(memory_space=pltpu.VMEM)] * 2,
        out_specs=pl.BlockSpec(memory_space=pltpu.HBM),
        scratch_shapes=[pltpu.VMEM((3, order.shape[1]), F32), pltpu.SemaphoreType.DMA((PIECES,))],
        compiler_params=pltpu.CompilerParams(vmem_limit_bytes=40 << 20),
    )(arrived, order)


def swap(x, axis):
    return lax.ppermute(x, axis, [(i, i ^ 1) for i in range(lax.axis_size(axis))])


def ring(x, axis, evens):
    count = lax.axis_size(axis)
    pairs = []
    for i in range(count):
        to = i + (evens if i % 2 == 0 else -evens)
        pairs.append((i, to if 0 <= to < count else i ^ 1))
    return lax.ppermute(x, axis, pairs)


def on_device(source_fields, slot_source, slot_weight, slot_target, cell_mass, send_order, place_order):
    n_src, n_tgt = lax.axis_size("src"), lax.axis_size("tgt")
    both = ("src", "tgt")
    owners = n_src * n_tgt
    cells = cell_mass.size
    quota = cells // owners

    values = gather_call(source_fields, slot_source.reshape(1, -1), slot_weight.reshape(1, -1))
    values = values.reshape(owners, FIELDS, SPAN // 128, 128)
    values = lax.all_to_all(values, both, split_axis=0, concat_axis=0, tiled=True).reshape(-1, 128)
    v, strips = scatter_call(values, slot_target.reshape(1, -1), cell_mass)
    strips = swap(strips, "tgt")
    even_block = swap(v, "src")
    far_block = ring(v, "src", -2)
    odd_strips = ring(strips[1], "tgt", 2)
    sides, ends = sides_call(n_tgt, strips, odd_strips, far_block)
    ends = swap(ends, "src")
    odd_ends = ring(ends[1], "src", 2)
    odd_block = swap(far_block, "src")
    projected, outgoing = solve_call(
        (n_src, n_tgt), v, sides, even_block, odd_block, ends, odd_ends, cell_mass, send_order
    )

    if quota == WIDE:
        outgoing = outgoing.reshape(owners, 3, 2, 128)
        incoming = lax.all_to_all(outgoing, both, split_axis=0, concat_axis=0, tiled=True)
    else:
        groups = cells // WIDE
        flat = outgoing.reshape(groups, 3, WIDE).transpose(1, 0, 2).reshape(3, owners, quota)
        flat = lax.all_to_all(flat, both, split_axis=1, concat_axis=1, tiled=True)
        incoming = flat.reshape(3, groups, WIDE).transpose(1, 0, 2)
    incoming = incoming.reshape(-1, 128)
    return projected, place_call(incoming, place_order)


def solution(mesh):
    split = P(("src", "tgt"))
    rows = P(("src", "tgt"), None)
    return jax.shard_map(
        on_device,
        mesh=mesh,
        in_specs=(P(None, ("src", "tgt")), split, split, split, P("src", "tgt", None), rows, rows),
        out_specs=(P(None, "src", "tgt", None), P(None, ("src", "tgt"))),
        check_vma=False,
    )
```

```python
import numpy as np

import jax
import jax.numpy as jnp
from jax import lax
from jax.experimental import pallas as pl
from jax.experimental.pallas import tpu as pltpu
from jax.sharding import PartitionSpec as P

ITERS = 4
FIELDS = 7
PIECES = 4
SPAN = 512
AT_ONCE = 32
TOGETHER = 8
WIDE = 256
BF16 = jnp.bfloat16
F32 = jnp.float32
NT = (((1,), (1,)), ((), ()))


def sweep_polynomial(iters, theta, delta):
    sigma = theta / delta
    rho = 1.0 / sigma
    mass = np.array([1.0, 0.125])
    poly = np.polynomial.polynomial
    resid = np.array([1.0])
    step = resid / theta
    total = np.array([0.0])
    for _ in range(iters):
        total = poly.polyadd(total, step)
        resid = poly.polysub(resid, poly.polymul(mass, step))
        rho_new = 1.0 / (2.0 * sigma - rho)
        step = poly.polyadd(rho_new * rho * step, 2.0 * rho_new / delta * resid)
        rho = rho_new
    return [float(c) for c in poly.polyadd(total, step)]


COEFS = sweep_polynomial(ITERS, 1.0, 0.75)


def halves(x):
    high = x.astype(BF16)
    return high, (x - high.astype(F32)).astype(BF16)


def log2(n):
    assert n & (n - 1) == 0
    return n.bit_length() - 1


def row_ids(rows, lanes):
    return lax.broadcasted_iota(jnp.int32, (rows, lanes), 0)


def low_onehot(low, ids):
    return jnp.where(ids == low.astype(F32).astype(BF16), jnp.ones((), BF16), jnp.zeros((), BF16))


def gather_kernel(fields_hbm, index_hbm, weight_hbm, out_ref, table, fields_ref, index_ref, weight_ref, sems):
    pairs = ((fields_hbm, fields_ref), (index_hbm, index_ref), (weight_hbm, weight_ref))
    copies = [pltpu.make_async_copy(src, dst, sems.at[i]) for i, (src, dst) in enumerate(pairs)]
    for copy in copies:
        copy.start()
    lanes = out_ref.shape[1]
    span = SPAN
    tiles = span // lanes
    owners = index_ref.shape[1] // span
    groups = fields_ref.shape[1] // WIDE
    table[...] = jnp.zeros_like(table)
    for copy in copies:
        copy.wait()
    for g in range(groups):
        table[g * 8 : g * 8 + FIELDS, :] = fields_ref[:, g * WIDE : (g + 1) * WIDE]
    high, low = halves(table[...])
    both = jnp.concatenate([high, low], axis=0)
    ids = row_ids(WIDE, span).astype(F32).astype(BF16)
    rows = groups * 8

    def one_owner(q):
        at = pl.multiple_of(q * span, span)
        index = index_ref[:, pl.ds(at, span)]
        weight = weight_ref[:, pl.ds(at, span)]
        onehot = low_onehot(index & (WIDE - 1), ids)
        got = jnp.dot(both, onehot, preferred_element_type=F32)
        group = jnp.broadcast_to(index >> log2(WIDE), (8, span))
        value = jnp.zeros((8, span), F32)
        for g in range(groups):
            part = got[g * 8 : (g + 1) * 8] + got[rows + g * 8 : rows + (g + 1) * 8]
            value = jnp.where(group == g, part, value)
        value = value * weight
        for t in range(tiles):
            out_ref[pl.ds(q * (FIELDS * tiles) + t, FIELDS, stride=tiles), :] = value[
                :FIELDS, t * lanes : (t + 1) * lanes
            ]

    @pl.loop(0, owners // AT_ONCE)
    def _(m):
        for i in range(AT_ONCE):
            one_owner(m * AT_ONCE + i)


def gather_call(fields, index, weight):
    rows = FIELDS * index.shape[1] // 128
    return pl.pallas_call(
        gather_kernel,
        out_shape=jax.ShapeDtypeStruct((rows, 128), F32),
        in_specs=[pl.BlockSpec(memory_space=pltpu.HBM)] * 3,
        out_specs=pl.BlockSpec(memory_space=pltpu.VMEM),
        scratch_shapes=[
            pltpu.VMEM((fields.shape[1] // WIDE * 8, WIDE), F32),
            pltpu.VMEM(fields.shape, F32),
            pltpu.VMEM(index.shape, jnp.int32),
            pltpu.VMEM(weight.shape, F32),
            pltpu.SemaphoreType.DMA((3,)),
        ],
        compiler_params=pltpu.CompilerParams(vmem_limit_bytes=40 << 20),
    )(*[pltpu.with_memory_space_constraint(x, pltpu.HBM) for x in (fields, index, weight)])


def scatter_kernel(value_ref, target_ref, mass_ref, v_ref, even_ref, odd_ref, total):
    lanes = value_ref.shape[1]
    tiles = SPAN // lanes
    owners = target_ref.shape[1] // SPAN
    span = TOGETHER * SPAN
    hx, hy, hz = mass_ref.shape
    groups = hx * hy * hz // WIDE
    total[...] = jnp.zeros_like(total)
    ids = row_ids(WIDE, span).astype(F32).astype(BF16)
    group_ids = row_ids(groups, span).astype(F32).astype(BF16)

    def step(p):
        at = pl.multiple_of(p * span, span)
        target = target_ref[:, pl.ds(at, span)]
        low = ((target >> log2(groups * hz)) << log2(hz)) + (target & (hz - 1))
        onehot = low_onehot(jnp.where(target < 0, -1, low), ids)
        group = ((target >> log2(hz)) & (groups - 1)).astype(F32).astype(BF16)
        here = group_ids == group
        row = p * (TOGETHER * FIELDS * tiles)
        pieces = [i * FIELDS * tiles + t for i in range(TOGETHER) for t in range(tiles)]
        value = jnp.concatenate([value_ref[pl.ds(row + i, FIELDS, stride=tiles), :] for i in pieces], axis=1)
        parts = []
        for half in halves(value):
            for f in range(FIELDS):
                parts.append(jnp.where(here, half[f : f + 1], jnp.zeros((), BF16)))
        spread = jnp.concatenate(parts, axis=0)
        total[...] += lax.dot_general(spread, onehot, NT, preferred_element_type=F32)

    @pl.loop(0, owners // TOGETHER // 4)
    def _(n):
        for i in range(4):
            step(n * 4 + i)

    even_ref[FIELDS * hx] = jnp.zeros((ITERS, hz), F32)
    scale = lax.rsqrt(mass_ref[...])
    half_x = hx // 2
    odd = lax.axis_index("tgt") % 2 == 1
    for f in range(FIELDS):
        s = total[f * groups : (f + 1) * groups] + total[(FIELDS + f) * groups : (FIELDS + f + 1) * groups]
        for b in range(2):
            for x in range(half_x):
                at = b * half_x + x
                v = s[x * hy : (x + 1) * hy, b * hz : (b + 1) * hz] * scale[at]
                v_ref[f, at] = v
                first, last = v[:ITERS], v[hy - ITERS :]
                even_ref[f * hx + at] = jnp.where(odd, first, last)
                odd_ref[f * hx + at] = jnp.where(odd, last, first)


def scatter_call(values, target, mass):
    hx, hy, hz = mass.shape
    groups = hx * hy * hz // WIDE
    even = jax.ShapeDtypeStruct((FIELDS * hx + 1, ITERS, hz), F32)
    odd = jax.ShapeDtypeStruct((FIELDS * hx, ITERS, hz), F32)
    return pl.pallas_call(
        scatter_kernel,
        out_shape=(jax.ShapeDtypeStruct((FIELDS, hx, hy, hz), F32), even, odd),
        in_specs=[pl.BlockSpec(memory_space=pltpu.VMEM)] * 3,
        out_specs=(pl.BlockSpec(memory_space=pltpu.VMEM),) * 3,
        scratch_shapes=[pltpu.VMEM((2 * FIELDS * groups, WIDE), F32)],
        compiler_params=pltpu.CompilerParams(vmem_limit_bytes=40 << 20),
    )(values, target, mass)


def lookup_rows(table, index, ids, group_ids, groups, at_parts):
    group, low = at_parts(index)
    got = jnp.dot(table, low_onehot(low, ids), preferred_element_type=F32)
    here = group_ids == group
    rows = 3 * groups
    out = []
    for m in range(3):
        part = got[m * groups : (m + 1) * groups] + got[rows + m * groups : rows + (m + 1) * groups]
        out.append(jnp.sum(jnp.where(here, part, 0.0), axis=0, keepdims=True))
    return out


def cell_moduli(vals):
    phi = vals[0]
    mean = (vals[1] + vals[2] + vals[3]) / 3.0
    q2 = 1.5 * (
        (vals[1] - mean) ** 2
        + (vals[2] - mean) ** 2
        + (vals[3] - mean) ** 2
        + 2.0 * (vals[4] ** 2 + vals[5] ** 2 + vals[6] ** 2)
    )
    bulk = 1.6 * jnp.exp(-3.0 * phi) * (1.0 + 0.25 * jnp.tanh(mean))
    shear = 0.9 * jnp.exp(-2.0 * phi) / (1.0 + q2 / 0.5)
    soften = shear * q2 / (0.5 + q2)
    return [bulk, shear, soften]


def corners(sides):
    line = row_ids(2 * ITERS, sides[0].shape[1])
    near = pltpu.roll(sides[1], 2, 0)
    far = jnp.where(line == 4, pltpu.roll(sides[2], 4, 0), pltpu.roll(sides[2], 6, 0))
    return sides[0], jnp.where(line < 4, near, far)


def sides_kernel(even_ref, odd_ref, sides_ref, to_even_ref, to_odd_ref):
    hx = sides_ref.shape[1]
    b_odd = lax.axis_index("tgt") % 2 == 1
    a_odd = lax.axis_index("src") % 2 == 1
    for f in range(FIELDS):
        sides = []
        for x in range(hx):
            even_side, odd_side = even_ref[f * hx + x], odd_ref[f * hx + x]
            right = jnp.where(b_odd, odd_side, even_side)
            left = jnp.where(b_odd, even_side, odd_side)
            sides.append(jnp.concatenate([right, left], axis=0))
            sides_ref[f, x] = sides[x]
        to_left, to_right = corners(sides), corners(sides[::-1])
        to_even_ref[f, :8] = jnp.where(a_odd, to_left[0], to_right[0])
        to_even_ref[f, 8:14] = jnp.where(a_odd, to_left[1], to_right[1])[:6]
        to_odd_ref[f, :8] = jnp.where(a_odd, to_right[0], to_left[0])
        to_odd_ref[f, 8:] = jnp.where(a_odd, to_right[1], to_left[1])


def sides_call(even, odd, hx):
    hz = even.shape[2]
    return pl.pallas_call(
        sides_kernel,
        out_shape=(
            jax.ShapeDtypeStruct((FIELDS, hx, 2 * ITERS, hz), F32),
            jax.ShapeDtypeStruct((FIELDS, 4 * ITERS - 2, hz), F32),
            jax.ShapeDtypeStruct((FIELDS, 4 * ITERS, hz), F32),
        ),
        in_specs=[pl.BlockSpec(memory_space=pltpu.VMEM)] * 2,
        out_specs=(pl.BlockSpec(memory_space=pltpu.VMEM),) * 3,
        compiler_params=pltpu.CompilerParams(vmem_limit_bytes=4 << 20),
        cost_estimate=pl.CostEstimate(flops=40 * 10**9, bytes_accessed=40 * 10**6, transcendentals=0),
    )(even, odd)


def solve_kernel(
    mesh_shape, v_ref, sides_ref, even_ref, odd_ref, even_corners_ref, odd_corners_ref, mass_ref, order_ref,
    projected_hbm, out_ref, projected_ref, sem,
):
    n_src, n_tgt = mesh_shape
    hx, hy, hz = mass_ref.shape
    k = ITERS
    rows = hy + 2 * k
    a, b = lax.axis_index("src"), lax.axis_index("tgt")

    def exists(flag):
        return jnp.where(flag, 1.0, 0.0).astype(F32)

    row = row_ids(rows, hz)
    lane = lax.broadcasted_iota(jnp.int32, (rows, hz), 1)
    inside = jnp.where(row < hy, 1.0, jnp.where(row < hy + k, exists(b < n_tgt - 1), exists(b > 0)))
    inside_left = inside * exists(a > 0)
    inside_right = inside * exists(a < n_src - 1)
    not_first = jnp.where(lane == 0, 0.0, 1.0)
    not_last = jnp.where(lane == hz - 1, 0.0, 1.0)
    scale = lax.rsqrt(mass_ref[...])

    line = row_ids(2 * k, hz)

    def slabs(own, first, packed, from_left):
        second = pltpu.roll(packed, 6, 0)
        third = jnp.where(line < 4, pltpu.roll(packed, 4, 0), pltpu.roll(packed, 2, 0))
        sides = [first, second, third] + [jnp.zeros((2 * k, hz), F32)] * (hx - 3)
        if from_left:
            sides = sides[::-1]
        return [jnp.concatenate([own[x], side], axis=0) for x, side in enumerate(sides)]

    a_odd = a % 2 == 1

    for f in range(FIELDS):
        packed = jnp.concatenate([even_corners_ref[f, 2 * k :], jnp.zeros((2, hz), F32)], axis=0)
        even = (even_ref[f], even_corners_ref[f, : 2 * k], packed)
        odd = (odd_ref[f], odd_corners_ref[f, : 2 * k], odd_corners_ref[f, 2 * k :])
        left = slabs(*[jnp.where(a_odd, p, q) for p, q in zip(even, odd)], True)
        right = slabs(*[jnp.where(a_odd, q, p) for p, q in zip(even, odd)], False)
        own = [jnp.concatenate([v_ref[f, x], sides_ref[f, x]], axis=0) for x in range(hx)]
        base = left + own + right
        u = [COEFS[k] * e for e in base]
        for sweep in range(1, k + 1):
            new = list(u)
            for x in range(sweep, hx + 2 * k - sweep):
                far = max(k - x, x - (k + hx - 1), 0)
                n = rows if sweep + far < k else hy
                w = u[x]
                near = u[x - 1][:n] + u[x + 1][:n]
                near = near + pltpu.roll(w, 1, 0)[:n] + pltpu.roll(w, rows - 1, 0)[:n]
                w = w[:n]
                near = near + pltpu.roll(w, 1, 1) * not_first[:n] + pltpu.roll(w, hz - 1, 1) * not_last[:n]
                if x < k:
                    near = near * inside_left[:n]
                elif x >= k + hx:
                    near = near * inside_right[:n]
                elif n > hy:
                    near = near * inside
                new[x] = COEFS[k - sweep] * base[x][:n] + near
            u = new
        for x in range(hx):
            projected_ref[f, x] = u[k + x][:hy] * scale[x]

    leave = pltpu.make_async_copy(projected_ref, projected_hbm, sem)
    leave.start()
    groups = hx * hy * hz // WIDE
    payload = cell_moduli([projected_ref[f].reshape(hx * hy, hz) for f in range(FIELDS)])
    table = jnp.concatenate([jnp.concatenate([m[:groups], m[groups:]], axis=1) for m in payload], axis=0)
    table = jnp.concatenate(halves(table), axis=0)
    ids = row_ids(WIDE, WIDE).astype(F32).astype(BF16)
    group_ids = row_ids(groups, WIDE)

    def at_parts(index):
        return (index >> log2(hz)) & (groups - 1), ((index >> log2(groups * hz)) << log2(hz)) + (index & (hz - 1))

    for q in range(0, groups, 4):
        lines = []
        for i in range(q, q + 4):
            index = order_ref[:, i * WIDE : (i + 1) * WIDE]
            got = lookup_rows(table, index, ids, group_ids, groups, at_parts)
            lines += [line[:, c * 128 : (c + 1) * 128] for line in got for c in range(2)]
        out_ref[q * 6 : q * 6 + 24, :] = jnp.concatenate(lines, axis=0)
    leave.wait()


def solve_call(mesh_shape, *args):
    mass, order = args[-2:]
    hx, hy, hz = mass.shape

    def kernel(*refs):
        solve_kernel(mesh_shape, *refs)

    return pl.pallas_call(
        kernel,
        out_shape=(
            jax.ShapeDtypeStruct((FIELDS, hx, hy, hz), F32),
            jax.ShapeDtypeStruct((order.shape[1] // WIDE * 6, 128), F32),
        ),
        in_specs=[pl.BlockSpec(memory_space=pltpu.VMEM)] * 8,
        out_specs=(pl.BlockSpec(memory_space=pltpu.HBM), pl.BlockSpec(memory_space=pltpu.VMEM)),
        scratch_shapes=[pltpu.VMEM((FIELDS, hx, hy, hz), F32), pltpu.SemaphoreType.DMA],
        compiler_params=pltpu.CompilerParams(vmem_limit_bytes=40 << 20),
    )(*args)


def place_kernel(arrived_ref, order_ref, out_hbm, out_ref, sems):
    groups = arrived_ref.shape[0] // 6
    table = jnp.concatenate(
        [
            jnp.concatenate([arrived_ref[pl.ds(2 * m + c, groups, stride=6), :] for c in range(2)], axis=1)
            for m in range(3)
        ],
        axis=0,
    )
    table = jnp.concatenate(halves(table), axis=0)
    ids = row_ids(WIDE, WIDE).astype(F32).astype(BF16)
    group_ids = row_ids(groups, WIDE)

    copies = []
    for n in range(PIECES):
        for q in range(n * groups // PIECES, (n + 1) * groups // PIECES):
            at = pl.ds(q * WIDE, WIDE)
            got = lookup_rows(
                table, order_ref[:, at], ids, group_ids, groups, lambda index: (index >> log2(WIDE), index & (WIDE - 1))
            )
            out_ref[:, at] = jnp.concatenate(got, axis=0)
        piece = pl.ds(n * groups // PIECES * WIDE, groups // PIECES * WIDE)
        copies.append(pltpu.make_async_copy(out_ref.at[:, piece], out_hbm.at[:, piece], sems.at[n]))
        copies[n].start()
    for copy in copies:
        copy.wait()


def place_call(arrived, order):
    return pl.pallas_call(
        place_kernel,
        out_shape=jax.ShapeDtypeStruct((3, order.shape[1]), F32),
        in_specs=[pl.BlockSpec(memory_space=pltpu.VMEM)] * 2,
        out_specs=pl.BlockSpec(memory_space=pltpu.HBM),
        scratch_shapes=[pltpu.VMEM((3, order.shape[1]), F32), pltpu.SemaphoreType.DMA((PIECES,))],
        compiler_params=pltpu.CompilerParams(vmem_limit_bytes=40 << 20),
    )(arrived, order)


def swap(x, axis, start):
    pairs = [(i, i + 1) for i in range(start, lax.axis_size(axis) - 1, 2)]
    return lax.ppermute(x, axis, pairs + [(j, i) for i, j in pairs])


def on_device(source_fields, slot_source, slot_weight, slot_target, cell_mass, send_order, place_order):
    n_src, n_tgt = lax.axis_size("src"), lax.axis_size("tgt")
    both = ("src", "tgt")
    owners = n_src * n_tgt
    cells = cell_mass.size
    quota = cells // owners

    values = gather_call(source_fields, slot_source.reshape(1, -1), slot_weight.reshape(1, -1))
    values = values.reshape(owners, FIELDS, SPAN // 128, 128)
    values = lax.all_to_all(values, both, split_axis=0, concat_axis=0, tiled=True).reshape(-1, 128)
    v, even, odd = scatter_call(values, slot_target.reshape(1, -1), cell_mass)
    even_block, odd_block = swap(v, "src", 0), swap(v, "src", 1)
    even, odd = swap(even, "tgt", 0), swap(odd, "tgt", 1)
    sides, even, odd = sides_call(even, odd, cell_mass.shape[0])
    even, odd = swap(even, "src", 0), swap(odd, "src", 1)
    projected, outgoing = solve_call(
        (n_src, n_tgt), v, sides, even_block, odd_block, even, odd, cell_mass, send_order
    )

    if quota == WIDE:
        outgoing = outgoing.reshape(owners, 3, 2, 128)
        incoming = lax.all_to_all(outgoing, both, split_axis=0, concat_axis=0, tiled=True)
    else:
        groups = cells // WIDE
        flat = outgoing.reshape(groups, 3, WIDE).transpose(1, 0, 2).reshape(3, owners, quota)
        flat = lax.all_to_all(flat, both, split_axis=1, concat_axis=1, tiled=True)
        incoming = flat.reshape(3, groups, WIDE).transpose(1, 0, 2)
    incoming = incoming.reshape(-1, 128)
    return projected, place_call(incoming, place_order)


def solution(mesh):
    split = P(("src", "tgt"))
    rows = P(("src", "tgt"), None)
    return jax.shard_map(
        on_device,
        mesh=mesh,
        in_specs=(P(None, ("src", "tgt")), split, split, split, P("src", "tgt", None), rows, rows),
        out_specs=(P(None, "src", "tgt", None), P(None, ("src", "tgt"))),
        check_vma=False,
    )
```

```python
import functools

import numpy as np

import jax
import jax.numpy as jnp
from jax import lax
from jax.experimental import pallas as pl
from jax.experimental.pallas import tpu as pltpu
from jax.sharding import PartitionSpec as P

ITERS = 4
FIELDS = 7
PIECES = 4
SPAN = 512
AT_ONCE = 32
TOGETHER = 8
WIDE = 256
BF16 = jnp.bfloat16
F32 = jnp.float32
NT = (((1,), (1,)), ((), ()))


def sweep_polynomial(iters, theta, delta):
    sigma = theta / delta
    rho = 1.0 / sigma
    mass = np.array([1.0, 0.125])
    poly = np.polynomial.polynomial
    resid = np.array([1.0])
    step = resid / theta
    total = np.array([0.0])
    for _ in range(iters):
        total = poly.polyadd(total, step)
        resid = poly.polysub(resid, poly.polymul(mass, step))
        rho_new = 1.0 / (2.0 * sigma - rho)
        step = poly.polyadd(rho_new * rho * step, 2.0 * rho_new / delta * resid)
        rho = rho_new
    return [float(c) for c in poly.polyadd(total, step)]


COEFS = sweep_polynomial(ITERS, 1.0, 0.75)


def halves(x):
    high = x.astype(BF16)
    return high, (x - high.astype(F32)).astype(BF16)


def log2(n):
    assert n & (n - 1) == 0
    return n.bit_length() - 1


def row_ids(rows, lanes):
    return lax.broadcasted_iota(jnp.int32, (rows, lanes), 0)


def low_onehot(low, ids):
    return jnp.where(ids == low.astype(F32).astype(BF16), jnp.ones((), BF16), jnp.zeros((), BF16))


def gather_kernel(fields_hbm, index_hbm, weight_hbm, out_ref, table, fields_ref, index_ref, weight_ref, sems):
    pairs = ((fields_hbm, fields_ref), (index_hbm, index_ref), (weight_hbm, weight_ref))
    copies = [pltpu.make_async_copy(src, dst, sems.at[i]) for i, (src, dst) in enumerate(pairs)]
    for copy in copies:
        copy.start()
    lanes = out_ref.shape[1]
    span = SPAN
    tiles = span // lanes
    owners = index_ref.shape[1] // span
    groups = fields_ref.shape[1] // WIDE
    table[...] = jnp.zeros_like(table)
    for copy in copies:
        copy.wait()
    for g in range(groups):
        table[g * 8 : g * 8 + FIELDS, :] = fields_ref[:, g * WIDE : (g + 1) * WIDE]
    high, low = halves(table[...])
    ids = row_ids(WIDE, span).astype(F32).astype(BF16)

    def one_owner(q):
        at = pl.multiple_of(q * span, span)
        index = index_ref[:, pl.ds(at, span)]
        weight = weight_ref[:, pl.ds(at, span)]
        onehot = low_onehot(index & (WIDE - 1), ids)
        got = jnp.dot(high, onehot, preferred_element_type=F32)
        got = got + jnp.dot(low, onehot, preferred_element_type=F32)
        group = jnp.broadcast_to(index >> log2(WIDE), (8, span))
        value = jnp.zeros((8, span), F32)
        for g in range(groups):
            value = jnp.where(group == g, got[g * 8 : (g + 1) * 8], value)
        value = value * weight
        for t in range(tiles):
            out_ref[pl.ds(q * (FIELDS * tiles) + t, FIELDS, stride=tiles), :] = value[
                :FIELDS, t * lanes : (t + 1) * lanes
            ]

    @pl.loop(0, owners // AT_ONCE)
    def _(m):
        for i in range(AT_ONCE):
            one_owner(m * AT_ONCE + i)


def gather_call(fields, index, weight):
    rows = FIELDS * index.shape[1] // 128
    return pl.pallas_call(
        gather_kernel,
        out_shape=jax.ShapeDtypeStruct((rows, 128), F32),
        in_specs=[pl.BlockSpec(memory_space=pltpu.HBM)] * 3,
        out_specs=pl.BlockSpec(memory_space=pltpu.VMEM),
        scratch_shapes=[
            pltpu.VMEM((fields.shape[1] // WIDE * 8, WIDE), F32),
            pltpu.VMEM(fields.shape, F32),
            pltpu.VMEM(index.shape, jnp.int32),
            pltpu.VMEM(weight.shape, F32),
            pltpu.SemaphoreType.DMA((3,)),
        ],
        compiler_params=pltpu.CompilerParams(vmem_limit_bytes=40 << 20),
    )(*[pltpu.with_memory_space_constraint(x, pltpu.HBM) for x in (fields, index, weight)])


def scatter_kernel(value_ref, target_ref, mass_ref, v_ref, even_ref, odd_ref, total):
    lanes = value_ref.shape[1]
    tiles = SPAN // lanes
    owners = target_ref.shape[1] // SPAN
    span = TOGETHER * SPAN
    hx, hy, hz = mass_ref.shape
    groups = hx * hy * hz // WIDE
    total[...] = jnp.zeros_like(total)
    ids = row_ids(WIDE, span).astype(F32).astype(BF16)
    group_ids = row_ids(groups, span).astype(F32).astype(BF16)

    def step(p):
        at = pl.multiple_of(p * span, span)
        target = target_ref[:, pl.ds(at, span)]
        low = ((target >> log2(groups * hz)) << log2(hz)) + (target & (hz - 1))
        onehot = low_onehot(jnp.where(target < 0, -1, low), ids)
        group = ((target >> log2(hz)) & (groups - 1)).astype(F32).astype(BF16)
        here = group_ids == group
        row = p * (TOGETHER * FIELDS * tiles)
        pieces = [i * FIELDS * tiles + t for i in range(TOGETHER) for t in range(tiles)]
        value = jnp.concatenate([value_ref[pl.ds(row + i, FIELDS, stride=tiles), :] for i in pieces], axis=1)
        parts = []
        for half in halves(value):
            for f in range(FIELDS):
                parts.append(jnp.where(here, half[f : f + 1], jnp.zeros((), BF16)))
        spread = jnp.concatenate(parts, axis=0)
        return lax.dot_general(spread, onehot, NT, preferred_element_type=F32)

    @pl.loop(0, owners // TOGETHER // 4)
    def _(n):
        total[...] += functools.reduce(lambda sums, i: sums + step(n * 4 + i), range(1, 4), step(n * 4))

    even_ref[FIELDS * hx] = jnp.zeros((ITERS, hz), F32)
    scale = lax.rsqrt(mass_ref[...])
    half_x = hx // 2
    odd = lax.axis_index("tgt") % 2 == 1
    for f in range(FIELDS):
        s = total[f * groups : (f + 1) * groups] + total[(FIELDS + f) * groups : (FIELDS + f + 1) * groups]
        for b in range(2):
            for x in range(half_x):
                at = b * half_x + x
                v = s[x * hy : (x + 1) * hy, b * hz : (b + 1) * hz] * scale[at]
                v_ref[f, at] = v
                first, last = v[:ITERS], v[hy - ITERS :]
                even_ref[f * hx + at] = jnp.where(odd, first, last)
                odd_ref[f * hx + at] = jnp.where(odd, last, first)


def scatter_call(values, target, mass):
    hx, hy, hz = mass.shape
    groups = hx * hy * hz // WIDE
    even = jax.ShapeDtypeStruct((FIELDS * hx + 1, ITERS, hz), F32)
    odd = jax.ShapeDtypeStruct((FIELDS * hx, ITERS, hz), F32)
    return pl.pallas_call(
        scatter_kernel,
        out_shape=(jax.ShapeDtypeStruct((FIELDS, hx, hy, hz), F32), even, odd),
        in_specs=[pl.BlockSpec(memory_space=pltpu.VMEM)] * 3,
        out_specs=(pl.BlockSpec(memory_space=pltpu.VMEM),) * 3,
        scratch_shapes=[pltpu.VMEM((2 * FIELDS * groups, WIDE), F32)],
        compiler_params=pltpu.CompilerParams(vmem_limit_bytes=40 << 20),
    )(values, target, mass)


def lookup_rows(table, index, ids, group_ids, groups, at_parts):
    group, low = at_parts(index)
    onehot = low_onehot(low, ids)
    got = jnp.dot(table[0], onehot, preferred_element_type=F32)
    got = got + jnp.dot(table[1], onehot, preferred_element_type=F32)
    here = group_ids == group
    out = []
    for m in range(3):
        part = got[m * groups : (m + 1) * groups]
        out.append(jnp.sum(jnp.where(here, part, 0.0), axis=0, keepdims=True))
    return out


def cell_moduli(vals):
    phi = vals[0]
    mean = (vals[1] + vals[2] + vals[3]) / 3.0
    q2 = 1.5 * (
        (vals[1] - mean) ** 2
        + (vals[2] - mean) ** 2
        + (vals[3] - mean) ** 2
        + 2.0 * (vals[4] ** 2 + vals[5] ** 2 + vals[6] ** 2)
    )
    bulk = 1.6 * jnp.exp(-3.0 * phi) * (1.0 + 0.25 * jnp.tanh(mean))
    shear = 0.9 * jnp.exp(-2.0 * phi) / (1.0 + q2 / 0.5)
    soften = shear * q2 / (0.5 + q2)
    return [bulk, shear, soften]


def corners(sides):
    line = row_ids(2 * ITERS, sides[0].shape[1])
    near = pltpu.roll(sides[1], 2, 0)
    far = jnp.where(line == 4, pltpu.roll(sides[2], 4, 0), pltpu.roll(sides[2], 6, 0))
    return sides[0], jnp.where(line < 4, near, far)


def sides_kernel(even_ref, odd_ref, sides_ref, to_even_ref, to_odd_ref):
    hx = sides_ref.shape[1]
    b_odd = lax.axis_index("tgt") % 2 == 1
    a_odd = lax.axis_index("src") % 2 == 1
    for f in range(FIELDS):
        sides = []
        for x in range(hx):
            even_side, odd_side = even_ref[f * hx + x], odd_ref[f * hx + x]
            right = jnp.where(b_odd, odd_side, even_side)
            left = jnp.where(b_odd, even_side, odd_side)
            sides.append(jnp.concatenate([right, left], axis=0))
            sides_ref[f, x] = sides[x]
        to_left, to_right = corners(sides), corners(sides[::-1])
        to_even_ref[f, :8] = jnp.where(a_odd, to_left[0], to_right[0])
        to_even_ref[f, 8:14] = jnp.where(a_odd, to_left[1], to_right[1])[:6]
        to_odd_ref[f, :8] = jnp.where(a_odd, to_right[0], to_left[0])
        to_odd_ref[f, 8:] = jnp.where(a_odd, to_right[1], to_left[1])


def sides_call(even, odd, hx):
    hz = even.shape[2]
    return pl.pallas_call(
        sides_kernel,
        out_shape=(
            jax.ShapeDtypeStruct((FIELDS, hx, 2 * ITERS, hz), F32),
            jax.ShapeDtypeStruct((FIELDS, 4 * ITERS - 2, hz), F32),
            jax.ShapeDtypeStruct((FIELDS, 4 * ITERS, hz), F32),
        ),
        in_specs=[pl.BlockSpec(memory_space=pltpu.VMEM)] * 2,
        out_specs=(pl.BlockSpec(memory_space=pltpu.VMEM),) * 3,
        compiler_params=pltpu.CompilerParams(vmem_limit_bytes=4 << 20),
        cost_estimate=pl.CostEstimate(flops=40 * 10**9, bytes_accessed=40 * 10**6, transcendentals=0),
    )(even, odd)


def solve_kernel(
    mesh_shape, v_ref, sides_ref, even_ref, odd_ref, even_corners_ref, odd_corners_ref, mass_ref, order_ref,
    projected_hbm, out_ref, projected_ref, sem,
):
    n_src, n_tgt = mesh_shape
    hx, hy, hz = mass_ref.shape
    k = ITERS
    rows = hy + 2 * k
    a, b = lax.axis_index("src"), lax.axis_index("tgt")

    def exists(flag):
        return jnp.where(flag, 1.0, 0.0).astype(F32)

    row = row_ids(rows, hz)
    lane = lax.broadcasted_iota(jnp.int32, (rows, hz), 1)
    inside = jnp.where(row < hy, 1.0, jnp.where(row < hy + k, exists(b < n_tgt - 1), exists(b > 0)))
    inside_left = inside * exists(a > 0)
    inside_right = inside * exists(a < n_src - 1)
    not_first = jnp.where(lane == 0, 0.0, 1.0)
    not_last = jnp.where(lane == hz - 1, 0.0, 1.0)
    scale = lax.rsqrt(mass_ref[...])

    line = row_ids(2 * k, hz)

    def slabs(own, first, packed, from_left):
        second = pltpu.roll(packed, 6, 0)
        third = jnp.where(line < 4, pltpu.roll(packed, 4, 0), pltpu.roll(packed, 2, 0))
        sides = [first, second, third] + [jnp.zeros((2 * k, hz), F32)] * (hx - 3)
        if from_left:
            sides = sides[::-1]
        return [jnp.concatenate([own[x], side], axis=0) for x, side in enumerate(sides)]

    a_odd = a % 2 == 1

    for f in range(FIELDS):
        packed = jnp.concatenate([even_corners_ref[f, 2 * k :], jnp.zeros((2, hz), F32)], axis=0)
        even = (even_ref[f], even_corners_ref[f, : 2 * k], packed)
        odd = (odd_ref[f], odd_corners_ref[f, : 2 * k], odd_corners_ref[f, 2 * k :])
        left = slabs(*[jnp.where(a_odd, p, q) for p, q in zip(even, odd)], True)
        right = slabs(*[jnp.where(a_odd, q, p) for p, q in zip(even, odd)], False)
        own = [jnp.concatenate([v_ref[f, x], sides_ref[f, x]], axis=0) for x in range(hx)]
        base = left + own + right
        u = [COEFS[k] * e for e in base]
        for sweep in range(1, k + 1):
            new = list(u)
            for x in range(sweep, hx + 2 * k - sweep):
                far = max(k - x, x - (k + hx - 1), 0)
                n = rows if sweep + far < k else hy
                w = u[x]
                near = u[x - 1][:n] + u[x + 1][:n]
                near = near + pltpu.roll(w, 1, 0)[:n] + pltpu.roll(w, rows - 1, 0)[:n]
                w = w[:n]
                near = near + pltpu.roll(w, 1, 1) * not_first[:n] + pltpu.roll(w, hz - 1, 1) * not_last[:n]
                if x < k:
                    near = near * inside_left[:n]
                elif x >= k + hx:
                    near = near * inside_right[:n]
                elif n > hy:
                    near = near * inside
                new[x] = COEFS[k - sweep] * base[x][:n] + near
            u = new
        for x in range(hx):
            projected_ref[f, x] = u[k + x][:hy] * scale[x]

    leave = pltpu.make_async_copy(projected_ref, projected_hbm, sem)
    leave.start()
    groups = hx * hy * hz // WIDE
    payload = cell_moduli([projected_ref[f].reshape(hx * hy, hz) for f in range(FIELDS)])
    table = jnp.concatenate([jnp.concatenate([m[:groups], m[groups:]], axis=1) for m in payload], axis=0)
    table = halves(table)
    ids = row_ids(WIDE, WIDE).astype(F32).astype(BF16)
    group_ids = row_ids(groups, WIDE)

    def at_parts(index):
        return (index >> log2(hz)) & (groups - 1), ((index >> log2(groups * hz)) << log2(hz)) + (index & (hz - 1))

    for q in range(0, groups, 4):
        lines = []
        for i in range(q, q + 4):
            index = order_ref[:, i * WIDE : (i + 1) * WIDE]
            got = lookup_rows(table, index, ids, group_ids, groups, at_parts)
            lines += [line[:, c * 128 : (c + 1) * 128] for line in got for c in range(2)]
        out_ref[q * 6 : q * 6 + 24, :] = jnp.concatenate(lines, axis=0)
    leave.wait()


def solve_call(mesh_shape, *args):
    mass, order = args[-2:]
    hx, hy, hz = mass.shape

    def kernel(*refs):
        solve_kernel(mesh_shape, *refs)

    return pl.pallas_call(
        kernel,
        out_shape=(
            jax.ShapeDtypeStruct((FIELDS, hx, hy, hz), F32),
            jax.ShapeDtypeStruct((order.shape[1] // WIDE * 6, 128), F32),
        ),
        in_specs=[pl.BlockSpec(memory_space=pltpu.VMEM)] * 8,
        out_specs=(pl.BlockSpec(memory_space=pltpu.HBM), pl.BlockSpec(memory_space=pltpu.VMEM)),
        scratch_shapes=[pltpu.VMEM((FIELDS, hx, hy, hz), F32), pltpu.SemaphoreType.DMA],
        compiler_params=pltpu.CompilerParams(vmem_limit_bytes=40 << 20),
    )(*args)


def place_kernel(arrived_ref, order_ref, out_hbm, out_ref, sems):
    groups = arrived_ref.shape[0] // 6
    table = jnp.concatenate(
        [
            jnp.concatenate([arrived_ref[pl.ds(2 * m + c, groups, stride=6), :] for c in range(2)], axis=1)
            for m in range(3)
        ],
        axis=0,
    )
    table = halves(table)
    ids = row_ids(WIDE, WIDE).astype(F32).astype(BF16)
    group_ids = row_ids(groups, WIDE)

    copies = []
    for n in range(PIECES):
        for q in range(n * groups // PIECES, (n + 1) * groups // PIECES):
            at = pl.ds(q * WIDE, WIDE)
            got = lookup_rows(
                table, order_ref[:, at], ids, group_ids, groups, lambda index: (index >> log2(WIDE), index & (WIDE - 1))
            )
            out_ref[:, at] = jnp.concatenate(got, axis=0)
        piece = pl.ds(n * groups // PIECES * WIDE, groups // PIECES * WIDE)
        copies.append(pltpu.make_async_copy(out_ref.at[:, piece], out_hbm.at[:, piece], sems.at[n]))
        copies[n].start()
    for copy in copies:
        copy.wait()


def place_call(arrived, order):
    return pl.pallas_call(
        place_kernel,
        out_shape=jax.ShapeDtypeStruct((3, order.shape[1]), F32),
        in_specs=[pl.BlockSpec(memory_space=pltpu.VMEM)] * 2,
        out_specs=pl.BlockSpec(memory_space=pltpu.HBM),
        scratch_shapes=[pltpu.VMEM((3, order.shape[1]), F32), pltpu.SemaphoreType.DMA((PIECES,))],
        compiler_params=pltpu.CompilerParams(vmem_limit_bytes=40 << 20),
    )(arrived, order)


def swap(x, axis, start):
    pairs = [(i, i + 1) for i in range(start, lax.axis_size(axis) - 1, 2)]
    return lax.ppermute(x, axis, pairs + [(j, i) for i, j in pairs])


def on_device(source_fields, slot_source, slot_weight, slot_target, cell_mass, send_order, place_order):
    n_src, n_tgt = lax.axis_size("src"), lax.axis_size("tgt")
    both = ("src", "tgt")
    owners = n_src * n_tgt
    cells = cell_mass.size
    quota = cells // owners

    values = gather_call(source_fields, slot_source.reshape(1, -1), slot_weight.reshape(1, -1))
    values = values.reshape(owners, FIELDS, SPAN // 128, 128)
    values = lax.all_to_all(values, both, split_axis=0, concat_axis=0, tiled=True).reshape(-1, 128)
    v, even, odd = scatter_call(values, slot_target.reshape(1, -1), cell_mass)
    even_block, odd_block = swap(v, "src", 0), swap(v, "src", 1)
    even, odd = swap(even, "tgt", 0), swap(odd, "tgt", 1)
    sides, even, odd = sides_call(even, odd, cell_mass.shape[0])
    even, odd = swap(even, "src", 0), swap(odd, "src", 1)
    projected, outgoing = solve_call(
        (n_src, n_tgt), v, sides, even_block, odd_block, even, odd, cell_mass, send_order
    )

    if quota == WIDE:
        outgoing = outgoing.reshape(owners, 3, 2, 128)
        incoming = lax.all_to_all(outgoing, both, split_axis=0, concat_axis=0, tiled=True)
    else:
        groups = cells // WIDE
        flat = outgoing.reshape(groups, 3, WIDE).transpose(1, 0, 2).reshape(3, owners, quota)
        flat = lax.all_to_all(flat, both, split_axis=1, concat_axis=1, tiled=True)
        incoming = flat.reshape(3, groups, WIDE).transpose(1, 0, 2)
    incoming = incoming.reshape(-1, 128)
    return projected, place_call(incoming, place_order)


def solution(mesh):
    split = P(("src", "tgt"))
    rows = P(("src", "tgt"), None)
    return jax.shard_map(
        on_device,
        mesh=mesh,
        in_specs=(P(None, ("src", "tgt")), split, split, split, P("src", "tgt", None), rows, rows),
        out_specs=(P(None, "src", "tgt", None), P(None, ("src", "tgt"))),
        check_vma=False,
    )
```

```python
import functools

import numpy as np

import jax
import jax.numpy as jnp
from jax import lax
from jax.experimental import pallas as pl
from jax.experimental.pallas import tpu as pltpu
from jax.sharding import PartitionSpec as P

ITERS = 4
FIELDS = 7
PIECES = 4
SPAN = 512
AT_ONCE = 32
TOGETHER = 8
WIDE = 256
BF16 = jnp.bfloat16
F32 = jnp.float32
NT = (((1,), (1,)), ((), ()))


def sweep_polynomial(iters, theta, delta):
    sigma = theta / delta
    rho = 1.0 / sigma
    mass = np.array([1.0, 0.125])
    poly = np.polynomial.polynomial
    resid = np.array([1.0])
    step = resid / theta
    total = np.array([0.0])
    for _ in range(iters):
        total = poly.polyadd(total, step)
        resid = poly.polysub(resid, poly.polymul(mass, step))
        rho_new = 1.0 / (2.0 * sigma - rho)
        step = poly.polyadd(rho_new * rho * step, 2.0 * rho_new / delta * resid)
        rho = rho_new
    return [float(c) for c in poly.polyadd(total, step)]


COEFS = sweep_polynomial(ITERS, 1.0, 0.75)


def halves(x):
    high = x.astype(BF16)
    return high, (x - high.astype(F32)).astype(BF16)


def log2(n):
    assert n & (n - 1) == 0
    return n.bit_length() - 1


def row_ids(rows, lanes):
    return lax.broadcasted_iota(jnp.int32, (rows, lanes), 0)


def low_onehot(low, ids):
    return jnp.where(ids == low.astype(F32).astype(BF16), jnp.ones((), BF16), jnp.zeros((), BF16))


def gather_kernel(fields_hbm, index_hbm, weight_hbm, out_ref, table, fields_ref, index_ref, weight_ref, sems):
    pairs = ((fields_hbm, fields_ref), (index_hbm, index_ref), (weight_hbm, weight_ref))
    copies = [pltpu.make_async_copy(src, dst, sems.at[i]) for i, (src, dst) in enumerate(pairs)]
    for copy in copies:
        copy.start()
    lanes = out_ref.shape[1]
    span = SPAN
    tiles = span // lanes
    owners = index_ref.shape[1] // span
    groups = fields_ref.shape[1] // WIDE
    table[...] = jnp.zeros_like(table)
    for copy in copies:
        copy.wait()
    for g in range(groups):
        table[g * 8 : g * 8 + FIELDS, :] = fields_ref[:, g * WIDE : (g + 1) * WIDE]
    high, low = halves(table[...])
    ids = row_ids(WIDE, span).astype(F32).astype(BF16)

    def one_owner(q):
        at = pl.multiple_of(q * span, span)
        index = index_ref[:, pl.ds(at, span)]
        weight = weight_ref[:, pl.ds(at, span)]
        onehot = low_onehot(index & (WIDE - 1), ids)
        got = jnp.dot(high, onehot, preferred_element_type=F32)
        got = got + jnp.dot(low, onehot, preferred_element_type=F32)
        group = jnp.broadcast_to(index >> log2(WIDE), (8, span))
        value = jnp.zeros((8, span), F32)
        for g in range(groups):
            value = jnp.where(group == g, got[g * 8 : (g + 1) * 8], value)
        value = value * weight
        for t in range(tiles):
            out_ref[pl.ds(q * (FIELDS * tiles) + t, FIELDS, stride=tiles), :] = value[
                :FIELDS, t * lanes : (t + 1) * lanes
            ]

    @pl.loop(0, owners // AT_ONCE)
    def _(m):
        for i in range(AT_ONCE):
            one_owner(m * AT_ONCE + i)


def gather_call(fields, index, weight):
    rows = FIELDS * index.shape[1] // 128
    return pl.pallas_call(
        gather_kernel,
        out_shape=jax.ShapeDtypeStruct((rows, 128), F32),
        in_specs=[pl.BlockSpec(memory_space=pltpu.HBM)] * 3,
        out_specs=pl.BlockSpec(memory_space=pltpu.VMEM),
        scratch_shapes=[
            pltpu.VMEM((fields.shape[1] // WIDE * 8, WIDE), F32),
            pltpu.VMEM(fields.shape, F32),
            pltpu.VMEM(index.shape, jnp.int32),
            pltpu.VMEM(weight.shape, F32),
            pltpu.SemaphoreType.DMA((3,)),
        ],
        compiler_params=pltpu.CompilerParams(vmem_limit_bytes=40 << 20),
    )(*[pltpu.with_memory_space_constraint(x, pltpu.HBM) for x in (fields, index, weight)])


def scatter_kernel(value_ref, target_ref, mass_ref, v_ref, even_ref, odd_ref, total):
    lanes = value_ref.shape[1]
    tiles = SPAN // lanes
    owners = target_ref.shape[1] // SPAN
    span = TOGETHER * SPAN
    hx, hy, hz = mass_ref.shape
    groups = hx * hy * hz // WIDE
    total[...] = jnp.zeros_like(total)
    ids = row_ids(WIDE, span).astype(F32).astype(BF16)
    group_ids = row_ids(groups, span).astype(F32).astype(BF16)

    def step(p):
        at = pl.multiple_of(p * span, span)
        target = target_ref[:, pl.ds(at, span)]
        low = ((target >> log2(groups * hz)) << log2(hz)) + (target & (hz - 1))
        onehot = low_onehot(jnp.where(target < 0, -1, low), ids)
        group = ((target >> log2(hz)) & (groups - 1)).astype(F32).astype(BF16)
        here = group_ids == group
        row = p * (TOGETHER * FIELDS * tiles)
        pieces = [i * FIELDS * tiles + t for i in range(TOGETHER) for t in range(tiles)]
        value = jnp.concatenate([value_ref[pl.ds(row + i, FIELDS, stride=tiles), :] for i in pieces], axis=1)
        parts = []
        for half in halves(value):
            for f in range(FIELDS):
                parts.append(jnp.where(here, half[f : f + 1], jnp.zeros((), BF16)))
        spread = jnp.concatenate(parts, axis=0)
        return lax.dot_general(spread, onehot, NT, preferred_element_type=F32)

    @pl.loop(0, owners // TOGETHER // 4)
    def _(n):
        total[...] += functools.reduce(lambda sums, i: sums + step(n * 4 + i), range(1, 4), step(n * 4))

    even_ref[FIELDS * hx] = jnp.zeros((ITERS, hz), F32)
    scale = lax.rsqrt(mass_ref[...])
    half_x = hx // 2
    odd = lax.axis_index("tgt") % 2 == 1
    for f in range(FIELDS):
        s = total[f * groups : (f + 1) * groups] + total[(FIELDS + f) * groups : (FIELDS + f + 1) * groups]
        for b in range(2):
            for x in range(half_x):
                at = b * half_x + x
                v = s[x * hy : (x + 1) * hy, b * hz : (b + 1) * hz] * scale[at]
                v_ref[f, at] = v
                first, last = v[:ITERS], v[hy - ITERS :]
                even_ref[f * hx + at] = jnp.where(odd, first, last)
                odd_ref[f * hx + at] = jnp.where(odd, last, first)


def scatter_call(values, target, mass):
    hx, hy, hz = mass.shape
    groups = hx * hy * hz // WIDE
    even = jax.ShapeDtypeStruct((FIELDS * hx + 1, ITERS, hz), F32)
    odd = jax.ShapeDtypeStruct((FIELDS * hx, ITERS, hz), F32)
    return pl.pallas_call(
        scatter_kernel,
        out_shape=(jax.ShapeDtypeStruct((FIELDS, hx, hy, hz), F32), even, odd),
        in_specs=[pl.BlockSpec(memory_space=pltpu.VMEM)] * 3,
        out_specs=(pl.BlockSpec(memory_space=pltpu.VMEM),) * 3,
        scratch_shapes=[pltpu.VMEM((2 * FIELDS * groups, WIDE), F32)],
        compiler_params=pltpu.CompilerParams(vmem_limit_bytes=40 << 20),
    )(values, target, mass)


def lookup_rows(tables, row, lane):
    row = jnp.broadcast_to(row, (8, 128))
    lane = jnp.broadcast_to(lane, (8, 128))
    tile = row >> 3
    here = row_ids(8, 128) == (row & 7)
    out = []
    for table in tables:
        got = jnp.zeros((8, 128), F32)
        for v in range(table.shape[0] // 8):
            piece = jnp.take_along_axis(table[v * 8 : (v + 1) * 8], lane, axis=1, mode="promise_in_bounds")
            got = jnp.where(tile == v, piece, got)
        out.append(jnp.sum(jnp.where(here, got, 0.0), axis=0, keepdims=True))
    return out


def cell_moduli(vals):
    phi = vals[0]
    mean = (vals[1] + vals[2] + vals[3]) / 3.0
    q2 = 1.5 * (
        (vals[1] - mean) ** 2
        + (vals[2] - mean) ** 2
        + (vals[3] - mean) ** 2
        + 2.0 * (vals[4] ** 2 + vals[5] ** 2 + vals[6] ** 2)
    )
    bulk = 1.6 * jnp.exp(-3.0 * phi) * (1.0 + 0.25 * jnp.tanh(mean))
    shear = 0.9 * jnp.exp(-2.0 * phi) / (1.0 + q2 / 0.5)
    soften = shear * q2 / (0.5 + q2)
    return [bulk, shear, soften]


def corners(sides):
    line = row_ids(2 * ITERS, sides[0].shape[1])
    near = pltpu.roll(sides[1], 2, 0)
    far = jnp.where(line == 4, pltpu.roll(sides[2], 4, 0), pltpu.roll(sides[2], 6, 0))
    return sides[0], jnp.where(line < 4, near, far)


def sides_kernel(even_ref, odd_ref, sides_ref, to_even_ref, to_odd_ref):
    hx = sides_ref.shape[1]
    b_odd = lax.axis_index("tgt") % 2 == 1
    a_odd = lax.axis_index("src") % 2 == 1
    for f in range(FIELDS):
        sides = []
        for x in range(hx):
            even_side, odd_side = even_ref[f * hx + x], odd_ref[f * hx + x]
            right = jnp.where(b_odd, odd_side, even_side)
            left = jnp.where(b_odd, even_side, odd_side)
            sides.append(jnp.concatenate([right, left], axis=0))
            sides_ref[f, x] = sides[x]
        to_left, to_right = corners(sides), corners(sides[::-1])
        to_even_ref[f, :8] = jnp.where(a_odd, to_left[0], to_right[0])
        to_even_ref[f, 8:14] = jnp.where(a_odd, to_left[1], to_right[1])[:6]
        to_odd_ref[f, :8] = jnp.where(a_odd, to_right[0], to_left[0])
        to_odd_ref[f, 8:] = jnp.where(a_odd, to_right[1], to_left[1])


def sides_call(even, odd, hx):
    hz = even.shape[2]
    return pl.pallas_call(
        sides_kernel,
        out_shape=(
            jax.ShapeDtypeStruct((FIELDS, hx, 2 * ITERS, hz), F32),
            jax.ShapeDtypeStruct((FIELDS, 4 * ITERS - 2, hz), F32),
            jax.ShapeDtypeStruct((FIELDS, 4 * ITERS, hz), F32),
        ),
        in_specs=[pl.BlockSpec(memory_space=pltpu.VMEM)] * 2,
        out_specs=(pl.BlockSpec(memory_space=pltpu.VMEM),) * 3,
        compiler_params=pltpu.CompilerParams(vmem_limit_bytes=4 << 20),
        cost_estimate=pl.CostEstimate(flops=40 * 10**9, bytes_accessed=40 * 10**6, transcendentals=0),
    )(even, odd)


def solve_kernel(
    mesh_shape, v_ref, sides_ref, even_ref, odd_ref, even_corners_ref, odd_corners_ref, mass_ref, order_ref,
    projected_hbm, out_ref, projected_ref, sem,
):
    n_src, n_tgt = mesh_shape
    hx, hy, hz = mass_ref.shape
    k = ITERS
    rows = hy + 2 * k
    a, b = lax.axis_index("src"), lax.axis_index("tgt")

    def exists(flag):
        return jnp.where(flag, 1.0, 0.0).astype(F32)

    row = row_ids(rows, hz)
    lane = lax.broadcasted_iota(jnp.int32, (rows, hz), 1)
    inside = jnp.where(row < hy, 1.0, jnp.where(row < hy + k, exists(b < n_tgt - 1), exists(b > 0)))
    inside_left = inside * exists(a > 0)
    inside_right = inside * exists(a < n_src - 1)
    not_first = jnp.where(lane == 0, 0.0, 1.0)
    not_last = jnp.where(lane == hz - 1, 0.0, 1.0)
    scale = lax.rsqrt(mass_ref[...])

    line = row_ids(2 * k, hz)

    def slabs(own, first, packed, from_left):
        second = pltpu.roll(packed, 6, 0)
        third = jnp.where(line < 4, pltpu.roll(packed, 4, 0), pltpu.roll(packed, 2, 0))
        sides = [first, second, third] + [jnp.zeros((2 * k, hz), F32)] * (hx - 3)
        if from_left:
            sides = sides[::-1]
        return [jnp.concatenate([own[x], side], axis=0) for x, side in enumerate(sides)]

    a_odd = a % 2 == 1

    for f in range(FIELDS):
        packed = jnp.concatenate([even_corners_ref[f, 2 * k :], jnp.zeros((2, hz), F32)], axis=0)
        even = (even_ref[f], even_corners_ref[f, : 2 * k], packed)
        odd = (odd_ref[f], odd_corners_ref[f, : 2 * k], odd_corners_ref[f, 2 * k :])
        left = slabs(*[jnp.where(a_odd, p, q) for p, q in zip(even, odd)], True)
        right = slabs(*[jnp.where(a_odd, q, p) for p, q in zip(even, odd)], False)
        own = [jnp.concatenate([v_ref[f, x], sides_ref[f, x]], axis=0) for x in range(hx)]
        base = left + own + right
        u = [COEFS[k] * e for e in base]
        for sweep in range(1, k + 1):
            new = list(u)
            for x in range(sweep, hx + 2 * k - sweep):
                far = max(k - x, x - (k + hx - 1), 0)
                n = rows if sweep + far < k else hy
                w = u[x]
                near = u[x - 1][:n] + u[x + 1][:n]
                near = near + pltpu.roll(w, 1, 0)[:n] + pltpu.roll(w, rows - 1, 0)[:n]
                w = w[:n]
                near = near + pltpu.roll(w, 1, 1) * not_first[:n] + pltpu.roll(w, hz - 1, 1) * not_last[:n]
                if x < k:
                    near = near * inside_left[:n]
                elif x >= k + hx:
                    near = near * inside_right[:n]
                elif n > hy:
                    near = near * inside
                new[x] = COEFS[k - sweep] * base[x][:n] + near
            u = new
        for x in range(hx):
            projected_ref[f, x] = u[k + x][:hy] * scale[x]

    leave = pltpu.make_async_copy(projected_ref, projected_hbm, sem)
    leave.start()
    tables = cell_moduli([projected_ref[f].reshape(hx * hy, hz) for f in range(FIELDS)])
    for q in range(0, order_ref.shape[1] // WIDE, 4):
        lines = []
        for i in range(q, q + 4):
            got = []
            for c in range(2):
                index = order_ref[:, i * WIDE + c * 128 : i * WIDE + (c + 1) * 128]
                got.append(lookup_rows(tables, index >> log2(hz), index & (hz - 1)))
            lines += [got[c][m] for m in range(3) for c in range(2)]
        out_ref[q * 6 : q * 6 + 24, :] = jnp.concatenate(lines, axis=0)
    leave.wait()


def solve_call(mesh_shape, *args):
    mass, order = args[-2:]
    hx, hy, hz = mass.shape

    def kernel(*refs):
        solve_kernel(mesh_shape, *refs)

    return pl.pallas_call(
        kernel,
        out_shape=(
            jax.ShapeDtypeStruct((FIELDS, hx, hy, hz), F32),
            jax.ShapeDtypeStruct((order.shape[1] // WIDE * 6, 128), F32),
        ),
        in_specs=[pl.BlockSpec(memory_space=pltpu.VMEM)] * 8,
        out_specs=(pl.BlockSpec(memory_space=pltpu.HBM), pl.BlockSpec(memory_space=pltpu.VMEM)),
        scratch_shapes=[pltpu.VMEM((FIELDS, hx, hy, hz), F32), pltpu.SemaphoreType.DMA],
        compiler_params=pltpu.CompilerParams(vmem_limit_bytes=40 << 20),
    )(*args)


def place_kernel(arrived_ref, order_ref, out_hbm, out_ref, sems):
    groups = arrived_ref.shape[0] // 6
    tables = [
        jnp.concatenate([arrived_ref[pl.ds(2 * m + c, groups, stride=6), :] for c in range(2)], axis=0)
        for m in range(3)
    ]

    copies = []
    for n in range(PIECES):
        for q in range(n * groups // PIECES * 2, (n + 1) * groups // PIECES * 2):
            at = pl.ds(q * 128, 128)
            index = order_ref[:, at]
            row = ((index >> 7) & 1) * groups + (index >> log2(WIDE))
            out_ref[:, at] = jnp.concatenate(lookup_rows(tables, row, index & 127), axis=0)
        piece = pl.ds(n * groups // PIECES * WIDE, groups // PIECES * WIDE)
        copies.append(pltpu.make_async_copy(out_ref.at[:, piece], out_hbm.at[:, piece], sems.at[n]))
        copies[n].start()
    for copy in copies:
        copy.wait()


def place_call(arrived, order):
    return pl.pallas_call(
        place_kernel,
        out_shape=jax.ShapeDtypeStruct((3, order.shape[1]), F32),
        in_specs=[pl.BlockSpec(memory_space=pltpu.VMEM)] * 2,
        out_specs=pl.BlockSpec(memory_space=pltpu.HBM),
        scratch_shapes=[pltpu.VMEM((3, order.shape[1]), F32), pltpu.SemaphoreType.DMA((PIECES,))],
        compiler_params=pltpu.CompilerParams(vmem_limit_bytes=40 << 20),
    )(arrived, order)


def swap(x, axis, start):
    pairs = [(i, i + 1) for i in range(start, lax.axis_size(axis) - 1, 2)]
    return lax.ppermute(x, axis, pairs + [(j, i) for i, j in pairs])


def on_device(source_fields, slot_source, slot_weight, slot_target, cell_mass, send_order, place_order):
    n_src, n_tgt = lax.axis_size("src"), lax.axis_size("tgt")
    both = ("src", "tgt")
    owners = n_src * n_tgt
    cells = cell_mass.size
    quota = cells // owners

    values = gather_call(source_fields, slot_source.reshape(1, -1), slot_weight.reshape(1, -1))
    values = values.reshape(owners, FIELDS, SPAN // 128, 128)
    values = lax.all_to_all(values, both, split_axis=0, concat_axis=0, tiled=True).reshape(-1, 128)
    v, even, odd = scatter_call(values, slot_target.reshape(1, -1), cell_mass)
    even_block, odd_block = swap(v, "src", 0), swap(v, "src", 1)
    even, odd = swap(even, "tgt", 0), swap(odd, "tgt", 1)
    sides, even, odd = sides_call(even, odd, cell_mass.shape[0])
    even, odd = swap(even, "src", 0), swap(odd, "src", 1)
    projected, outgoing = solve_call(
        (n_src, n_tgt), v, sides, even_block, odd_block, even, odd, cell_mass, send_order
    )

    if quota == WIDE:
        outgoing = outgoing.reshape(owners, 3, 2, 128)
        incoming = lax.all_to_all(outgoing, both, split_axis=0, concat_axis=0, tiled=True)
    else:
        groups = cells // WIDE
        flat = outgoing.reshape(groups, 3, WIDE).transpose(1, 0, 2).reshape(3, owners, quota)
        flat = lax.all_to_all(flat, both, split_axis=1, concat_axis=1, tiled=True)
        incoming = flat.reshape(3, groups, WIDE).transpose(1, 0, 2)
    incoming = incoming.reshape(-1, 128)
    return projected, place_call(incoming, place_order)


def solution(mesh):
    split = P(("src", "tgt"))
    rows = P(("src", "tgt"), None)
    return jax.shard_map(
        on_device,
        mesh=mesh,
        in_specs=(P(None, ("src", "tgt")), split, split, split, P("src", "tgt", None), rows, rows),
        out_specs=(P(None, "src", "tgt", None), P(None, ("src", "tgt"))),
        check_vma=False,
    )
```

```python
import functools

import numpy as np

import jax
import jax.numpy as jnp
from jax import lax
from jax.experimental import pallas as pl
from jax.experimental.pallas import tpu as pltpu
from jax.sharding import PartitionSpec as P

ITERS = 4
FIELDS = 7
PIECES = 4
SPAN = 512
AT_ONCE = 32
TOGETHER = 8
WIDE = 256
BF16 = jnp.bfloat16
F32 = jnp.float32
NT = (((1,), (1,)), ((), ()))


def sweep_polynomial(iters, theta, delta):
    sigma = theta / delta
    rho = 1.0 / sigma
    mass = np.array([1.0, 0.125])
    poly = np.polynomial.polynomial
    resid = np.array([1.0])
    step = resid / theta
    total = np.array([0.0])
    for _ in range(iters):
        total = poly.polyadd(total, step)
        resid = poly.polysub(resid, poly.polymul(mass, step))
        rho_new = 1.0 / (2.0 * sigma - rho)
        step = poly.polyadd(rho_new * rho * step, 2.0 * rho_new / delta * resid)
        rho = rho_new
    return [float(c) for c in poly.polyadd(total, step)]


COEFS = sweep_polynomial(ITERS, 1.0, 0.75)


def halves(x):
    high = x.astype(BF16)
    return high, (x - high.astype(F32)).astype(BF16)


def log2(n):
    assert n & (n - 1) == 0
    return n.bit_length() - 1


def row_ids(rows, lanes):
    return lax.broadcasted_iota(jnp.int32, (rows, lanes), 0)


def low_onehot(low, ids):
    return jnp.where(ids == low.astype(F32).astype(BF16), jnp.ones((), BF16), jnp.zeros((), BF16))


def gather_kernel(fields_hbm, index_hbm, weight_hbm, out_ref, table, padded, fields_ref, index_ref, weight_ref, sems):
    pairs = ((fields_hbm, fields_ref), (index_hbm, index_ref), (weight_hbm, weight_ref))
    copies = [pltpu.make_async_copy(src, dst, sems.at[i]) for i, (src, dst) in enumerate(pairs)]
    for copy in copies:
        copy.start()
    lanes = out_ref.shape[1]
    span = SPAN
    tiles = span // lanes
    owners = index_ref.shape[1] // span
    groups = fields_ref.shape[1] // WIDE
    table[...] = jnp.zeros_like(table)
    padded[...] = jnp.zeros_like(padded)
    for copy in copies:
        copy.wait()
    for g in range(groups):
        table[g * 8 : g * 8 + FIELDS, :] = fields_ref[:, g * WIDE : (g + 1) * WIDE]
    both = jnp.concatenate(halves(table[...]), axis=0)
    rows = groups * 8
    ids = row_ids(WIDE, WIDE).astype(F32).astype(BF16)
    padded[:FIELDS, :] = fields_ref[...]

    def by_matmul(index):
        got = jnp.dot(both, low_onehot(index & (WIDE - 1), ids), preferred_element_type=F32)
        group = jnp.broadcast_to(index >> log2(WIDE), (8, WIDE))
        value = jnp.zeros((8, WIDE), F32)
        for g in range(groups):
            part = got[g * 8 : (g + 1) * 8] + got[rows + g * 8 : rows + (g + 1) * 8]
            value = jnp.where(group == g, part, value)
        return value

    def by_lanes(index):
        lane = jnp.broadcast_to(index & 127, (8, 128))
        tile = jnp.broadcast_to(index >> 7, (8, 128))
        value = jnp.zeros((8, 128), F32)
        for g in range(padded.shape[1] // 128):
            piece = padded[:, g * 128 : (g + 1) * 128]
            piece = jnp.take_along_axis(piece, lane, axis=1, mode="promise_in_bounds")
            value = jnp.where(tile == g, piece, value)
        return value

    def one_owner(q, matmuls):
        at = pl.multiple_of(q * SPAN, SPAN)
        index = index_ref[:, pl.ds(at, SPAN)]
        weight = weight_ref[:, pl.ds(at, SPAN)]
        values = [by_matmul(index[:, i * WIDE : (i + 1) * WIDE]) for i in range(matmuls)]
        for t in range(matmuls * WIDE // 128, tiles):
            values.append(by_lanes(index[:, t * 128 : (t + 1) * 128]))
        value = jnp.concatenate(values, axis=1) * weight
        for t in range(tiles):
            out_ref[pl.ds(q * (FIELDS * tiles) + t, FIELDS, stride=tiles), :] = value[
                :FIELDS, t * lanes : (t + 1) * lanes
            ]

    @pl.loop(0, owners // AT_ONCE)
    def _(m):
        for i in range(AT_ONCE):
            one_owner(m * AT_ONCE + i, SPAN // WIDE - i % 2)


def gather_call(fields, index, weight):
    rows = FIELDS * index.shape[1] // 128
    return pl.pallas_call(
        gather_kernel,
        out_shape=jax.ShapeDtypeStruct((rows, 128), F32),
        in_specs=[pl.BlockSpec(memory_space=pltpu.HBM)] * 3,
        out_specs=pl.BlockSpec(memory_space=pltpu.VMEM),
        scratch_shapes=[
            pltpu.VMEM((fields.shape[1] // WIDE * 8, WIDE), F32),
            pltpu.VMEM((8, fields.shape[1]), F32),
            pltpu.VMEM(fields.shape, F32),
            pltpu.VMEM(index.shape, jnp.int32),
            pltpu.VMEM(weight.shape, F32),
            pltpu.SemaphoreType.DMA((3,)),
        ],
        compiler_params=pltpu.CompilerParams(vmem_limit_bytes=40 << 20),
    )(*[pltpu.with_memory_space_constraint(x, pltpu.HBM) for x in (fields, index, weight)])


def scatter_kernel(value_ref, target_ref, mass_ref, v_ref, even_ref, odd_ref, total):
    lanes = value_ref.shape[1]
    tiles = SPAN // lanes
    owners = target_ref.shape[1] // SPAN
    span = TOGETHER * SPAN
    hx, hy, hz = mass_ref.shape
    groups = hx * hy * hz // WIDE
    total[...] = jnp.zeros_like(total)
    ids = row_ids(WIDE, span).astype(F32).astype(BF16)
    group_ids = row_ids(groups, span).astype(F32).astype(BF16)

    def step(p):
        at = pl.multiple_of(p * span, span)
        target = target_ref[:, pl.ds(at, span)]
        low = ((target >> log2(groups * hz)) << log2(hz)) + (target & (hz - 1))
        onehot = low_onehot(jnp.where(target < 0, -1, low), ids)
        group = ((target >> log2(hz)) & (groups - 1)).astype(F32).astype(BF16)
        here = group_ids == group
        row = p * (TOGETHER * FIELDS * tiles)
        pieces = [i * FIELDS * tiles + t for i in range(TOGETHER) for t in range(tiles)]
        value = jnp.concatenate([value_ref[pl.ds(row + i, FIELDS, stride=tiles), :] for i in pieces], axis=1)
        parts = []
        for half in halves(value):
            for f in range(FIELDS):
                parts.append(jnp.where(here, half[f : f + 1], jnp.zeros((), BF16)))
        spread = jnp.concatenate(parts, axis=0)
        return lax.dot_general(spread, onehot, NT, preferred_element_type=F32)

    @pl.loop(0, owners // TOGETHER // 4)
    def _(n):
        total[...] += functools.reduce(lambda sums, i: sums + step(n * 4 + i), range(1, 4), step(n * 4))

    even_ref[FIELDS * hx] = jnp.zeros((ITERS, hz), F32)
    scale = lax.rsqrt(mass_ref[...])
    half_x = hx // 2
    odd = lax.axis_index("tgt") % 2 == 1
    for f in range(FIELDS):
        s = total[f * groups : (f + 1) * groups] + total[(FIELDS + f) * groups : (FIELDS + f + 1) * groups]
        for b in range(2):
            for x in range(half_x):
                at = b * half_x + x
                v = s[x * hy : (x + 1) * hy, b * hz : (b + 1) * hz] * scale[at]
                v_ref[f, at] = v
                first, last = v[:ITERS], v[hy - ITERS :]
                even_ref[f * hx + at] = jnp.where(odd, first, last)
                odd_ref[f * hx + at] = jnp.where(odd, last, first)


def scatter_call(values, target, mass):
    hx, hy, hz = mass.shape
    groups = hx * hy * hz // WIDE
    even = jax.ShapeDtypeStruct((FIELDS * hx + 1, ITERS, hz), F32)
    odd = jax.ShapeDtypeStruct((FIELDS * hx, ITERS, hz), F32)
    return pl.pallas_call(
        scatter_kernel,
        out_shape=(jax.ShapeDtypeStruct((FIELDS, hx, hy, hz), F32), even, odd),
        in_specs=[pl.BlockSpec(memory_space=pltpu.VMEM)] * 3,
        out_specs=(pl.BlockSpec(memory_space=pltpu.VMEM),) * 3,
        scratch_shapes=[pltpu.VMEM((2 * FIELDS * groups, WIDE), F32)],
        compiler_params=pltpu.CompilerParams(vmem_limit_bytes=40 << 20),
    )(values, target, mass)


def lookup_rows(table, index, ids, group_ids, groups, at_parts):
    group, low = at_parts(index)
    got = jnp.dot(table, low_onehot(low, ids), preferred_element_type=F32)
    here = group_ids == group
    rows = 3 * groups
    out = []
    for m in range(3):
        part = got[m * groups : (m + 1) * groups] + got[rows + m * groups : rows + (m + 1) * groups]
        out.append(jnp.sum(jnp.where(here, part, 0.0), axis=0, keepdims=True))
    return out


def pick_rows(tables, row, lane):
    row = jnp.broadcast_to(row, (8, 128))
    lane = jnp.broadcast_to(lane, (8, 128))
    tile = row >> 3
    here = row_ids(8, 128) == (row & 7)
    out = []
    for table in tables:
        got = jnp.zeros((8, 128), F32)
        for v in range(table.shape[0] // 8):
            piece = jnp.take_along_axis(table[v * 8 : (v + 1) * 8], lane, axis=1, mode="promise_in_bounds")
            got = jnp.where(tile == v, piece, got)
        out.append(jnp.sum(jnp.where(here, got, 0.0), axis=0, keepdims=True))
    return out


def either_way(i, index, table, ids, group_ids, groups, at_parts, tables, row_and_lane):
    halves_of = [slice(c * 128, (c + 1) * 128) for c in range(2)]
    if i % 8 in (2, 5, 7):
        got = [pick_rows(tables, *row_and_lane(index[:, c])) for c in halves_of]
        return [got[c][m] for m in range(3) for c in range(2)]
    got = lookup_rows(table, index, ids, group_ids, groups, at_parts)
    return [line[:, c] for line in got for c in halves_of]


def cell_moduli(vals):
    phi = vals[0]
    mean = (vals[1] + vals[2] + vals[3]) / 3.0
    q2 = 1.5 * (
        (vals[1] - mean) ** 2
        + (vals[2] - mean) ** 2
        + (vals[3] - mean) ** 2
        + 2.0 * (vals[4] ** 2 + vals[5] ** 2 + vals[6] ** 2)
    )
    bulk = 1.6 * jnp.exp(-3.0 * phi) * (1.0 + 0.25 * jnp.tanh(mean))
    shear = 0.9 * jnp.exp(-2.0 * phi) / (1.0 + q2 / 0.5)
    soften = shear * q2 / (0.5 + q2)
    return [bulk, shear, soften]


def corners(sides):
    line = row_ids(2 * ITERS, sides[0].shape[1])
    near = pltpu.roll(sides[1], 2, 0)
    far = jnp.where(line == 4, pltpu.roll(sides[2], 4, 0), pltpu.roll(sides[2], 6, 0))
    return sides[0], jnp.where(line < 4, near, far)


def sides_kernel(even_ref, odd_ref, sides_ref, to_even_ref, to_odd_ref):
    hx = sides_ref.shape[1]
    b_odd = lax.axis_index("tgt") % 2 == 1
    a_odd = lax.axis_index("src") % 2 == 1
    for f in range(FIELDS):
        sides = []
        for x in range(hx):
            even_side, odd_side = even_ref[f * hx + x], odd_ref[f * hx + x]
            right = jnp.where(b_odd, odd_side, even_side)
            left = jnp.where(b_odd, even_side, odd_side)
            sides.append(jnp.concatenate([right, left], axis=0))
            sides_ref[f, x] = sides[x]
        to_left, to_right = corners(sides), corners(sides[::-1])
        to_even_ref[f, :8] = jnp.where(a_odd, to_left[0], to_right[0])
        to_even_ref[f, 8:14] = jnp.where(a_odd, to_left[1], to_right[1])[:6]
        to_odd_ref[f, :8] = jnp.where(a_odd, to_right[0], to_left[0])
        to_odd_ref[f, 8:] = jnp.where(a_odd, to_right[1], to_left[1])


def sides_call(even, odd, hx):
    hz = even.shape[2]
    return pl.pallas_call(
        sides_kernel,
        out_shape=(
            jax.ShapeDtypeStruct((FIELDS, hx, 2 * ITERS, hz), F32),
            jax.ShapeDtypeStruct((FIELDS, 4 * ITERS - 2, hz), F32),
            jax.ShapeDtypeStruct((FIELDS, 4 * ITERS, hz), F32),
        ),
        in_specs=[pl.BlockSpec(memory_space=pltpu.VMEM)] * 2,
        out_specs=(pl.BlockSpec(memory_space=pltpu.VMEM),) * 3,
        compiler_params=pltpu.CompilerParams(vmem_limit_bytes=4 << 20),
        cost_estimate=pl.CostEstimate(flops=40 * 10**9, bytes_accessed=40 * 10**6, transcendentals=0),
    )(even, odd)


def solve_kernel(
    mesh_shape, v_ref, sides_ref, even_ref, odd_ref, even_corners_ref, odd_corners_ref, mass_ref, order_ref,
    projected_hbm, out_ref, projected_ref, sem,
):
    n_src, n_tgt = mesh_shape
    hx, hy, hz = mass_ref.shape
    k = ITERS
    rows = hy + 2 * k
    a, b = lax.axis_index("src"), lax.axis_index("tgt")

    def exists(flag):
        return jnp.where(flag, 1.0, 0.0).astype(F32)

    row = row_ids(rows, hz)
    lane = lax.broadcasted_iota(jnp.int32, (rows, hz), 1)
    inside = jnp.where(row < hy, 1.0, jnp.where(row < hy + k, exists(b < n_tgt - 1), exists(b > 0)))
    inside_left = inside * exists(a > 0)
    inside_right = inside * exists(a < n_src - 1)
    not_first = jnp.where(lane == 0, 0.0, 1.0)
    not_last = jnp.where(lane == hz - 1, 0.0, 1.0)
    scale = lax.rsqrt(mass_ref[...])

    line = row_ids(2 * k, hz)

    def slabs(own, first, packed, from_left):
        second = pltpu.roll(packed, 6, 0)
        third = jnp.where(line < 4, pltpu.roll(packed, 4, 0), pltpu.roll(packed, 2, 0))
        sides = [first, second, third] + [jnp.zeros((2 * k, hz), F32)] * (hx - 3)
        if from_left:
            sides = sides[::-1]
        return [jnp.concatenate([own[x], side], axis=0) for x, side in enumerate(sides)]

    a_odd = a % 2 == 1

    for f in range(FIELDS):
        packed = jnp.concatenate([even_corners_ref[f, 2 * k :], jnp.zeros((2, hz), F32)], axis=0)
        even = (even_ref[f], even_corners_ref[f, : 2 * k], packed)
        odd = (odd_ref[f], odd_corners_ref[f, : 2 * k], odd_corners_ref[f, 2 * k :])
        left = slabs(*[jnp.where(a_odd, p, q) for p, q in zip(even, odd)], True)
        right = slabs(*[jnp.where(a_odd, q, p) for p, q in zip(even, odd)], False)
        own = [jnp.concatenate([v_ref[f, x], sides_ref[f, x]], axis=0) for x in range(hx)]
        base = left + own + right
        u = [COEFS[k] * e for e in base]
        for sweep in range(1, k + 1):
            new = list(u)
            for x in range(sweep, hx + 2 * k - sweep):
                far = max(k - x, x - (k + hx - 1), 0)
                n = rows if sweep + far < k else hy
                w = u[x]
                near = u[x - 1][:n] + u[x + 1][:n]
                near = near + pltpu.roll(w, 1, 0)[:n] + pltpu.roll(w, rows - 1, 0)[:n]
                w = w[:n]
                near = near + pltpu.roll(w, 1, 1) * not_first[:n] + pltpu.roll(w, hz - 1, 1) * not_last[:n]
                if x < k:
                    near = near * inside_left[:n]
                elif x >= k + hx:
                    near = near * inside_right[:n]
                elif n > hy:
                    near = near * inside
                new[x] = COEFS[k - sweep] * base[x][:n] + near
            u = new
        for x in range(hx):
            projected_ref[f, x] = u[k + x][:hy] * scale[x]

    leave = pltpu.make_async_copy(projected_ref, projected_hbm, sem)
    leave.start()
    groups = hx * hy * hz // WIDE
    payload = cell_moduli([projected_ref[f].reshape(hx * hy, hz) for f in range(FIELDS)])
    table = jnp.concatenate([jnp.concatenate([m[:groups], m[groups:]], axis=1) for m in payload], axis=0)
    table = jnp.concatenate(halves(table), axis=0)
    ids = row_ids(WIDE, WIDE).astype(F32).astype(BF16)
    group_ids = row_ids(groups, WIDE)

    def at_parts(index):
        return (index >> log2(hz)) & (groups - 1), ((index >> log2(groups * hz)) << log2(hz)) + (index & (hz - 1))

    def row_and_lane(index):
        return index >> log2(hz), index & (hz - 1)

    for q in range(0, groups, 4):
        lines = []
        for i in range(q, q + 4):
            index = order_ref[:, i * WIDE : (i + 1) * WIDE]
            lines += either_way(i, index, table, ids, group_ids, groups, at_parts, payload, row_and_lane)
        out_ref[q * 6 : q * 6 + 24, :] = jnp.concatenate(lines, axis=0)
    leave.wait()


def solve_call(mesh_shape, *args):
    mass, order = args[-2:]
    hx, hy, hz = mass.shape

    def kernel(*refs):
        solve_kernel(mesh_shape, *refs)

    return pl.pallas_call(
        kernel,
        out_shape=(
            jax.ShapeDtypeStruct((FIELDS, hx, hy, hz), F32),
            jax.ShapeDtypeStruct((order.shape[1] // WIDE * 6, 128), F32),
        ),
        in_specs=[pl.BlockSpec(memory_space=pltpu.VMEM)] * 8,
        out_specs=(pl.BlockSpec(memory_space=pltpu.HBM), pl.BlockSpec(memory_space=pltpu.VMEM)),
        scratch_shapes=[pltpu.VMEM((FIELDS, hx, hy, hz), F32), pltpu.SemaphoreType.DMA],
        compiler_params=pltpu.CompilerParams(vmem_limit_bytes=40 << 20),
    )(*args)


def place_kernel(arrived_ref, order_ref, out_hbm, out_ref, sems):
    groups = arrived_ref.shape[0] // 6
    parts = [[arrived_ref[pl.ds(2 * m + c, groups, stride=6), :] for c in range(2)] for m in range(3)]
    table = jnp.concatenate([jnp.concatenate(part, axis=1) for part in parts], axis=0)
    table = jnp.concatenate(halves(table), axis=0)
    tables = [jnp.concatenate(part, axis=0) for part in parts]
    ids = row_ids(WIDE, WIDE).astype(F32).astype(BF16)
    group_ids = row_ids(groups, WIDE)

    def at_parts(index):
        return index >> log2(WIDE), index & (WIDE - 1)

    def row_and_lane(index):
        return ((index >> 7) & 1) * groups + (index >> log2(WIDE)), index & 127

    copies = []
    for n in range(PIECES):
        for q in range(n * groups // PIECES, (n + 1) * groups // PIECES):
            index = order_ref[:, q * WIDE : (q + 1) * WIDE]
            lines = either_way(q, index, table, ids, group_ids, groups, at_parts, tables, row_and_lane)
            for c in range(2):
                out_ref[:, q * WIDE + c * 128 : q * WIDE + (c + 1) * 128] = jnp.concatenate(lines[c::2], axis=0)
        piece = pl.ds(n * groups // PIECES * WIDE, groups // PIECES * WIDE)
        copies.append(pltpu.make_async_copy(out_ref.at[:, piece], out_hbm.at[:, piece], sems.at[n]))
        copies[n].start()
    for copy in copies:
        copy.wait()


def place_call(arrived, order):
    return pl.pallas_call(
        place_kernel,
        out_shape=jax.ShapeDtypeStruct((3, order.shape[1]), F32),
        in_specs=[pl.BlockSpec(memory_space=pltpu.VMEM)] * 2,
        out_specs=pl.BlockSpec(memory_space=pltpu.HBM),
        scratch_shapes=[pltpu.VMEM((3, order.shape[1]), F32), pltpu.SemaphoreType.DMA((PIECES,))],
        compiler_params=pltpu.CompilerParams(vmem_limit_bytes=40 << 20),
    )(arrived, order)


def swap(x, axis, start):
    pairs = [(i, i + 1) for i in range(start, lax.axis_size(axis) - 1, 2)]
    return lax.ppermute(x, axis, pairs + [(j, i) for i, j in pairs])


def on_device(source_fields, slot_source, slot_weight, slot_target, cell_mass, send_order, place_order):
    n_src, n_tgt = lax.axis_size("src"), lax.axis_size("tgt")
    both = ("src", "tgt")
    owners = n_src * n_tgt
    cells = cell_mass.size
    quota = cells // owners

    values = gather_call(source_fields, slot_source.reshape(1, -1), slot_weight.reshape(1, -1))
    values = values.reshape(owners, FIELDS, SPAN // 128, 128)
    values = lax.all_to_all(values, both, split_axis=0, concat_axis=0, tiled=True).reshape(-1, 128)
    v, even, odd = scatter_call(values, slot_target.reshape(1, -1), cell_mass)
    even_block, odd_block = swap(v, "src", 0), swap(v, "src", 1)
    even, odd = swap(even, "tgt", 0), swap(odd, "tgt", 1)
    sides, even, odd = sides_call(even, odd, cell_mass.shape[0])
    even, odd = swap(even, "src", 0), swap(odd, "src", 1)
    projected, outgoing = solve_call(
        (n_src, n_tgt), v, sides, even_block, odd_block, even, odd, cell_mass, send_order
    )

    if quota == WIDE:
        outgoing = outgoing.reshape(owners, 3, 2, 128)
        incoming = lax.all_to_all(outgoing, both, split_axis=0, concat_axis=0, tiled=True)
    else:
        groups = cells // WIDE
        flat = outgoing.reshape(groups, 3, WIDE).transpose(1, 0, 2).reshape(3, owners, quota)
        flat = lax.all_to_all(flat, both, split_axis=1, concat_axis=1, tiled=True)
        incoming = flat.reshape(3, groups, WIDE).transpose(1, 0, 2)
    incoming = incoming.reshape(-1, 128)
    return projected, place_call(incoming, place_order)


def solution(mesh):
    split = P(("src", "tgt"))
    rows = P(("src", "tgt"), None)
    return jax.shard_map(
        on_device,
        mesh=mesh,
        in_specs=(P(None, ("src", "tgt")), split, split, split, P("src", "tgt", None), rows, rows),
        out_specs=(P(None, "src", "tgt", None), P(None, ("src", "tgt"))),
        check_vma=False,
    )
```

```python
import functools

import numpy as np

import jax
import jax.numpy as jnp
from jax import lax
from jax.experimental import pallas as pl
from jax.experimental.pallas import tpu as pltpu
from jax.sharding import PartitionSpec as P

ITERS = 4
FIELDS = 7
PIECES = 4
SPAN = 512
AT_ONCE = 32
TOGETHER = 8
WIDE = 256
BF16 = jnp.bfloat16
F32 = jnp.float32
NT = (((1,), (1,)), ((), ()))


def sweep_polynomial(iters, theta, delta):
    sigma = theta / delta
    rho = 1.0 / sigma
    mass = np.array([1.0, 0.125])
    poly = np.polynomial.polynomial
    resid = np.array([1.0])
    step = resid / theta
    total = np.array([0.0])
    for _ in range(iters):
        total = poly.polyadd(total, step)
        resid = poly.polysub(resid, poly.polymul(mass, step))
        rho_new = 1.0 / (2.0 * sigma - rho)
        step = poly.polyadd(rho_new * rho * step, 2.0 * rho_new / delta * resid)
        rho = rho_new
    return [float(c) for c in poly.polyadd(total, step)]


COEFS = sweep_polynomial(ITERS, 1.0, 0.75)


def halves(x):
    high = x.astype(BF16)
    return high, (x - high.astype(F32)).astype(BF16)


def log2(n):
    assert n & (n - 1) == 0
    return n.bit_length() - 1


def row_ids(rows, lanes):
    return lax.broadcasted_iota(jnp.int32, (rows, lanes), 0)


def low_onehot(low, ids):
    return jnp.where(ids == low.astype(F32).astype(BF16), jnp.ones((), BF16), jnp.zeros((), BF16))


def gather_kernel(fields_hbm, index_hbm, weight_hbm, out_ref, table, padded, fields_ref, index_ref, weight_ref, sems):
    pairs = ((fields_hbm, fields_ref), (index_hbm, index_ref), (weight_hbm, weight_ref))
    copies = [pltpu.make_async_copy(src, dst, sems.at[i]) for i, (src, dst) in enumerate(pairs)]
    for copy in copies:
        copy.start()
    lanes = out_ref.shape[1]
    span = SPAN
    tiles = span // lanes
    owners = index_ref.shape[1] // span
    groups = fields_ref.shape[1] // WIDE
    table[...] = jnp.zeros_like(table)
    padded[...] = jnp.zeros_like(padded)
    for copy in copies:
        copy.wait()
    for g in range(groups):
        table[g * 8 : g * 8 + FIELDS, :] = fields_ref[:, g * WIDE : (g + 1) * WIDE]
    both = jnp.concatenate(halves(table[...]), axis=0)
    rows = groups * 8
    ids = row_ids(WIDE, WIDE).astype(F32).astype(BF16)
    padded[:FIELDS, :] = fields_ref[...]

    def by_matmul(index):
        got = jnp.dot(both, low_onehot(index & (WIDE - 1), ids), preferred_element_type=F32)
        group = jnp.broadcast_to(index >> log2(WIDE), (8, WIDE))
        value = jnp.zeros((8, WIDE), F32)
        for g in range(groups):
            part = got[g * 8 : (g + 1) * 8] + got[rows + g * 8 : rows + (g + 1) * 8]
            value = jnp.where(group == g, part, value)
        return value

    def by_lanes(index):
        lane = jnp.broadcast_to(index & 127, (8, 128))
        tile = jnp.broadcast_to(index >> 7, (8, 128))
        value = jnp.zeros((8, 128), F32)
        for g in range(padded.shape[1] // 128):
            piece = padded[:, g * 128 : (g + 1) * 128]
            piece = jnp.take_along_axis(piece, lane, axis=1, mode="promise_in_bounds")
            value = jnp.where(tile == g, piece, value)
        return value

    def one_owner(q, matmuls):
        at = pl.multiple_of(q * SPAN, SPAN)
        index = index_ref[:, pl.ds(at, SPAN)]
        weight = weight_ref[:, pl.ds(at, SPAN)]
        values = [by_matmul(index[:, i * WIDE : (i + 1) * WIDE]) for i in range(matmuls)]
        for t in range(matmuls * WIDE // 128, tiles):
            values.append(by_lanes(index[:, t * 128 : (t + 1) * 128]))
        value = jnp.concatenate(values, axis=1) * weight
        for t in range(tiles):
            out_ref[pl.ds(q * (FIELDS * tiles) + t, FIELDS, stride=tiles), :] = value[
                :FIELDS, t * lanes : (t + 1) * lanes
            ]

    @pl.loop(0, owners // AT_ONCE)
    def _(m):
        for i in range(AT_ONCE):
            one_owner(m * AT_ONCE + i, SPAN // WIDE - (i % 4 > 0))


def gather_call(fields, index, weight):
    rows = FIELDS * index.shape[1] // 128
    return pl.pallas_call(
        gather_kernel,
        out_shape=jax.ShapeDtypeStruct((rows, 128), F32),
        in_specs=[pl.BlockSpec(memory_space=pltpu.HBM)] * 3,
        out_specs=pl.BlockSpec(memory_space=pltpu.VMEM),
        scratch_shapes=[
            pltpu.VMEM((fields.shape[1] // WIDE * 8, WIDE), F32),
            pltpu.VMEM((8, fields.shape[1]), F32),
            pltpu.VMEM(fields.shape, F32),
            pltpu.VMEM(index.shape, jnp.int32),
            pltpu.VMEM(weight.shape, F32),
            pltpu.SemaphoreType.DMA((3,)),
        ],
        compiler_params=pltpu.CompilerParams(vmem_limit_bytes=40 << 20),
    )(*[pltpu.with_memory_space_constraint(x, pltpu.HBM) for x in (fields, index, weight)])


def scatter_kernel(value_ref, target_ref, mass_ref, v_ref, even_ref, odd_ref, total):
    lanes = value_ref.shape[1]
    tiles = SPAN // lanes
    owners = target_ref.shape[1] // SPAN
    span = TOGETHER * SPAN
    hx, hy, hz = mass_ref.shape
    groups = hx * hy * hz // WIDE
    total[...] = jnp.zeros_like(total)
    ids = row_ids(WIDE, span).astype(F32).astype(BF16)
    group_ids = row_ids(groups, span).astype(F32).astype(BF16)

    def step(p):
        at = pl.multiple_of(p * span, span)
        target = target_ref[:, pl.ds(at, span)]
        low = ((target >> log2(groups * hz)) << log2(hz)) + (target & (hz - 1))
        onehot = low_onehot(jnp.where(target < 0, -1, low), ids)
        group = ((target >> log2(hz)) & (groups - 1)).astype(F32).astype(BF16)
        here = group_ids == group
        row = p * (TOGETHER * FIELDS * tiles)
        pieces = [i * FIELDS * tiles + t for i in range(TOGETHER) for t in range(tiles)]
        value = jnp.concatenate([value_ref[pl.ds(row + i, FIELDS, stride=tiles), :] for i in pieces], axis=1)
        parts = []
        for half in halves(value):
            for f in range(FIELDS):
                parts.append(jnp.where(here, half[f : f + 1], jnp.zeros((), BF16)))
        spread = jnp.concatenate(parts, axis=0)
        return lax.dot_general(spread, onehot, NT, preferred_element_type=F32)

    @pl.loop(0, owners // TOGETHER // 4)
    def _(n):
        total[...] += functools.reduce(lambda sums, i: sums + step(n * 4 + i), range(1, 4), step(n * 4))

    even_ref[FIELDS * hx] = jnp.zeros((ITERS, hz), F32)
    scale = lax.rsqrt(mass_ref[...])
    half_x = hx // 2
    odd = lax.axis_index("tgt") % 2 == 1
    for f in range(FIELDS):
        s = total[f * groups : (f + 1) * groups] + total[(FIELDS + f) * groups : (FIELDS + f + 1) * groups]
        for b in range(2):
            for x in range(half_x):
                at = b * half_x + x
                v = s[x * hy : (x + 1) * hy, b * hz : (b + 1) * hz] * scale[at]
                v_ref[f, at] = v
                first, last = v[:ITERS], v[hy - ITERS :]
                even_ref[f * hx + at] = jnp.where(odd, first, last)
                odd_ref[f * hx + at] = jnp.where(odd, last, first)


def scatter_call(values, target, mass):
    hx, hy, hz = mass.shape
    groups = hx * hy * hz // WIDE
    even = jax.ShapeDtypeStruct((FIELDS * hx + 1, ITERS, hz), F32)
    odd = jax.ShapeDtypeStruct((FIELDS * hx, ITERS, hz), F32)
    return pl.pallas_call(
        scatter_kernel,
        out_shape=(jax.ShapeDtypeStruct((FIELDS, hx, hy, hz), F32), even, odd),
        in_specs=[pl.BlockSpec(memory_space=pltpu.VMEM)] * 3,
        out_specs=(pl.BlockSpec(memory_space=pltpu.VMEM),) * 3,
        scratch_shapes=[pltpu.VMEM((2 * FIELDS * groups, WIDE), F32)],
        compiler_params=pltpu.CompilerParams(vmem_limit_bytes=40 << 20),
    )(values, target, mass)


def lookup_rows(table, index, ids, group_ids, groups, at_parts):
    group, low = at_parts(index)
    got = jnp.dot(table, low_onehot(low, ids), preferred_element_type=F32)
    here = group_ids == group
    rows = 3 * groups
    out = []
    for m in range(3):
        part = got[m * groups : (m + 1) * groups] + got[rows + m * groups : rows + (m + 1) * groups]
        out.append(jnp.sum(jnp.where(here, part, 0.0), axis=0, keepdims=True))
    return out


def pick_rows(tables, row, lane):
    row = jnp.broadcast_to(row, (8, 128))
    lane = jnp.broadcast_to(lane, (8, 128))
    tile = row >> 3
    here = row_ids(8, 128) == (row & 7)
    out = []
    for table in tables:
        got = jnp.zeros((8, 128), F32)
        for v in range(table.shape[0] // 8):
            piece = jnp.take_along_axis(table[v * 8 : (v + 1) * 8], lane, axis=1, mode="promise_in_bounds")
            got = jnp.where(tile == v, piece, got)
        out.append(jnp.sum(jnp.where(here, got, 0.0), axis=0, keepdims=True))
    return out


def either_way(i, index, table, ids, group_ids, groups, at_parts, tables, row_and_lane):
    halves_of = [slice(c * 128, (c + 1) * 128) for c in range(2)]
    if i % 8 in (2, 5, 7):
        got = [pick_rows(tables, *row_and_lane(index[:, c])) for c in halves_of]
        return [got[c][m] for m in range(3) for c in range(2)]
    got = lookup_rows(table, index, ids, group_ids, groups, at_parts)
    return [line[:, c] for line in got for c in halves_of]


def cell_moduli(vals):
    phi = vals[0]
    mean = (vals[1] + vals[2] + vals[3]) / 3.0
    q2 = 1.5 * (
        (vals[1] - mean) ** 2
        + (vals[2] - mean) ** 2
        + (vals[3] - mean) ** 2
        + 2.0 * (vals[4] ** 2 + vals[5] ** 2 + vals[6] ** 2)
    )
    bulk = 1.6 * jnp.exp(-3.0 * phi) * (1.0 + 0.25 * jnp.tanh(mean))
    shear = 0.9 * jnp.exp(-2.0 * phi) / (1.0 + q2 / 0.5)
    soften = shear * q2 / (0.5 + q2)
    return [bulk, shear, soften]


def corners(sides):
    line = row_ids(2 * ITERS, sides[0].shape[1])
    near = pltpu.roll(sides[1], 2, 0)
    far = jnp.where(line == 4, pltpu.roll(sides[2], 4, 0), pltpu.roll(sides[2], 6, 0))
    return sides[0], jnp.where(line < 4, near, far)


def sides_kernel(even_ref, odd_ref, sides_ref, to_even_ref, to_odd_ref):
    hx = sides_ref.shape[1]
    b_odd = lax.axis_index("tgt") % 2 == 1
    a_odd = lax.axis_index("src") % 2 == 1
    for f in range(FIELDS):
        sides = []
        for x in range(hx):
            even_side, odd_side = even_ref[f * hx + x], odd_ref[f * hx + x]
            right = jnp.where(b_odd, odd_side, even_side)
            left = jnp.where(b_odd, even_side, odd_side)
            sides.append(jnp.concatenate([right, left], axis=0))
            sides_ref[f, x] = sides[x]
        to_left, to_right = corners(sides), corners(sides[::-1])
        to_even_ref[f, :8] = jnp.where(a_odd, to_left[0], to_right[0])
        to_even_ref[f, 8:14] = jnp.where(a_odd, to_left[1], to_right[1])[:6]
        to_odd_ref[f, :8] = jnp.where(a_odd, to_right[0], to_left[0])
        to_odd_ref[f, 8:] = jnp.where(a_odd, to_right[1], to_left[1])


def sides_call(even, odd, hx):
    hz = even.shape[2]
    return pl.pallas_call(
        sides_kernel,
        out_shape=(
            jax.ShapeDtypeStruct((FIELDS, hx, 2 * ITERS, hz), F32),
            jax.ShapeDtypeStruct((FIELDS, 4 * ITERS - 2, hz), F32),
            jax.ShapeDtypeStruct((FIELDS, 4 * ITERS, hz), F32),
        ),
        in_specs=[pl.BlockSpec(memory_space=pltpu.VMEM)] * 2,
        out_specs=(pl.BlockSpec(memory_space=pltpu.VMEM),) * 3,
        compiler_params=pltpu.CompilerParams(vmem_limit_bytes=4 << 20),
        cost_estimate=pl.CostEstimate(flops=40 * 10**9, bytes_accessed=40 * 10**6, transcendentals=0),
    )(even, odd)


def solve_kernel(
    mesh_shape, v_ref, sides_ref, even_ref, odd_ref, even_corners_ref, odd_corners_ref, mass_ref, order_ref,
    projected_hbm, out_ref, projected_ref, sem,
):
    n_src, n_tgt = mesh_shape
    hx, hy, hz = mass_ref.shape
    k = ITERS
    rows = hy + 2 * k
    a, b = lax.axis_index("src"), lax.axis_index("tgt")

    def exists(flag):
        return jnp.where(flag, 1.0, 0.0).astype(F32)

    row = row_ids(rows, hz)
    lane = lax.broadcasted_iota(jnp.int32, (rows, hz), 1)
    inside = jnp.where(row < hy, 1.0, jnp.where(row < hy + k, exists(b < n_tgt - 1), exists(b > 0)))
    inside_left = inside * exists(a > 0)
    inside_right = inside * exists(a < n_src - 1)
    not_first = jnp.where(lane == 0, 0.0, 1.0)
    not_last = jnp.where(lane == hz - 1, 0.0, 1.0)
    scale = lax.rsqrt(mass_ref[...])

    line = row_ids(2 * k, hz)

    def slabs(own, first, packed, from_left):
        second = pltpu.roll(packed, 6, 0)
        third = jnp.where(line < 4, pltpu.roll(packed, 4, 0), pltpu.roll(packed, 2, 0))
        sides = [first, second, third] + [jnp.zeros((2 * k, hz), F32)] * (hx - 3)
        if from_left:
            sides = sides[::-1]
        return [jnp.concatenate([own[x], side], axis=0) for x, side in enumerate(sides)]

    a_odd = a % 2 == 1

    for f in range(FIELDS):
        packed = jnp.concatenate([even_corners_ref[f, 2 * k :], jnp.zeros((2, hz), F32)], axis=0)
        even = (even_ref[f], even_corners_ref[f, : 2 * k], packed)
        odd = (odd_ref[f], odd_corners_ref[f, : 2 * k], odd_corners_ref[f, 2 * k :])
        left = slabs(*[jnp.where(a_odd, p, q) for p, q in zip(even, odd)], True)
        right = slabs(*[jnp.where(a_odd, q, p) for p, q in zip(even, odd)], False)
        own = [jnp.concatenate([v_ref[f, x], sides_ref[f, x]], axis=0) for x in range(hx)]
        base = left + own + right
        u = [COEFS[k] * e for e in base]
        for sweep in range(1, k + 1):
            new = list(u)
            for x in range(sweep, hx + 2 * k - sweep):
                far = max(k - x, x - (k + hx - 1), 0)
                n = rows if sweep + far < k else hy
                w = u[x]
                near = u[x - 1][:n] + u[x + 1][:n]
                near = near + pltpu.roll(w, 1, 0)[:n] + pltpu.roll(w, rows - 1, 0)[:n]
                w = w[:n]
                near = near + pltpu.roll(w, 1, 1) * not_first[:n] + pltpu.roll(w, hz - 1, 1) * not_last[:n]
                if x < k:
                    near = near * inside_left[:n]
                elif x >= k + hx:
                    near = near * inside_right[:n]
                elif n > hy:
                    near = near * inside
                new[x] = COEFS[k - sweep] * base[x][:n] + near
            u = new
        for x in range(hx):
            projected_ref[f, x] = u[k + x][:hy] * scale[x]

    leave = pltpu.make_async_copy(projected_ref, projected_hbm, sem)
    leave.start()
    groups = hx * hy * hz // WIDE
    payload = cell_moduli([projected_ref[f].reshape(hx * hy, hz) for f in range(FIELDS)])
    table = jnp.concatenate([jnp.concatenate([m[:groups], m[groups:]], axis=1) for m in payload], axis=0)
    table = jnp.concatenate(halves(table), axis=0)
    ids = row_ids(WIDE, WIDE).astype(F32).astype(BF16)
    group_ids = row_ids(groups, WIDE)

    def at_parts(index):
        return (index >> log2(hz)) & (groups - 1), ((index >> log2(groups * hz)) << log2(hz)) + (index & (hz - 1))

    for q in range(0, groups, 4):
        lines = []
        for i in range(q, q + 4):
            index = order_ref[:, i * WIDE : (i + 1) * WIDE]
            got = lookup_rows(table, index, ids, group_ids, groups, at_parts)
            lines += [line[:, c * 128 : (c + 1) * 128] for line in got for c in range(2)]
        out_ref[q * 6 : q * 6 + 24, :] = jnp.concatenate(lines, axis=0)
    leave.wait()


def solve_call(mesh_shape, *args):
    mass, order = args[-2:]
    hx, hy, hz = mass.shape

    def kernel(*refs):
        solve_kernel(mesh_shape, *refs)

    return pl.pallas_call(
        kernel,
        out_shape=(
            jax.ShapeDtypeStruct((FIELDS, hx, hy, hz), F32),
            jax.ShapeDtypeStruct((order.shape[1] // WIDE * 6, 128), F32),
        ),
        in_specs=[pl.BlockSpec(memory_space=pltpu.VMEM)] * 8,
        out_specs=(pl.BlockSpec(memory_space=pltpu.HBM), pl.BlockSpec(memory_space=pltpu.VMEM)),
        scratch_shapes=[pltpu.VMEM((FIELDS, hx, hy, hz), F32), pltpu.SemaphoreType.DMA],
        compiler_params=pltpu.CompilerParams(vmem_limit_bytes=40 << 20),
    )(*args)


def place_kernel(arrived_ref, order_ref, out_hbm, out_ref, sems):
    groups = arrived_ref.shape[0] // 6
    parts = [[arrived_ref[pl.ds(2 * m + c, groups, stride=6), :] for c in range(2)] for m in range(3)]
    table = jnp.concatenate([jnp.concatenate(part, axis=1) for part in parts], axis=0)
    table = jnp.concatenate(halves(table), axis=0)
    tables = [jnp.concatenate(part, axis=0) for part in parts]
    ids = row_ids(WIDE, WIDE).astype(F32).astype(BF16)
    group_ids = row_ids(groups, WIDE)

    def at_parts(index):
        return index >> log2(WIDE), index & (WIDE - 1)

    def row_and_lane(index):
        return ((index >> 7) & 1) * groups + (index >> log2(WIDE)), index & 127

    copies = []
    for n in range(PIECES):
        for q in range(n * groups // PIECES, (n + 1) * groups // PIECES):
            index = order_ref[:, q * WIDE : (q + 1) * WIDE]
            lines = either_way(q, index, table, ids, group_ids, groups, at_parts, tables, row_and_lane)
            for c in range(2):
                out_ref[:, q * WIDE + c * 128 : q * WIDE + (c + 1) * 128] = jnp.concatenate(lines[c::2], axis=0)
        piece = pl.ds(n * groups // PIECES * WIDE, groups // PIECES * WIDE)
        copies.append(pltpu.make_async_copy(out_ref.at[:, piece], out_hbm.at[:, piece], sems.at[n]))
        copies[n].start()
    for copy in copies:
        copy.wait()


def place_call(arrived, order):
    return pl.pallas_call(
        place_kernel,
        out_shape=jax.ShapeDtypeStruct((3, order.shape[1]), F32),
        in_specs=[pl.BlockSpec(memory_space=pltpu.VMEM)] * 2,
        out_specs=pl.BlockSpec(memory_space=pltpu.HBM),
        scratch_shapes=[pltpu.VMEM((3, order.shape[1]), F32), pltpu.SemaphoreType.DMA((PIECES,))],
        compiler_params=pltpu.CompilerParams(vmem_limit_bytes=40 << 20),
    )(arrived, order)


def swap(x, axis, start):
    pairs = [(i, i + 1) for i in range(start, lax.axis_size(axis) - 1, 2)]
    return lax.ppermute(x, axis, pairs + [(j, i) for i, j in pairs])


def on_device(source_fields, slot_source, slot_weight, slot_target, cell_mass, send_order, place_order):
    n_src, n_tgt = lax.axis_size("src"), lax.axis_size("tgt")
    both = ("src", "tgt")
    owners = n_src * n_tgt
    cells = cell_mass.size
    quota = cells // owners

    values = gather_call(source_fields, slot_source.reshape(1, -1), slot_weight.reshape(1, -1))
    values = values.reshape(owners, FIELDS, SPAN // 128, 128)
    values = lax.all_to_all(values, both, split_axis=0, concat_axis=0, tiled=True).reshape(-1, 128)
    v, even, odd = scatter_call(values, slot_target.reshape(1, -1), cell_mass)
    even_block, odd_block = swap(v, "src", 0), swap(v, "src", 1)
    even, odd = swap(even, "tgt", 0), swap(odd, "tgt", 1)
    sides, even, odd = sides_call(even, odd, cell_mass.shape[0])
    even, odd = swap(even, "src", 0), swap(odd, "src", 1)
    projected, outgoing = solve_call(
        (n_src, n_tgt), v, sides, even_block, odd_block, even, odd, cell_mass, send_order
    )

    if quota == WIDE:
        outgoing = outgoing.reshape(owners, 3, 2, 128)
        incoming = lax.all_to_all(outgoing, both, split_axis=0, concat_axis=0, tiled=True)
    else:
        groups = cells // WIDE
        flat = outgoing.reshape(groups, 3, WIDE).transpose(1, 0, 2).reshape(3, owners, quota)
        flat = lax.all_to_all(flat, both, split_axis=1, concat_axis=1, tiled=True)
        incoming = flat.reshape(3, groups, WIDE).transpose(1, 0, 2)
    incoming = incoming.reshape(-1, 128)
    return projected, place_call(incoming, place_order)


def solution(mesh):
    split = P(("src", "tgt"))
    rows = P(("src", "tgt"), None)
    return jax.shard_map(
        on_device,
        mesh=mesh,
        in_specs=(P(None, ("src", "tgt")), split, split, split, P("src", "tgt", None), rows, rows),
        out_specs=(P(None, "src", "tgt", None), P(None, ("src", "tgt"))),
        check_vma=False,
    )
```

```python
import functools

import numpy as np

import jax
import jax.numpy as jnp
from jax import lax
from jax.experimental import pallas as pl
from jax.experimental.pallas import tpu as pltpu
from jax.sharding import PartitionSpec as P

ITERS = 4
FIELDS = 7
PIECES = 4
SPAN = 512
AT_ONCE = 32
TOGETHER = 8
WIDE = 256
BF16 = jnp.bfloat16
F32 = jnp.float32
NT = (((1,), (1,)), ((), ()))


def sweep_polynomial(iters, theta, delta):
    sigma = theta / delta
    rho = 1.0 / sigma
    mass = np.array([1.0, 0.125])
    poly = np.polynomial.polynomial
    resid = np.array([1.0])
    step = resid / theta
    total = np.array([0.0])
    for _ in range(iters):
        total = poly.polyadd(total, step)
        resid = poly.polysub(resid, poly.polymul(mass, step))
        rho_new = 1.0 / (2.0 * sigma - rho)
        step = poly.polyadd(rho_new * rho * step, 2.0 * rho_new / delta * resid)
        rho = rho_new
    return [float(c) for c in poly.polyadd(total, step)]


COEFS = sweep_polynomial(ITERS, 1.0, 0.75)


def halves(x):
    high = x.astype(BF16)
    return high, (x - high.astype(F32)).astype(BF16)


def log2(n):
    assert n & (n - 1) == 0
    return n.bit_length() - 1


def row_ids(rows, lanes):
    return lax.broadcasted_iota(jnp.int32, (rows, lanes), 0)


def low_onehot(low, ids):
    return jnp.where(ids == low.astype(F32).astype(BF16), jnp.ones((), BF16), jnp.zeros((), BF16))


def gather_kernel(fields_hbm, index_hbm, weight_hbm, out_ref, table, padded, fields_ref, index_ref, weight_ref, sems):
    pairs = ((fields_hbm, fields_ref), (index_hbm, index_ref), (weight_hbm, weight_ref))
    copies = [pltpu.make_async_copy(src, dst, sems.at[i]) for i, (src, dst) in enumerate(pairs)]
    for copy in copies:
        copy.start()
    lanes = out_ref.shape[1]
    span = SPAN
    tiles = span // lanes
    owners = index_ref.shape[1] // span
    groups = fields_ref.shape[1] // WIDE
    table[...] = jnp.zeros_like(table)
    padded[...] = jnp.zeros_like(padded)
    for copy in copies:
        copy.wait()
    for g in range(groups):
        table[g * 8 : g * 8 + FIELDS, :] = fields_ref[:, g * WIDE : (g + 1) * WIDE]
    both = jnp.concatenate(halves(table[...]), axis=0)
    rows = groups * 8
    ids = row_ids(WIDE, WIDE).astype(F32).astype(BF16)
    padded[:FIELDS, :] = fields_ref[...]

    def by_matmul(index):
        got = jnp.dot(both, low_onehot(index & (WIDE - 1), ids), preferred_element_type=F32)
        group = jnp.broadcast_to(index >> log2(WIDE), (8, WIDE))
        value = jnp.zeros((8, WIDE), F32)
        for g in range(groups):
            part = got[g * 8 : (g + 1) * 8] + got[rows + g * 8 : rows + (g + 1) * 8]
            value = jnp.where(group == g, part, value)
        return value

    def by_lanes(index):
        lane = jnp.broadcast_to(index & 127, (8, 128))
        tile = jnp.broadcast_to(index >> 7, (8, 128))
        value = jnp.zeros((8, 128), F32)
        for g in range(padded.shape[1] // 128):
            piece = padded[:, g * 128 : (g + 1) * 128]
            piece = jnp.take_along_axis(piece, lane, axis=1, mode="promise_in_bounds")
            value = jnp.where(tile == g, piece, value)
        return value

    def one_owner(q, matmuls):
        at = pl.multiple_of(q * SPAN, SPAN)
        index = index_ref[:, pl.ds(at, SPAN)]
        weight = weight_ref[:, pl.ds(at, SPAN)]
        values = [by_matmul(index[:, i * WIDE : (i + 1) * WIDE]) for i in range(matmuls)]
        for t in range(matmuls * WIDE // 128, tiles):
            values.append(by_lanes(index[:, t * 128 : (t + 1) * 128]))
        value = jnp.concatenate(values, axis=1) * weight
        return [value[:FIELDS, t * lanes : (t + 1) * lanes] for t in range(tiles)]

    @pl.loop(0, owners // AT_ONCE)
    def _(m):
        lines = []
        for i in range(AT_ONCE):
            q = m * AT_ONCE + i
            value = one_owner(q, SPAN // WIDE - (i % 4 > 0))
            if i < AT_ONCE - 2:
                for t in range(tiles):
                    out_ref[pl.ds(q * (FIELDS * tiles) + t, FIELDS, stride=tiles), :] = value[t]
            else:
                lines += [value[t][f : f + 1] for f in range(FIELDS) for t in range(tiles)]
        at = pl.multiple_of((m * AT_ONCE + AT_ONCE - 2) * (FIELDS * tiles), 8)
        out_ref[pl.ds(at, len(lines)), :] = jnp.concatenate(lines, axis=0)


def gather_call(fields, index, weight):
    rows = FIELDS * index.shape[1] // 128
    return pl.pallas_call(
        gather_kernel,
        out_shape=jax.ShapeDtypeStruct((rows, 128), F32),
        in_specs=[pl.BlockSpec(memory_space=pltpu.HBM)] * 3,
        out_specs=pl.BlockSpec(memory_space=pltpu.VMEM),
        scratch_shapes=[
            pltpu.VMEM((fields.shape[1] // WIDE * 8, WIDE), F32),
            pltpu.VMEM((8, fields.shape[1]), F32),
            pltpu.VMEM(fields.shape, F32),
            pltpu.VMEM(index.shape, jnp.int32),
            pltpu.VMEM(weight.shape, F32),
            pltpu.SemaphoreType.DMA((3,)),
        ],
        compiler_params=pltpu.CompilerParams(vmem_limit_bytes=40 << 20),
    )(*[pltpu.with_memory_space_constraint(x, pltpu.HBM) for x in (fields, index, weight)])


def scatter_kernel(value_ref, target_ref, mass_ref, v_ref, even_ref, odd_ref, total):
    lanes = value_ref.shape[1]
    tiles = SPAN // lanes
    owners = target_ref.shape[1] // SPAN
    span = TOGETHER * SPAN
    hx, hy, hz = mass_ref.shape
    groups = hx * hy * hz // WIDE
    total[...] = jnp.zeros_like(total)
    ids = row_ids(WIDE, span).astype(F32).astype(BF16)
    group_ids = row_ids(groups, span).astype(F32).astype(BF16)

    def step(p, last):
        at = pl.multiple_of(p * span, span)
        target = target_ref[:, pl.ds(at, span)]
        low = ((target >> log2(groups * hz)) << log2(hz)) + (target & (hz - 1))
        onehot = low_onehot(jnp.where(target < 0, -1, low), ids)
        group = ((target >> log2(hz)) & (groups - 1)).astype(F32).astype(BF16)
        here = group_ids == group
        row = p * (TOGETHER * FIELDS * tiles)
        plain = TOGETHER - 2 if last else TOGETHER
        pieces = [i * FIELDS * tiles + t for i in range(plain) for t in range(tiles)]
        pieces = [value_ref[pl.ds(row + i, FIELDS, stride=tiles), :] for i in pieces]
        if last:
            at_end = pl.multiple_of(row + plain * FIELDS * tiles, 8)
            block = value_ref[pl.ds(at_end, 2 * FIELDS * tiles), :]
            for first in [i * FIELDS * tiles + t for i in range(2) for t in range(tiles)]:
                lines = [first + f * tiles for f in range(FIELDS)]
                pieces.append(jnp.concatenate([block[r : r + 1] for r in lines], axis=0))
        value = jnp.concatenate(pieces, axis=1)
        parts = []
        for half in halves(value):
            for f in range(FIELDS):
                parts.append(jnp.where(here, half[f : f + 1], jnp.zeros((), BF16)))
        spread = jnp.concatenate(parts, axis=0)
        return lax.dot_general(spread, onehot, NT, preferred_element_type=F32)

    @pl.loop(0, owners // TOGETHER // 4)
    def _(n):
        total[...] += functools.reduce(lambda sums, i: sums + step(n * 4 + i, i == 3), range(1, 4), step(n * 4, False))

    even_ref[FIELDS * hx] = jnp.zeros((ITERS, hz), F32)
    scale = lax.rsqrt(mass_ref[...])
    half_x = hx // 2
    odd = lax.axis_index("tgt") % 2 == 1
    for f in range(FIELDS):
        s = total[f * groups : (f + 1) * groups] + total[(FIELDS + f) * groups : (FIELDS + f + 1) * groups]
        for b in range(2):
            for x in range(half_x):
                at = b * half_x + x
                v = s[x * hy : (x + 1) * hy, b * hz : (b + 1) * hz] * scale[at]
                v_ref[f, at] = v
                first, last = v[:ITERS], v[hy - ITERS :]
                even_ref[f * hx + at] = jnp.where(odd, first, last)
                odd_ref[f * hx + at] = jnp.where(odd, last, first)


def scatter_call(values, target, mass):
    hx, hy, hz = mass.shape
    groups = hx * hy * hz // WIDE
    even = jax.ShapeDtypeStruct((FIELDS * hx + 1, ITERS, hz), F32)
    odd = jax.ShapeDtypeStruct((FIELDS * hx, ITERS, hz), F32)
    return pl.pallas_call(
        scatter_kernel,
        out_shape=(jax.ShapeDtypeStruct((FIELDS, hx, hy, hz), F32), even, odd),
        in_specs=[pl.BlockSpec(memory_space=pltpu.VMEM)] * 3,
        out_specs=(pl.BlockSpec(memory_space=pltpu.VMEM),) * 3,
        scratch_shapes=[pltpu.VMEM((2 * FIELDS * groups, WIDE), F32)],
        compiler_params=pltpu.CompilerParams(vmem_limit_bytes=40 << 20),
    )(values, target, mass)


def lookup_rows(table, index, ids, group_ids, groups, at_parts):
    group, low = at_parts(index)
    got = jnp.dot(table, low_onehot(low, ids), preferred_element_type=F32)
    here = group_ids == group
    rows = 3 * groups
    out = []
    for m in range(3):
        part = got[m * groups : (m + 1) * groups] + got[rows + m * groups : rows + (m + 1) * groups]
        out.append(jnp.sum(jnp.where(here, part, 0.0), axis=0, keepdims=True))
    return out


def pick_rows(tables, row, lane):
    row = jnp.broadcast_to(row, (8, 128))
    lane = jnp.broadcast_to(lane, (8, 128))
    tile = row >> 3
    here = row_ids(8, 128) == (row & 7)
    out = []
    for table in tables:
        got = jnp.zeros((8, 128), F32)
        for v in range(table.shape[0] // 8):
            piece = jnp.take_along_axis(table[v * 8 : (v + 1) * 8], lane, axis=1, mode="promise_in_bounds")
            got = jnp.where(tile == v, piece, got)
        out.append(jnp.sum(jnp.where(here, got, 0.0), axis=0, keepdims=True))
    return out


def either_way(i, index, table, ids, group_ids, groups, at_parts, tables, row_and_lane):
    halves_of = [slice(c * 128, (c + 1) * 128) for c in range(2)]
    if i % 8 in (2, 5, 7):
        got = [pick_rows(tables, *row_and_lane(index[:, c])) for c in halves_of]
        return [got[c][m] for m in range(3) for c in range(2)]
    got = lookup_rows(table, index, ids, group_ids, groups, at_parts)
    return [line[:, c] for line in got for c in halves_of]


def cell_moduli(vals):
    phi = vals[0]
    mean = (vals[1] + vals[2] + vals[3]) / 3.0
    q2 = 1.5 * (
        (vals[1] - mean) ** 2
        + (vals[2] - mean) ** 2
        + (vals[3] - mean) ** 2
        + 2.0 * (vals[4] ** 2 + vals[5] ** 2 + vals[6] ** 2)
    )
    bulk = 1.6 * jnp.exp(-3.0 * phi) * (1.0 + 0.25 * jnp.tanh(mean))
    shear = 0.9 * jnp.exp(-2.0 * phi) / (1.0 + q2 / 0.5)
    soften = shear * q2 / (0.5 + q2)
    return [bulk, shear, soften]


def corners(sides):
    line = row_ids(2 * ITERS, sides[0].shape[1])
    near = pltpu.roll(sides[1], 2, 0)
    far = jnp.where(line == 4, pltpu.roll(sides[2], 4, 0), pltpu.roll(sides[2], 6, 0))
    return sides[0], jnp.where(line < 4, near, far)


def sides_kernel(even_ref, odd_ref, sides_ref, to_even_ref, to_odd_ref):
    hx = sides_ref.shape[1]
    b_odd = lax.axis_index("tgt") % 2 == 1
    a_odd = lax.axis_index("src") % 2 == 1
    for f in range(FIELDS):
        sides = []
        for x in range(hx):
            even_side, odd_side = even_ref[f * hx + x], odd_ref[f * hx + x]
            right = jnp.where(b_odd, odd_side, even_side)
            left = jnp.where(b_odd, even_side, odd_side)
            sides.append(jnp.concatenate([right, left], axis=0))
            sides_ref[f, x] = sides[x]
        to_left, to_right = corners(sides), corners(sides[::-1])
        to_even_ref[f, :8] = jnp.where(a_odd, to_left[0], to_right[0])
        to_even_ref[f, 8:14] = jnp.where(a_odd, to_left[1], to_right[1])[:6]
        to_odd_ref[f, :8] = jnp.where(a_odd, to_right[0], to_left[0])
        to_odd_ref[f, 8:] = jnp.where(a_odd, to_right[1], to_left[1])


def sides_call(even, odd, hx):
    hz = even.shape[2]
    return pl.pallas_call(
        sides_kernel,
        out_shape=(
            jax.ShapeDtypeStruct((FIELDS, hx, 2 * ITERS, hz), F32),
            jax.ShapeDtypeStruct((FIELDS, 4 * ITERS - 2, hz), F32),
            jax.ShapeDtypeStruct((FIELDS, 4 * ITERS, hz), F32),
        ),
        in_specs=[pl.BlockSpec(memory_space=pltpu.VMEM)] * 2,
        out_specs=(pl.BlockSpec(memory_space=pltpu.VMEM),) * 3,
        compiler_params=pltpu.CompilerParams(vmem_limit_bytes=4 << 20),
        cost_estimate=pl.CostEstimate(flops=40 * 10**9, bytes_accessed=40 * 10**6, transcendentals=0),
    )(even, odd)


def solve_kernel(
    mesh_shape, v_ref, sides_ref, even_ref, odd_ref, even_corners_ref, odd_corners_ref, mass_ref, order_ref,
    projected_hbm, out_ref, projected_ref, sem,
):
    n_src, n_tgt = mesh_shape
    hx, hy, hz = mass_ref.shape
    k = ITERS
    rows = hy + 2 * k
    a, b = lax.axis_index("src"), lax.axis_index("tgt")

    def exists(flag):
        return jnp.where(flag, 1.0, 0.0).astype(F32)

    row = row_ids(rows, hz)
    lane = lax.broadcasted_iota(jnp.int32, (rows, hz), 1)
    inside = jnp.where(row < hy, 1.0, jnp.where(row < hy + k, exists(b < n_tgt - 1), exists(b > 0)))
    inside_left = inside * exists(a > 0)
    inside_right = inside * exists(a < n_src - 1)
    not_first = jnp.where(lane == 0, 0.0, 1.0)
    not_last = jnp.where(lane == hz - 1, 0.0, 1.0)
    scale = lax.rsqrt(mass_ref[...])

    line = row_ids(2 * k, hz)

    def slabs(own, first, packed, from_left):
        second = pltpu.roll(packed, 6, 0)
        third = jnp.where(line < 4, pltpu.roll(packed, 4, 0), pltpu.roll(packed, 2, 0))
        sides = [first, second, third] + [jnp.zeros((2 * k, hz), F32)] * (hx - 3)
        if from_left:
            sides = sides[::-1]
        return [jnp.concatenate([own[x], side], axis=0) for x, side in enumerate(sides)]

    a_odd = a % 2 == 1

    for f in range(FIELDS):
        packed = jnp.concatenate([even_corners_ref[f, 2 * k :], jnp.zeros((2, hz), F32)], axis=0)
        even = (even_ref[f], even_corners_ref[f, : 2 * k], packed)
        odd = (odd_ref[f], odd_corners_ref[f, : 2 * k], odd_corners_ref[f, 2 * k :])
        left = slabs(*[jnp.where(a_odd, p, q) for p, q in zip(even, odd)], True)
        right = slabs(*[jnp.where(a_odd, q, p) for p, q in zip(even, odd)], False)
        own = [jnp.concatenate([v_ref[f, x], sides_ref[f, x]], axis=0) for x in range(hx)]
        base = left + own + right
        u = [COEFS[k] * e for e in base]
        for sweep in range(1, k + 1):
            new = list(u)
            for x in range(sweep, hx + 2 * k - sweep):
                far = max(k - x, x - (k + hx - 1), 0)
                n = rows if sweep + far < k else hy
                w = u[x]
                near = u[x - 1][:n] + u[x + 1][:n]
                near = near + pltpu.roll(w, 1, 0)[:n] + pltpu.roll(w, rows - 1, 0)[:n]
                w = w[:n]
                near = near + pltpu.roll(w, 1, 1) * not_first[:n] + pltpu.roll(w, hz - 1, 1) * not_last[:n]
                if x < k:
                    near = near * inside_left[:n]
                elif x >= k + hx:
                    near = near * inside_right[:n]
                elif n > hy:
                    near = near * inside
                new[x] = COEFS[k - sweep] * base[x][:n] + near
            u = new
        for x in range(hx):
            projected_ref[f, x] = u[k + x][:hy] * scale[x]

    leave = pltpu.make_async_copy(projected_ref, projected_hbm, sem)
    leave.start()
    groups = hx * hy * hz // WIDE
    payload = cell_moduli([projected_ref[f].reshape(hx * hy, hz) for f in range(FIELDS)])
    table = jnp.concatenate([jnp.concatenate([m[:groups], m[groups:]], axis=1) for m in payload], axis=0)
    table = jnp.concatenate(halves(table), axis=0)
    ids = row_ids(WIDE, WIDE).astype(F32).astype(BF16)
    group_ids = row_ids(groups, WIDE)

    def at_parts(index):
        return (index >> log2(hz)) & (groups - 1), ((index >> log2(groups * hz)) << log2(hz)) + (index & (hz - 1))

    for q in range(0, groups, 4):
        lines = []
        for i in range(q, q + 4):
            index = order_ref[:, i * WIDE : (i + 1) * WIDE]
            got = lookup_rows(table, index, ids, group_ids, groups, at_parts)
            lines += [line[:, c * 128 : (c + 1) * 128] for line in got for c in range(2)]
        out_ref[q * 6 : q * 6 + 24, :] = jnp.concatenate(lines, axis=0)
    leave.wait()


def solve_call(mesh_shape, *args):
    mass, order = args[-2:]
    hx, hy, hz = mass.shape

    def kernel(*refs):
        solve_kernel(mesh_shape, *refs)

    return pl.pallas_call(
        kernel,
        out_shape=(
            jax.ShapeDtypeStruct((FIELDS, hx, hy, hz), F32),
            jax.ShapeDtypeStruct((order.shape[1] // WIDE * 6, 128), F32),
        ),
        in_specs=[pl.BlockSpec(memory_space=pltpu.VMEM)] * 8,
        out_specs=(pl.BlockSpec(memory_space=pltpu.HBM), pl.BlockSpec(memory_space=pltpu.VMEM)),
        scratch_shapes=[pltpu.VMEM((FIELDS, hx, hy, hz), F32), pltpu.SemaphoreType.DMA],
        compiler_params=pltpu.CompilerParams(vmem_limit_bytes=40 << 20),
    )(*args)


def place_kernel(arrived_ref, order_ref, out_hbm, out_ref, sems):
    groups = arrived_ref.shape[0] // 6
    parts = [[arrived_ref[pl.ds(2 * m + c, groups, stride=6), :] for c in range(2)] for m in range(3)]
    table = jnp.concatenate([jnp.concatenate(part, axis=1) for part in parts], axis=0)
    table = jnp.concatenate(halves(table), axis=0)
    tables = [jnp.concatenate(part, axis=0) for part in parts]
    ids = row_ids(WIDE, WIDE).astype(F32).astype(BF16)
    group_ids = row_ids(groups, WIDE)

    def at_parts(index):
        return index >> log2(WIDE), index & (WIDE - 1)

    def row_and_lane(index):
        return ((index >> 7) & 1) * groups + (index >> log2(WIDE)), index & 127

    copies = []
    for n in range(PIECES):
        for q in range(n * groups // PIECES, (n + 1) * groups // PIECES):
            index = order_ref[:, q * WIDE : (q + 1) * WIDE]
            lines = either_way(q, index, table, ids, group_ids, groups, at_parts, tables, row_and_lane)
            for c in range(2):
                out_ref[:, q * WIDE + c * 128 : q * WIDE + (c + 1) * 128] = jnp.concatenate(lines[c::2], axis=0)
        piece = pl.ds(n * groups // PIECES * WIDE, groups // PIECES * WIDE)
        copies.append(pltpu.make_async_copy(out_ref.at[:, piece], out_hbm.at[:, piece], sems.at[n]))
        copies[n].start()
    for copy in copies:
        copy.wait()


def place_call(arrived, order):
    return pl.pallas_call(
        place_kernel,
        out_shape=jax.ShapeDtypeStruct((3, order.shape[1]), F32),
        in_specs=[pl.BlockSpec(memory_space=pltpu.VMEM)] * 2,
        out_specs=pl.BlockSpec(memory_space=pltpu.HBM),
        scratch_shapes=[pltpu.VMEM((3, order.shape[1]), F32), pltpu.SemaphoreType.DMA((PIECES,))],
        compiler_params=pltpu.CompilerParams(vmem_limit_bytes=40 << 20),
    )(arrived, order)


def swap(x, axis, start):
    pairs = [(i, i + 1) for i in range(start, lax.axis_size(axis) - 1, 2)]
    return lax.ppermute(x, axis, pairs + [(j, i) for i, j in pairs])


def on_device(source_fields, slot_source, slot_weight, slot_target, cell_mass, send_order, place_order):
    n_src, n_tgt = lax.axis_size("src"), lax.axis_size("tgt")
    both = ("src", "tgt")
    owners = n_src * n_tgt
    cells = cell_mass.size
    quota = cells // owners

    values = gather_call(source_fields, slot_source.reshape(1, -1), slot_weight.reshape(1, -1))
    values = values.reshape(owners, FIELDS, SPAN // 128, 128)
    values = lax.all_to_all(values, both, split_axis=0, concat_axis=0, tiled=True).reshape(-1, 128)
    v, even, odd = scatter_call(values, slot_target.reshape(1, -1), cell_mass)
    even_block, odd_block = swap(v, "src", 0), swap(v, "src", 1)
    even, odd = swap(even, "tgt", 0), swap(odd, "tgt", 1)
    sides, even, odd = sides_call(even, odd, cell_mass.shape[0])
    even, odd = swap(even, "src", 0), swap(odd, "src", 1)
    projected, outgoing = solve_call(
        (n_src, n_tgt), v, sides, even_block, odd_block, even, odd, cell_mass, send_order
    )

    if quota == WIDE:
        outgoing = outgoing.reshape(owners, 3, 2, 128)
        incoming = lax.all_to_all(outgoing, both, split_axis=0, concat_axis=0, tiled=True)
    else:
        groups = cells // WIDE
        flat = outgoing.reshape(groups, 3, WIDE).transpose(1, 0, 2).reshape(3, owners, quota)
        flat = lax.all_to_all(flat, both, split_axis=1, concat_axis=1, tiled=True)
        incoming = flat.reshape(3, groups, WIDE).transpose(1, 0, 2)
    incoming = incoming.reshape(-1, 128)
    return projected, place_call(incoming, place_order)


def solution(mesh):
    split = P(("src", "tgt"))
    rows = P(("src", "tgt"), None)
    return jax.shard_map(
        on_device,
        mesh=mesh,
        in_specs=(P(None, ("src", "tgt")), split, split, split, P("src", "tgt", None), rows, rows),
        out_specs=(P(None, "src", "tgt", None), P(None, ("src", "tgt"))),
        check_vma=False,
    )
```

```python
import functools

import numpy as np

import jax
import jax.numpy as jnp
from jax import lax
from jax.experimental import pallas as pl
from jax.experimental.pallas import tpu as pltpu
from jax.sharding import PartitionSpec as P

ITERS = 4
FIELDS = 7
PIECES = 4
SPAN = 512
AT_ONCE = 32
TOGETHER = 8
WIDE = 256
BF16 = jnp.bfloat16
F32 = jnp.float32
NT = (((1,), (1,)), ((), ()))


def sweep_polynomial(iters, theta, delta):
    sigma = theta / delta
    rho = 1.0 / sigma
    mass = np.array([1.0, 0.125])
    poly = np.polynomial.polynomial
    resid = np.array([1.0])
    step = resid / theta
    total = np.array([0.0])
    for _ in range(iters):
        total = poly.polyadd(total, step)
        resid = poly.polysub(resid, poly.polymul(mass, step))
        rho_new = 1.0 / (2.0 * sigma - rho)
        step = poly.polyadd(rho_new * rho * step, 2.0 * rho_new / delta * resid)
        rho = rho_new
    return [float(c) for c in poly.polyadd(total, step)]


COEFS = sweep_polynomial(ITERS, 1.0, 0.75)


def halves(x):
    high = x.astype(BF16)
    return high, (x - high.astype(F32)).astype(BF16)


def log2(n):
    assert n & (n - 1) == 0
    return n.bit_length() - 1


def row_ids(rows, lanes):
    return lax.broadcasted_iota(jnp.int32, (rows, lanes), 0)


def low_onehot(low, ids):
    return jnp.where(ids == low.astype(F32).astype(BF16), jnp.ones((), BF16), jnp.zeros((), BF16))


def gather_kernel(fields_hbm, index_hbm, weight_hbm, out_ref, table, padded, fields_ref, index_ref, weight_ref, sems):
    pairs = ((fields_hbm, fields_ref), (index_hbm, index_ref), (weight_hbm, weight_ref))
    copies = [pltpu.make_async_copy(src, dst, sems.at[i]) for i, (src, dst) in enumerate(pairs)]
    for copy in copies:
        copy.start()
    lanes = out_ref.shape[1]
    span = SPAN
    tiles = span // lanes
    owners = index_ref.shape[1] // span
    groups = fields_ref.shape[1] // WIDE
    table[...] = jnp.zeros_like(table)
    padded[...] = jnp.zeros_like(padded)
    for copy in copies:
        copy.wait()
    for g in range(groups):
        table[g * 8 : g * 8 + FIELDS, :] = fields_ref[:, g * WIDE : (g + 1) * WIDE]
    both = jnp.concatenate(halves(table[...]), axis=0)
    rows = groups * 8
    ids = row_ids(WIDE, WIDE).astype(F32).astype(BF16)
    padded[:FIELDS, :] = fields_ref[...]

    def by_matmul(index):
        got = jnp.dot(both, low_onehot(index & (WIDE - 1), ids), preferred_element_type=F32)
        group = jnp.broadcast_to(index >> log2(WIDE), (8, WIDE))
        value = jnp.zeros((8, WIDE), F32)
        for g in range(groups):
            part = got[g * 8 : (g + 1) * 8] + got[rows + g * 8 : rows + (g + 1) * 8]
            value = jnp.where(group == g, part, value)
        return value

    def by_lanes(index):
        lane = jnp.broadcast_to(index & 127, (8, 128))
        tile = jnp.broadcast_to(index >> 7, (8, 128))
        value = jnp.zeros((8, 128), F32)
        for g in range(padded.shape[1] // 128):
            piece = padded[:, g * 128 : (g + 1) * 128]
            piece = jnp.take_along_axis(piece, lane, axis=1, mode="promise_in_bounds")
            value = jnp.where(tile == g, piece, value)
        return value

    def one_owner(q, matmuls):
        at = pl.multiple_of(q * SPAN, SPAN)
        index = index_ref[:, pl.ds(at, SPAN)]
        weight = weight_ref[:, pl.ds(at, SPAN)]
        values = [by_matmul(index[:, i * WIDE : (i + 1) * WIDE]) for i in range(matmuls)]
        for t in range(matmuls * WIDE // 128, tiles):
            values.append(by_lanes(index[:, t * 128 : (t + 1) * 128]))
        value = jnp.concatenate(values, axis=1) * weight
        return [value[:FIELDS, t * lanes : (t + 1) * lanes] for t in range(tiles)]

    @pl.loop(0, owners // AT_ONCE)
    def _(m):
        lines = []
        for i in range(AT_ONCE):
            q = m * AT_ONCE + i
            value = one_owner(q, SPAN // WIDE - (i % 4 > 0))
            if i < AT_ONCE - 2:
                for t in range(tiles):
                    out_ref[pl.ds(q * (FIELDS * tiles) + t, FIELDS, stride=tiles), :] = value[t]
            else:
                lines += [value[t][f : f + 1] for f in range(FIELDS) for t in range(tiles)]
        at = pl.multiple_of((m * AT_ONCE + AT_ONCE - 2) * (FIELDS * tiles), 8)
        out_ref[pl.ds(at, len(lines)), :] = jnp.concatenate(lines, axis=0)


def gather_call(fields, index, weight):
    rows = FIELDS * index.shape[1] // 128
    return pl.pallas_call(
        gather_kernel,
        out_shape=jax.ShapeDtypeStruct((rows, 128), F32),
        in_specs=[pl.BlockSpec(memory_space=pltpu.HBM)] * 3,
        out_specs=pl.BlockSpec(memory_space=pltpu.VMEM),
        scratch_shapes=[
            pltpu.VMEM((fields.shape[1] // WIDE * 8, WIDE), F32),
            pltpu.VMEM((8, fields.shape[1]), F32),
            pltpu.VMEM(fields.shape, F32),
            pltpu.VMEM(index.shape, jnp.int32),
            pltpu.VMEM(weight.shape, F32),
            pltpu.SemaphoreType.DMA((3,)),
        ],
        compiler_params=pltpu.CompilerParams(vmem_limit_bytes=40 << 20),
    )(*[pltpu.with_memory_space_constraint(x, pltpu.HBM) for x in (fields, index, weight)])


def scatter_kernel(value_ref, target_ref, mass_ref, v_ref, even_ref, odd_ref, total):
    lanes = value_ref.shape[1]
    tiles = SPAN // lanes
    owners = target_ref.shape[1] // SPAN
    span = TOGETHER * SPAN
    hx, hy, hz = mass_ref.shape
    groups = hx * hy * hz // WIDE
    total[...] = jnp.zeros_like(total)
    ids = row_ids(WIDE, span).astype(F32).astype(BF16)
    group_ids = row_ids(groups, span).astype(F32).astype(BF16)

    def step(p, last):
        at = pl.multiple_of(p * span, span)
        target = target_ref[:, pl.ds(at, span)]
        low = ((target >> log2(groups * hz)) << log2(hz)) + (target & (hz - 1))
        onehot = low_onehot(jnp.where(target < 0, -1, low), ids)
        group = ((target >> log2(hz)) & (groups - 1)).astype(F32).astype(BF16)
        here = group_ids == group
        row = p * (TOGETHER * FIELDS * tiles)
        plain = TOGETHER - 2 if last else TOGETHER
        pieces = [i * FIELDS * tiles + t for i in range(plain) for t in range(tiles)]
        pieces = [value_ref[pl.ds(row + i, FIELDS, stride=tiles), :] for i in pieces]
        if last:
            at_end = pl.multiple_of(row + plain * FIELDS * tiles, 8)
            block = value_ref[pl.ds(at_end, 2 * FIELDS * tiles), :]
            for first in [i * FIELDS * tiles + t for i in range(2) for t in range(tiles)]:
                lines = [first + f * tiles for f in range(FIELDS)]
                pieces.append(jnp.concatenate([block[r : r + 1] for r in lines], axis=0))
        value = jnp.concatenate(pieces, axis=1)
        parts = []
        for half in halves(value):
            for f in range(FIELDS):
                parts.append(jnp.where(here, half[f : f + 1], jnp.zeros((), BF16)))
        spread = jnp.concatenate(parts, axis=0)
        return lax.dot_general(spread, onehot, NT, preferred_element_type=F32)

    @pl.loop(0, owners // TOGETHER // 4)
    def _(n):
        total[...] += functools.reduce(lambda sums, i: sums + step(n * 4 + i, i == 3), range(1, 4), step(n * 4, False))

    even_ref[FIELDS * hx] = jnp.zeros((ITERS, hz), F32)
    scale = lax.rsqrt(mass_ref[...])
    half_x = hx // 2
    odd = lax.axis_index("tgt") % 2 == 1
    for f in range(FIELDS):
        s = total[f * groups : (f + 1) * groups] + total[(FIELDS + f) * groups : (FIELDS + f + 1) * groups]
        for b in range(2):
            for x in range(half_x):
                at = b * half_x + x
                v = s[x * hy : (x + 1) * hy, b * hz : (b + 1) * hz] * scale[at]
                v_ref[f, at] = v
                first, last = v[:ITERS], v[hy - ITERS :]
                even_ref[f * hx + at] = jnp.where(odd, first, last)
                odd_ref[f * hx + at] = jnp.where(odd, last, first)


def scatter_call(values, target, mass):
    hx, hy, hz = mass.shape
    groups = hx * hy * hz // WIDE
    even = jax.ShapeDtypeStruct((FIELDS * hx + 1, ITERS, hz), F32)
    odd = jax.ShapeDtypeStruct((FIELDS * hx, ITERS, hz), F32)
    return pl.pallas_call(
        scatter_kernel,
        out_shape=(jax.ShapeDtypeStruct((FIELDS, hx, hy, hz), F32), even, odd),
        in_specs=[pl.BlockSpec(memory_space=pltpu.VMEM)] * 3,
        out_specs=(pl.BlockSpec(memory_space=pltpu.VMEM),) * 3,
        scratch_shapes=[pltpu.VMEM((2 * FIELDS * groups, WIDE), F32)],
        compiler_params=pltpu.CompilerParams(vmem_limit_bytes=40 << 20),
    )(values, target, mass)


def lookup_rows(table, index, ids, group_ids, groups, at_parts):
    group, low = at_parts(index)
    got = jnp.dot(table, low_onehot(low, ids), preferred_element_type=F32)
    here = group_ids == group
    rows = 3 * groups
    out = []
    for m in range(3):
        part = got[m * groups : (m + 1) * groups] + got[rows + m * groups : rows + (m + 1) * groups]
        out.append(jnp.sum(jnp.where(here, part, 0.0), axis=0, keepdims=True))
    return out


def pick_rows(tables, row, lane):
    row = jnp.broadcast_to(row, (8, 128))
    lane = jnp.broadcast_to(lane, (8, 128))
    tile = row >> 3
    here = row_ids(8, 128) == (row & 7)
    out = []
    for table in tables:
        got = jnp.zeros((8, 128), F32)
        for v in range(table.shape[0] // 8):
            piece = jnp.take_along_axis(table[v * 8 : (v + 1) * 8], lane, axis=1, mode="promise_in_bounds")
            got = jnp.where(tile == v, piece, got)
        out.append(jnp.sum(jnp.where(here, got, 0.0), axis=0, keepdims=True))
    return out


def either_way(i, index, table, ids, group_ids, groups, at_parts, tables, row_and_lane):
    halves_of = [slice(c * 128, (c + 1) * 128) for c in range(2)]
    if i % 8 in (2, 5, 7):
        got = [pick_rows(tables, *row_and_lane(index[:, c])) for c in halves_of]
        return [got[c][m] for m in range(3) for c in range(2)]
    got = lookup_rows(table, index, ids, group_ids, groups, at_parts)
    return [line[:, c] for line in got for c in halves_of]


def cell_moduli(vals):
    phi = vals[0]
    mean = (vals[1] + vals[2] + vals[3]) / 3.0
    q2 = 1.5 * (
        (vals[1] - mean) ** 2
        + (vals[2] - mean) ** 2
        + (vals[3] - mean) ** 2
        + 2.0 * (vals[4] ** 2 + vals[5] ** 2 + vals[6] ** 2)
    )
    bulk = 1.6 * jnp.exp(-3.0 * phi) * (1.0 + 0.25 * jnp.tanh(mean))
    shear = 0.9 * jnp.exp(-2.0 * phi) / (1.0 + q2 / 0.5)
    soften = shear * q2 / (0.5 + q2)
    return [bulk, shear, soften]


def corners(sides):
    line = row_ids(2 * ITERS, sides[0].shape[1])
    near = pltpu.roll(sides[1], 2, 0)
    far = jnp.where(line == 4, pltpu.roll(sides[2], 4, 0), pltpu.roll(sides[2], 6, 0))
    return sides[0], jnp.where(line < 4, near, far)


def sides_kernel(even_ref, odd_ref, sides_ref, to_even_ref, to_odd_ref):
    hx = sides_ref.shape[1]
    b_odd = lax.axis_index("tgt") % 2 == 1
    a_odd = lax.axis_index("src") % 2 == 1
    for f in range(FIELDS):
        sides = []
        for x in range(hx):
            even_side, odd_side = even_ref[f * hx + x], odd_ref[f * hx + x]
            right = jnp.where(b_odd, odd_side, even_side)
            left = jnp.where(b_odd, even_side, odd_side)
            sides.append(jnp.concatenate([right, left], axis=0))
            sides_ref[f, x] = sides[x]
        to_left, to_right = corners(sides), corners(sides[::-1])
        to_even_ref[f, :8] = jnp.where(a_odd, to_left[0], to_right[0])
        to_even_ref[f, 8:14] = jnp.where(a_odd, to_left[1], to_right[1])[:6]
        to_odd_ref[f, :8] = jnp.where(a_odd, to_right[0], to_left[0])
        to_odd_ref[f, 8:] = jnp.where(a_odd, to_right[1], to_left[1])


def sides_call(even, odd, hx):
    hz = even.shape[2]
    return pl.pallas_call(
        sides_kernel,
        out_shape=(
            jax.ShapeDtypeStruct((FIELDS, hx, 2 * ITERS, hz), F32),
            jax.ShapeDtypeStruct((FIELDS, 4 * ITERS - 2, hz), F32),
            jax.ShapeDtypeStruct((FIELDS, 4 * ITERS, hz), F32),
        ),
        in_specs=[pl.BlockSpec(memory_space=pltpu.VMEM)] * 2,
        out_specs=(pl.BlockSpec(memory_space=pltpu.VMEM),) * 3,
        compiler_params=pltpu.CompilerParams(vmem_limit_bytes=4 << 20),
        cost_estimate=pl.CostEstimate(flops=40 * 10**9, bytes_accessed=40 * 10**6, transcendentals=0),
    )(even, odd)


def solve_kernel(
    mesh_shape, v_ref, sides_ref, even_ref, odd_ref, even_corners_ref, odd_corners_ref, mass_ref, order_ref,
    projected_hbm, out_ref, projected_ref, sem,
):
    n_src, n_tgt = mesh_shape
    hx, hy, hz = mass_ref.shape
    k = ITERS
    rows = hy + 2 * k
    a, b = lax.axis_index("src"), lax.axis_index("tgt")

    def exists(flag):
        return jnp.where(flag, 1.0, 0.0).astype(F32)

    row = row_ids(rows, hz)
    inside = jnp.where(row < hy, 1.0, jnp.where(row < hy + k, exists(b < n_tgt - 1), exists(b > 0)))
    inside_left = inside * exists(a > 0)
    inside_right = inside * exists(a < n_src - 1)
    gap = row_ids(hz, hz) - lax.broadcasted_iota(jnp.int32, (hz, hz), 1)
    beside = jnp.where(jnp.abs(gap) == 1, 1.0, 0.0).astype(BF16)
    beside = jnp.concatenate([beside, beside], axis=0)

    def rows_of(sweep, x):
        return rows if sweep + max(k - x, x - (k + hx - 1), 0) < k else hy

    def deep_sums(parts):
        both = jnp.concatenate(halves(jnp.concatenate(parts, axis=0)), axis=1)
        sums = jnp.dot(both, beside, preferred_element_type=F32)
        starts = np.cumsum([0] + [part.shape[0] for part in parts])
        return [sums[at : at + part.shape[0]] for at, part in zip(starts, parts)]

    scale = lax.rsqrt(mass_ref[...])

    line = row_ids(2 * k, hz)

    def slabs(own, first, packed, from_left):
        second = pltpu.roll(packed, 6, 0)
        third = jnp.where(line < 4, pltpu.roll(packed, 4, 0), pltpu.roll(packed, 2, 0))
        sides = [first, second, third] + [jnp.zeros((2 * k, hz), F32)] * (hx - 3)
        if from_left:
            sides = sides[::-1]
        return [jnp.concatenate([own[x], side], axis=0) for x, side in enumerate(sides)]

    a_odd = a % 2 == 1

    for f in range(FIELDS):
        packed = jnp.concatenate([even_corners_ref[f, 2 * k :], jnp.zeros((2, hz), F32)], axis=0)
        even = (even_ref[f], even_corners_ref[f, : 2 * k], packed)
        odd = (odd_ref[f], odd_corners_ref[f, : 2 * k], odd_corners_ref[f, 2 * k :])
        left = slabs(*[jnp.where(a_odd, p, q) for p, q in zip(even, odd)], True)
        right = slabs(*[jnp.where(a_odd, q, p) for p, q in zip(even, odd)], False)
        own = [jnp.concatenate([v_ref[f, x], sides_ref[f, x]], axis=0) for x in range(hx)]
        base = left + own + right
        u = [COEFS[k] * e for e in base]
        for sweep in range(1, k + 1):
            new = list(u)
            xs = range(sweep, hx + 2 * k - sweep)
            deep = deep_sums([u[x][: rows_of(sweep, x)] for x in xs])
            for x in xs:
                n = rows_of(sweep, x)
                w = u[x]
                near = u[x - 1][:n] + u[x + 1][:n]
                near = near + pltpu.roll(w, 1, 0)[:n] + pltpu.roll(w, rows - 1, 0)[:n]
                near = near + deep[x - sweep]
                if x < k:
                    near = near * inside_left[:n]
                elif x >= k + hx:
                    near = near * inside_right[:n]
                elif n > hy:
                    near = near * inside
                new[x] = COEFS[k - sweep] * base[x][:n] + near
            u = new
        for x in range(hx):
            projected_ref[f, x] = u[k + x][:hy] * scale[x]

    leave = pltpu.make_async_copy(projected_ref, projected_hbm, sem)
    leave.start()
    groups = hx * hy * hz // WIDE
    payload = cell_moduli([projected_ref[f].reshape(hx * hy, hz) for f in range(FIELDS)])
    table = jnp.concatenate([jnp.concatenate([m[:groups], m[groups:]], axis=1) for m in payload], axis=0)
    table = jnp.concatenate(halves(table), axis=0)
    ids = row_ids(WIDE, WIDE).astype(F32).astype(BF16)
    group_ids = row_ids(groups, WIDE)

    def at_parts(index):
        return (index >> log2(hz)) & (groups - 1), ((index >> log2(groups * hz)) << log2(hz)) + (index & (hz - 1))

    for q in range(0, groups, 4):
        lines = []
        for i in range(q, q + 4):
            index = order_ref[:, i * WIDE : (i + 1) * WIDE]
            got = lookup_rows(table, index, ids, group_ids, groups, at_parts)
            lines += [line[:, c * 128 : (c + 1) * 128] for line in got for c in range(2)]
        out_ref[q * 6 : q * 6 + 24, :] = jnp.concatenate(lines, axis=0)
    leave.wait()


def solve_call(mesh_shape, *args):
    mass, order = args[-2:]
    hx, hy, hz = mass.shape

    def kernel(*refs):
        solve_kernel(mesh_shape, *refs)

    return pl.pallas_call(
        kernel,
        out_shape=(
            jax.ShapeDtypeStruct((FIELDS, hx, hy, hz), F32),
            jax.ShapeDtypeStruct((order.shape[1] // WIDE * 6, 128), F32),
        ),
        in_specs=[pl.BlockSpec(memory_space=pltpu.VMEM)] * 8,
        out_specs=(pl.BlockSpec(memory_space=pltpu.HBM), pl.BlockSpec(memory_space=pltpu.VMEM)),
        scratch_shapes=[pltpu.VMEM((FIELDS, hx, hy, hz), F32), pltpu.SemaphoreType.DMA],
        compiler_params=pltpu.CompilerParams(vmem_limit_bytes=40 << 20),
    )(*args)


def place_kernel(arrived_ref, order_ref, out_hbm, out_ref, sems):
    groups = arrived_ref.shape[0] // 6
    parts = [[arrived_ref[pl.ds(2 * m + c, groups, stride=6), :] for c in range(2)] for m in range(3)]
    table = jnp.concatenate([jnp.concatenate(part, axis=1) for part in parts], axis=0)
    table = jnp.concatenate(halves(table), axis=0)
    tables = [jnp.concatenate(part, axis=0) for part in parts]
    ids = row_ids(WIDE, WIDE).astype(F32).astype(BF16)
    group_ids = row_ids(groups, WIDE)

    def at_parts(index):
        return index >> log2(WIDE), index & (WIDE - 1)

    def row_and_lane(index):
        return ((index >> 7) & 1) * groups + (index >> log2(WIDE)), index & 127

    copies = []
    for n in range(PIECES):
        for q in range(n * groups // PIECES, (n + 1) * groups // PIECES):
            index = order_ref[:, q * WIDE : (q + 1) * WIDE]
            lines = either_way(q, index, table, ids, group_ids, groups, at_parts, tables, row_and_lane)
            for c in range(2):
                out_ref[:, q * WIDE + c * 128 : q * WIDE + (c + 1) * 128] = jnp.concatenate(lines[c::2], axis=0)
        piece = pl.ds(n * groups // PIECES * WIDE, groups // PIECES * WIDE)
        copies.append(pltpu.make_async_copy(out_ref.at[:, piece], out_hbm.at[:, piece], sems.at[n]))
        copies[n].start()
    for copy in copies:
        copy.wait()


def place_call(arrived, order):
    return pl.pallas_call(
        place_kernel,
        out_shape=jax.ShapeDtypeStruct((3, order.shape[1]), F32),
        in_specs=[pl.BlockSpec(memory_space=pltpu.VMEM)] * 2,
        out_specs=pl.BlockSpec(memory_space=pltpu.HBM),
        scratch_shapes=[pltpu.VMEM((3, order.shape[1]), F32), pltpu.SemaphoreType.DMA((PIECES,))],
        compiler_params=pltpu.CompilerParams(vmem_limit_bytes=40 << 20),
    )(arrived, order)


def swap(x, axis, start):
    pairs = [(i, i + 1) for i in range(start, lax.axis_size(axis) - 1, 2)]
    return lax.ppermute(x, axis, pairs + [(j, i) for i, j in pairs])


def on_device(source_fields, slot_source, slot_weight, slot_target, cell_mass, send_order, place_order):
    n_src, n_tgt = lax.axis_size("src"), lax.axis_size("tgt")
    both = ("src", "tgt")
    owners = n_src * n_tgt
    cells = cell_mass.size
    quota = cells // owners

    values = gather_call(source_fields, slot_source.reshape(1, -1), slot_weight.reshape(1, -1))
    values = values.reshape(owners, FIELDS, SPAN // 128, 128)
    values = lax.all_to_all(values, both, split_axis=0, concat_axis=0, tiled=True).reshape(-1, 128)
    v, even, odd = scatter_call(values, slot_target.reshape(1, -1), cell_mass)
    even_block, odd_block = swap(v, "src", 0), swap(v, "src", 1)
    even, odd = swap(even, "tgt", 0), swap(odd, "tgt", 1)
    sides, even, odd = sides_call(even, odd, cell_mass.shape[0])
    even, odd = swap(even, "src", 0), swap(odd, "src", 1)
    projected, outgoing = solve_call(
        (n_src, n_tgt), v, sides, even_block, odd_block, even, odd, cell_mass, send_order
    )

    if quota == WIDE:
        outgoing = outgoing.reshape(owners, 3, 2, 128)
        incoming = lax.all_to_all(outgoing, both, split_axis=0, concat_axis=0, tiled=True)
    else:
        groups = cells // WIDE
        flat = outgoing.reshape(groups, 3, WIDE).transpose(1, 0, 2).reshape(3, owners, quota)
        flat = lax.all_to_all(flat, both, split_axis=1, concat_axis=1, tiled=True)
        incoming = flat.reshape(3, groups, WIDE).transpose(1, 0, 2)
    incoming = incoming.reshape(-1, 128)
    return projected, place_call(incoming, place_order)


def solution(mesh):
    split = P(("src", "tgt"))
    rows = P(("src", "tgt"), None)
    return jax.shard_map(
        on_device,
        mesh=mesh,
        in_specs=(P(None, ("src", "tgt")), split, split, split, P("src", "tgt", None), rows, rows),
        out_specs=(P(None, "src", "tgt", None), P(None, ("src", "tgt"))),
        check_vma=False,
    )
```

```python
import functools

import numpy as np

import jax
import jax.numpy as jnp
from jax import lax
from jax.experimental import pallas as pl
from jax.experimental.pallas import tpu as pltpu
from jax.sharding import PartitionSpec as P

ITERS = 4
FIELDS = 7
PIECES = 4
SPAN = 512
AT_ONCE = 32
TOGETHER = 8
WIDE = 256
BF16 = jnp.bfloat16
F32 = jnp.float32
NT = (((1,), (1,)), ((), ()))


def sweep_polynomial(iters, theta, delta):
    sigma = theta / delta
    rho = 1.0 / sigma
    mass = np.array([1.0, 0.125])
    poly = np.polynomial.polynomial
    resid = np.array([1.0])
    step = resid / theta
    total = np.array([0.0])
    for _ in range(iters):
        total = poly.polyadd(total, step)
        resid = poly.polysub(resid, poly.polymul(mass, step))
        rho_new = 1.0 / (2.0 * sigma - rho)
        step = poly.polyadd(rho_new * rho * step, 2.0 * rho_new / delta * resid)
        rho = rho_new
    return [float(c) for c in poly.polyadd(total, step)]


COEFS = sweep_polynomial(ITERS, 1.0, 0.75)


def halves(x):
    high = x.astype(BF16)
    return high, (x - high.astype(F32)).astype(BF16)


def log2(n):
    assert n & (n - 1) == 0
    return n.bit_length() - 1


def row_ids(rows, lanes):
    return lax.broadcasted_iota(jnp.int32, (rows, lanes), 0)


def low_onehot(low, ids):
    return jnp.where(ids == low.astype(F32).astype(BF16), jnp.ones((), BF16), jnp.zeros((), BF16))


def gather_kernel(fields_hbm, index_hbm, weight_hbm, out_ref, table, padded, fields_ref, index_ref, weight_ref, sems):
    pairs = ((fields_hbm, fields_ref), (index_hbm, index_ref), (weight_hbm, weight_ref))
    copies = [pltpu.make_async_copy(src, dst, sems.at[i]) for i, (src, dst) in enumerate(pairs)]
    for copy in copies:
        copy.start()
    lanes = out_ref.shape[1]
    span = SPAN
    tiles = span // lanes
    owners = index_ref.shape[1] // span
    groups = fields_ref.shape[1] // WIDE
    table[...] = jnp.zeros_like(table)
    padded[...] = jnp.zeros_like(padded)
    for copy in copies:
        copy.wait()
    for g in range(groups):
        table[g * 8 : g * 8 + FIELDS, :] = fields_ref[:, g * WIDE : (g + 1) * WIDE]
    both = jnp.concatenate(halves(table[...]), axis=0)
    rows = groups * 8
    ids = row_ids(WIDE, WIDE).astype(F32).astype(BF16)
    padded[:FIELDS, :] = fields_ref[...]

    def by_matmul(index):
        got = jnp.dot(both, low_onehot(index & (WIDE - 1), ids), preferred_element_type=F32)
        group = jnp.broadcast_to(index >> log2(WIDE), (8, WIDE))
        value = jnp.zeros((8, WIDE), F32)
        for g in range(groups):
            part = got[g * 8 : (g + 1) * 8] + got[rows + g * 8 : rows + (g + 1) * 8]
            value = jnp.where(group == g, part, value)
        return value

    def by_lanes(index):
        lane = jnp.broadcast_to(index & 127, (8, 128))
        tile = jnp.broadcast_to(index >> 7, (8, 128))
        value = jnp.zeros((8, 128), F32)
        for g in range(padded.shape[1] // 128):
            piece = padded[:, g * 128 : (g + 1) * 128]
            piece = jnp.take_along_axis(piece, lane, axis=1, mode="promise_in_bounds")
            value = jnp.where(tile == g, piece, value)
        return value

    def one_owner(q, matmuls):
        at = pl.multiple_of(q * SPAN, SPAN)
        index = index_ref[:, pl.ds(at, SPAN)]
        weight = weight_ref[:, pl.ds(at, SPAN)]
        values = [by_matmul(index[:, i * WIDE : (i + 1) * WIDE]) for i in range(matmuls)]
        for t in range(matmuls * WIDE // 128, tiles):
            values.append(by_lanes(index[:, t * 128 : (t + 1) * 128]))
        value = jnp.concatenate(values, axis=1) * weight
        return [value[:FIELDS, t * lanes : (t + 1) * lanes] for t in range(tiles)]

    @pl.loop(0, owners // AT_ONCE)
    def _(m):
        lines = []
        for i in range(AT_ONCE):
            q = m * AT_ONCE + i
            value = one_owner(q, SPAN // WIDE - (i % 4 > 0))
            if i < AT_ONCE - 2:
                for t in range(tiles):
                    out_ref[pl.ds(q * (FIELDS * tiles) + t, FIELDS, stride=tiles), :] = value[t]
            else:
                lines += [value[t][f : f + 1] for f in range(FIELDS) for t in range(tiles)]
        at = pl.multiple_of((m * AT_ONCE + AT_ONCE - 2) * (FIELDS * tiles), 8)
        out_ref[pl.ds(at, len(lines)), :] = jnp.concatenate(lines, axis=0)


def gather_call(fields, index, weight):
    rows = FIELDS * index.shape[1] // 128
    return pl.pallas_call(
        gather_kernel,
        out_shape=jax.ShapeDtypeStruct((rows, 128), F32),
        in_specs=[pl.BlockSpec(memory_space=pltpu.HBM)] * 3,
        out_specs=pl.BlockSpec(memory_space=pltpu.VMEM),
        scratch_shapes=[
            pltpu.VMEM((fields.shape[1] // WIDE * 8, WIDE), F32),
            pltpu.VMEM((8, fields.shape[1]), F32),
            pltpu.VMEM(fields.shape, F32),
            pltpu.VMEM(index.shape, jnp.int32),
            pltpu.VMEM(weight.shape, F32),
            pltpu.SemaphoreType.DMA((3,)),
        ],
        compiler_params=pltpu.CompilerParams(vmem_limit_bytes=40 << 20),
    )(*[pltpu.with_memory_space_constraint(x, pltpu.HBM) for x in (fields, index, weight)])


def scatter_kernel(value_ref, target_ref, mass_ref, v_ref, even_ref, odd_ref, total):
    lanes = value_ref.shape[1]
    tiles = SPAN // lanes
    owners = target_ref.shape[1] // SPAN
    span = TOGETHER * SPAN
    hx, hy, hz = mass_ref.shape
    groups = hx * hy * hz // WIDE
    total[...] = jnp.zeros_like(total)
    ids = row_ids(WIDE, span).astype(F32).astype(BF16)
    group_ids = row_ids(groups, span).astype(F32).astype(BF16)

    def step(p, last):
        at = pl.multiple_of(p * span, span)
        target = target_ref[:, pl.ds(at, span)]
        low = ((target >> log2(groups * hz)) << log2(hz)) + (target & (hz - 1))
        onehot = low_onehot(jnp.where(target < 0, -1, low), ids)
        group = ((target >> log2(hz)) & (groups - 1)).astype(F32).astype(BF16)
        here = group_ids == group
        row = p * (TOGETHER * FIELDS * tiles)
        plain = TOGETHER - 2 if last else TOGETHER
        pieces = [i * FIELDS * tiles + t for i in range(plain) for t in range(tiles)]
        pieces = [value_ref[pl.ds(row + i, FIELDS, stride=tiles), :] for i in pieces]
        if last:
            at_end = pl.multiple_of(row + plain * FIELDS * tiles, 8)
            block = value_ref[pl.ds(at_end, 2 * FIELDS * tiles), :]
            for first in [i * FIELDS * tiles + t for i in range(2) for t in range(tiles)]:
                lines = [first + f * tiles for f in range(FIELDS)]
                pieces.append(jnp.concatenate([block[r : r + 1] for r in lines], axis=0))
        value = jnp.concatenate(pieces, axis=1)
        parts = []
        for half in halves(value):
            for f in range(FIELDS):
                parts.append(jnp.where(here, half[f : f + 1], jnp.zeros((), BF16)))
        spread = jnp.concatenate(parts, axis=0)
        return lax.dot_general(spread, onehot, NT, preferred_element_type=F32)

    @pl.loop(0, owners // TOGETHER // 4)
    def _(n):
        total[...] += functools.reduce(lambda sums, i: sums + step(n * 4 + i, i == 3), range(1, 4), step(n * 4, False))

    even_ref[FIELDS * hx] = jnp.zeros((ITERS, hz), F32)
    scale = lax.rsqrt(mass_ref[...])
    half_x = hx // 2
    odd = lax.axis_index("tgt") % 2 == 1
    for f in range(FIELDS):
        s = total[f * groups : (f + 1) * groups] + total[(FIELDS + f) * groups : (FIELDS + f + 1) * groups]
        for b in range(2):
            for x in range(half_x):
                at = b * half_x + x
                v = s[x * hy : (x + 1) * hy, b * hz : (b + 1) * hz] * scale[at]
                v_ref[f, at] = v
                first, last = v[:ITERS], v[hy - ITERS :]
                even_ref[f * hx + at] = jnp.where(odd, first, last)
                odd_ref[f * hx + at] = jnp.where(odd, last, first)


def scatter_call(values, target, mass):
    hx, hy, hz = mass.shape
    groups = hx * hy * hz // WIDE
    even = jax.ShapeDtypeStruct((FIELDS * hx + 1, ITERS, hz), F32)
    odd = jax.ShapeDtypeStruct((FIELDS * hx, ITERS, hz), F32)
    return pl.pallas_call(
        scatter_kernel,
        out_shape=(jax.ShapeDtypeStruct((FIELDS, hx, hy, hz), F32), even, odd),
        in_specs=[pl.BlockSpec(memory_space=pltpu.VMEM)] * 3,
        out_specs=(pl.BlockSpec(memory_space=pltpu.VMEM),) * 3,
        scratch_shapes=[pltpu.VMEM((2 * FIELDS * groups, WIDE), F32)],
        compiler_params=pltpu.CompilerParams(vmem_limit_bytes=40 << 20),
    )(values, target, mass)


def lookup_rows(table, index, ids, group_ids, groups, at_parts):
    group, low = at_parts(index)
    got = jnp.dot(table, low_onehot(low, ids), preferred_element_type=F32)
    here = group_ids == group
    rows = 3 * groups
    out = []
    for m in range(3):
        part = got[m * groups : (m + 1) * groups] + got[rows + m * groups : rows + (m + 1) * groups]
        out.append(jnp.sum(jnp.where(here, part, 0.0), axis=0, keepdims=True))
    return out


def pick_rows(tables, row, lane):
    row = jnp.broadcast_to(row, (8, 128))
    lane = jnp.broadcast_to(lane, (8, 128))
    tile = row >> 3
    here = row_ids(8, 128) == (row & 7)
    out = []
    for table in tables:
        got = jnp.zeros((8, 128), F32)
        for v in range(table.shape[0] // 8):
            piece = jnp.take_along_axis(table[v * 8 : (v + 1) * 8], lane, axis=1, mode="promise_in_bounds")
            got = jnp.where(tile == v, piece, got)
        out.append(jnp.sum(jnp.where(here, got, 0.0), axis=0, keepdims=True))
    return out


def either_way(i, index, table, ids, group_ids, groups, at_parts, tables, row_and_lane):
    halves_of = [slice(c * 128, (c + 1) * 128) for c in range(2)]
    if i % 8 in (2, 5, 7):
        got = [pick_rows(tables, *row_and_lane(index[:, c])) for c in halves_of]
        return [got[c][m] for m in range(3) for c in range(2)]
    got = lookup_rows(table, index, ids, group_ids, groups, at_parts)
    return [line[:, c] for line in got for c in halves_of]


def cell_moduli(vals):
    phi = vals[0]
    mean = (vals[1] + vals[2] + vals[3]) / 3.0
    q2 = 1.5 * (
        (vals[1] - mean) ** 2
        + (vals[2] - mean) ** 2
        + (vals[3] - mean) ** 2
        + 2.0 * (vals[4] ** 2 + vals[5] ** 2 + vals[6] ** 2)
    )
    bulk = 1.6 * jnp.exp(-3.0 * phi) * (1.0 + 0.25 * jnp.tanh(mean))
    shear = 0.9 * jnp.exp(-2.0 * phi) / (1.0 + q2 / 0.5)
    soften = shear * q2 / (0.5 + q2)
    return [bulk, shear, soften]


def corners(sides):
    line = row_ids(2 * ITERS, sides[0].shape[1])
    near = pltpu.roll(sides[1], 2, 0)
    far = jnp.where(line == 4, pltpu.roll(sides[2], 4, 0), pltpu.roll(sides[2], 6, 0))
    return sides[0], jnp.where(line < 4, near, far)


def sides_kernel(even_ref, odd_ref, sides_ref, to_even_ref, to_odd_ref):
    hx = sides_ref.shape[1]
    b_odd = lax.axis_index("tgt") % 2 == 1
    a_odd = lax.axis_index("src") % 2 == 1
    for f in range(FIELDS):
        sides = []
        for x in range(hx):
            even_side, odd_side = even_ref[f * hx + x], odd_ref[f * hx + x]
            right = jnp.where(b_odd, odd_side, even_side)
            left = jnp.where(b_odd, even_side, odd_side)
            sides.append(jnp.concatenate([right, left], axis=0))
            sides_ref[f, x] = sides[x]
        to_left, to_right = corners(sides), corners(sides[::-1])
        to_even_ref[f, :8] = jnp.where(a_odd, to_left[0], to_right[0])
        to_even_ref[f, 8:14] = jnp.where(a_odd, to_left[1], to_right[1])[:6]
        to_odd_ref[f, :8] = jnp.where(a_odd, to_right[0], to_left[0])
        to_odd_ref[f, 8:] = jnp.where(a_odd, to_right[1], to_left[1])


def sides_call(even, odd, hx):
    hz = even.shape[2]
    return pl.pallas_call(
        sides_kernel,
        out_shape=(
            jax.ShapeDtypeStruct((FIELDS, hx, 2 * ITERS, hz), F32),
            jax.ShapeDtypeStruct((FIELDS, 4 * ITERS - 2, hz), F32),
            jax.ShapeDtypeStruct((FIELDS, 4 * ITERS, hz), F32),
        ),
        in_specs=[pl.BlockSpec(memory_space=pltpu.VMEM)] * 2,
        out_specs=(pl.BlockSpec(memory_space=pltpu.VMEM),) * 3,
        compiler_params=pltpu.CompilerParams(vmem_limit_bytes=4 << 20),
        cost_estimate=pl.CostEstimate(flops=40 * 10**9, bytes_accessed=40 * 10**6, transcendentals=0),
    )(even, odd)


def solve_kernel(
    mesh_shape, v_ref, sides_ref, even_ref, odd_ref, even_corners_ref, odd_corners_ref, mass_ref, order_ref,
    projected_hbm, out_ref, projected_ref, sem,
):
    n_src, n_tgt = mesh_shape
    hx, hy, hz = mass_ref.shape
    k = ITERS
    rows = hy + 2 * k
    a, b = lax.axis_index("src"), lax.axis_index("tgt")

    def exists(flag):
        return jnp.where(flag, 1.0, 0.0).astype(F32)

    row = row_ids(rows, hz)
    lane = lax.broadcasted_iota(jnp.int32, (rows, hz), 1)
    inside = jnp.where(row < hy, 1.0, jnp.where(row < hy + k, exists(b < n_tgt - 1), exists(b > 0)))
    inside_left = inside * exists(a > 0)
    inside_right = inside * exists(a < n_src - 1)
    not_first = jnp.where(lane == 0, 0.0, 1.0)
    not_last = jnp.where(lane == hz - 1, 0.0, 1.0)
    scale = lax.rsqrt(mass_ref[...])

    line = row_ids(2 * k, hz)

    def slabs(own, first, packed, from_left):
        second = pltpu.roll(packed, 6, 0)
        third = jnp.where(line < 4, pltpu.roll(packed, 4, 0), pltpu.roll(packed, 2, 0))
        sides = [first, second, third] + [jnp.zeros((2 * k, hz), F32)] * (hx - 3)
        if from_left:
            sides = sides[::-1]
        return [jnp.concatenate([own[x], side], axis=0) for x, side in enumerate(sides)]

    a_odd = a % 2 == 1

    def slabs_of(f):
        packed = jnp.concatenate([even_corners_ref[f, 2 * k :], jnp.zeros((2, hz), F32)], axis=0)
        even = (even_ref[f], even_corners_ref[f, : 2 * k], packed)
        odd = (odd_ref[f], odd_corners_ref[f, : 2 * k], odd_corners_ref[f, 2 * k :])
        left = slabs(*[jnp.where(a_odd, p, q) for p, q in zip(even, odd)], True)
        right = slabs(*[jnp.where(a_odd, q, p) for p, q in zip(even, odd)], False)
        own = [jnp.concatenate([v_ref[f, x], sides_ref[f, x]], axis=0) for x in range(hx)]
        return left + own + right

    def one_sweep(sweep, base, u):
        new = list(u)
        for x in range(sweep, hx + 2 * k - sweep):
            far = max(k - x, x - (k + hx - 1), 0)
            n = rows if sweep + far < k else hy
            w = u[x]
            near = u[x - 1][:n] + u[x + 1][:n]
            near = near + pltpu.roll(w, 1, 0)[:n] + pltpu.roll(w, rows - 1, 0)[:n]
            w = w[:n]
            near = near + pltpu.roll(w, 1, 1) * not_first[:n] + pltpu.roll(w, hz - 1, 1) * not_last[:n]
            if x < k:
                near = near * inside_left[:n]
            elif x >= k + hx:
                near = near * inside_right[:n]
            elif n > hy:
                near = near * inside
            new[x] = COEFS[k - sweep] * base[x][:n] + near
        return new

    for first in range(0, FIELDS, 2):
        pair = range(first, min(first + 2, FIELDS))
        bases = [slabs_of(f) for f in pair]
        us = [[COEFS[k] * e for e in base] for base in bases]
        for sweep in range(1, k + 1):
            us = [one_sweep(sweep, base, u) for base, u in zip(bases, us)]
        for f, u in zip(pair, us):
            for x in range(hx):
                projected_ref[f, x] = u[k + x][:hy] * scale[x]

    leave = pltpu.make_async_copy(projected_ref, projected_hbm, sem)
    leave.start()
    groups = hx * hy * hz // WIDE
    payload = cell_moduli([projected_ref[f].reshape(hx * hy, hz) for f in range(FIELDS)])
    table = jnp.concatenate([jnp.concatenate([m[:groups], m[groups:]], axis=1) for m in payload], axis=0)
    table = jnp.concatenate(halves(table), axis=0)
    ids = row_ids(WIDE, WIDE).astype(F32).astype(BF16)
    group_ids = row_ids(groups, WIDE)

    def at_parts(index):
        return (index >> log2(hz)) & (groups - 1), ((index >> log2(groups * hz)) << log2(hz)) + (index & (hz - 1))

    for q in range(0, groups, 4):
        lines = []
        for i in range(q, q + 4):
            index = order_ref[:, i * WIDE : (i + 1) * WIDE]
            got = lookup_rows(table, index, ids, group_ids, groups, at_parts)
            lines += [line[:, c * 128 : (c + 1) * 128] for line in got for c in range(2)]
        out_ref[q * 6 : q * 6 + 24, :] = jnp.concatenate(lines, axis=0)
    leave.wait()


def solve_call(mesh_shape, *args):
    mass, order = args[-2:]
    hx, hy, hz = mass.shape

    def kernel(*refs):
        solve_kernel(mesh_shape, *refs)

    return pl.pallas_call(
        kernel,
        out_shape=(
            jax.ShapeDtypeStruct((FIELDS, hx, hy, hz), F32),
            jax.ShapeDtypeStruct((order.shape[1] // WIDE * 6, 128), F32),
        ),
        in_specs=[pl.BlockSpec(memory_space=pltpu.VMEM)] * 8,
        out_specs=(pl.BlockSpec(memory_space=pltpu.HBM), pl.BlockSpec(memory_space=pltpu.VMEM)),
        scratch_shapes=[pltpu.VMEM((FIELDS, hx, hy, hz), F32), pltpu.SemaphoreType.DMA],
        compiler_params=pltpu.CompilerParams(vmem_limit_bytes=40 << 20),
    )(*args)


def place_kernel(arrived_ref, order_ref, out_hbm, out_ref, sems):
    groups = arrived_ref.shape[0] // 6
    parts = [[arrived_ref[pl.ds(2 * m + c, groups, stride=6), :] for c in range(2)] for m in range(3)]
    table = jnp.concatenate([jnp.concatenate(part, axis=1) for part in parts], axis=0)
    table = jnp.concatenate(halves(table), axis=0)
    tables = [jnp.concatenate(part, axis=0) for part in parts]
    ids = row_ids(WIDE, WIDE).astype(F32).astype(BF16)
    group_ids = row_ids(groups, WIDE)

    def at_parts(index):
        return index >> log2(WIDE), index & (WIDE - 1)

    def row_and_lane(index):
        return ((index >> 7) & 1) * groups + (index >> log2(WIDE)), index & 127

    copies = []
    for n in range(PIECES):
        for q in range(n * groups // PIECES, (n + 1) * groups // PIECES):
            index = order_ref[:, q * WIDE : (q + 1) * WIDE]
            lines = either_way(q, index, table, ids, group_ids, groups, at_parts, tables, row_and_lane)
            for c in range(2):
                out_ref[:, q * WIDE + c * 128 : q * WIDE + (c + 1) * 128] = jnp.concatenate(lines[c::2], axis=0)
        piece = pl.ds(n * groups // PIECES * WIDE, groups // PIECES * WIDE)
        copies.append(pltpu.make_async_copy(out_ref.at[:, piece], out_hbm.at[:, piece], sems.at[n]))
        copies[n].start()
    for copy in copies:
        copy.wait()


def place_call(arrived, order):
    return pl.pallas_call(
        place_kernel,
        out_shape=jax.ShapeDtypeStruct((3, order.shape[1]), F32),
        in_specs=[pl.BlockSpec(memory_space=pltpu.VMEM)] * 2,
        out_specs=pl.BlockSpec(memory_space=pltpu.HBM),
        scratch_shapes=[pltpu.VMEM((3, order.shape[1]), F32), pltpu.SemaphoreType.DMA((PIECES,))],
        compiler_params=pltpu.CompilerParams(vmem_limit_bytes=40 << 20),
    )(arrived, order)


def swap(x, axis, start):
    pairs = [(i, i + 1) for i in range(start, lax.axis_size(axis) - 1, 2)]
    return lax.ppermute(x, axis, pairs + [(j, i) for i, j in pairs])


def on_device(source_fields, slot_source, slot_weight, slot_target, cell_mass, send_order, place_order):
    n_src, n_tgt = lax.axis_size("src"), lax.axis_size("tgt")
    both = ("src", "tgt")
    owners = n_src * n_tgt
    cells = cell_mass.size
    quota = cells // owners

    values = gather_call(source_fields, slot_source.reshape(1, -1), slot_weight.reshape(1, -1))
    values = values.reshape(owners, FIELDS, SPAN // 128, 128)
    values = lax.all_to_all(values, both, split_axis=0, concat_axis=0, tiled=True).reshape(-1, 128)
    v, even, odd = scatter_call(values, slot_target.reshape(1, -1), cell_mass)
    even_block, odd_block = swap(v, "src", 0), swap(v, "src", 1)
    even, odd = swap(even, "tgt", 0), swap(odd, "tgt", 1)
    sides, even, odd = sides_call(even, odd, cell_mass.shape[0])
    even, odd = swap(even, "src", 0), swap(odd, "src", 1)
    projected, outgoing = solve_call(
        (n_src, n_tgt), v, sides, even_block, odd_block, even, odd, cell_mass, send_order
    )

    if quota == WIDE:
        outgoing = outgoing.reshape(owners, 3, 2, 128)
        incoming = lax.all_to_all(outgoing, both, split_axis=0, concat_axis=0, tiled=True)
    else:
        groups = cells // WIDE
        flat = outgoing.reshape(groups, 3, WIDE).transpose(1, 0, 2).reshape(3, owners, quota)
        flat = lax.all_to_all(flat, both, split_axis=1, concat_axis=1, tiled=True)
        incoming = flat.reshape(3, groups, WIDE).transpose(1, 0, 2)
    incoming = incoming.reshape(-1, 128)
    return projected, place_call(incoming, place_order)


def solution(mesh):
    split = P(("src", "tgt"))
    rows = P(("src", "tgt"), None)
    return jax.shard_map(
        on_device,
        mesh=mesh,
        in_specs=(P(None, ("src", "tgt")), split, split, split, P("src", "tgt", None), rows, rows),
        out_specs=(P(None, "src", "tgt", None), P(None, ("src", "tgt"))),
        check_vma=False,
    )
```

```python
import functools

import numpy as np

import jax
import jax.numpy as jnp
from jax import lax
from jax.experimental import pallas as pl
from jax.experimental.pallas import tpu as pltpu
from jax.sharding import PartitionSpec as P

ITERS = 4
FIELDS = 7
PIECES = 4
SPAN = 512
AT_ONCE = 32
TOGETHER = 8
WIDE = 256
BF16 = jnp.bfloat16
F32 = jnp.float32
NT = (((1,), (1,)), ((), ()))


def sweep_polynomial(iters, theta, delta):
    sigma = theta / delta
    rho = 1.0 / sigma
    mass = np.array([1.0, 0.125])
    poly = np.polynomial.polynomial
    resid = np.array([1.0])
    step = resid / theta
    total = np.array([0.0])
    for _ in range(iters):
        total = poly.polyadd(total, step)
        resid = poly.polysub(resid, poly.polymul(mass, step))
        rho_new = 1.0 / (2.0 * sigma - rho)
        step = poly.polyadd(rho_new * rho * step, 2.0 * rho_new / delta * resid)
        rho = rho_new
    return [float(c) for c in poly.polyadd(total, step)]


COEFS = sweep_polynomial(ITERS, 1.0, 0.75)


def halves(x):
    high = x.astype(BF16)
    return high, (x - high.astype(F32)).astype(BF16)


def log2(n):
    assert n & (n - 1) == 0
    return n.bit_length() - 1


def choose(part, index, count):
    bits = [(index & (1 << bit)) != 0 for bit in range(log2(count))]

    def among(first, depth):
        if depth == 0:
            return part(first)
        low = among(first, depth - 1)
        return jnp.where(bits[depth - 1], among(first + (1 << (depth - 1)), depth - 1), low)

    return among(0, log2(count))


def row_ids(rows, lanes):
    return lax.broadcasted_iota(jnp.int32, (rows, lanes), 0)


def low_onehot(low, ids):
    return jnp.where(ids == low.astype(F32).astype(BF16), jnp.ones((), BF16), jnp.zeros((), BF16))


def gather_kernel(fields_hbm, index_hbm, weight_hbm, out_ref, table, padded, fields_ref, index_ref, weight_ref, sems):
    pairs = ((fields_hbm, fields_ref), (index_hbm, index_ref), (weight_hbm, weight_ref))
    copies = [pltpu.make_async_copy(src, dst, sems.at[i]) for i, (src, dst) in enumerate(pairs)]
    for copy in copies:
        copy.start()
    lanes = out_ref.shape[1]
    span = SPAN
    tiles = span // lanes
    owners = index_ref.shape[1] // span
    groups = fields_ref.shape[1] // WIDE
    table[...] = jnp.zeros_like(table)
    padded[...] = jnp.zeros_like(padded)
    for copy in copies:
        copy.wait()
    for g in range(groups):
        table[g * 8 : g * 8 + FIELDS, :] = fields_ref[:, g * WIDE : (g + 1) * WIDE]
    both = jnp.concatenate(halves(table[...]), axis=0)
    rows = groups * 8
    ids = row_ids(WIDE, WIDE).astype(F32).astype(BF16)
    padded[:FIELDS, :] = fields_ref[...]

    def by_matmul(index):
        got = jnp.dot(both, low_onehot(index & (WIDE - 1), ids), preferred_element_type=F32)
        group = jnp.broadcast_to(index >> log2(WIDE), (8, WIDE))
        return choose(lambda g: got[g * 8 : (g + 1) * 8] + got[rows + g * 8 : rows + (g + 1) * 8], group, groups)

    def by_lanes(index):
        lane = jnp.broadcast_to(index & 127, (8, 128))
        tile = jnp.broadcast_to(index >> 7, (8, 128))

        def piece(g):
            columns = padded[:, g * 128 : (g + 1) * 128]
            return jnp.take_along_axis(columns, lane, axis=1, mode="promise_in_bounds")

        return choose(piece, tile, padded.shape[1] // 128)

    def one_owner(q, matmuls):
        at = pl.multiple_of(q * SPAN, SPAN)
        index = index_ref[:, pl.ds(at, SPAN)]
        weight = weight_ref[:, pl.ds(at, SPAN)]
        values = [by_matmul(index[:, i * WIDE : (i + 1) * WIDE]) for i in range(matmuls)]
        for t in range(matmuls * WIDE // 128, tiles):
            values.append(by_lanes(index[:, t * 128 : (t + 1) * 128]))
        value = jnp.concatenate(values, axis=1) * weight
        return [value[:FIELDS, t * lanes : (t + 1) * lanes] for t in range(tiles)]

    @pl.loop(0, owners // AT_ONCE)
    def _(m):
        lines = []
        for i in range(AT_ONCE):
            q = m * AT_ONCE + i
            value = one_owner(q, SPAN // WIDE - (i % 4 > 0))
            if i < AT_ONCE - 2:
                for t in range(tiles):
                    out_ref[pl.ds(q * (FIELDS * tiles) + t, FIELDS, stride=tiles), :] = value[t]
            else:
                lines += [value[t][f : f + 1] for f in range(FIELDS) for t in range(tiles)]
        at = pl.multiple_of((m * AT_ONCE + AT_ONCE - 2) * (FIELDS * tiles), 8)
        out_ref[pl.ds(at, len(lines)), :] = jnp.concatenate(lines, axis=0)


def gather_call(fields, index, weight):
    rows = FIELDS * index.shape[1] // 128
    return pl.pallas_call(
        gather_kernel,
        out_shape=jax.ShapeDtypeStruct((rows, 128), F32),
        in_specs=[pl.BlockSpec(memory_space=pltpu.HBM)] * 3,
        out_specs=pl.BlockSpec(memory_space=pltpu.VMEM),
        scratch_shapes=[
            pltpu.VMEM((fields.shape[1] // WIDE * 8, WIDE), F32),
            pltpu.VMEM((8, fields.shape[1]), F32),
            pltpu.VMEM(fields.shape, F32),
            pltpu.VMEM(index.shape, jnp.int32),
            pltpu.VMEM(weight.shape, F32),
            pltpu.SemaphoreType.DMA((3,)),
        ],
        compiler_params=pltpu.CompilerParams(vmem_limit_bytes=40 << 20),
    )(*[pltpu.with_memory_space_constraint(x, pltpu.HBM) for x in (fields, index, weight)])


def scatter_kernel(value_ref, target_ref, mass_ref, v_ref, even_ref, odd_ref, total):
    lanes = value_ref.shape[1]
    tiles = SPAN // lanes
    owners = target_ref.shape[1] // SPAN
    span = TOGETHER * SPAN
    hx, hy, hz = mass_ref.shape
    groups = hx * hy * hz // WIDE
    total[...] = jnp.zeros_like(total)
    ids = row_ids(WIDE, span).astype(F32).astype(BF16)
    group_ids = row_ids(groups, span).astype(F32).astype(BF16)

    def step(p, last):
        at = pl.multiple_of(p * span, span)
        target = target_ref[:, pl.ds(at, span)]
        low = ((target >> log2(groups * hz)) << log2(hz)) + (target & (hz - 1))
        onehot = low_onehot(jnp.where(target < 0, -1, low), ids)
        group = ((target >> log2(hz)) & (groups - 1)).astype(F32).astype(BF16)
        here = group_ids == group
        row = p * (TOGETHER * FIELDS * tiles)
        plain = TOGETHER - 2 if last else TOGETHER
        pieces = [i * FIELDS * tiles + t for i in range(plain) for t in range(tiles)]
        pieces = [value_ref[pl.ds(row + i, FIELDS, stride=tiles), :] for i in pieces]
        if last:
            at_end = pl.multiple_of(row + plain * FIELDS * tiles, 8)
            block = value_ref[pl.ds(at_end, 2 * FIELDS * tiles), :]
            for first in [i * FIELDS * tiles + t for i in range(2) for t in range(tiles)]:
                lines = [first + f * tiles for f in range(FIELDS)]
                pieces.append(jnp.concatenate([block[r : r + 1] for r in lines], axis=0))
        value = jnp.concatenate(pieces, axis=1)
        parts = []
        for half in halves(value):
            for f in range(FIELDS):
                parts.append(jnp.where(here, half[f : f + 1], jnp.zeros((), BF16)))
        spread = jnp.concatenate(parts, axis=0)
        return lax.dot_general(spread, onehot, NT, preferred_element_type=F32)

    @pl.loop(0, owners // TOGETHER // 4)
    def _(n):
        total[...] += functools.reduce(lambda sums, i: sums + step(n * 4 + i, i == 3), range(1, 4), step(n * 4, False))

    even_ref[FIELDS * hx] = jnp.zeros((ITERS, hz), F32)
    scale = lax.rsqrt(mass_ref[...])
    half_x = hx // 2
    odd = lax.axis_index("tgt") % 2 == 1
    for f in range(FIELDS):
        s = total[f * groups : (f + 1) * groups] + total[(FIELDS + f) * groups : (FIELDS + f + 1) * groups]
        for b in range(2):
            for x in range(half_x):
                at = b * half_x + x
                v = s[x * hy : (x + 1) * hy, b * hz : (b + 1) * hz] * scale[at]
                v_ref[f, at] = v
                first, last = v[:ITERS], v[hy - ITERS :]
                even_ref[f * hx + at] = jnp.where(odd, first, last)
                odd_ref[f * hx + at] = jnp.where(odd, last, first)


def scatter_call(values, target, mass):
    hx, hy, hz = mass.shape
    groups = hx * hy * hz // WIDE
    even = jax.ShapeDtypeStruct((FIELDS * hx + 1, ITERS, hz), F32)
    odd = jax.ShapeDtypeStruct((FIELDS * hx, ITERS, hz), F32)
    return pl.pallas_call(
        scatter_kernel,
        out_shape=(jax.ShapeDtypeStruct((FIELDS, hx, hy, hz), F32), even, odd),
        in_specs=[pl.BlockSpec(memory_space=pltpu.VMEM)] * 3,
        out_specs=(pl.BlockSpec(memory_space=pltpu.VMEM),) * 3,
        scratch_shapes=[pltpu.VMEM((2 * FIELDS * groups, WIDE), F32)],
        compiler_params=pltpu.CompilerParams(vmem_limit_bytes=40 << 20),
    )(values, target, mass)


def lookup_rows(table, index, ids, group_ids, groups, at_parts):
    group, low = at_parts(index)
    got = jnp.dot(table, low_onehot(low, ids), preferred_element_type=F32)
    here = group_ids == group
    rows = 3 * groups
    out = []
    for m in range(3):
        part = got[m * groups : (m + 1) * groups] + got[rows + m * groups : rows + (m + 1) * groups]
        out.append(jnp.sum(jnp.where(here, part, 0.0), axis=0, keepdims=True))
    return out


def pick_rows(tables, row, lane):
    row = jnp.broadcast_to(row, (8, 128))
    lane = jnp.broadcast_to(lane, (8, 128))
    tile = row >> 3
    here = row_ids(8, 128) == (row & 7)
    out = []
    for table in tables:

        def piece(v, table=table):
            return jnp.take_along_axis(table[v * 8 : (v + 1) * 8], lane, axis=1, mode="promise_in_bounds")

        got = choose(piece, tile, table.shape[0] // 8)
        out.append(jnp.sum(jnp.where(here, got, 0.0), axis=0, keepdims=True))
    return out


def either_way(i, index, table, ids, group_ids, groups, at_parts, tables, row_and_lane):
    halves_of = [slice(c * 128, (c + 1) * 128) for c in range(2)]
    if i % 8 in (2, 5, 7):
        got = [pick_rows(tables, *row_and_lane(index[:, c])) for c in halves_of]
        return [got[c][m] for m in range(3) for c in range(2)]
    got = lookup_rows(table, index, ids, group_ids, groups, at_parts)
    return [line[:, c] for line in got for c in halves_of]


def cell_moduli(vals):
    phi = vals[0]
    mean = (vals[1] + vals[2] + vals[3]) / 3.0
    q2 = 1.5 * (
        (vals[1] - mean) ** 2
        + (vals[2] - mean) ** 2
        + (vals[3] - mean) ** 2
        + 2.0 * (vals[4] ** 2 + vals[5] ** 2 + vals[6] ** 2)
    )
    bulk = 1.6 * jnp.exp(-3.0 * phi) * (1.0 + 0.25 * jnp.tanh(mean))
    shear = 0.9 * jnp.exp(-2.0 * phi) / (1.0 + q2 / 0.5)
    soften = shear * q2 / (0.5 + q2)
    return [bulk, shear, soften]


def corners(sides):
    line = row_ids(2 * ITERS, sides[0].shape[1])
    near = pltpu.roll(sides[1], 2, 0)
    far = jnp.where(line == 4, pltpu.roll(sides[2], 4, 0), pltpu.roll(sides[2], 6, 0))
    return sides[0], jnp.where(line < 4, near, far)


def sides_kernel(even_ref, odd_ref, sides_ref, to_even_ref, to_odd_ref):
    hx = sides_ref.shape[1]
    b_odd = lax.axis_index("tgt") % 2 == 1
    a_odd = lax.axis_index("src") % 2 == 1
    for f in range(FIELDS):
        sides = []
        for x in range(hx):
            even_side, odd_side = even_ref[f * hx + x], odd_ref[f * hx + x]
            right = jnp.where(b_odd, odd_side, even_side)
            left = jnp.where(b_odd, even_side, odd_side)
            sides.append(jnp.concatenate([right, left], axis=0))
            sides_ref[f, x] = sides[x]
        to_left, to_right = corners(sides), corners(sides[::-1])
        to_even_ref[f, :8] = jnp.where(a_odd, to_left[0], to_right[0])
        to_even_ref[f, 8:14] = jnp.where(a_odd, to_left[1], to_right[1])[:6]
        to_odd_ref[f, :8] = jnp.where(a_odd, to_right[0], to_left[0])
        to_odd_ref[f, 8:] = jnp.where(a_odd, to_right[1], to_left[1])


def sides_call(even, odd, hx):
    hz = even.shape[2]
    return pl.pallas_call(
        sides_kernel,
        out_shape=(
            jax.ShapeDtypeStruct((FIELDS, hx, 2 * ITERS, hz), F32),
            jax.ShapeDtypeStruct((FIELDS, 4 * ITERS - 2, hz), F32),
            jax.ShapeDtypeStruct((FIELDS, 4 * ITERS, hz), F32),
        ),
        in_specs=[pl.BlockSpec(memory_space=pltpu.VMEM)] * 2,
        out_specs=(pl.BlockSpec(memory_space=pltpu.VMEM),) * 3,
        compiler_params=pltpu.CompilerParams(vmem_limit_bytes=4 << 20),
        cost_estimate=pl.CostEstimate(flops=40 * 10**9, bytes_accessed=40 * 10**6, transcendentals=0),
    )(even, odd)


def solve_kernel(
    mesh_shape, v_ref, sides_ref, even_ref, odd_ref, even_corners_ref, odd_corners_ref, mass_ref, order_ref,
    projected_hbm, out_ref, projected_ref, sem,
):
    n_src, n_tgt = mesh_shape
    hx, hy, hz = mass_ref.shape
    k = ITERS
    rows = hy + 2 * k
    a, b = lax.axis_index("src"), lax.axis_index("tgt")

    def exists(flag):
        return jnp.where(flag, 1.0, 0.0).astype(F32)

    row = row_ids(rows, hz)
    lane = lax.broadcasted_iota(jnp.int32, (rows, hz), 1)
    inside = jnp.where(row < hy, 1.0, jnp.where(row < hy + k, exists(b < n_tgt - 1), exists(b > 0)))
    inside_left = inside * exists(a > 0)
    inside_right = inside * exists(a < n_src - 1)
    not_first = jnp.where(lane == 0, 0.0, 1.0)
    not_last = jnp.where(lane == hz - 1, 0.0, 1.0)
    scale = lax.rsqrt(mass_ref[...])

    line = row_ids(2 * k, hz)

    def slabs(own, first, packed, from_left):
        second = pltpu.roll(packed, 6, 0)
        third = jnp.where(line < 4, pltpu.roll(packed, 4, 0), pltpu.roll(packed, 2, 0))
        sides = [first, second, third] + [jnp.zeros((2 * k, hz), F32)] * (hx - 3)
        if from_left:
            sides = sides[::-1]
        return [jnp.concatenate([own[x], side], axis=0) for x, side in enumerate(sides)]

    a_odd = a % 2 == 1

    for f in range(FIELDS):
        packed = jnp.concatenate([even_corners_ref[f, 2 * k :], jnp.zeros((2, hz), F32)], axis=0)
        even = (even_ref[f], even_corners_ref[f, : 2 * k], packed)
        odd = (odd_ref[f], odd_corners_ref[f, : 2 * k], odd_corners_ref[f, 2 * k :])
        left = slabs(*[jnp.where(a_odd, p, q) for p, q in zip(even, odd)], True)
        right = slabs(*[jnp.where(a_odd, q, p) for p, q in zip(even, odd)], False)
        own = [jnp.concatenate([v_ref[f, x], sides_ref[f, x]], axis=0) for x in range(hx)]
        base = left + own + right
        u = [COEFS[k] * e for e in base]
        for sweep in range(1, k + 1):
            new = list(u)
            for x in range(sweep, hx + 2 * k - sweep):
                far = max(k - x, x - (k + hx - 1), 0)
                n = rows if sweep + far < k else hy
                w = u[x]
                near = u[x - 1][:n] + u[x + 1][:n]
                near = near + pltpu.roll(w, 1, 0)[:n] + pltpu.roll(w, rows - 1, 0)[:n]
                w = w[:n]
                near = near + pltpu.roll(w, 1, 1) * not_first[:n] + pltpu.roll(w, hz - 1, 1) * not_last[:n]
                if x < k:
                    near = near * inside_left[:n]
                elif x >= k + hx:
                    near = near * inside_right[:n]
                elif n > hy:
                    near = near * inside
                new[x] = COEFS[k - sweep] * base[x][:n] + near
            u = new
        for x in range(hx):
            projected_ref[f, x] = u[k + x][:hy] * scale[x]

    leave = pltpu.make_async_copy(projected_ref, projected_hbm, sem)
    leave.start()
    groups = hx * hy * hz // WIDE
    payload = cell_moduli([projected_ref[f].reshape(hx * hy, hz) for f in range(FIELDS)])
    table = jnp.concatenate([jnp.concatenate([m[:groups], m[groups:]], axis=1) for m in payload], axis=0)
    table = jnp.concatenate(halves(table), axis=0)
    ids = row_ids(WIDE, WIDE).astype(F32).astype(BF16)
    group_ids = row_ids(groups, WIDE)

    def at_parts(index):
        return (index >> log2(hz)) & (groups - 1), ((index >> log2(groups * hz)) << log2(hz)) + (index & (hz - 1))

    for q in range(0, groups, 4):
        lines = []
        for i in range(q, q + 4):
            index = order_ref[:, i * WIDE : (i + 1) * WIDE]
            got = lookup_rows(table, index, ids, group_ids, groups, at_parts)
            lines += [line[:, c * 128 : (c + 1) * 128] for line in got for c in range(2)]
        out_ref[q * 6 : q * 6 + 24, :] = jnp.concatenate(lines, axis=0)
    leave.wait()


def solve_call(mesh_shape, *args):
    mass, order = args[-2:]
    hx, hy, hz = mass.shape

    def kernel(*refs):
        solve_kernel(mesh_shape, *refs)

    return pl.pallas_call(
        kernel,
        out_shape=(
            jax.ShapeDtypeStruct((FIELDS, hx, hy, hz), F32),
            jax.ShapeDtypeStruct((order.shape[1] // WIDE * 6, 128), F32),
        ),
        in_specs=[pl.BlockSpec(memory_space=pltpu.VMEM)] * 8,
        out_specs=(pl.BlockSpec(memory_space=pltpu.HBM), pl.BlockSpec(memory_space=pltpu.VMEM)),
        scratch_shapes=[pltpu.VMEM((FIELDS, hx, hy, hz), F32), pltpu.SemaphoreType.DMA],
        compiler_params=pltpu.CompilerParams(vmem_limit_bytes=40 << 20),
    )(*args)


def place_kernel(arrived_ref, order_ref, out_hbm, out_ref, sems):
    groups = arrived_ref.shape[0] // 6
    parts = [[arrived_ref[pl.ds(2 * m + c, groups, stride=6), :] for c in range(2)] for m in range(3)]
    table = jnp.concatenate([jnp.concatenate(part, axis=1) for part in parts], axis=0)
    table = jnp.concatenate(halves(table), axis=0)
    tables = [jnp.concatenate(part, axis=0) for part in parts]
    ids = row_ids(WIDE, WIDE).astype(F32).astype(BF16)
    group_ids = row_ids(groups, WIDE)

    def at_parts(index):
        return index >> log2(WIDE), index & (WIDE - 1)

    def row_and_lane(index):
        return ((index >> 7) & 1) * groups + (index >> log2(WIDE)), index & 127

    copies = []
    for n in range(PIECES):
        for q in range(n * groups // PIECES, (n + 1) * groups // PIECES):
            index = order_ref[:, q * WIDE : (q + 1) * WIDE]
            lines = either_way(q, index, table, ids, group_ids, groups, at_parts, tables, row_and_lane)
            for c in range(2):
                out_ref[:, q * WIDE + c * 128 : q * WIDE + (c + 1) * 128] = jnp.concatenate(lines[c::2], axis=0)
        piece = pl.ds(n * groups // PIECES * WIDE, groups // PIECES * WIDE)
        copies.append(pltpu.make_async_copy(out_ref.at[:, piece], out_hbm.at[:, piece], sems.at[n]))
        copies[n].start()
    for copy in copies:
        copy.wait()


def place_call(arrived, order):
    return pl.pallas_call(
        place_kernel,
        out_shape=jax.ShapeDtypeStruct((3, order.shape[1]), F32),
        in_specs=[pl.BlockSpec(memory_space=pltpu.VMEM)] * 2,
        out_specs=pl.BlockSpec(memory_space=pltpu.HBM),
        scratch_shapes=[pltpu.VMEM((3, order.shape[1]), F32), pltpu.SemaphoreType.DMA((PIECES,))],
        compiler_params=pltpu.CompilerParams(vmem_limit_bytes=40 << 20),
    )(arrived, order)


def swap(x, axis, start):
    pairs = [(i, i + 1) for i in range(start, lax.axis_size(axis) - 1, 2)]
    return lax.ppermute(x, axis, pairs + [(j, i) for i, j in pairs])


def on_device(source_fields, slot_source, slot_weight, slot_target, cell_mass, send_order, place_order):
    n_src, n_tgt = lax.axis_size("src"), lax.axis_size("tgt")
    both = ("src", "tgt")
    owners = n_src * n_tgt
    cells = cell_mass.size
    quota = cells // owners

    values = gather_call(source_fields, slot_source.reshape(1, -1), slot_weight.reshape(1, -1))
    values = values.reshape(owners, FIELDS, SPAN // 128, 128)
    values = lax.all_to_all(values, both, split_axis=0, concat_axis=0, tiled=True).reshape(-1, 128)
    v, even, odd = scatter_call(values, slot_target.reshape(1, -1), cell_mass)
    even_block, odd_block = swap(v, "src", 0), swap(v, "src", 1)
    even, odd = swap(even, "tgt", 0), swap(odd, "tgt", 1)
    sides, even, odd = sides_call(even, odd, cell_mass.shape[0])
    even, odd = swap(even, "src", 0), swap(odd, "src", 1)
    projected, outgoing = solve_call(
        (n_src, n_tgt), v, sides, even_block, odd_block, even, odd, cell_mass, send_order
    )

    if quota == WIDE:
        outgoing = outgoing.reshape(owners, 3, 2, 128)
        incoming = lax.all_to_all(outgoing, both, split_axis=0, concat_axis=0, tiled=True)
    else:
        groups = cells // WIDE
        flat = outgoing.reshape(groups, 3, WIDE).transpose(1, 0, 2).reshape(3, owners, quota)
        flat = lax.all_to_all(flat, both, split_axis=1, concat_axis=1, tiled=True)
        incoming = flat.reshape(3, groups, WIDE).transpose(1, 0, 2)
    incoming = incoming.reshape(-1, 128)
    return projected, place_call(incoming, place_order)


def solution(mesh):
    split = P(("src", "tgt"))
    rows = P(("src", "tgt"), None)
    return jax.shard_map(
        on_device,
        mesh=mesh,
        in_specs=(P(None, ("src", "tgt")), split, split, split, P("src", "tgt", None), rows, rows),
        out_specs=(P(None, "src", "tgt", None), P(None, ("src", "tgt"))),
        check_vma=False,
    )
```

```python
import functools

import numpy as np

import jax
import jax.numpy as jnp
from jax import lax
from jax.experimental import pallas as pl
from jax.experimental.pallas import tpu as pltpu
from jax.sharding import PartitionSpec as P

ITERS = 4
FIELDS = 7
PIECES = 4
SPAN = 512
AT_ONCE = 32
TOGETHER = 16
WIDE = 256
BF16 = jnp.bfloat16
F32 = jnp.float32
NT = (((1,), (1,)), ((), ()))


def sweep_polynomial(iters, theta, delta):
    sigma = theta / delta
    rho = 1.0 / sigma
    mass = np.array([1.0, 0.125])
    poly = np.polynomial.polynomial
    resid = np.array([1.0])
    step = resid / theta
    total = np.array([0.0])
    for _ in range(iters):
        total = poly.polyadd(total, step)
        resid = poly.polysub(resid, poly.polymul(mass, step))
        rho_new = 1.0 / (2.0 * sigma - rho)
        step = poly.polyadd(rho_new * rho * step, 2.0 * rho_new / delta * resid)
        rho = rho_new
    return [float(c) for c in poly.polyadd(total, step)]


COEFS = sweep_polynomial(ITERS, 1.0, 0.75)


def halves(x):
    high = x.astype(BF16)
    return high, (x - high.astype(F32)).astype(BF16)


def log2(n):
    assert n & (n - 1) == 0
    return n.bit_length() - 1


def row_ids(rows, lanes):
    return lax.broadcasted_iota(jnp.int32, (rows, lanes), 0)


def low_onehot(low, ids):
    return jnp.where(ids == low.astype(F32).astype(BF16), jnp.ones((), BF16), jnp.zeros((), BF16))


def gather_kernel(fields_hbm, index_hbm, weight_hbm, out_ref, table, padded, fields_ref, index_ref, weight_ref, sems):
    pairs = ((fields_hbm, fields_ref), (index_hbm, index_ref), (weight_hbm, weight_ref))
    copies = [pltpu.make_async_copy(src, dst, sems.at[i]) for i, (src, dst) in enumerate(pairs)]
    for copy in copies:
        copy.start()
    lanes = out_ref.shape[1]
    span = SPAN
    tiles = span // lanes
    owners = index_ref.shape[1] // span
    groups = fields_ref.shape[1] // WIDE
    table[...] = jnp.zeros_like(table)
    padded[...] = jnp.zeros_like(padded)
    copies[0].wait()
    for g in range(groups):
        table[g * 8 : g * 8 + FIELDS, :] = fields_ref[:, g * WIDE : (g + 1) * WIDE]
    both = jnp.concatenate(halves(table[...]), axis=0)
    rows = groups * 8
    ids = row_ids(WIDE, WIDE).astype(F32).astype(BF16)
    padded[:FIELDS, :] = fields_ref[...]
    copies[1].wait()
    copies[2].wait()

    def by_matmul(index):
        got = jnp.dot(both, low_onehot(index & (WIDE - 1), ids), preferred_element_type=F32)
        group = jnp.broadcast_to(index >> log2(WIDE), (8, WIDE))
        value = jnp.zeros((8, WIDE), F32)
        for g in range(groups):
            part = got[g * 8 : (g + 1) * 8] + got[rows + g * 8 : rows + (g + 1) * 8]
            value = jnp.where(group == g, part, value)
        return value

    def by_lanes(index):
        lane = jnp.broadcast_to(index & 127, (8, 128))
        tile = jnp.broadcast_to(index >> 7, (8, 128))
        value = jnp.zeros((8, 128), F32)
        for g in range(padded.shape[1] // 128):
            piece = padded[:, g * 128 : (g + 1) * 128]
            piece = jnp.take_along_axis(piece, lane, axis=1, mode="promise_in_bounds")
            value = jnp.where(tile == g, piece, value)
        return value

    def one_owner(q, matmuls):
        at = pl.multiple_of(q * SPAN, SPAN)
        index = index_ref[:, pl.ds(at, SPAN)]
        weight = weight_ref[:, pl.ds(at, SPAN)]
        values = [by_matmul(index[:, i * WIDE : (i + 1) * WIDE]) for i in range(matmuls)]
        for t in range(matmuls * WIDE // 128, tiles):
            values.append(by_lanes(index[:, t * 128 : (t + 1) * 128]))
        value = jnp.concatenate(values, axis=1) * weight
        return [value[:FIELDS, t * lanes : (t + 1) * lanes] for t in range(tiles)]

    @pl.loop(0, owners // AT_ONCE)
    def _(m):
        lines = []
        for i in range(AT_ONCE):
            q = m * AT_ONCE + i
            value = one_owner(q, SPAN // WIDE - (i % 4 > 0))
            if i < AT_ONCE - 2:
                for t in range(tiles):
                    out_ref[pl.ds(q * (FIELDS * tiles) + t, FIELDS, stride=tiles), :] = value[t]
            else:
                lines += [value[t][f : f + 1] for f in range(FIELDS) for t in range(tiles)]
        at = pl.multiple_of((m * AT_ONCE + AT_ONCE - 2) * (FIELDS * tiles), 8)
        out_ref[pl.ds(at, len(lines)), :] = jnp.concatenate(lines, axis=0)


def gather_call(fields, index, weight):
    rows = FIELDS * index.shape[1] // 128
    return pl.pallas_call(
        gather_kernel,
        out_shape=jax.ShapeDtypeStruct((rows, 128), F32),
        in_specs=[pl.BlockSpec(memory_space=pltpu.HBM)] * 3,
        out_specs=pl.BlockSpec(memory_space=pltpu.VMEM),
        scratch_shapes=[
            pltpu.VMEM((fields.shape[1] // WIDE * 8, WIDE), F32),
            pltpu.VMEM((8, fields.shape[1]), F32),
            pltpu.VMEM(fields.shape, F32),
            pltpu.VMEM(index.shape, jnp.int32),
            pltpu.VMEM(weight.shape, F32),
            pltpu.SemaphoreType.DMA((3,)),
        ],
        compiler_params=pltpu.CompilerParams(vmem_limit_bytes=40 << 20),
    )(*[pltpu.with_memory_space_constraint(x, pltpu.HBM) for x in (fields, index, weight)])


def scatter_kernel(value_ref, target_ref, mass_ref, v_ref, even_ref, odd_ref, total):
    lanes = value_ref.shape[1]
    tiles = SPAN // lanes
    owners = target_ref.shape[1] // SPAN
    span = TOGETHER * SPAN
    hx, hy, hz = mass_ref.shape
    groups = hx * hy * hz // WIDE
    total[...] = jnp.zeros_like(total)
    ids = row_ids(WIDE, span).astype(F32).astype(BF16)
    group_ids = row_ids(groups, span).astype(F32).astype(BF16)

    def step(p, last):
        at = pl.multiple_of(p * span, span)
        target = target_ref[:, pl.ds(at, span)]
        low = ((target >> log2(groups * hz)) << log2(hz)) + (target & (hz - 1))
        onehot = low_onehot(jnp.where(target < 0, -1, low), ids)
        group = ((target >> log2(hz)) & (groups - 1)).astype(F32).astype(BF16)
        here = group_ids == group
        row = p * (TOGETHER * FIELDS * tiles)
        plain = TOGETHER - 2 if last else TOGETHER
        pieces = [i * FIELDS * tiles + t for i in range(plain) for t in range(tiles)]
        pieces = [value_ref[pl.ds(row + i, FIELDS, stride=tiles), :] for i in pieces]
        if last:
            at_end = pl.multiple_of(row + plain * FIELDS * tiles, 8)
            block = value_ref[pl.ds(at_end, 2 * FIELDS * tiles), :]
            for first in [i * FIELDS * tiles + t for i in range(2) for t in range(tiles)]:
                lines = [first + f * tiles for f in range(FIELDS)]
                pieces.append(jnp.concatenate([block[r : r + 1] for r in lines], axis=0))
        value = jnp.concatenate(pieces, axis=1)
        parts = []
        for half in halves(value):
            for f in range(FIELDS):
                parts.append(jnp.where(here, half[f : f + 1], jnp.zeros((), BF16)))
        spread = jnp.concatenate(parts, axis=0)
        return lax.dot_general(spread, onehot, NT, preferred_element_type=F32)

    @pl.loop(0, owners // TOGETHER // 2)
    def _(n):
        total[...] += step(n * 2, False) + step(n * 2 + 1, True)

    even_ref[FIELDS * hx] = jnp.zeros((ITERS, hz), F32)
    scale = lax.rsqrt(mass_ref[...])
    half_x = hx // 2
    odd = lax.axis_index("tgt") % 2 == 1
    for f in range(FIELDS):
        s = total[f * groups : (f + 1) * groups] + total[(FIELDS + f) * groups : (FIELDS + f + 1) * groups]
        for b in range(2):
            for x in range(half_x):
                at = b * half_x + x
                v = s[x * hy : (x + 1) * hy, b * hz : (b + 1) * hz] * scale[at]
                v_ref[f, at] = v
                first, last = v[:ITERS], v[hy - ITERS :]
                even_ref[f * hx + at] = jnp.where(odd, first, last)
                odd_ref[f * hx + at] = jnp.where(odd, last, first)


def scatter_call(values, target, mass):
    hx, hy, hz = mass.shape
    groups = hx * hy * hz // WIDE
    even = jax.ShapeDtypeStruct((FIELDS * hx + 1, ITERS, hz), F32)
    odd = jax.ShapeDtypeStruct((FIELDS * hx, ITERS, hz), F32)
    return pl.pallas_call(
        scatter_kernel,
        out_shape=(jax.ShapeDtypeStruct((FIELDS, hx, hy, hz), F32), even, odd),
        in_specs=[pl.BlockSpec(memory_space=pltpu.VMEM)] * 3,
        out_specs=(pl.BlockSpec(memory_space=pltpu.VMEM),) * 3,
        scratch_shapes=[pltpu.VMEM((2 * FIELDS * groups, WIDE), F32)],
        compiler_params=pltpu.CompilerParams(vmem_limit_bytes=40 << 20),
    )(values, target, mass)


def lookup_rows(table, index, ids, group_ids, groups, at_parts):
    group, low = at_parts(index)
    got = jnp.dot(table, low_onehot(low, ids), preferred_element_type=F32)
    here = group_ids == group
    rows = 3 * groups
    out = []
    for m in range(3):
        part = got[m * groups : (m + 1) * groups] + got[rows + m * groups : rows + (m + 1) * groups]
        out.append(jnp.sum(jnp.where(here, part, 0.0), axis=0, keepdims=True))
    return out


def pick_rows(tables, row, lane):
    row = jnp.broadcast_to(row, (8, 128))
    lane = jnp.broadcast_to(lane, (8, 128))
    tile = row >> 3
    here = row_ids(8, 128) == (row & 7)
    out = []
    for table in tables:
        got = jnp.zeros((8, 128), F32)
        for v in range(table.shape[0] // 8):
            piece = jnp.take_along_axis(table[v * 8 : (v + 1) * 8], lane, axis=1, mode="promise_in_bounds")
            got = jnp.where(tile == v, piece, got)
        out.append(jnp.sum(jnp.where(here, got, 0.0), axis=0, keepdims=True))
    return out


def either_way(i, index, table, ids, group_ids, groups, at_parts, tables, row_and_lane):
    halves_of = [slice(c * 128, (c + 1) * 128) for c in range(2)]
    if i % 8 in (2, 5, 7):
        got = [pick_rows(tables, *row_and_lane(index[:, c])) for c in halves_of]
        return [got[c][m] for m in range(3) for c in range(2)]
    got = lookup_rows(table, index, ids, group_ids, groups, at_parts)
    return [line[:, c] for line in got for c in halves_of]


def cell_moduli(vals):
    phi = vals[0]
    mean = (vals[1] + vals[2] + vals[3]) / 3.0
    q2 = 1.5 * (
        (vals[1] - mean) ** 2
        + (vals[2] - mean) ** 2
        + (vals[3] - mean) ** 2
        + 2.0 * (vals[4] ** 2 + vals[5] ** 2 + vals[6] ** 2)
    )
    bulk = 1.6 * jnp.exp(-3.0 * phi) * (1.0 + 0.25 * jnp.tanh(mean))
    shear = 0.9 * jnp.exp(-2.0 * phi) / (1.0 + q2 / 0.5)
    soften = shear * q2 / (0.5 + q2)
    return [bulk, shear, soften]


def corners(sides):
    line = row_ids(2 * ITERS, sides[0].shape[1])
    near = pltpu.roll(sides[1], 2, 0)
    far = jnp.where(line == 4, pltpu.roll(sides[2], 4, 0), pltpu.roll(sides[2], 6, 0))
    return sides[0], jnp.where(line < 4, near, far)


def sides_kernel(even_ref, odd_ref, sides_ref, to_even_ref, to_odd_ref):
    hx = sides_ref.shape[1]
    b_odd = lax.axis_index("tgt") % 2 == 1
    a_odd = lax.axis_index("src") % 2 == 1
    for f in range(FIELDS):
        sides = []
        for x in range(hx):
            even_side, odd_side = even_ref[f * hx + x], odd_ref[f * hx + x]
            right = jnp.where(b_odd, odd_side, even_side)
            left = jnp.where(b_odd, even_side, odd_side)
            sides.append(jnp.concatenate([right, left], axis=0))
            sides_ref[f, x] = sides[x]
        to_left, to_right = corners(sides), corners(sides[::-1])
        to_even_ref[f, :8] = jnp.where(a_odd, to_left[0], to_right[0])
        to_even_ref[f, 8:14] = jnp.where(a_odd, to_left[1], to_right[1])[:6]
        to_odd_ref[f, :8] = jnp.where(a_odd, to_right[0], to_left[0])
        to_odd_ref[f, 8:] = jnp.where(a_odd, to_right[1], to_left[1])


def sides_call(even, odd, hx):
    hz = even.shape[2]
    return pl.pallas_call(
        sides_kernel,
        out_shape=(
            jax.ShapeDtypeStruct((FIELDS, hx, 2 * ITERS, hz), F32),
            jax.ShapeDtypeStruct((FIELDS, 4 * ITERS - 2, hz), F32),
            jax.ShapeDtypeStruct((FIELDS, 4 * ITERS, hz), F32),
        ),
        in_specs=[pl.BlockSpec(memory_space=pltpu.VMEM)] * 2,
        out_specs=(pl.BlockSpec(memory_space=pltpu.VMEM),) * 3,
        compiler_params=pltpu.CompilerParams(vmem_limit_bytes=4 << 20),
        cost_estimate=pl.CostEstimate(flops=40 * 10**9, bytes_accessed=40 * 10**6, transcendentals=0),
    )(even, odd)


def solve_kernel(
    mesh_shape, v_ref, sides_ref, even_ref, odd_ref, even_corners_ref, odd_corners_ref, mass_ref, order_ref,
    projected_hbm, out_ref, projected_ref, sem,
):
    n_src, n_tgt = mesh_shape
    hx, hy, hz = mass_ref.shape
    k = ITERS
    rows = hy + 2 * k
    a, b = lax.axis_index("src"), lax.axis_index("tgt")

    def exists(flag):
        return jnp.where(flag, 1.0, 0.0).astype(F32)

    row = row_ids(rows, hz)
    lane = lax.broadcasted_iota(jnp.int32, (rows, hz), 1)
    inside = jnp.where(row < hy, 1.0, jnp.where(row < hy + k, exists(b < n_tgt - 1), exists(b > 0)))
    inside_left = inside * exists(a > 0)
    inside_right = inside * exists(a < n_src - 1)
    not_first = jnp.where(lane == 0, 0.0, 1.0)
    not_last = jnp.where(lane == hz - 1, 0.0, 1.0)
    scale = lax.rsqrt(mass_ref[...])

    line = row_ids(2 * k, hz)

    def slabs(own, first, packed, from_left):
        second = pltpu.roll(packed, 6, 0)
        third = jnp.where(line < 4, pltpu.roll(packed, 4, 0), pltpu.roll(packed, 2, 0))
        sides = [first, second, third] + [jnp.zeros((2 * k, hz), F32)] * (hx - 3)
        if from_left:
            sides = sides[::-1]
        return [jnp.concatenate([own[x], side], axis=0) for x, side in enumerate(sides)]

    a_odd = a % 2 == 1

    for f in range(FIELDS):
        packed = jnp.concatenate([even_corners_ref[f, 2 * k :], jnp.zeros((2, hz), F32)], axis=0)
        even = (even_ref[f], even_corners_ref[f, : 2 * k], packed)
        odd = (odd_ref[f], odd_corners_ref[f, : 2 * k], odd_corners_ref[f, 2 * k :])
        left = slabs(*[jnp.where(a_odd, p, q) for p, q in zip(even, odd)], True)
        right = slabs(*[jnp.where(a_odd, q, p) for p, q in zip(even, odd)], False)
        own = [jnp.concatenate([v_ref[f, x], sides_ref[f, x]], axis=0) for x in range(hx)]
        base = left + own + right
        u = [COEFS[k] * e for e in base]
        for sweep in range(1, k + 1):
            new = list(u)
            for x in range(sweep, hx + 2 * k - sweep):
                far = max(k - x, x - (k + hx - 1), 0)
                n = rows if sweep + far < k else hy
                w = u[x]
                near = u[x - 1][:n] + u[x + 1][:n]
                near = near + pltpu.roll(w, 1, 0)[:n] + pltpu.roll(w, rows - 1, 0)[:n]
                w = w[:n]
                near = near + pltpu.roll(w, 1, 1) * not_first[:n] + pltpu.roll(w, hz - 1, 1) * not_last[:n]
                if x < k:
                    near = near * inside_left[:n]
                elif x >= k + hx:
                    near = near * inside_right[:n]
                elif n > hy:
                    near = near * inside
                new[x] = COEFS[k - sweep] * base[x][:n] + near
            u = new
        for x in range(hx):
            projected_ref[f, x] = u[k + x][:hy] * scale[x]

    leave = pltpu.make_async_copy(projected_ref, projected_hbm, sem)
    leave.start()
    groups = hx * hy * hz // WIDE
    payload = cell_moduli([projected_ref[f].reshape(hx * hy, hz) for f in range(FIELDS)])
    table = jnp.concatenate([jnp.concatenate([m[:groups], m[groups:]], axis=1) for m in payload], axis=0)
    table = jnp.concatenate(halves(table), axis=0)
    ids = row_ids(WIDE, WIDE).astype(F32).astype(BF16)
    group_ids = row_ids(groups, WIDE)

    def at_parts(index):
        return (index >> log2(hz)) & (groups - 1), ((index >> log2(groups * hz)) << log2(hz)) + (index & (hz - 1))

    for q in range(0, groups, 4):
        lines = []
        for i in range(q, q + 4):
            index = order_ref[:, i * WIDE : (i + 1) * WIDE]
            got = lookup_rows(table, index, ids, group_ids, groups, at_parts)
            lines += [line[:, c * 128 : (c + 1) * 128] for line in got for c in range(2)]
        out_ref[q * 6 : q * 6 + 24, :] = jnp.concatenate(lines, axis=0)
    leave.wait()


def solve_call(mesh_shape, *args):
    mass, order = args[-2:]
    hx, hy, hz = mass.shape

    def kernel(*refs):
        solve_kernel(mesh_shape, *refs)

    return pl.pallas_call(
        kernel,
        out_shape=(
            jax.ShapeDtypeStruct((FIELDS, hx, hy, hz), F32),
            jax.ShapeDtypeStruct((order.shape[1] // WIDE * 6, 128), F32),
        ),
        in_specs=[pl.BlockSpec(memory_space=pltpu.VMEM)] * 8,
        out_specs=(pl.BlockSpec(memory_space=pltpu.HBM), pl.BlockSpec(memory_space=pltpu.VMEM)),
        scratch_shapes=[pltpu.VMEM((FIELDS, hx, hy, hz), F32), pltpu.SemaphoreType.DMA],
        compiler_params=pltpu.CompilerParams(vmem_limit_bytes=40 << 20),
    )(*args)


def place_kernel(arrived_ref, order_ref, out_hbm, out_ref, sems):
    groups = arrived_ref.shape[0] // 6
    parts = [[arrived_ref[pl.ds(2 * m + c, groups, stride=6), :] for c in range(2)] for m in range(3)]
    table = jnp.concatenate([jnp.concatenate(part, axis=1) for part in parts], axis=0)
    table = jnp.concatenate(halves(table), axis=0)
    tables = [jnp.concatenate(part, axis=0) for part in parts]
    ids = row_ids(WIDE, WIDE).astype(F32).astype(BF16)
    group_ids = row_ids(groups, WIDE)

    def at_parts(index):
        return index >> log2(WIDE), index & (WIDE - 1)

    def row_and_lane(index):
        return ((index >> 7) & 1) * groups + (index >> log2(WIDE)), index & 127

    copies = []
    for n in range(PIECES):
        for q in range(n * groups // PIECES, (n + 1) * groups // PIECES):
            index = order_ref[:, q * WIDE : (q + 1) * WIDE]
            lines = either_way(q, index, table, ids, group_ids, groups, at_parts, tables, row_and_lane)
            for c in range(2):
                out_ref[:, q * WIDE + c * 128 : q * WIDE + (c + 1) * 128] = jnp.concatenate(lines[c::2], axis=0)
        piece = pl.ds(n * groups // PIECES * WIDE, groups // PIECES * WIDE)
        copies.append(pltpu.make_async_copy(out_ref.at[:, piece], out_hbm.at[:, piece], sems.at[n]))
        copies[n].start()
    for copy in copies:
        copy.wait()


def place_call(arrived, order):
    return pl.pallas_call(
        place_kernel,
        out_shape=jax.ShapeDtypeStruct((3, order.shape[1]), F32),
        in_specs=[pl.BlockSpec(memory_space=pltpu.VMEM)] * 2,
        out_specs=pl.BlockSpec(memory_space=pltpu.HBM),
        scratch_shapes=[pltpu.VMEM((3, order.shape[1]), F32), pltpu.SemaphoreType.DMA((PIECES,))],
        compiler_params=pltpu.CompilerParams(vmem_limit_bytes=40 << 20),
    )(arrived, order)


def swap(x, axis, start):
    pairs = [(i, i + 1) for i in range(start, lax.axis_size(axis) - 1, 2)]
    return lax.ppermute(x, axis, pairs + [(j, i) for i, j in pairs])


def on_device(source_fields, slot_source, slot_weight, slot_target, cell_mass, send_order, place_order):
    n_src, n_tgt = lax.axis_size("src"), lax.axis_size("tgt")
    both = ("src", "tgt")
    owners = n_src * n_tgt
    cells = cell_mass.size
    quota = cells // owners

    values = gather_call(source_fields, slot_source.reshape(1, -1), slot_weight.reshape(1, -1))
    values = values.reshape(owners, FIELDS, SPAN // 128, 128)
    values = lax.all_to_all(values, both, split_axis=0, concat_axis=0, tiled=True).reshape(-1, 128)
    v, even, odd = scatter_call(values, slot_target.reshape(1, -1), cell_mass)
    even_block, odd_block = swap(v, "src", 0), swap(v, "src", 1)
    even, odd = swap(even, "tgt", 0), swap(odd, "tgt", 1)
    sides, even, odd = sides_call(even, odd, cell_mass.shape[0])
    even, odd = swap(even, "src", 0), swap(odd, "src", 1)
    projected, outgoing = solve_call(
        (n_src, n_tgt), v, sides, even_block, odd_block, even, odd, cell_mass, send_order
    )

    if quota == WIDE:
        outgoing = outgoing.reshape(owners, 3, 2, 128)
        incoming = lax.all_to_all(outgoing, both, split_axis=0, concat_axis=0, tiled=True)
    else:
        groups = cells // WIDE
        flat = outgoing.reshape(groups, 3, WIDE).transpose(1, 0, 2).reshape(3, owners, quota)
        flat = lax.all_to_all(flat, both, split_axis=1, concat_axis=1, tiled=True)
        incoming = flat.reshape(3, groups, WIDE).transpose(1, 0, 2)
    incoming = incoming.reshape(-1, 128)
    return projected, place_call(incoming, place_order)


def solution(mesh):
    split = P(("src", "tgt"))
    rows = P(("src", "tgt"), None)
    return jax.shard_map(
        on_device,
        mesh=mesh,
        in_specs=(P(None, ("src", "tgt")), split, split, split, P("src", "tgt", None), rows, rows),
        out_specs=(P(None, "src", "tgt", None), P(None, ("src", "tgt"))),
        check_vma=False,
    )
```
